128 devices in a mesh: dp: 4 (over y), seq: 16 (over z, x_lo, core), wshard: 2 (over x_hi).
Axes of the slice: x: 4 (x_hi: 2, x_lo: 2; x = x_hi * 2 + x_lo), y: 4, z: 4, core: 2. Of those that a mesh axis runs over, the one named last changes fastest.
Arguments:
- tokens: bfloat16 [8, 4096, 1024], P('dp', ('seq', 'wshard')), may hold values from -6 to 6
- segments: int32 [8, 4096], P('dp', ('seq', 'wshard')), may hold values from 0 to 20, as said below
- valid_flags: int32 [8, 4096], P('dp', ('seq', 'wshard')), may hold values from 0 to 1, as said below
- teacher: bfloat16 [8, 4096, 1024], P('dp', ('seq', 'wshard')), may hold values from -6 to 6
- w_qkv: bfloat16 [1024, 3072], P(('dp', 'wshard')), may hold values from -0.1875 to 0.1875
- b_query: bfloat16 [1024], P(('dp', 'wshard')), may hold values from -3 to 3
- b_value: bfloat16 [1024], P(('dp', 'wshard')), may hold values from -3 to 3
- w_out: bfloat16 [1024, 1024], P(('dp', 'wshard')), may hold values from -1.5 to 1.5
- b_out: bfloat16 [1024], P(('dp', 'wshard')), may hold values from -3 to 3
- ln1_gain: bfloat16 [1024], P(('dp', 'wshard')), may hold values from 0.099609375 to 1.8984375
- ln1_bias: bfloat16 [1024], P(('dp', 'wshard')), may hold values from -3 to 3
- w_up: bfloat16 [1024, 4096], P(('dp', 'wshard')), may hold values from -0.1875 to 0.1875
- b_up: bfloat16 [4096], P(('dp', 'wshard')), may hold values from -3 to 3
- w_down: bfloat16 [4096, 1024], P(('dp', 'wshard')), may hold values from -0.09375 to 0.09375
- b_down: bfloat16 [1024], P(('dp', 'wshard')), may hold values from -3 to 3
- ln2_gain: bfloat16 [1024], P(('dp', 'wshard')), may hold values from 0.099609375 to 1.8984375
- ln2_bias: bfloat16 [1024], P(('dp', 'wshard')), may hold values from -3 to 3
Outputs:
- states: bfloat16 [8, 4096, 1024], P('dp', ('seq', 'wshard'))
- mean_loss: float32 [], replicated
- grad_tokens: float32 [8, 4096, 1024], P('dp', ('seq', 'wshard'))
- grad_w_qkv: float32 [1024, 3072], P(('dp', 'wshard'))
- grad_b_query: float32 [1024], P(('dp', 'wshard'))
- grad_b_value: float32 [1024], P(('dp', 'wshard'))
- grad_w_out: float32 [1024, 1024], P(('dp', 'wshard'))
- grad_b_out: float32 [1024], P(('dp', 'wshard'))
- grad_ln1_gain: float32 [1024], P(('dp', 'wshard'))
- grad_ln1_bias: float32 [1024], P(('dp', 'wshard'))
- grad_w_up: float32 [1024, 4096], P(('dp', 'wshard'))
- grad_b_up: float32 [4096], P(('dp', 'wshard'))
- grad_w_down: float32 [4096, 1024], P(('dp', 'wshard'))
- grad_b_down: float32 [1024], P(('dp', 'wshard'))
- grad_ln2_gain: float32 [1024], P(('dp', 'wshard'))
- grad_ln2_bias: float32 [1024], P(('dp', 'wshard'))
The draws below stay inside these ranges and needn't reach their ends.
Inputs may be any that keep to these rules, and one draw needn't show every extreme that they name: `segments`: segment numbers start at 0 in each sequence and never fall along it; a document has 204 to 2048 tokens except the last one of a sequence, which may be cut. In every run of 2 sequences held by one index of dp, one sequence is a single document. In some sequence every document but the last has exactly 204 tokens. `valid_flags`: the first token of every sequence is valid.
All inputs are finite; a program needn't handle non-finite values.
Results may differ from the reference program's by a relative error of at most 0.017.
Values may be sent and summed in bfloat16 or wider, within the bound.
A program may use at most 128 MiB of HBM per device.

```python
import math
import jax
import jax.numpy as jnp
from jax import lax

D = 1024
H = 16
HD = 64
FF = 4096
LENGTH = 4096
SEQS = 2
SEQUENCES = 8


def draw_segments(key, part):
    key = jax.random.fold_in(key, 11)
    pick_key, length_key = jax.random.split(key)
    doc_lengths = jax.random.randint(length_key, (SEQUENCES, 24), LENGTH // 20, LENGTH // 2 + 1)
    doc_ends = jnp.cumsum(doc_lengths, axis=1)
    position = jnp.arange(LENGTH, dtype=jnp.int32)
    packed = jnp.sum((doc_ends[:, None, :] <= position[None, :, None]).astype(jnp.int32), axis=2)
    whole_pick = jax.random.randint(pick_key, (SEQUENCES // SEQS, 1), 0, SEQS)
    whole_seq = (jnp.arange(SEQS, dtype=jnp.int32)[None, :] == whole_pick).reshape(SEQUENCES)
    short_index = (whole_pick[0, 0] + 1) % SEQS
    short_seq = jnp.arange(SEQUENCES, dtype=jnp.int32) == short_index
    shortest = position // (LENGTH // 20)
    packed = jnp.where(short_seq[:, None], shortest[None, :], packed)
    return jnp.where(whole_seq[:, None], 0, packed).astype(jnp.int32)


def draw_valid_flags(key, part):
    key = jax.random.fold_in(key, 23)
    tickets = jax.random.randint(key, (SEQUENCES, LENGTH), 0, 4 * LENGTH)
    position = jnp.arange(LENGTH, dtype=jnp.int32)[None, :]
    marked = (tickets < LENGTH + 2 * position) | (position == 0)
    return marked.astype(jnp.int32)


def block_levels(own_key, extent, cuts, smallest, high):
    factor_of = 1.0
    for axis_at, blocks in cuts:
        steps = jax.random.uniform(jax.random.fold_in(jax.random.fold_in(own_key, 6), axis_at), (blocks,), jnp.float32, smallest / len(cuts), high / len(cuts))
        factor_of = factor_of * jnp.repeat(jnp.exp(steps), extent[axis_at] // blocks).reshape((-1,) + (1,) * (len(extent) - 1 - axis_at))
    return factor_of


def normal_values(own_key, dims, spread, limit, pieces=(), kind=jnp.bfloat16):
    array = spread * jax.random.normal(own_key, dims, jnp.float32)
    if pieces:
        array = array * block_levels(own_key, dims, pieces, -0.22, 0.18)
    return jnp.clip(array, -limit, limit).astype(kind)


def setup_inputs(seed: int = 0) -> dict:
    splits = jax.random.split(jax.random.key(seed), 18)
    return {
        "tokens": normal_values(splits[0], (SEQUENCES, LENGTH, D), 1.0, 6.0, ((0, 4), (1, 32))),
        "segments": draw_segments(jax.random.fold_in(splits[17], 71), 0),
        "valid_flags": draw_valid_flags(jax.random.fold_in(splits[17], 71), 0),
        "teacher": normal_values(splits[3], (SEQUENCES, LENGTH, D), 1.0, 6.0, ((0, 4), (1, 32))),
        "w_qkv": normal_values(splits[4], (D, 3 * D), D ** -0.5, 0.1875, ((0, 8),)),
        "b_query": normal_values(splits[5], (D,), 0.5, 3.0, ((0, 8),)),
        "b_value": normal_values(splits[6], (D,), 0.5, 3.0, ((0, 8),)),
        "w_out": normal_values(splits[7], (D, D), (D // 64) ** -0.5, 1.5, ((0, 8),)),
        "b_out": normal_values(splits[8], (D,), 0.5, 3.0, ((0, 8),)),
        "ln1_gain": jnp.clip(1.0 + 0.18 * jax.random.normal(splits[9], (D,), jnp.float32), 0.099609375, 1.8984375).astype(jnp.bfloat16),
        "ln1_bias": normal_values(splits[10], (D,), 0.5, 3.0, ((0, 8),)),
        "w_up": normal_values(splits[11], (D, FF), D ** -0.5, 0.1875, ((0, 8),)),
        "b_up": normal_values(splits[12], (FF,), 0.5, 3.0, ((0, 8),)),
        "w_down": normal_values(splits[13], (FF, D), FF ** -0.5, 0.09375, ((0, 8),)),
        "b_down": normal_values(splits[14], (D,), 0.5, 3.0, ((0, 8),)),
        "ln2_gain": jnp.clip(1.0 + 0.18 * jax.random.normal(splits[15], (D,), jnp.float32), 0.099609375, 1.8984375).astype(jnp.bfloat16),
        "ln2_bias": normal_values(splits[16], (D,), 0.5, 3.0, ((0, 8),)),
    }


EPS = 1e-06
HIGHEST = lax.Precision.HIGHEST

@jax.custom_vjp
def low(v):
    return lax.optimization_barrier(v.astype(jnp.bfloat16)).astype(jnp.float32)

@jax.custom_vjp
def low_back(v):
    return v

def low_keep(v):
    return (low(v), None)

def low_pass(kept, grad):
    return (grad,)

def back_keep(v):
    return (v, None)

def back_low(kept, grad):
    return (low(grad),)
low.defvjp(low_keep, low_pass)
low_back.defvjp(back_keep, back_low)

def product(first_op, second_op):
    return jnp.dot(first_op, second_op, precision=HIGHEST)

def layer_norm(values, norm_gain, norm_offset):
    centre = values - lax.optimization_barrier(jnp.mean(values, axis=-1, keepdims=True))
    normed = centre * lax.rsqrt(lax.optimization_barrier(jnp.mean(centre * centre, axis=-1, keepdims=True)) + EPS)
    return normed * norm_gain + norm_offset

def attention(queries, keys_all, values_all, segment_ids):
    block_rows = math.gcd(LENGTH, 512)
    scale = 1.0 / math.sqrt(HD)
    keys_heads = keys_all.reshape(LENGTH, H, HD)
    values_heads = values_all.reshape(LENGTH, H, HD)

    def one_block(arrays):
        query_block, segment_block = arrays
        raw_scores = low_back(jnp.einsum('qhd,khd->hqk', query_block, keys_heads, precision=HIGHEST))
        matching = (segment_block[:, None] == segment_ids[None, :])[None]
        logits = jnp.where(matching, raw_scores * scale, -1000000000.0)
        probs = low(jax.nn.softmax(logits, axis=-1))
        return jnp.einsum('hqk,khd->qhd', probs, values_heads, precision=HIGHEST)
    blocks = lax.map(jax.checkpoint(one_block), (queries.reshape(LENGTH // block_rows, block_rows, H, HD), segment_ids.reshape(LENGTH // block_rows, block_rows)))
    return blocks.reshape(LENGTH, D)

def sequence(params, inputs, segment_ids, teacher_rows, flag_rows):
    w_qkv, b_query, b_value, w_out, b_out, gain_one, offset_one, w_up, b_up, w_down, b_down, gain_two, offset_two = params
    projected = product(low(inputs), w_qkv)
    queries = low(low_back(projected[:, :D] + b_query))
    keys_all = low(low_back(projected[:, D:2 * D]))
    values_all = low(low_back(projected[:, 2 * D:] + b_value))
    context = low(low_back(attention(queries, keys_all, values_all, segment_ids)))
    attended = low_back(product(context, w_out) + b_out)
    hidden = layer_norm(inputs + attended, gain_one, offset_one)
    up_proj = low_back(product(low(hidden), w_up) + b_up)
    activated = low(jax.nn.gelu(up_proj, approximate=True))
    branch = low_back(product(activated, w_down) + b_down)
    states = layer_norm(hidden + branch, gain_two, offset_two)
    differ = states - teacher_rows
    return (jnp.sum(flag_rows[:, None] * differ * differ), states)

def reference(tokens, segments, valid_flags, teacher, w_qkv, b_query, b_value, w_out, b_out, ln1_gain, ln1_bias, w_up, b_up, w_down, b_down, ln2_gain, ln2_bias):
    params = (w_qkv.astype(jnp.float32), b_query.astype(jnp.float32), b_value.astype(jnp.float32), w_out.astype(jnp.float32), b_out.astype(jnp.float32), ln1_gain.astype(jnp.float32), ln1_bias.astype(jnp.float32), w_up.astype(jnp.float32), b_up.astype(jnp.float32), w_down.astype(jnp.float32), b_down.astype(jnp.float32), ln2_gain.astype(jnp.float32), ln2_bias.astype(jnp.float32))
    inputs_all = tokens.astype(jnp.float32)
    teacher_all = teacher.astype(jnp.float32)
    flags_all = valid_flags.astype(jnp.float32)
    valid_count = jnp.sum(flags_all)
    factor = SEQUENCES * LENGTH / (2.0 * valid_count)

    def forward(weights, inputs_seq):

        def one_sequence(error_sum, arrays):
            seq_inputs, seq_segments, seq_teacher, seq_flags = arrays
            seq_error, seq_states = sequence(weights, seq_inputs, seq_segments, seq_teacher, seq_flags)
            return (error_sum + seq_error, seq_states)
        error_sum, states_all = lax.scan(one_sequence, jnp.zeros((), jnp.float32), (inputs_seq, segments, teacher_all, flags_all))
        return (error_sum * factor, (error_sum, states_all))
    scaled, pullback, (error_sum, states_all) = jax.vjp(forward, params, inputs_all, has_aux=True)
    weight_grads, grad_inputs = pullback(jnp.ones((), jnp.float32))
    mean_loss = error_sum / (D * valid_count)
    return (states_all.astype(jnp.bfloat16), mean_loss, grad_inputs, weight_grads[0], weight_grads[1], weight_grads[2], weight_grads[3], weight_grads[4], weight_grads[5], weight_grads[6], weight_grads[7], weight_grads[8], weight_grads[9], weight_grads[10], weight_grads[11], weight_grads[12])
```

```python
import functools

import jax
import jax.numpy as jnp
from jax import lax
from jax.experimental import pallas as pl
from jax.experimental.pallas import tpu as pltpu
from jax.sharding import PartitionSpec as P

D = 1024
H = 16
HD = 64
FF = 4096
L = 4096
EPS = 1e-06
F32 = jnp.float32
BF = jnp.bfloat16
MASKED = 1000000000.0
VMEM_CAP = 60 * 1024 * 1024
MESH = pl.DeviceIdType.MESH
ANY = pl.BlockSpec(memory_space=pl.ANY)
TB = 128
NB = L // TB


def dot(first, second, dims=((1,), (0,))):
    return lax.dot_general(first, second, (dims, ((), ())), preferred_element_type=F32)


def project_kernel(
    x_ref, heads_ref, smalls_ref, meta_ref, qat_ref, ka_ref, vat_ref, va_ref, kt_ref, q_ref, w_ref, wt_ref, b_ref
):
    _, _, _, core = place()

    @pl.when(pl.program_id(0) == 0)
    def _():
        pair = lax.axis_index("seq") // 2
        first = core == 0
        both = heads_ref[...]
        own = [jnp.where(first, both[:, 128 * p : 128 * p + HD], both[:, 128 * p + HD : 128 * (p + 1)]) for p in range(3)]
        w_ref[...] = jnp.concatenate(own, axis=1)
        wt_ref[...] = w_ref[...].astype(F32).T.astype(BF)
        mine = smalls_ref[pair]
        bias = [jnp.where(first, mine[k : k + 1, :HD], mine[k : k + 1, HD:]) for k in range(2)]
        b_ref[...] = jnp.broadcast_to(jnp.concatenate([bias[0], jnp.zeros((1, HD), F32), bias[1]], axis=1), (8, 3 * HD))

    x = x_ref[...]
    rows = x.shape[0]
    side = dot(x, w_ref[...]) + b_ref[:1, :]
    turned = dot(wt_ref[...], x, ((1,), (1,))) + b_ref[...].T[:, :1]
    q8 = (side[:, :HD].astype(BF).astype(F32) * 0.125).astype(BF)
    q8t = (turned[:HD].astype(BF).astype(F32) * 0.125).astype(BF)
    k = side[:, HD : 2 * HD].astype(BF)
    v = side[:, 2 * HD :].astype(BF)
    segment = jnp.concatenate([meta_ref[i, 0:1, :] for i in range(rows // TB)], axis=1)
    hot = jnp.where(lax.broadcasted_iota(jnp.int32, (32, rows), 0) == segment, 1.0, 0.0)
    apart = (hot.T - 1.0) * MASKED
    lane = lax.broadcasted_iota(jnp.int32, (rows, 32), 1)
    ones3 = jnp.where(lane < 3, 1.0, 0.0)
    zero_side = jnp.zeros((rows, 32), F32)
    q_ref[...] = q8
    qat_ref[...] = jnp.concatenate([q8t, hot.astype(BF), jnp.zeros((32, rows), BF)], axis=0)
    ka_ref[...] = jnp.concatenate([k, apart.astype(BF), ones3.astype(BF)], axis=1)
    va_ref[...] = jnp.concatenate([v, ones3.astype(BF), zero_side.astype(BF)], axis=1)
    kt_ref[...] = turned[HD : 2 * HD].astype(BF)
    ones_row = jnp.where(lax.broadcasted_iota(jnp.int32, (16, rows), 0) == 0, 1.0, 0.0)
    vat_ref[...] = jnp.concatenate([turned[2 * HD :].astype(BF), ones_row.astype(BF)], axis=0)


def project(x, heads, smalls, meta, rows=1024):
    return pl.pallas_call(
        project_kernel,
        grid=(L // rows,),
        in_specs=[
            pl.BlockSpec((rows, D), lambda i: (i, 0)),
            pl.BlockSpec((D, 384), lambda i: (0, 0)),
            pl.BlockSpec((8, 16, 128), lambda i: (0, 0, 0)),
            pl.BlockSpec((rows // TB, 8, TB), lambda i: (i, 0, 0)),
        ],
        out_specs=[
            pl.BlockSpec((128, rows), lambda i: (0, i)),
            pl.BlockSpec((rows, 128), lambda i: (i, 0)),
            pl.BlockSpec((80, rows), lambda i: (0, i)),
            pl.BlockSpec((rows, 128), lambda i: (i, 0)),
            pl.BlockSpec((HD, rows), lambda i: (0, i)),
            pl.BlockSpec((rows, HD), lambda i: (i, 0)),
        ],
        out_shape=[
            jax.ShapeDtypeStruct((128, L), BF),
            jax.ShapeDtypeStruct((L, 128), BF),
            jax.ShapeDtypeStruct((80, L), BF),
            jax.ShapeDtypeStruct((L, 128), BF),
            jax.ShapeDtypeStruct((HD, L), BF),
            jax.ShapeDtypeStruct((L, HD), BF),
        ],
        scratch_shapes=[pltpu.VMEM((D, 3 * HD), BF), pltpu.VMEM((3 * HD, D), BF), pltpu.VMEM((8, 3 * HD), F32)],
        name="project_head",
        compiler_params=pltpu.CompilerParams(vmem_limit_bytes=VMEM_CAP),
    )(x, heads, smalls, meta)


def attend_kernel(key_rows, qat_ref, ka_ref, vat_ref, blocks_ref, wide_ref, lse_ref):
    queries = qat_ref[...]
    width = queries.shape[1]
    peak = jnp.full((1, width), -jnp.inf, F32)
    total = jnp.zeros((80, width), F32)
    for j in range(L // key_rows):
        rows = slice(j * key_rows, (j + 1) * key_rows)
        logits = dot(ka_ref[rows, :], queries)
        new_peak = jnp.maximum(peak, jnp.max(logits, axis=0, keepdims=True))
        expos = jnp.exp(logits - new_peak).astype(BF)
        total = total * jnp.exp(peak - new_peak) + dot(vat_ref[:, rows], expos)
        peak = new_peak
    sums = total[HD : HD + 1]
    context = total[:HD] / sums
    wide_ref[...] = context
    lse_ref[...] = peak + jnp.log(sums)
    low = context.astype(BF)
    for j in range(width // TB):
        blocks_ref[j] = low[:, j * TB : (j + 1) * TB]


def attend(qat, ka, vat, width=1024, key_rows=512):
    return pl.pallas_call(
        functools.partial(attend_kernel, key_rows),
        grid=(L // width,),
        in_specs=[
            pl.BlockSpec((128, width), lambda i: (0, i)),
            pl.BlockSpec((L, 128), lambda i: (0, 0)),
            pl.BlockSpec((80, L), lambda i: (0, 0)),
        ],
        out_specs=[
            pl.BlockSpec((width // TB, HD, TB), lambda i: (i, 0, 0)),
            pl.BlockSpec((HD, width), lambda i: (0, i)),
            pl.BlockSpec((1, width), lambda i: (0, i)),
        ],
        out_shape=[
            jax.ShapeDtypeStruct((NB, HD, TB), BF),
            jax.ShapeDtypeStruct((HD, L), F32),
            jax.ShapeDtypeStruct((1, L), F32),
        ],
        name="attend",
        compiler_params=pltpu.CompilerParams(vmem_limit_bytes=VMEM_CAP),
    )(qat, ka, vat)


def three_pieces(row):
    high = row.astype(BF)
    rest = row - high.astype(F32)
    middle = rest.astype(BF)
    lowest = (rest - middle.astype(F32)).astype(BF)
    return jnp.concatenate([high, middle, lowest], axis=0)


def attend_back_kernel(
    key_rows, qat_ref, ka_ref, va_ref, kt_ref, q_ref, do_ref, wide_ref, lse_ref, dqkv_ref, dk_ref, dv_ref
):
    step = pl.program_id(0)

    @pl.when(step == 0)
    def _():
        dk_ref[...] = jnp.zeros_like(dk_ref)
        dv_ref[...] = jnp.zeros_like(dv_ref)

    width = qat_ref.shape[1]
    grad_t = jnp.concatenate([do_ref[j] for j in range(width // TB)], axis=1)
    delta = jnp.sum(grad_t.astype(F32) * wide_ref[...], axis=0, keepdims=True)
    queries = jnp.concatenate(
        [qat_ref[:96, :], three_pieces(-lse_ref[...]), jnp.zeros((29, width), BF)], axis=0
    )
    grads = jnp.concatenate([grad_t, three_pieces(-delta), jnp.zeros((61, width), BF)], axis=0)
    grad_rows = grad_t.astype(F32).T.astype(BF)
    query_rows = q_ref[...]
    dq = jnp.zeros((HD, width), F32)
    for j in range(L // key_rows):
        rows = slice(j * key_rows, (j + 1) * key_rows)
        probs = jnp.exp(dot(ka_ref[rows, :], queries))
        raw = (probs * dot(va_ref[rows, :], grads)).astype(BF)
        dv_ref[rows, :] += dot(probs.astype(BF), grad_rows)
        dk_ref[rows, :] += dot(raw, query_rows)
        dq = dq + dot(kt_ref[:, rows], raw)
    dq_low = (dq * 0.125).astype(BF)
    for j in range(width // TB):
        dqkv_ref[step * (width // TB) + j, 0:HD, :] = dq_low[:, j * TB : (j + 1) * TB]

    @pl.when(step == pl.num_programs(0) - 1)
    def _():
        for j in range(NB):
            rows = slice(j * TB, (j + 1) * TB)
            dqkv_ref[j, HD : 2 * HD, :] = dk_ref[rows, :].T.astype(BF)
            dqkv_ref[j, 2 * HD :, :] = dv_ref[rows, :].T.astype(BF)


def attend_back(qat, ka, va, kt, q8, do, wide, lse, width=1024, key_rows=512):
    def whole(shape):
        return pl.BlockSpec(shape, lambda i: (0,) * len(shape))

    return pl.pallas_call(
        functools.partial(attend_back_kernel, key_rows),
        grid=(L // width,),
        in_specs=[
            pl.BlockSpec((128, width), lambda i: (0, i)),
            whole((L, 128)),
            whole((L, 128)),
            whole((HD, L)),
            pl.BlockSpec((width, HD), lambda i: (i, 0)),
            pl.BlockSpec((width // TB, HD, TB), lambda i: (i, 0, 0)),
            pl.BlockSpec((HD, width), lambda i: (0, i)),
            pl.BlockSpec((1, width), lambda i: (0, i)),
        ],
        out_specs=whole((NB, 3 * HD, TB)),
        out_shape=jax.ShapeDtypeStruct((NB, 3 * HD, TB), BF),
        scratch_shapes=[pltpu.VMEM((L, HD), F32), pltpu.VMEM((L, HD), F32)],
        name="attend_back",
        compiler_params=pltpu.CompilerParams(vmem_limit_bytes=VMEM_CAP),
    )(qat, ka, va, kt, q8, do, wide, lse)


def place():
    at = lax.axis_index("seq")
    return (lax.axis_index("wshard") * 2 + (at // 2) % 2, lax.axis_index("dp"), at // 4, at % 2)


def device_at(x, y, z, core):
    return (y, (z * 2 + x % 2) * 2 + core, x // 2)


def along(axis, shift):
    x, y, z, core = place()
    if axis == "x":
        return device_at((x + shift) % 4, y, z, core)
    if axis == "y":
        return device_at(x, (y + shift) % 4, z, core)
    return device_at(x, y, (z + shift) % 4, core)


def sibling():
    x, y, z, core = place()
    return device_at(x, y, z, 1 - core)


def greet(partners):
    barrier = pltpu.get_barrier_semaphore()
    for partner in partners:
        pl.semaphore_signal(barrier, inc=1, device_id=partner, device_id_type=MESH)
    pl.semaphore_wait(barrier, len(partners))


def remote(src, dst, send_sem, recv_sem, target):
    return pltpu.make_async_remote_copy(
        src_ref=src, dst_ref=dst, send_sem=send_sem, recv_sem=recv_sem, device_id=target, device_id_type=MESH
    )


ORDERS = ("yzx", "zxy", "xyz")


def ring_partners():
    return [along(axis, shift) for axis in "xyz" for shift in (1, 2, 3)] + [sibling()]


def reduce_scratch():
    return [
        pltpu.VMEM((4, 2, 384, 512), BF),
        pltpu.VMEM((4, 4, 2, 96, 512), BF),
        pltpu.VMEM((4, 4, 192, 512), BF),
        pltpu.VMEM((4, 2, 96, 512), BF),
        pltpu.VMEM((4, 4, 48, 512), BF),
        pltpu.VMEM((4, 192, 512), BF),
        pltpu.VMEM((3, 4, 48, 512), BF),
        pltpu.SemaphoreType.DMA((3, 3, 3)),
        pltpu.SemaphoreType.DMA((3, 3, 3)),
        pltpu.SemaphoreType.DMA((3,)),
        pltpu.SemaphoreType.DMA((3, 8)),
        pltpu.SemaphoreType.DMA((3, 8)),
    ]


def aligned(value, unit):
    return pl.multiple_of(value, unit)


def reduce_pieces(stage, part, refs, at):
    g_ref, a1, b1, c1, a2, b2, c2, last = refs[:8]
    half, low = at // 2, at % 2
    if stage == 0:
        return (
            lambda: g_ref.at[at, :, pl.ds(0, 384), :],
            lambda: g_ref.at[:, :, pl.ds(aligned(384 + at * 96, 96), 96), :],
            lambda: g_ref.at[:, half, pl.ds(aligned(768 + low * 192, 192), 192), :],
        )[part]()
    if stage == 1:
        return (
            lambda: a1.at[0, :, pl.ds(aligned(at * 96, 96), 96), :],
            lambda: b1.at[0, :, half, pl.ds(aligned(low * 48, 48), 48), :],
            lambda: c1.at[0, at],
        )[part]()
    return (
        lambda: a2.at[0, half, pl.ds(aligned(low * 48, 48), 48), :],
        lambda: b2.at[0, at],
        lambda: c2.at[0, pl.ds(aligned(at * 48, 48), 48), :],
    )[part]()


def reduce_landing(stage, part, refs, slot):
    g_ref, a1, b1, c1, a2, b2, c2, last = refs[:8]
    if stage == 0:
        return (a1, b1, c1)[part].at[slot]
    if stage == 1:
        return (a2, b2, c2)[part].at[slot]
    return last.at[part, slot]


def ring_at(axis):
    x, y, z, _ = place()
    return {"x": x, "y": y, "z": z}[axis]


def reduce_copies(stage, refs):
    send, recv = refs[8], refs[9]
    copies = []
    for shift in (1, 2, 3):
        for part in range(3):
            axis = ORDERS[part][stage]
            target_at = (ring_at(axis) + shift) % 4
            copies.append(
                remote(
                    reduce_pieces(stage, part, refs, target_at),
                    reduce_landing(stage, part, refs, shift),
                    send.at[stage, part, shift - 1],
                    recv.at[stage, part, shift - 1],
                    along(axis, shift),
                )
            )
    return copies


def reduce_own(refs):
    return [
        pltpu.make_async_copy(
            reduce_pieces(0, part, refs, ring_at(ORDERS[part][0])), reduce_landing(0, part, refs, 0), refs[10].at[part]
        )
        for part in range(3)
    ]


def reduce_start(refs):
    for copy in reduce_copies(0, refs):
        copy.start()
    for copy in reduce_own(refs):
        copy.start()


def add_four(values):
    total = values[0].astype(F32) + values[1].astype(F32)
    return (total + values[2].astype(F32) + values[3].astype(F32)).astype(BF)


def reduce_step(stage, refs):
    g_ref, a1, b1, c1, a2, b2, c2, last = refs[:8]
    for copy in reduce_copies(stage, refs):
        copy.wait()
    x, y, z, _ = place()
    if stage == 0:
        for copy in reduce_own(refs):
            copy.wait()

        @pl.loop(0, 16)
        def _(i):
            k = aligned((i % 8) * 48, 48)
            a1[0, i // 8, pl.ds(k, 48), :] = add_four([a1[s, i // 8, pl.ds(k, 48), :] for s in range(4)])
            k = aligned((i % 2) * 48, 48)
            b1[0, i // 4, (i // 2) % 2, pl.ds(k, 48), :] = add_four(
                [b1[s, i // 4, (i // 2) % 2, pl.ds(k, 48), :] for s in range(4)]
            )
            k = aligned((i % 4) * 48, 48)
            c1[0, i // 4, pl.ds(k, 48), :] = add_four([c1[s, i // 4, pl.ds(k, 48), :] for s in range(4)])

    elif stage == 1:

        @pl.loop(0, 4)
        def _(i):
            k = aligned((i % 2) * 48, 48)
            own = a1[0, i // 2, pl.ds(aligned(z * 96 + (i % 2) * 48, 48), 48), :]
            a2[0, i // 2, pl.ds(k, 48), :] = add_four([own] + [a2[s, i // 2, pl.ds(k, 48), :] for s in (1, 2, 3)])
            own = b1[0, i, x // 2, pl.ds(aligned((x % 2) * 48, 48), 48), :]
            b2[0, i] = add_four([own] + [b2[s, i] for s in (1, 2, 3)])
            k = aligned(i * 48, 48)
            own = c1[0, y, pl.ds(k, 48), :]
            c2[0, pl.ds(k, 48), :] = add_four([own] + [c2[s, pl.ds(k, 48), :] for s in (1, 2, 3)])

    else:
        own = a2[0, x // 2, pl.ds(aligned((x % 2) * 48, 48), 48), :]
        last[0, 0] = add_four([own] + [last[0, s] for s in (1, 2, 3)])
        last[1, 0] = add_four([b2[0, y]] + [last[1, s] for s in (1, 2, 3)])
        own = c2[0, pl.ds(aligned(z * 48, 48), 48), :]
        last[2, 0] = add_four([own] + [last[2, s] for s in (1, 2, 3)])
    if stage < 2:
        for copy in reduce_copies(stage + 1, refs):
            copy.start()


def shard_rows(o_ref, part, x_low, z, core):
    sub = x_low * 4 + z if part == 2 else z * 2 + x_low
    return o_ref.at[core, pl.ds(aligned(part * 384 + sub * 48, 48), 48), :]


def spread(refs, o_ref):
    last, local = refs[7], refs[10]
    send, recv = refs[11], refs[12]
    x, y, z, core = place()
    low = x % 2
    pair = device_at(x // 2 * 2 + 1 - low, y, z, core)
    first, own, second, third = [], [], [], []
    for part in range(3):
        mine = last.at[part, 0]
        own.append(pltpu.make_async_copy(mine, shard_rows(o_ref, part, low, z, core), local.at[part]))
        first.append(remote(mine, shard_rows(o_ref, part, low, z, core), send.at[part, 0], recv.at[part, 0], pair))
        for shift in (1, 2, 3):
            place_there = shard_rows(o_ref, part, low, z, core)
            second.append(remote(mine, place_there, send.at[part, shift], recv.at[part, shift], along("z", shift)))
            place_there = shard_rows(o_ref, part, 1 - low, z, core)
            third.append(
                remote(place_there, place_there, send.at[part, 3 + shift], recv.at[part, 3 + shift], along("z", shift))
            )
    for copy in own + first + second:
        copy.start()
    for copy in first:
        copy.wait()
    for copy in third:
        copy.start()
    for copy in own + second + third:
        copy.wait()
    rows = o_ref.at[core]
    across = remote(rows, rows, send.at[0, 7], recv.at[0, 7], sibling())
    across.start()
    across.wait()


def swap_partner(shift):
    mine = lax.axis_index("seq") * 2 + lax.axis_index("wshard")
    other = (mine + shift) % NB
    return other, (lax.axis_index("dp"), other // 2, other % 2)


def swap_greet():
    barrier = pltpu.get_barrier_semaphore()

    @pl.loop(1, NB)
    def _(shift):
        pl.semaphore_signal(barrier, inc=1, device_id=swap_partner(shift)[1], device_id_type=MESH)

    pl.semaphore_wait(barrier, NB - 1)


def swap_copies(piece_for, landing_from, sems):
    mine = lax.axis_index("seq") * 2 + lax.axis_index("wshard")
    send, recv, local = sems

    def copy(shift):
        other, device = swap_partner(shift)
        return remote(piece_for(other), landing_from(mine), send.at[shift], recv.at[shift], device)

    own = pltpu.make_async_copy(piece_for(mine), landing_from(mine), local)

    def start():
        @pl.loop(1, NB)
        def _(shift):
            copy(shift).start()

        own.start()

    def wait():
        @pl.loop(1, NB)
        def _(shift):
            copy(shift).wait()

        own.wait()

    return start, wait


def swap_sems():
    return [pltpu.SemaphoreType.DMA((NB,)), pltpu.SemaphoreType.DMA((NB,)), pltpu.SemaphoreType.DMA]


def block_of(ref, b):
    return ref.at[b]


def head_tile(ref, b):
    return ref.at[pl.ds(aligned((b // 2) * HD, HD), HD), pl.ds(aligned((b % 2) * TB, TB), TB)]


def head_tile3(ref, b):
    return ref.at[:, pl.ds(aligned((b // 2) * HD, HD), HD), pl.ds(aligned((b % 2) * TB, TB), TB)]


HALVES = ((128, 2048), (256, 1024))


class Transfers:
    def __init__(self, send, recv):
        self.send, self.recv, self.used = send, recv, 0

    def copy(self, src, dst, target):
        made = remote(src, dst, self.send.at[self.used], self.recv.at[self.used], target)
        self.used += 1
        return made


def start_all(copies):
    for copy in copies:
        copy.start()


def wait_all(copies):
    for copy in copies:
        copy.wait()


def unit_rows(matrix, unit, count=1):
    rows = HALVES[matrix][0] // 4
    return pl.ds(unit * rows, count * rows)


def columns_part(matrix, at, parts):
    width = HALVES[matrix][1] // parts
    return pl.ds(aligned(at * width, 128), width)


def half_rows(core, rows=64):
    return pl.ds(aligned(core * rows, rows), rows)


def shard_greet():
    x, y, z, core = place()
    return [device_at(x, (y + d) % 4, z, core) for d in (1, 2, 3)] + [
        device_at(3 - x, (y + d) % 4, z, core) for d in range(4)
    ]


def greet_all(others):
    barrier = pltpu.get_barrier_semaphore()

    @pl.loop(1, NB)
    def _(shift):
        pl.semaphore_signal(barrier, inc=1, device_id=swap_partner(shift)[1], device_id_type=MESH)

    for other in others:
        pl.semaphore_signal(barrier, inc=1, device_id=other, device_id_type=MESH)
    pl.semaphore_wait(barrier, NB - 1 + len(others))


FRONT_COPIES = 160


def front_kernel(
    tokens, segments, flags, vectors, b_up, w_out, w_up, w_down, w_qkv,
    x_ref, meta_all, heads_all, smalls_all, out_all, up_all, down_all, qkv_all,
    tok_buf, out_buf, up_buf, down_buf, qkv_buf, meta, heads, smalls,
    send, recv, local, meta_send, meta_recv, meta_local,
):
    x, y, z, core = place()
    hi, lo = x // 2, x % 2
    mine, across = y * 2 + hi, y * 2 + 1 - hi
    wrap, pair, other_core = device_at(3 - x, y, z, core), device_at(hi * 2 + 1 - lo, y, z, core), sibling()
    shards, wholes = (up_buf.at[core], down_buf), (up_all, down_all)
    rows_out = half_rows(core)
    loads = [pltpu.make_async_copy(tokens, tok_buf, local.at[0])]
    for j in range(8):
        piece = w_up.at[:, pl.ds(aligned(j * 512 + core * 256, 256), 256)]
        loads.append(pltpu.make_async_copy(piece, up_buf.at[core, :, pl.ds(j * 256, 256)], local.at[1 + j]))
    loads.append(pltpu.make_async_copy(w_out, out_buf, local.at[9]))
    loads.append(pltpu.make_async_copy(w_down.at[half_rows(core, 256)], down_buf, local.at[10]))
    loads.append(pltpu.make_async_copy(w_qkv, qkv_buf, local.at[11]))
    start_all(loads)
    meta[...] = jnp.zeros_like(meta)
    for s in range(2):
        meta[s, 0:1, :] = segments[s : s + 1, :]
        meta[s, 1:2, :] = flags[s : s + 1, :]
    smalls[...] = jnp.zeros_like(smalls)
    smalls[0:8, :] = vectors[...]
    smalls[8:12, :] = b_up[...]
    greet_all(shard_greet())
    loads[0].wait()
    net = Transfers(send, recv)
    first, second = pl.ds(0, 64), pl.ds(64, 64)

    def block(at, low, w, rows=slice(None)):
        return x_ref.at[at, low, core, w, rows]

    swap = net.copy(tok_buf.at[1 - hi], block(z, lo, hi), wrap)
    swap.start()
    own = tok_buf.at[hi]
    own_z = [net.copy(own, block(z, lo, hi), along("z", d)) for d in (1, 3, 2)]
    own_pair = [net.copy(own.at[rows], block(z, lo, hi, rows), pair) for rows in (first, second)]
    start_all([own_pair[0]] + own_z)
    wait_all(loads[1:])
    for p in range(3):
        for k, pair_at in ((0, z * 2 + lo), (1, z * 2 + 1 - lo)):
            heads[k, :, 128 * p : 128 * (p + 1)] = qkv_buf[:, pl.ds(aligned(p * D + pair_at * 128, 128), 128)]
    keep = [
        pltpu.make_async_copy(own, block(z, lo, hi), local.at[0]),
        pltpu.make_async_copy(heads.at[0], heads_all.at[mine], local.at[1]),
        pltpu.make_async_copy(smalls, smalls_all.at[mine], local.at[2]),
        pltpu.make_async_copy(qkv_buf, qkv_all.at[mine], local.at[3]),
    ]
    keep += [pltpu.make_async_copy(shards[m], wholes[m].at[mine], local.at[4 + m]) for m in range(2)]
    keep.append(pltpu.make_async_copy(out_buf, out_all.at[mine], local.at[6]))
    start_all(keep)

    cross_early, cross_late = [], []
    for m in range(2):
        for unit, columns in ((0, columns_part(m, z, 4)), (3, columns_part(m, 1 - lo, 2))):
            rows = unit_rows(m, unit)
            cross_early.append(net.copy(shards[m].at[rows, columns], wholes[m].at[mine, rows, columns], wrap))
        rows = unit_rows(m, 1, 2)
        cross_late.append(net.copy(shards[m].at[rows], wholes[m].at[mine, rows], wrap))
    cross_early.append(net.copy(out_buf.at[rows_out], out_all.at[mine, rows_out], wrap))
    cross_early.append(net.copy(heads.at[1], heads_all.at[mine], wrap))
    cross_early.append(net.copy(smalls, smalls_all.at[mine], wrap))
    start_all(cross_early + cross_late)

    def along_y(shard, source, out_source, heads_source, smalls_source):
        copies = []
        for d in (1, 3, 2):
            there = along("y", d)
            for m in range(2):
                for unit, columns in (
                    (0, columns_part(m, z, 4)),
                    (3, columns_part(m, lo, 2)),
                    (1, slice(None)),
                ):
                    rows = unit_rows(m, unit)
                    copies.append(net.copy(source(m).at[rows, columns], wholes[m].at[shard, rows, columns], there))
            copies.append(net.copy(out_source.at[rows_out], out_all.at[shard, rows_out], there))
            copies.append(net.copy(heads_source, heads_all.at[shard], there))
            copies.append(net.copy(smalls_source, smalls_all.at[shard], there))
        return copies

    meta_start, meta_wait = swap_copies(
        lambda b: meta.at[b % 2], lambda b: meta_all.at[b], (meta_send, meta_recv, meta_local)
    )
    meta_start()
    own_y = along_y(mine, lambda m: shards[m], out_buf, heads.at[0], smalls)
    start_all(own_y)

    swap.wait_recv()
    came = block(z, 1 - lo, 1 - hi)
    came_pair = [
        net.copy(block(z, 1 - lo, 1 - hi, rows), block(z, 1 - lo, 1 - hi, rows), pair) for rows in (first, second)
    ]
    came_z = [net.copy(came, came, along("z", d)) for d in (1, 3, 2)]
    start_all([came_pair[0]] + came_z)
    start_all([own_pair[1], came_pair[1]])

    for copy in cross_early + cross_late:
        copy.wait_recv()
    across_y = along_y(
        across, lambda m: wholes[m].at[across], out_all.at[across], heads_all.at[across], smalls_all.at[across]
    )
    start_all(across_y)

    half_z = []
    for got, low, w in ((own_pair[0], 1 - lo, hi), (came_pair[0], lo, 1 - hi)):
        got.wait_recv()
        piece = block(z, low, w, first)
        half_z += [net.copy(piece, piece, along("z", d)) for d in (1, 3, 2)]
    start_all(half_z)
    pair_late = []
    for i, d in enumerate((1, 3, 2)):
        at = (z + 4 - d) % 4
        for got, low, w in ((own_z[i], lo, hi), (came_z[i], 1 - lo, 1 - hi)):
            got.wait_recv()
            piece = block(at, low, w, second)
            late = net.copy(piece, piece, pair)
            late.start()
            pair_late.append(late)
    keep[0].wait()
    share = []
    for low, w in ((lo, hi), (1 - lo, 1 - hi)):
        piece = x_ref.at[:, low, core, w]
        share.append(net.copy(piece, piece, other_core))
    start_all(share)
    for copy in half_z + [own_pair[1], came_pair[1]] + pair_late:
        copy.wait_recv()
    rest = []
    for low, w in ((1 - lo, hi), (lo, 1 - hi)):
        piece = x_ref.at[:, low, core, w]
        rest.append(net.copy(piece, piece, other_core))
    start_all(rest)
    wait_all(keep[1:])
    meta_wait()
    wait_all(own_y + across_y + share + rest)
    for copy in [swap] + own_pair + own_z + came_pair + came_z + half_z + pair_late + cross_early + cross_late:
        copy.wait_send()


def front(tokens, segments, flags, vectors, b_up, w_out, w_up, w_down, w_qkv):
    shape = jax.ShapeDtypeStruct
    in_vmem = pl.BlockSpec(memory_space=pltpu.VMEM)
    return pl.pallas_call(
        front_kernel,
        in_specs=[ANY] + [in_vmem] * 4 + [ANY] * 4,
        out_specs=[ANY] * 8,
        out_shape=[
            shape((4, 2, 2, 2, TB, D), BF),
            shape((NB, 8, TB), jnp.int32),
            shape((8, 128, 384), BF),
            shape((8, 16, 128), F32),
            shape((8, 128, D), BF),
            shape((8, 128, 2048), BF),
            shape((8, 256, D), BF),
            shape((8, 128, 3 * D), BF),
        ],
        scratch_shapes=[
            pltpu.VMEM((2, TB, D), BF),
            pltpu.VMEM((128, D), BF),
            pltpu.VMEM((2, 128, 2048), BF),
            pltpu.VMEM((256, D), BF),
            pltpu.VMEM((128, 3 * D), BF),
            pltpu.VMEM((2, 8, TB), jnp.int32),
            pltpu.VMEM((2, 128, 384), BF),
            pltpu.VMEM((16, 128), F32),
            pltpu.SemaphoreType.DMA((FRONT_COPIES,)),
            pltpu.SemaphoreType.DMA((FRONT_COPIES,)),
            pltpu.SemaphoreType.DMA((12,)),
            *swap_sems(),
        ],
        name="front_gather",
        compiler_params=pltpu.CompilerParams(
            collective_id=1, has_side_effects=True, vmem_limit_bytes=VMEM_CAP
        ),
    )(tokens, segments, flags, vectors, b_up, w_out, w_up, w_down, w_qkv)


def weights_second(up_all, down_all, out_all, qkv_all, net):
    x, y, z, core = place()
    hi, lo = x // 2, x % 2
    pair, wrap = device_at(hi * 2 + 1 - lo, y, z, core), device_at(3 - x, y, z, core)
    wholes = (up_all, down_all)
    copies = []
    for m in range(2):
        piece = wholes[m].at[:, unit_rows(m, 3), columns_part(m, lo, 2)]
        copies.append(net.copy(piece, piece, pair))
        for d in (1, 3, 2):
            for w in range(2):
                piece = wholes[m].at[y * 2 + w, unit_rows(m, 2)]
                copies.append(net.copy(piece, piece, along("y", d)))
            piece = wholes[m].at[:, unit_rows(m, 0), columns_part(m, z, 4)]
            copies.append(net.copy(piece, piece, along("z", d)))
    piece = out_all.at[:, half_rows(core)]
    copies.append(net.copy(piece, piece, sibling()))
    piece = qkv_all.at[y * 2 + hi, half_rows(core)]
    copies.append(net.copy(piece, piece, wrap))
    return copies


def attend_send_kernel(key_rows, *refs):
    inputs, outputs, wholes, sems = refs[:3], refs[7:10], refs[10:14], refs[14:]
    step = pl.program_id(0)

    def copies():
        return weights_second(*wholes, Transfers(*sems))

    @pl.when(step == 0)
    def _():
        greet(ring_partners())
        start_all(copies())

    attend_kernel(key_rows, *inputs, *outputs)

    @pl.when(step == pl.num_programs(0) - 1)
    def _():
        wait_all(copies())


def attend_send(qat, ka, vat, weights, width=1024, key_rows=512):
    shape = jax.ShapeDtypeStruct
    return pl.pallas_call(
        functools.partial(attend_send_kernel, key_rows),
        grid=(L // width,),
        in_specs=[
            pl.BlockSpec((128, width), lambda i: (0, i)),
            pl.BlockSpec((L, 128), lambda i: (0, 0)),
            pl.BlockSpec((80, L), lambda i: (0, 0)),
        ]
        + [ANY] * 4,
        out_specs=[
            pl.BlockSpec((width // TB, HD, TB), lambda i: (i, 0, 0)),
            pl.BlockSpec((HD, width), lambda i: (0, i)),
            pl.BlockSpec((1, width), lambda i: (0, i)),
        ]
        + [ANY] * 4,
        out_shape=[shape((NB, HD, TB), BF), shape((HD, L), F32), shape((1, L), F32)]
        + [shape(w.shape, w.dtype) for w in weights],
        input_output_aliases={3: 3, 4: 4, 5: 5, 6: 6},
        scratch_shapes=[pltpu.SemaphoreType.DMA((24,)), pltpu.SemaphoreType.DMA((24,))],
        name="attend",
        compiler_params=pltpu.CompilerParams(
            collective_id=2, has_side_effects=True, vmem_limit_bytes=VMEM_CAP
        ),
    )(qat, ka, vat, *weights)


def qkv_along_y(qkv_all, net):
    _, y, _, core = place()
    copies = []
    for d in (1, 3, 2):
        for w in range(2):
            piece = qkv_all.at[y * 2 + w, half_rows(core)]
            copies.append(net.copy(piece, piece, along("y", d)))
    return copies


def turned(first, second):
    return dot(first, second, ((0,), (0,)))


def gelu_both(u):
    rate = 0.7978845608028654
    square = u * u
    curve = jnp.tanh(rate * (u + 0.044715 * (square * u)))
    half = 0.5 * (1.0 + curve)
    slope = half + 0.5 * u * (1.0 - curve * curve) * (rate * (1.0 + 0.134145 * square))
    return u * half, slope


def fold(values):
    return jnp.sum(values.reshape(values.shape[0] // 8, 8, values.shape[1]), axis=0)


ROWS = 256
CHUNK = 32
SMALLS = 16


def middle_kernel(
    blocks, meta, tokens, teacher, flags, smalls, out_all, up_all, down_all, a0,
    states, resid_out, do, g_ref, sums_out, count_out, qkv_all,
    context, context_s, w_out, w_up, w_down, h, act, slope, send_one, come_one, send_two, come_two,
    gb, gu, ga, ga_s, normed, hidden, rate, work, resid, gct, stage, count, counts, valid,
    send, recv, local, go_send, go_recv, go_local, back_send, back_recv, back_local,
):
    x, y, z, core = place()
    mine = y * 2 + x // 2
    twin = sibling()
    loads = [
        pltpu.make_async_copy(out_all, w_out, local.at[0]),
        pltpu.make_async_copy(up_all, w_up, local.at[1]),
        pltpu.make_async_copy(down_all, w_down, local.at[2]),
    ]
    start_all(loads)
    greet_all(shard_greet())
    net = Transfers(send, recv)
    go_start, go_wait = swap_copies(
        lambda b: blocks.at[b], lambda b: head_tile(context, b), (go_send, go_recv, go_local)
    )
    go_start()
    valid_here = jnp.sum(meta[:, 1, :].astype(F32), axis=0, keepdims=True)
    count[...] = jnp.broadcast_to(jnp.sum(valid_here, axis=1, keepdims=True), (8, 128))
    ahead = [net.copy(count, counts.at[mine], target) for target in shard_greet()]
    start_all(ahead)
    own_count = pltpu.make_async_copy(count, counts.at[mine], local.at[3])
    own_count.start()
    later = qkv_along_y(qkv_all, net)
    start_all(later)
    for s in range(2):
        column = jnp.broadcast_to(flags[s : s + 1, :].astype(F32), (128, 128)).T
        valid[128 * s : 128 * (s + 1), :] = column

    def vector(row):
        return jnp.concatenate([smalls[i, row : row + 1, :] for i in range(8)], axis=1)

    out_bias, gain_one, offset_one, down_bias, gain_two, offset_two = [vector(row) for row in range(2, 8)]
    zeros = jnp.zeros((8, D), F32)
    go_wait()
    give_context = net.copy(context, context_s, twin)
    give_context.start()
    wait_all(loads)
    work[...] = turned(context[...], w_out[...].reshape(D, D))

    @pl.loop(0, ROWS // CHUNK)
    def _(i):
        rows = pl.ds(aligned(i * CHUNK, CHUNK), CHUNK)
        total = tokens[rows, :].astype(F32) + work[rows, :] + out_bias
        centre = total - jnp.mean(total, axis=1, keepdims=True)
        scale = lax.rsqrt(jnp.mean(centre * centre, axis=1, keepdims=True) + EPS)
        unit = centre * scale
        normed[rows, :] = unit
        rate[rows, :] = jnp.broadcast_to(scale, (CHUNK, 128))
        full = unit * gain_one + offset_one
        hidden[rows, :] = full
        h[0, rows, :] = full.astype(BF)

    give_hidden = net.copy(h.at[0], h.at[1], twin)
    give_hidden.start()
    for slot in range(2):
        if slot == 1:
            give_hidden.wait()
        for k in range(8):
            columns = slice(256 * k, 256 * (k + 1))
            bias = jnp.concatenate([smalls[k, pl.ds(8 + 2 * core + e, 1), :] for e in range(2)], axis=1)
            u = dot(h[slot], w_up[:, :, columns].reshape(D, 256)) + bias
            value, incline = gelu_both(u)
            act[slot, :, columns] = value.astype(BF)
            slope[slot, :, columns] = incline
    send_one[...] = dot(act[1], w_down[...].reshape(2048, D))
    give_one = net.copy(send_one, come_one, twin)
    give_one.start()
    work[...] = dot(act[0], w_down[...].reshape(2048, D))
    give_one.wait()
    wait_all(ahead)
    own_count.wait()
    total_count = jnp.sum(counts[...], axis=0)
    count_out[...] = total_count
    factor = (128 * ROWS) / total_count[:1, :1]

    def loss_rows(i, carried):
        rows = pl.ds(aligned(i * CHUNK, CHUNK), CHUNK)
        total = hidden[rows, :] + (work[rows, :] + come_one[rows, :] + down_bias)
        centre = total - jnp.mean(total, axis=1, keepdims=True)
        scale = lax.rsqrt(jnp.mean(centre * centre, axis=1, keepdims=True) + EPS)
        unit = centre * scale
        final = unit * gain_two + offset_two
        states[rows, :] = final.astype(BF)
        differ = final - teacher[rows, :].astype(F32)
        held = valid[rows, :1] * differ
        grad = factor * held
        weighted = grad * gain_two
        back = weighted - jnp.mean(weighted, axis=1, keepdims=True)
        back = scale * (back - unit * jnp.mean(weighted * unit, axis=1, keepdims=True))
        resid[rows, :] = back
        low = back.astype(BF)
        gb[0, rows, :] = low
        return (
            carried[0] + fold(grad * unit),
            carried[1] + fold(grad),
            carried[2] + fold(low.astype(F32)),
            carried[3] + fold(held * differ),
        )

    gain_two_sum, offset_two_sum, down_sum, error = lax.fori_loop(
        0, ROWS // CHUNK, loss_rows, (zeros, zeros, zeros, zeros)
    )
    give_branch = net.copy(gb.at[0], gb.at[1], twin)
    give_branch.start()
    up_sums = []
    for slot in range(2):
        if slot == 1:
            give_branch.wait()
        for k in range(8):
            columns = slice(256 * k, 256 * (k + 1))
            pulled = dot(gb[slot], w_down[k], ((1,), (1,))) * slope[slot, :, columns]
            low = pulled.astype(BF)
            gu[slot, :, columns] = low
            up_sums.append(fold(low.astype(F32)))
    for i in range(8):
        send_two[:, 128 * i : 128 * (i + 1)] = dot(gu[1], w_up[i], ((1,), (1,)))
    give_two = net.copy(send_two, come_two, twin)
    give_two.start()
    for i in range(8):
        work[:, 128 * i : 128 * (i + 1)] = dot(gu[0], w_up[i], ((1,), (1,)))
    give_two.wait()

    def first_norm_rows(i, carried):
        rows = pl.ds(aligned(i * CHUNK, CHUNK), CHUNK)
        grad = resid[rows, :] + (work[rows, :] + come_two[rows, :])
        unit = normed[rows, :]
        weighted = grad * gain_one
        back = weighted - jnp.mean(weighted, axis=1, keepdims=True)
        back = rate[rows, :1] * (back - unit * jnp.mean(weighted * unit, axis=1, keepdims=True))
        resid_out[rows, :] = back
        low = back.astype(BF)
        ga[rows, :] = low
        return (carried[0] + fold(grad * unit), carried[1] + fold(grad), carried[2] + fold(low.astype(F32)))

    gain_one_sum, offset_one_sum, out_sum = lax.fori_loop(0, ROWS // CHUNK, first_norm_rows, (zeros, zeros, zeros))
    give_attended = net.copy(ga.at[:, pl.ds(aligned((1 - core) * 512, 512), 512)], ga_s, twin)
    give_attended.start()
    gct[...] = dot(w_out[...].reshape(D, D), ga[...], ((1,), (1,))).astype(BF)
    back_start, back_wait = swap_copies(
        lambda b: head_tile(gct, b), lambda b: do.at[b], (back_send, back_recv, back_local)
    )
    back_start()

    error = jnp.broadcast_to(jnp.sum(jnp.sum(error, axis=0, keepdims=True), axis=1, keepdims=True), (1, 128))
    lines = [out_sum, gain_one_sum, offset_one_sum, down_sum, gain_two_sum, offset_two_sum]
    lines = [jnp.sum(line, axis=0, keepdims=True) for line in lines]
    for i in range(8):
        columns = slice(128 * i, 128 * (i + 1))
        sums_out[i] = jnp.zeros((SMALLS, 128), F32)
        for row, line in enumerate(lines):
            sums_out[i, row : row + 1, :] = line[:, columns]
        both = jnp.sum(up_sums[i] + up_sums[8 + i], axis=0, keepdims=True)
        for e in range(2):
            sums_out[i, pl.ds(6 + 2 * core + e, 1), :] = both[:, 128 * e : 128 * (e + 1)]
        sums_out[i, 10:11, :] = error

    give_context.wait()
    give_attended.wait()

    def stored(i):
        return pltpu.make_async_copy(stage.at[i % 2], g_ref.at[i // 2, i % 2], local.at[4 + i % 2])

    for i in range(8):
        if i >= 2:
            stored(i - 2).wait()
        tall = slice(128 * i, 128 * (i + 1))
        wide = slice(256 * i, 256 * (i + 1))
        up = turned(h[0, :, tall], gu[0]) + turned(h[1, :, tall], gu[1])
        for k in range(4):
            stage[i % 2, 128 * k : 128 * (k + 1), :] = up[:, 512 * k : 512 * (k + 1)].astype(BF)
        down = turned(act[0, :, wide], gb[0]) + turned(act[1, :, wide], gb[1])
        for k in range(2):
            stage[i % 2, 512 + 256 * k : 768 + 256 * k, :] = down[:, 512 * k : 512 * (k + 1)].astype(BF)
        own_half = ga[:, pl.ds(aligned(core * 512, 512), 512)]
        out = dot(context[tall, :], own_half) + dot(context_s[tall, :], ga_s[...])
        stage[i % 2, 1024:, :] = out.astype(BF)
        stored(i).start()
    stored(6).wait()
    stored(7).wait()
    back_wait()
    wait_all(later)


def middle(blocks, meta, tokens, teacher, flags, smalls, out_all, up_all, down_all, qkv_all):
    shape = jax.ShapeDtypeStruct
    in_vmem = pl.BlockSpec(memory_space=pltpu.VMEM)
    dma = pltpu.SemaphoreType.DMA
    wide = pltpu.VMEM((ROWS, D), F32)
    return pl.pallas_call(
        middle_kernel,
        in_specs=[ANY] + [in_vmem] * 5 + [ANY] * 4,
        out_specs=[in_vmem, in_vmem, ANY, ANY, in_vmem, in_vmem, ANY],
        out_shape=[
            shape((ROWS, D), BF),
            shape((ROWS, D), F32),
            shape((NB, HD, TB), BF),
            shape((4, 2, 1152, 512), BF),
            shape((8, SMALLS, 128), F32),
            shape((8, 128), F32),
            shape(qkv_all.shape, BF),
        ],
        input_output_aliases={9: 6},
        scratch_shapes=[
            pltpu.VMEM((D, ROWS), BF),
            pltpu.VMEM((D, ROWS), BF),
            pltpu.VMEM((8, 128, D), BF),
            pltpu.VMEM((8, 128, 2048), BF),
            pltpu.VMEM((8, 256, D), BF),
            pltpu.VMEM((2, ROWS, D), BF),
            pltpu.VMEM((2, ROWS, 2048), BF),
            pltpu.VMEM((2, ROWS, 2048), F32),
            wide,
            wide,
            wide,
            wide,
            pltpu.VMEM((2, ROWS, D), BF),
            pltpu.VMEM((2, ROWS, 2048), BF),
            pltpu.VMEM((ROWS, D), BF),
            pltpu.VMEM((ROWS, 512), BF),
            wide,
            wide,
            pltpu.VMEM((ROWS, 128), F32),
            wide,
            wide,
            pltpu.VMEM((D, ROWS), BF),
            pltpu.VMEM((2, 1152, 512), BF),
            pltpu.VMEM((8, 128), F32),
            pltpu.VMEM((8, 8, 128), F32),
            pltpu.VMEM((ROWS, 128), F32),
            dma((24,)),
            dma((24,)),
            dma((8,)),
            *swap_sems(),
            *swap_sems(),
        ],
        name="middle",
        compiler_params=pltpu.CompilerParams(
            collective_id=3, has_side_effects=True, vmem_limit_bytes=VMEM_CAP
        ),
    )(blocks, meta, tokens, teacher, flags, smalls, out_all, up_all, down_all, qkv_all)


def attend_back_send_kernel(key_rows, *refs):
    inputs, g_ref, dqkv_ref, f_ref = refs[:8], refs[8], refs[9], refs[10]
    dk_ref, dv_ref = refs[11:13]
    net = (g_ref,) + refs[13:]
    step = pl.program_id(0)
    steps = pl.num_programs(0)

    @pl.when(step == 0)
    def _():
        greet(ring_partners()[:9])
        reduce_start(net)

    attend_back_kernel(key_rows, *inputs, dqkv_ref, dk_ref, dv_ref)

    @pl.when(step == steps - 2)
    def _():
        reduce_step(0, net)

    @pl.when(step == steps - 1)
    def _():
        reduce_step(1, net)
        reduce_step(2, net)
        f_ref[...] = net[7][:, 0]


def attend_back_send(qat, ka, va, kt, q8, do, wide, lse, g, width=512, key_rows=512):
    def whole(shape):
        return pl.BlockSpec(shape, lambda i: (0,) * len(shape))

    return pl.pallas_call(
        functools.partial(attend_back_send_kernel, key_rows),
        grid=(L // width,),
        in_specs=[
            pl.BlockSpec((128, width), lambda i: (0, i)),
            whole((L, 128)),
            whole((L, 128)),
            whole((HD, L)),
            pl.BlockSpec((width, HD), lambda i: (i, 0)),
            pl.BlockSpec((width // TB, HD, TB), lambda i: (i, 0, 0)),
            pl.BlockSpec((HD, width), lambda i: (0, i)),
            pl.BlockSpec((1, width), lambda i: (0, i)),
            ANY,
        ],
        out_specs=[whole((NB, 3 * HD, TB)), whole((3, 48, 512))],
        out_shape=[jax.ShapeDtypeStruct((NB, 3 * HD, TB), BF), jax.ShapeDtypeStruct((3, 48, 512), BF)],
        scratch_shapes=[pltpu.VMEM((L, HD), F32), pltpu.VMEM((L, HD), F32)] + reduce_scratch(),
        name="attend_back",
        compiler_params=pltpu.CompilerParams(
            collective_id=5, has_side_effects=True, vmem_limit_bytes=VMEM_CAP
        ),
    )(qat, ka, va, kt, q8, do, wide, lse, g)


def last_kernel(
    dqkv, x_seq, pieces, smalls, a0,
    projected, heads_out, shard_out, smalls_out, qkv_all,
    d_ref, x_buf, mine_ref, parts_ref, sum_ref, small_buf, small_sum, small_all, f_ref, heads_buf,
    spread_send, spread_recv, local, send, recv, swap_send, swap_recv, swap_local,
):
    x, y, z, core = place()
    shard_at = y * 2 + x // 2
    seq = lax.axis_index("seq")

    def shard_device(d):
        other = (shard_at + d) % 8
        return other, (other // 2, seq, other % 2)

    greet_all([shard_device(d)[1] for d in range(1, 8)])
    net = Transfers(send, recv)
    start, wait = swap_copies(
        lambda b: dqkv.at[b], lambda b: head_tile3(projected, b), (swap_send, swap_recv, swap_local)
    )
    start()
    load = [
        pltpu.make_async_copy(dqkv, d_ref, local.at[3]),
        pltpu.make_async_copy(pieces, f_ref, local.at[4]),
    ]
    start_all(load)
    small_out = [net.copy(smalls.at[shard_device(d)[0]], small_buf.at[shard_at], shard_device(d)[1]) for d in range(1, 8)]
    small_own = pltpu.make_async_copy(smalls.at[shard_at], small_buf.at[shard_at], local.at[5])
    start_all(small_out + [small_own])
    rows = pl.ds(aligned(core * 64, 64), 64)
    weights = net.copy(qkv_all.at[:, rows], qkv_all.at[:, rows], sibling())
    weights.start()

    def chunk(j):
        return pltpu.make_async_copy(x_seq.at[pl.ds(j * 4, 4)], x_buf.at[j % 2], local.at[6 + j % 2])

    chunk(0).start()
    load[1].wait()
    spread_begin, spread_middle, spread_end = spread_steps((f_ref, local, spread_send, spread_recv), shard_out)
    spread_begin()
    load[0].wait()
    total = jnp.zeros((3 * HD, D), F32)
    sums = jnp.zeros((8, 3 * HD), F32)
    for j in range(8):
        chunk(j).wait()
        if j < 7:
            chunk(j + 1).start()
        left = jnp.concatenate([d_ref[4 * j + k].reshape(3 * HD, TB) for k in range(4)], axis=1)
        total = total + dot(left, x_buf[j % 2].reshape(4 * TB, D))
        sums = sums + dot(jnp.ones((8, 4 * TB), BF), left, ((1,), (1,)))
    gap = jnp.zeros((1, 128 - HD), F32)
    tail = jnp.concatenate(
        [
            jnp.concatenate([sums[:1, :HD], gap], axis=1),
            jnp.concatenate([sums[:1, 2 * HD :], gap], axis=1),
            jnp.zeros((14, 128), F32),
        ],
        axis=0,
    ).astype(BF)
    for i in range(8):
        mine_ref[i, : 3 * HD, :] = total[:, 128 * i : 128 * (i + 1)].astype(BF)
        mine_ref[i, 3 * HD :, :] = tail
    part_out = [net.copy(mine_ref.at[shard_device(d)[0]], parts_ref.at[d], shard_device(d)[1]) for d in range(1, 8)]
    start_all(part_out)
    wait_all(small_out + [small_own])
    small_sum[...] = jnp.sum(small_buf[...], axis=0)
    spread_middle()
    wait_all(part_out)
    added = mine_ref[shard_at].astype(F32)
    for d in range(1, 8):
        added = added + parts_ref[d].astype(F32)
    sum_ref[...] = added.astype(BF)
    head_out = []
    for d in range(1, 16):
        other = (seq + d) % 16
        target = (y, other, x // 2)
        head_out.append(net.copy(sum_ref, heads_buf.at[seq], target))
        head_out.append(net.copy(small_sum, small_all.at[seq], target))
    head_own = [
        pltpu.make_async_copy(sum_ref, heads_buf.at[seq], local.at[3]),
        pltpu.make_async_copy(small_sum, small_all.at[seq], local.at[4]),
    ]
    start_all(head_out + head_own)
    wait()
    spread_end()
    weights.wait()
    wait_all(head_out + head_own)
    heads_out[...] = heads_buf[...]
    smalls_out[...] = jnp.sum(small_all[...], axis=0)


def spread_steps(refs, o_ref):
    mine_ref, local, send, recv = refs
    x, y, z, core = place()
    low = x % 2
    pair = device_at(x // 2 * 2 + 1 - low, y, z, core)
    first, own, second, third = [], [], [], []
    for part in range(3):
        mine = mine_ref.at[part]
        own.append(pltpu.make_async_copy(mine, shard_rows(o_ref, part, low, z, core), local.at[part]))
        first.append(remote(mine, shard_rows(o_ref, part, low, z, core), send.at[part, 0], recv.at[part, 0], pair))
        for shift in (1, 2, 3):
            spot = shard_rows(o_ref, part, low, z, core)
            second.append(remote(mine, spot, send.at[part, shift], recv.at[part, shift], along("z", shift)))
            spot = shard_rows(o_ref, part, 1 - low, z, core)
            third.append(remote(spot, spot, send.at[part, 3 + shift], recv.at[part, 3 + shift], along("z", shift)))

    def begin():
        start_all(own + first + second)

    def middle():
        wait_all(first)
        start_all(third)

    def end():
        wait_all(own + second + third)
        rows = o_ref.at[core]
        across = remote(rows, rows, send.at[0, 7], recv.at[0, 7], sibling())
        across.start()
        across.wait()

    return begin, middle, end


def last_swap(dqkv, x_seq, pieces, smalls, qkv_all):
    shape = jax.ShapeDtypeStruct
    in_vmem = pl.BlockSpec(memory_space=pltpu.VMEM)
    dma = pltpu.SemaphoreType.DMA
    return pl.pallas_call(
        last_kernel,
        in_specs=[ANY] * 5,
        out_specs=[ANY, in_vmem, ANY, in_vmem, ANY],
        out_shape=[
            shape((3, D, 2 * TB), BF),
            shape((H, 208, 128), BF),
            shape((2, 1152, 512), BF),
            shape((16, 128), F32),
            shape(qkv_all.shape, BF),
        ],
        input_output_aliases={4: 4},
        scratch_shapes=[
            pltpu.VMEM((NB, 3, HD, TB), BF),
            pltpu.VMEM((2, 4, TB, D), BF),
            pltpu.VMEM((8, 208, 128), BF),
            pltpu.VMEM((8, 208, 128), BF),
            pltpu.VMEM((208, 128), BF),
            pltpu.VMEM((8, 16, 128), F32),
            pltpu.VMEM((16, 128), F32),
            pltpu.VMEM((16, 16, 128), F32),
            pltpu.VMEM((3, 48, 512), BF),
            pltpu.VMEM((H, 208, 128), BF),
            dma((3, 8)),
            dma((3, 8)),
            dma((8,)),
            dma((48,)),
            dma((48,)),
            *swap_sems(),
        ],
        name="last_swap",
        compiler_params=pltpu.CompilerParams(
            collective_id=6, has_side_effects=True, vmem_limit_bytes=VMEM_CAP
        ),
    )(dqkv, x_seq, pieces, smalls, qkv_all)


def finish_kernel(
    projected, qkv_ref, resid_ref, heads_ref, shard_ref, tokens_ref, grad_qkv, grad_out, grad_up, grad_down
):
    step = pl.program_id(0)
    tokens_ref[...] = resid_ref[...] + dot(projected[...], qkv_ref[...], ((0,), (1,)))
    for c in range(2):
        columns = slice(512 * c, 512 * (c + 1))
        for j in range(2):
            piece = shard_ref[c, pl.ds(aligned(step * 128, 128), 128), 256 * j : 256 * (j + 1)]
            grad_up[:, 512 * j + 256 * c : 512 * j + 256 * (c + 1)] = piece.astype(F32)
        rows = pl.ds(aligned(512 + 256 * c + (step % 2) * 128, 128), 128)
        grad_down[:, columns] = shard_ref[step // 2, rows, :].astype(F32)
        grad_out[:, columns] = shard_ref[c, pl.ds(aligned(1024 + step * 32, 32), 32), :].astype(F32)

    @pl.when(step == 0)
    def _():
        for p in range(3):
            for pair in range(8):
                both = [heads_ref[2 * pair + k, p * HD : (p + 1) * HD, :].astype(F32) for k in range(2)]
                at = p * D + pair * 128
                grad_qkv[:, at : at + 128] = jnp.concatenate(both, axis=0).T


def finish(projected, qkv, resid, heads, shard):
    shape = jax.ShapeDtypeStruct

    def whole(dims):
        return pl.BlockSpec(dims, lambda i: (0,) * len(dims))

    return pl.pallas_call(
        finish_kernel,
        grid=(4,),
        in_specs=[
            whole((3 * D, 2 * TB)),
            pl.BlockSpec((256, 3 * D), lambda i: (i, 0)),
            pl.BlockSpec((2 * TB, 256), lambda i: (0, i)),
            whole((H, 208, 128)),
            whole((2, 1152, 512)),
        ],
        out_specs=[
            pl.BlockSpec((2 * TB, 256), lambda i: (0, i)),
            whole((128, 3 * D)),
            pl.BlockSpec((32, D), lambda i: (i, 0)),
            pl.BlockSpec((128, 1024), lambda i: (0, i)),
            pl.BlockSpec((128, D), lambda i: (i, 0)),
        ],
        out_shape=[
            shape((2 * TB, D), F32),
            shape((128, 3 * D), F32),
            shape((128, D), F32),
            shape((128, FF), F32),
            shape((512, D), F32),
        ],
        name="finish",
        compiler_params=pltpu.CompilerParams(vmem_limit_bytes=VMEM_CAP),
    )(projected, qkv, resid, heads, shard)


def on_device(
    tokens,
    segments,
    valid_flags,
    teacher,
    w_qkv,
    b_query,
    b_value,
    w_out,
    b_out,
    ln1_gain,
    ln1_bias,
    w_up,
    b_up,
    w_down,
    b_down,
    ln2_gain,
    ln2_bias,
):
    seq_local, row_local, _ = tokens.shape
    token_rows = seq_local * row_local
    shard_at = lax.axis_index("dp") * 2 + lax.axis_index("wshard")

    vectors = jnp.stack([b_query, b_value, b_out, ln1_gain, ln1_bias, b_down, ln2_gain, ln2_bias]).astype(F32)
    x_seq, meta_all, heads_all, smalls_all, out_all, up_all, down_all, qkv_all = front(
        tokens, segments, valid_flags, vectors, b_up.reshape(4, 128).astype(F32), w_out, w_up, w_down, w_qkv
    )
    x_seq = x_seq.reshape(NB, TB, D)
    qat, ka, vat, va, kt, q8 = project(x_seq.reshape(L, D), heads_all.reshape(D, 384), smalls_all, meta_all)
    blocks, wide, lse, up_all, down_all, out_all, qkv_all = attend_send(
        qat, ka, vat, (up_all, down_all, out_all, qkv_all)
    )
    states, grad_resid_one, do, g, small_sums, count, qkv_all = middle(
        blocks,
        meta_all,
        tokens.reshape(token_rows, D),
        teacher.reshape(token_rows, D),
        valid_flags,
        smalls_all,
        out_all,
        up_all,
        down_all,
        qkv_all,
    )
    dqkv, pieces = attend_back_send(qat, ka, va, kt, q8, do, wide, lse, g)
    projected, heads_out, shard_out, small_out, qkv_all = last_swap(
        dqkv.reshape(NB, 3, HD, TB), x_seq, pieces, small_sums, qkv_all
    )
    grad_tokens, grad_qkv, grad_out, grad_up, grad_down = finish(
        projected.reshape(3 * D, token_rows), qkv_all.reshape(D, 3 * D), grad_resid_one, heads_out, shard_out
    )
    own_heads = lax.dynamic_slice(heads_out, (shard_at * 2, 3 * HD, 0), (2, 2, HD)).astype(F32)
    mean_loss = small_out[10, 0] / (D * count[0, 0])
    return (
        states.reshape(seq_local, row_local, D),
        mean_loss,
        grad_tokens.reshape(seq_local, row_local, D),
        grad_qkv,
        own_heads[:, 0].reshape(128),
        own_heads[:, 1].reshape(128),
        grad_out,
        small_out[0],
        small_out[1],
        small_out[2],
        grad_up,
        small_out[6:10].reshape(512),
        grad_down,
        small_out[3],
        small_out[4],
        small_out[5],
    )


def solution(mesh):
    rows = P("dp", ("seq", "wshard"), None)
    flags = P("dp", ("seq", "wshard"))
    matrix = P(("dp", "wshard"), None)
    vector = P(("dp", "wshard"))
    return jax.shard_map(
        on_device,
        mesh=mesh,
        in_specs=(
            rows,
            flags,
            flags,
            rows,
            matrix,
            vector,
            vector,
            matrix,
            vector,
            vector,
            vector,
            matrix,
            vector,
            matrix,
            vector,
            vector,
            vector,
        ),
        out_specs=(
            rows,
            P(),
            rows,
            matrix,
            vector,
            vector,
            matrix,
            vector,
            vector,
            vector,
            matrix,
            vector,
            matrix,
            vector,
            vector,
            vector,
        ),
        check_vma=False,
    )
```

```python
import functools

import jax
import jax.numpy as jnp
from jax import lax
from jax.experimental import pallas as pl
from jax.experimental.pallas import tpu as pltpu
from jax.sharding import PartitionSpec as P

D = 1024
H = 16
HD = 64
FF = 4096
L = 4096
EPS = 1e-06
F32 = jnp.float32
BF = jnp.bfloat16
MASKED = 1000000000.0
VMEM_CAP = 60 * 1024 * 1024
MESH = pl.DeviceIdType.MESH
ANY = pl.BlockSpec(memory_space=pl.ANY)
TB = 128
NB = L // TB


def dot(first, second, dims=((1,), (0,))):
    return lax.dot_general(first, second, (dims, ((), ())), preferred_element_type=F32)


def project_kernel(
    x_ref, heads_ref, smalls_ref, meta_ref, qat_ref, ka_ref, vat_ref, va_ref, kt_ref, q_ref, w_ref, wt_ref, b_ref
):
    _, _, _, core = place()

    @pl.when(pl.program_id(0) == 0)
    def _():
        pair = lax.axis_index("seq") // 2
        first = core == 0
        both = heads_ref[...]
        own = [jnp.where(first, both[:, 128 * p : 128 * p + HD], both[:, 128 * p + HD : 128 * (p + 1)]) for p in range(3)]
        w_ref[...] = jnp.concatenate(own, axis=1)
        wt_ref[...] = w_ref[...].astype(F32).T.astype(BF)
        mine = smalls_ref[pair]
        bias = [jnp.where(first, mine[k : k + 1, :HD], mine[k : k + 1, HD:]) for k in range(2)]
        b_ref[...] = jnp.broadcast_to(jnp.concatenate([bias[0], jnp.zeros((1, HD), F32), bias[1]], axis=1), (8, 3 * HD))

    x = x_ref[...]
    rows = x.shape[0]
    side = dot(x, w_ref[...]) + b_ref[:1, :]
    turned = dot(wt_ref[...], x, ((1,), (1,))) + b_ref[...].T[:, :1]
    q8 = (side[:, :HD].astype(BF).astype(F32) * 0.125).astype(BF)
    q8t = (turned[:HD].astype(BF).astype(F32) * 0.125).astype(BF)
    k = side[:, HD : 2 * HD].astype(BF)
    v = side[:, 2 * HD :].astype(BF)
    segment = jnp.concatenate([meta_ref[i, 0:1, :] for i in range(rows // TB)], axis=1)
    hot = jnp.where(lax.broadcasted_iota(jnp.int32, (32, rows), 0) == segment, 1.0, 0.0)
    apart = (hot.T - 1.0) * MASKED
    lane = lax.broadcasted_iota(jnp.int32, (rows, 32), 1)
    ones3 = jnp.where(lane < 3, 1.0, 0.0)
    zero_side = jnp.zeros((rows, 32), F32)
    q_ref[...] = q8
    qat_ref[...] = jnp.concatenate([q8t, hot.astype(BF), jnp.zeros((32, rows), BF)], axis=0)
    ka_ref[...] = jnp.concatenate([k, apart.astype(BF), ones3.astype(BF)], axis=1)
    va_ref[...] = jnp.concatenate([v, ones3.astype(BF), zero_side.astype(BF)], axis=1)
    kt_ref[...] = turned[HD : 2 * HD].astype(BF)
    ones_row = jnp.where(lax.broadcasted_iota(jnp.int32, (16, rows), 0) == 0, 1.0, 0.0)
    vat_ref[...] = jnp.concatenate([turned[2 * HD :].astype(BF), ones_row.astype(BF)], axis=0)


def project(x, heads, smalls, meta, rows=1024):
    return pl.pallas_call(
        project_kernel,
        grid=(L // rows,),
        in_specs=[
            pl.BlockSpec((rows, D), lambda i: (i, 0)),
            pl.BlockSpec((D, 384), lambda i: (0, 0)),
            pl.BlockSpec((8, 16, 128), lambda i: (0, 0, 0)),
            pl.BlockSpec((rows // TB, 8, TB), lambda i: (i, 0, 0)),
        ],
        out_specs=[
            pl.BlockSpec((128, rows), lambda i: (0, i)),
            pl.BlockSpec((rows, 128), lambda i: (i, 0)),
            pl.BlockSpec((80, rows), lambda i: (0, i)),
            pl.BlockSpec((rows, 128), lambda i: (i, 0)),
            pl.BlockSpec((HD, rows), lambda i: (0, i)),
            pl.BlockSpec((rows, HD), lambda i: (i, 0)),
        ],
        out_shape=[
            jax.ShapeDtypeStruct((128, L), BF),
            jax.ShapeDtypeStruct((L, 128), BF),
            jax.ShapeDtypeStruct((80, L), BF),
            jax.ShapeDtypeStruct((L, 128), BF),
            jax.ShapeDtypeStruct((HD, L), BF),
            jax.ShapeDtypeStruct((L, HD), BF),
        ],
        scratch_shapes=[pltpu.VMEM((D, 3 * HD), BF), pltpu.VMEM((3 * HD, D), BF), pltpu.VMEM((8, 3 * HD), F32)],
        name="project_head",
        compiler_params=pltpu.CompilerParams(vmem_limit_bytes=VMEM_CAP),
    )(x, heads, smalls, meta)


def attend_kernel(key_rows, qat_ref, ka_ref, vat_ref, blocks_ref, wide_ref, lse_ref):
    queries = qat_ref[...]
    width = queries.shape[1]
    peak = jnp.full((1, width), -jnp.inf, F32)
    total = jnp.zeros((80, width), F32)
    for j in range(L // key_rows):
        rows = slice(j * key_rows, (j + 1) * key_rows)
        logits = dot(ka_ref[rows, :], queries)
        new_peak = jnp.maximum(peak, jnp.max(logits, axis=0, keepdims=True))
        expos = jnp.exp(logits - new_peak).astype(BF)
        total = total * jnp.exp(peak - new_peak) + dot(vat_ref[:, rows], expos)
        peak = new_peak
    sums = total[HD : HD + 1]
    context = total[:HD] / sums
    wide_ref[...] = context
    lse_ref[...] = peak + jnp.log(sums)
    low = context.astype(BF)
    for j in range(width // TB):
        blocks_ref[j] = low[:, j * TB : (j + 1) * TB]


def attend(qat, ka, vat, width=1024, key_rows=512):
    return pl.pallas_call(
        functools.partial(attend_kernel, key_rows),
        grid=(L // width,),
        in_specs=[
            pl.BlockSpec((128, width), lambda i: (0, i)),
            pl.BlockSpec((L, 128), lambda i: (0, 0)),
            pl.BlockSpec((80, L), lambda i: (0, 0)),
        ],
        out_specs=[
            pl.BlockSpec((width // TB, HD, TB), lambda i: (i, 0, 0)),
            pl.BlockSpec((HD, width), lambda i: (0, i)),
            pl.BlockSpec((1, width), lambda i: (0, i)),
        ],
        out_shape=[
            jax.ShapeDtypeStruct((NB, HD, TB), BF),
            jax.ShapeDtypeStruct((HD, L), F32),
            jax.ShapeDtypeStruct((1, L), F32),
        ],
        name="attend",
        compiler_params=pltpu.CompilerParams(vmem_limit_bytes=VMEM_CAP),
    )(qat, ka, vat)


def three_pieces(row):
    high = row.astype(BF)
    rest = row - high.astype(F32)
    middle = rest.astype(BF)
    lowest = (rest - middle.astype(F32)).astype(BF)
    return jnp.concatenate([high, middle, lowest], axis=0)


def place():
    at = lax.axis_index("seq")
    return (lax.axis_index("wshard") * 2 + (at // 2) % 2, lax.axis_index("dp"), at // 4, at % 2)


def device_at(x, y, z, core):
    return (y, (z * 2 + x % 2) * 2 + core, x // 2)


def along(axis, shift):
    x, y, z, core = place()
    if axis == "x":
        return device_at((x + shift) % 4, y, z, core)
    if axis == "y":
        return device_at(x, (y + shift) % 4, z, core)
    return device_at(x, y, (z + shift) % 4, core)


def sibling():
    x, y, z, core = place()
    return device_at(x, y, z, 1 - core)


def greet(partners):
    barrier = pltpu.get_barrier_semaphore()
    for partner in partners:
        pl.semaphore_signal(barrier, inc=1, device_id=partner, device_id_type=MESH)
    pl.semaphore_wait(barrier, len(partners))


def remote(src, dst, send_sem, recv_sem, target):
    return pltpu.make_async_remote_copy(
        src_ref=src, dst_ref=dst, send_sem=send_sem, recv_sem=recv_sem, device_id=target, device_id_type=MESH
    )


ORDERS = ("yzx", "zxy", "xyz")
PIECE = (64, 32, 48)
FIRST = (0, 512, 768)


def ring_partners():
    return [along(axis, shift) for axis in "xyz" for shift in (1, 2, 3)] + [sibling()]


def reduce_scratch():
    a, b, c = PIECE
    return [
        pltpu.VMEM((4, 2, 8 * a, 512), BF),
        pltpu.VMEM((4, 4, 2, 2 * b, 512), BF),
        pltpu.VMEM((4, 4, 4 * c, 512), BF),
        pltpu.VMEM((4, 2, 2 * a, 512), BF),
        pltpu.VMEM((4, 4, b, 512), BF),
        pltpu.VMEM((4, 4 * c, 512), BF),
        pltpu.VMEM((4, a, 512), BF),
        pltpu.VMEM((4, b, 512), BF),
        pltpu.VMEM((4, c, 512), BF),
        pltpu.SemaphoreType.DMA((3, 3, 3)),
        pltpu.SemaphoreType.DMA((3, 3, 3)),
        pltpu.SemaphoreType.DMA((3,)),
    ]


def aligned(value, unit):
    return pl.multiple_of(value, unit)


def reduce_piece(stage, part, refs, at):
    g_ref = refs[0]
    half, low, n = at // 2, at % 2, PIECE[part]
    if stage == 0:
        first = FIRST[part]
        if part == 0:
            return g_ref.at[at, :, pl.ds(first, 8 * n), :]
        if part == 1:
            return g_ref.at[:, :, pl.ds(aligned(first + at * 2 * n, 16), 2 * n), :]
        return g_ref.at[:, half, pl.ds(aligned(first + low * 4 * n, 16), 4 * n), :]
    held = refs[1 + 3 * (stage - 1) + part]
    if stage == 1:
        if part == 0:
            return held.at[0, :, pl.ds(aligned(at * 2 * n, 16), 2 * n), :]
        if part == 1:
            return held.at[0, :, half, pl.ds(aligned(low * n, 16), n), :]
        return held.at[0, at]
    if part == 0:
        return held.at[0, half, pl.ds(aligned(low * n, 16), n), :]
    if part == 1:
        return held.at[0, at]
    return held.at[0, pl.ds(aligned(at * n, 16), n), :]


def ring_at(axis):
    x, y, z, _ = place()
    return {"x": x, "y": y, "z": z}[axis]


def reduce_copies(stage, part, refs):
    send, recv = refs[10], refs[11]
    axis = ORDERS[part][stage]
    return [
        remote(
            reduce_piece(stage, part, refs, (ring_at(axis) + shift) % 4),
            refs[1 + 3 * stage + part].at[shift],
            send.at[stage, part, shift - 1],
            recv.at[stage, part, shift - 1],
            along(axis, shift),
        )
        for shift in (1, 3, 2)
    ]


def reduce_own(part, refs):
    return pltpu.make_async_copy(
        reduce_piece(0, part, refs, ring_at(ORDERS[part][0])), refs[1 + part].at[0], refs[12].at[part]
    )


def reduce_start(part, refs):
    start_all(reduce_copies(0, part, refs))
    reduce_own(part, refs).start()


def add_four(values):
    total = values[0].astype(F32) + values[1].astype(F32)
    return (total + values[2].astype(F32) + values[3].astype(F32)).astype(BF)


def reduce_step(stage, part, refs):
    a1, b1, c1, a2, b2, c2, a3, b3, c3 = refs[1:10]
    wait_all(reduce_copies(stage, part, refs))
    x, y, z, _ = place()
    n = PIECE[part]
    rest = (1, 2, 3)
    if stage == 0:
        reduce_own(part, refs).wait()

        @pl.loop(0, 16)
        def _(i):
            if part == 0:
                rows = pl.ds(aligned((i % 8) * n, 16), n)
                a1[0, i // 8, rows, :] = add_four([a1[s, i // 8, rows, :] for s in range(4)])
            elif part == 1:
                rows = pl.ds(aligned((i % 2) * n, 16), n)
                b1[0, i // 4, (i // 2) % 2, rows, :] = add_four([b1[s, i // 4, (i // 2) % 2, rows, :] for s in range(4)])
            else:
                rows = pl.ds(aligned((i % 4) * n, 16), n)
                c1[0, i // 4, rows, :] = add_four([c1[s, i // 4, rows, :] for s in range(4)])

    elif stage == 1:

        @pl.loop(0, 4)
        def _(i):
            if part == 0:
                rows = pl.ds(aligned((i % 2) * n, 16), n)
                own = a1[0, i // 2, pl.ds(aligned(z * 2 * n + (i % 2) * n, 16), n), :]
                a2[0, i // 2, rows, :] = add_four([own] + [a2[s, i // 2, rows, :] for s in rest])
            elif part == 1:
                own = b1[0, i, x // 2, pl.ds(aligned((x % 2) * n, 16), n), :]
                b2[0, i] = add_four([own] + [b2[s, i] for s in rest])
            else:
                rows = pl.ds(aligned(i * n, 16), n)
                own = c1[0, y, rows, :]
                c2[0, rows, :] = add_four([own] + [c2[s, rows, :] for s in rest])

    elif part == 0:
        own = a2[0, x // 2, pl.ds(aligned((x % 2) * n, 16), n), :]
        a3[0] = add_four([own] + [a3[s] for s in rest])
    elif part == 1:
        b3[0] = add_four([b2[0, y]] + [b3[s] for s in rest])
    else:
        own = c2[0, pl.ds(aligned(z * n, 16), n), :]
        c3[0] = add_four([own] + [c3[s] for s in rest])
    if stage < 2:
        start_all(reduce_copies(stage + 1, part, refs))


def shard_rows(o_ref, part, x_low, z, core):
    sub = x_low * 4 + z if part == 2 else z * 2 + x_low
    return o_ref.at[core, pl.ds(aligned(FIRST[part] + sub * PIECE[part], 16), PIECE[part]), :]


def spread_steps(part, mine, sems, o_ref):
    local, send, recv = sems
    x, y, z, core = place()
    low = x % 2
    pair = device_at(x // 2 * 2 + 1 - low, y, z, core)
    spot = shard_rows(o_ref, part, low, z, core)
    own = pltpu.make_async_copy(mine, spot, local.at[part])
    first = remote(mine, spot, send.at[part, 0], recv.at[part, 0], pair)
    second = [remote(mine, spot, send.at[part, d], recv.at[part, d], along("z", d)) for d in (1, 3, 2)]
    spot = shard_rows(o_ref, part, 1 - low, z, core)
    third = [remote(spot, spot, send.at[part, 3 + d], recv.at[part, 3 + d], along("z", d)) for d in (1, 3, 2)]

    def begin():
        start_all([own, first] + second)

    def middle():
        first.wait()
        start_all(third)

    def end():
        wait_all([own] + second + third)

    return begin, middle, end


def swap_partner(shift):
    mine = lax.axis_index("seq") * 2 + lax.axis_index("wshard")
    other = (mine + shift) % NB
    return other, (lax.axis_index("dp"), other // 2, other % 2)


def swap_greet():
    barrier = pltpu.get_barrier_semaphore()

    @pl.loop(1, NB)
    def _(shift):
        pl.semaphore_signal(barrier, inc=1, device_id=swap_partner(shift)[1], device_id_type=MESH)

    pl.semaphore_wait(barrier, NB - 1)


def swap_copies(piece_for, landing_from, sems):
    mine = lax.axis_index("seq") * 2 + lax.axis_index("wshard")
    send, recv, local = sems

    def copy(shift):
        other, device = swap_partner(shift)
        return remote(piece_for(other), landing_from(mine), send.at[shift], recv.at[shift], device)

    own = pltpu.make_async_copy(piece_for(mine), landing_from(mine), local)

    def start():
        @pl.loop(1, NB)
        def _(shift):
            copy(shift).start()

        own.start()

    def wait():
        @pl.loop(1, NB)
        def _(shift):
            copy(shift).wait()

        own.wait()

    return start, wait


def swap_sems():
    return [pltpu.SemaphoreType.DMA((NB,)), pltpu.SemaphoreType.DMA((NB,)), pltpu.SemaphoreType.DMA]


def block_of(ref, b):
    return ref.at[b]


def head_tile(ref, b):
    return ref.at[pl.ds(aligned((b // 2) * HD, HD), HD), pl.ds(aligned((b % 2) * TB, TB), TB)]


def head_tile3(ref, b):
    return ref.at[:, pl.ds(aligned((b // 2) * HD, HD), HD), pl.ds(aligned((b % 2) * TB, TB), TB)]


HALVES = ((128, 2048), (256, 1024))


class Transfers:
    def __init__(self, send, recv):
        self.send, self.recv, self.used = send, recv, 0

    def copy(self, src, dst, target):
        made = remote(src, dst, self.send.at[self.used], self.recv.at[self.used], target)
        self.used += 1
        return made


def start_all(copies):
    for copy in copies:
        copy.start()


def wait_all(copies):
    for copy in copies:
        copy.wait()


def unit_rows(matrix, unit, count=1):
    rows = HALVES[matrix][0] // 4
    return pl.ds(unit * rows, count * rows)


def columns_part(matrix, at, parts):
    width = HALVES[matrix][1] // parts
    return pl.ds(aligned(at * width, 128), width)


def half_rows(core, rows=64):
    return pl.ds(aligned(core * rows, rows), rows)


def shard_greet():
    x, y, z, core = place()
    return [device_at(x, (y + d) % 4, z, core) for d in (1, 2, 3)] + [
        device_at(3 - x, (y + d) % 4, z, core) for d in range(4)
    ]


def greet_all(others):
    barrier = pltpu.get_barrier_semaphore()

    @pl.loop(1, NB)
    def _(shift):
        pl.semaphore_signal(barrier, inc=1, device_id=swap_partner(shift)[1], device_id_type=MESH)

    for other in others:
        pl.semaphore_signal(barrier, inc=1, device_id=other, device_id_type=MESH)
    pl.semaphore_wait(barrier, NB - 1 + len(others))


FRONT_COPIES = 160


def front_kernel(
    tokens, segments, flags, vectors, b_up, w_out, w_up, w_down, w_qkv,
    x_ref, meta_all, heads_all, smalls_all, out_all, up_all, down_all, qkv_all,
    tok_buf, out_buf, up_buf, down_buf, qkv_buf, meta, heads, smalls,
    send, recv, local, meta_send, meta_recv, meta_local,
):
    x, y, z, core = place()
    hi, lo = x // 2, x % 2
    mine, across = y * 2 + hi, y * 2 + 1 - hi
    wrap, pair, other_core = device_at(3 - x, y, z, core), device_at(hi * 2 + 1 - lo, y, z, core), sibling()
    shards, wholes = (up_buf.at[core], down_buf), (up_all, down_all)
    rows_out = half_rows(core)
    loads = [pltpu.make_async_copy(tokens, tok_buf, local.at[0])]
    for j in range(8):
        piece = w_up.at[:, pl.ds(aligned(j * 512 + core * 256, 256), 256)]
        loads.append(pltpu.make_async_copy(piece, up_buf.at[core, :, pl.ds(j * 256, 256)], local.at[1 + j]))
    loads.append(pltpu.make_async_copy(w_out, out_buf, local.at[9]))
    loads.append(pltpu.make_async_copy(w_down.at[half_rows(core, 256)], down_buf, local.at[10]))
    loads.append(pltpu.make_async_copy(w_qkv, qkv_buf, local.at[11]))
    start_all(loads)
    meta[...] = jnp.zeros_like(meta)
    for s in range(2):
        meta[s, 0:1, :] = segments[s : s + 1, :]
        meta[s, 1:2, :] = flags[s : s + 1, :]
    smalls[...] = jnp.zeros_like(smalls)
    smalls[0:8, :] = vectors[...]
    smalls[8:12, :] = b_up[...]
    greet_all(shard_greet())
    loads[0].wait()
    net = Transfers(send, recv)
    first, second = pl.ds(0, 64), pl.ds(64, 64)

    def block(at, low, w, rows=slice(None)):
        return x_ref.at[at, low, core, w, rows]

    swap = net.copy(tok_buf.at[1 - hi], block(z, lo, hi), wrap)
    swap.start()
    own = tok_buf.at[hi]
    own_z = [net.copy(own, block(z, lo, hi), along("z", d)) for d in (1, 3, 2)]
    own_pair = [net.copy(own.at[rows], block(z, lo, hi, rows), pair) for rows in (first, second)]
    start_all([own_pair[0]] + own_z)
    wait_all(loads[1:])
    for p in range(3):
        for k, pair_at in ((0, z * 2 + lo), (1, z * 2 + 1 - lo)):
            heads[k, :, 128 * p : 128 * (p + 1)] = qkv_buf[:, pl.ds(aligned(p * D + pair_at * 128, 128), 128)]
    keep = [
        pltpu.make_async_copy(own, block(z, lo, hi), local.at[0]),
        pltpu.make_async_copy(heads.at[0], heads_all.at[mine], local.at[1]),
        pltpu.make_async_copy(smalls, smalls_all.at[mine], local.at[2]),
        pltpu.make_async_copy(qkv_buf, qkv_all.at[mine], local.at[3]),
    ]
    keep += [pltpu.make_async_copy(shards[m], wholes[m].at[mine], local.at[4 + m]) for m in range(2)]
    keep.append(pltpu.make_async_copy(out_buf, out_all.at[mine], local.at[6]))
    start_all(keep)

    cross_early, cross_late = [], []
    for m in range(2):
        for unit, columns in ((0, columns_part(m, z, 4)), (3, columns_part(m, 1 - lo, 2))):
            rows = unit_rows(m, unit)
            cross_early.append(net.copy(shards[m].at[rows, columns], wholes[m].at[mine, rows, columns], wrap))
        rows = unit_rows(m, 1, 2)
        cross_late.append(net.copy(shards[m].at[rows], wholes[m].at[mine, rows], wrap))
    cross_early.append(net.copy(out_buf.at[rows_out], out_all.at[mine, rows_out], wrap))
    cross_early.append(net.copy(heads.at[1], heads_all.at[mine], wrap))
    cross_early.append(net.copy(smalls, smalls_all.at[mine], wrap))
    start_all(cross_early + cross_late)

    def along_y(shard, source, out_source, heads_source, smalls_source):
        copies = []
        for d in (1, 3, 2):
            there = along("y", d)
            for m in range(2):
                for unit, columns in (
                    (0, columns_part(m, z, 4)),
                    (3, columns_part(m, lo, 2)),
                    (1, slice(None)),
                ):
                    rows = unit_rows(m, unit)
                    copies.append(net.copy(source(m).at[rows, columns], wholes[m].at[shard, rows, columns], there))
            copies.append(net.copy(out_source.at[rows_out], out_all.at[shard, rows_out], there))
            copies.append(net.copy(heads_source, heads_all.at[shard], there))
            copies.append(net.copy(smalls_source, smalls_all.at[shard], there))
        return copies

    meta_start, meta_wait = swap_copies(
        lambda b: meta.at[b % 2], lambda b: meta_all.at[b], (meta_send, meta_recv, meta_local)
    )
    meta_start()
    own_y = along_y(mine, lambda m: shards[m], out_buf, heads.at[0], smalls)
    start_all(own_y)

    swap.wait_recv()
    came = block(z, 1 - lo, 1 - hi)
    came_pair = [
        net.copy(block(z, 1 - lo, 1 - hi, rows), block(z, 1 - lo, 1 - hi, rows), pair) for rows in (first, second)
    ]
    came_z = [net.copy(came, came, along("z", d)) for d in (1, 3, 2)]
    start_all([came_pair[0]] + came_z)
    start_all([own_pair[1], came_pair[1]])

    for copy in cross_early + cross_late:
        copy.wait_recv()
    across_y = along_y(
        across, lambda m: wholes[m].at[across], out_all.at[across], heads_all.at[across], smalls_all.at[across]
    )
    start_all(across_y)

    half_z = []
    for got, low, w in ((own_pair[0], 1 - lo, hi), (came_pair[0], lo, 1 - hi)):
        got.wait_recv()
        piece = block(z, low, w, first)
        half_z += [net.copy(piece, piece, along("z", d)) for d in (1, 3, 2)]
    start_all(half_z)
    pair_late = []
    for i, d in enumerate((1, 3, 2)):
        at = (z + 4 - d) % 4
        for got, low, w in ((own_z[i], lo, hi), (came_z[i], 1 - lo, 1 - hi)):
            got.wait_recv()
            piece = block(at, low, w, second)
            late = net.copy(piece, piece, pair)
            late.start()
            pair_late.append(late)
    keep[0].wait()
    share = []
    for low, w in ((lo, hi), (1 - lo, 1 - hi)):
        piece = x_ref.at[:, low, core, w]
        share.append(net.copy(piece, piece, other_core))
    start_all(share)
    for copy in half_z + [own_pair[1], came_pair[1]] + pair_late:
        copy.wait_recv()
    rest = []
    for low, w in ((1 - lo, hi), (lo, 1 - hi)):
        piece = x_ref.at[:, low, core, w]
        rest.append(net.copy(piece, piece, other_core))
    start_all(rest)
    wait_all(keep[1:])
    meta_wait()
    wait_all(own_y + across_y + share + rest)
    for copy in [swap] + own_pair + own_z + came_pair + came_z + half_z + pair_late + cross_early + cross_late:
        copy.wait_send()


def front(tokens, segments, flags, vectors, b_up, w_out, w_up, w_down, w_qkv):
    shape = jax.ShapeDtypeStruct
    in_vmem = pl.BlockSpec(memory_space=pltpu.VMEM)
    return pl.pallas_call(
        front_kernel,
        in_specs=[ANY] + [in_vmem] * 4 + [ANY] * 4,
        out_specs=[ANY] * 8,
        out_shape=[
            shape((4, 2, 2, 2, TB, D), BF),
            shape((NB, 8, TB), jnp.int32),
            shape((8, 128, 384), BF),
            shape((8, 16, 128), F32),
            shape((8, 128, D), BF),
            shape((8, 128, 2048), BF),
            shape((8, 256, D), BF),
            shape((8, 128, 3 * D), BF),
        ],
        scratch_shapes=[
            pltpu.VMEM((2, TB, D), BF),
            pltpu.VMEM((128, D), BF),
            pltpu.VMEM((2, 128, 2048), BF),
            pltpu.VMEM((256, D), BF),
            pltpu.VMEM((128, 3 * D), BF),
            pltpu.VMEM((2, 8, TB), jnp.int32),
            pltpu.VMEM((2, 128, 384), BF),
            pltpu.VMEM((16, 128), F32),
            pltpu.SemaphoreType.DMA((FRONT_COPIES,)),
            pltpu.SemaphoreType.DMA((FRONT_COPIES,)),
            pltpu.SemaphoreType.DMA((12,)),
            *swap_sems(),
        ],
        name="front_gather",
        compiler_params=pltpu.CompilerParams(
            collective_id=1, has_side_effects=True, vmem_limit_bytes=VMEM_CAP
        ),
    )(tokens, segments, flags, vectors, b_up, w_out, w_up, w_down, w_qkv)


def weights_second(up_all, down_all, out_all, qkv_all, net):
    x, y, z, core = place()
    hi, lo = x // 2, x % 2
    pair, wrap = device_at(hi * 2 + 1 - lo, y, z, core), device_at(3 - x, y, z, core)
    wholes = (up_all, down_all)
    copies = []
    for m in range(2):
        piece = wholes[m].at[:, unit_rows(m, 3), columns_part(m, lo, 2)]
        copies.append(net.copy(piece, piece, pair))
        for d in (1, 3, 2):
            for w in range(2):
                piece = wholes[m].at[y * 2 + w, unit_rows(m, 2)]
                copies.append(net.copy(piece, piece, along("y", d)))
            piece = wholes[m].at[:, unit_rows(m, 0), columns_part(m, z, 4)]
            copies.append(net.copy(piece, piece, along("z", d)))
    piece = out_all.at[:, half_rows(core)]
    copies.append(net.copy(piece, piece, sibling()))
    piece = qkv_all.at[y * 2 + hi, half_rows(core)]
    copies.append(net.copy(piece, piece, wrap))
    return copies


def attend_send_kernel(key_rows, *refs):
    inputs, outputs, wholes, sems = refs[:3], refs[7:10], refs[10:14], refs[14:]
    step = pl.program_id(0)

    def copies():
        return weights_second(*wholes, Transfers(*sems))

    @pl.when(step == 0)
    def _():
        greet(ring_partners())
        start_all(copies())

    attend_kernel(key_rows, *inputs, *outputs)

    @pl.when(step == pl.num_programs(0) - 1)
    def _():
        wait_all(copies())


def attend_send(qat, ka, vat, weights, width=1024, key_rows=512):
    shape = jax.ShapeDtypeStruct
    return pl.pallas_call(
        functools.partial(attend_send_kernel, key_rows),
        grid=(L // width,),
        in_specs=[
            pl.BlockSpec((128, width), lambda i: (0, i)),
            pl.BlockSpec((L, 128), lambda i: (0, 0)),
            pl.BlockSpec((80, L), lambda i: (0, 0)),
        ]
        + [ANY] * 4,
        out_specs=[
            pl.BlockSpec((width // TB, HD, TB), lambda i: (i, 0, 0)),
            pl.BlockSpec((HD, width), lambda i: (0, i)),
            pl.BlockSpec((1, width), lambda i: (0, i)),
        ]
        + [ANY] * 4,
        out_shape=[shape((NB, HD, TB), BF), shape((HD, L), F32), shape((1, L), F32)]
        + [shape(w.shape, w.dtype) for w in weights],
        input_output_aliases={3: 3, 4: 4, 5: 5, 6: 6},
        scratch_shapes=[pltpu.SemaphoreType.DMA((24,)), pltpu.SemaphoreType.DMA((24,))],
        name="attend",
        compiler_params=pltpu.CompilerParams(
            collective_id=2, has_side_effects=True, vmem_limit_bytes=VMEM_CAP
        ),
    )(qat, ka, vat, *weights)


def qkv_along_y(qkv_all, net):
    _, y, _, core = place()
    copies = []
    for d in (1, 3, 2):
        for w in range(2):
            piece = qkv_all.at[y * 2 + w, half_rows(core)]
            copies.append(net.copy(piece, piece, along("y", d)))
    return copies


def turned(first, second):
    return dot(first, second, ((0,), (0,)))


def gelu_both(u):
    rate = 0.7978845608028654
    square = u * u
    curve = jnp.tanh(rate * (u + 0.044715 * (square * u)))
    half = 0.5 * (1.0 + curve)
    slope = half + 0.5 * u * (1.0 - curve * curve) * (rate * (1.0 + 0.134145 * square))
    return u * half, slope


def fold(values):
    return jnp.sum(values.reshape(values.shape[0] // 8, 8, values.shape[1]), axis=0)


ROWS = 256
CHUNK = 32
SMALLS = 16


def middle_kernel(
    blocks, meta, tokens, teacher, flags, smalls, out_all, up_all, down_all, a0,
    states, resid_out, do, g_ref, sums_out, count_out, qkv_all,
    context, context_s, w_out, w_up, w_down, h, act, slope, send_one, come_one, send_two, come_two,
    gb, gu, ga, ga_s, normed, hidden, rate, work, resid, gct, stage, count, counts, valid,
    send, recv, local, go_send, go_recv, go_local, back_send, back_recv, back_local,
):
    x, y, z, core = place()
    mine = y * 2 + x // 2
    twin = sibling()
    loads = [
        pltpu.make_async_copy(out_all, w_out, local.at[0]),
        pltpu.make_async_copy(up_all, w_up, local.at[1]),
        pltpu.make_async_copy(down_all, w_down, local.at[2]),
    ]
    start_all(loads)
    greet_all(shard_greet())
    net = Transfers(send, recv)
    go_start, go_wait = swap_copies(
        lambda b: blocks.at[b], lambda b: head_tile(context, b), (go_send, go_recv, go_local)
    )
    go_start()
    valid_here = jnp.sum(meta[:, 1, :].astype(F32), axis=0, keepdims=True)
    count[...] = jnp.broadcast_to(jnp.sum(valid_here, axis=1, keepdims=True), (8, 128))
    ahead = [net.copy(count, counts.at[mine], target) for target in shard_greet()]
    start_all(ahead)
    own_count = pltpu.make_async_copy(count, counts.at[mine], local.at[3])
    own_count.start()
    later = qkv_along_y(qkv_all, net)
    start_all(later)
    for s in range(2):
        column = jnp.broadcast_to(flags[s : s + 1, :].astype(F32), (128, 128)).T
        valid[128 * s : 128 * (s + 1), :] = column

    def vector(row):
        return jnp.concatenate([smalls[i, row : row + 1, :] for i in range(8)], axis=1)

    out_bias, gain_one, offset_one, down_bias, gain_two, offset_two = [vector(row) for row in range(2, 8)]
    zeros = jnp.zeros((8, D), F32)
    go_wait()
    give_context = net.copy(context, context_s, twin)
    give_context.start()
    wait_all(loads)
    work[...] = turned(context[...], w_out[...].reshape(D, D))

    @pl.loop(0, ROWS // CHUNK)
    def _(i):
        rows = pl.ds(aligned(i * CHUNK, CHUNK), CHUNK)
        total = tokens[rows, :].astype(F32) + work[rows, :] + out_bias
        centre = total - jnp.mean(total, axis=1, keepdims=True)
        scale = lax.rsqrt(jnp.mean(centre * centre, axis=1, keepdims=True) + EPS)
        unit = centre * scale
        normed[rows, :] = unit
        rate[rows, :] = jnp.broadcast_to(scale, (CHUNK, 128))
        full = unit * gain_one + offset_one
        hidden[rows, :] = full
        h[0, rows, :] = full.astype(BF)

    give_hidden = net.copy(h.at[0], h.at[1], twin)
    give_hidden.start()
    for slot in range(2):
        if slot == 1:
            give_hidden.wait()
        for k in range(8):
            columns = slice(256 * k, 256 * (k + 1))
            bias = jnp.concatenate([smalls[k, pl.ds(8 + 2 * core + e, 1), :] for e in range(2)], axis=1)
            u = dot(h[slot], w_up[:, :, columns].reshape(D, 256)) + bias
            value, incline = gelu_both(u)
            act[slot, :, columns] = value.astype(BF)
            slope[slot, :, columns] = incline
    send_one[...] = dot(act[1], w_down[...].reshape(2048, D))
    give_one = net.copy(send_one, come_one, twin)
    give_one.start()
    work[...] = dot(act[0], w_down[...].reshape(2048, D))
    give_one.wait()
    wait_all(ahead)
    own_count.wait()
    total_count = jnp.sum(counts[...], axis=0)
    count_out[...] = total_count
    factor = (128 * ROWS) / total_count[:1, :1]

    def loss_rows(i, carried):
        rows = pl.ds(aligned(i * CHUNK, CHUNK), CHUNK)
        total = hidden[rows, :] + (work[rows, :] + come_one[rows, :] + down_bias)
        centre = total - jnp.mean(total, axis=1, keepdims=True)
        scale = lax.rsqrt(jnp.mean(centre * centre, axis=1, keepdims=True) + EPS)
        unit = centre * scale
        final = unit * gain_two + offset_two
        states[rows, :] = final.astype(BF)
        differ = final - teacher[rows, :].astype(F32)
        held = valid[rows, :1] * differ
        grad = factor * held
        weighted = grad * gain_two
        back = weighted - jnp.mean(weighted, axis=1, keepdims=True)
        back = scale * (back - unit * jnp.mean(weighted * unit, axis=1, keepdims=True))
        resid[rows, :] = back
        low = back.astype(BF)
        gb[0, rows, :] = low
        return (
            carried[0] + fold(grad * unit),
            carried[1] + fold(grad),
            carried[2] + fold(low.astype(F32)),
            carried[3] + fold(held * differ),
        )

    gain_two_sum, offset_two_sum, down_sum, error = lax.fori_loop(
        0, ROWS // CHUNK, loss_rows, (zeros, zeros, zeros, zeros)
    )
    give_branch = net.copy(gb.at[0], gb.at[1], twin)
    give_branch.start()
    up_sums = []
    for slot in range(2):
        if slot == 1:
            give_branch.wait()
        for k in range(8):
            columns = slice(256 * k, 256 * (k + 1))
            pulled = dot(gb[slot], w_down[k], ((1,), (1,))) * slope[slot, :, columns]
            low = pulled.astype(BF)
            gu[slot, :, columns] = low
            up_sums.append(fold(low.astype(F32)))
    for i in range(8):
        send_two[:, 128 * i : 128 * (i + 1)] = dot(gu[1], w_up[i], ((1,), (1,)))
    give_two = net.copy(send_two, come_two, twin)
    give_two.start()
    for i in range(8):
        work[:, 128 * i : 128 * (i + 1)] = dot(gu[0], w_up[i], ((1,), (1,)))
    give_two.wait()

    def first_norm_rows(i, carried):
        rows = pl.ds(aligned(i * CHUNK, CHUNK), CHUNK)
        grad = resid[rows, :] + (work[rows, :] + come_two[rows, :])
        unit = normed[rows, :]
        weighted = grad * gain_one
        back = weighted - jnp.mean(weighted, axis=1, keepdims=True)
        back = rate[rows, :1] * (back - unit * jnp.mean(weighted * unit, axis=1, keepdims=True))
        resid_out[rows, :] = back
        low = back.astype(BF)
        ga[rows, :] = low
        return (carried[0] + fold(grad * unit), carried[1] + fold(grad), carried[2] + fold(low.astype(F32)))

    gain_one_sum, offset_one_sum, out_sum = lax.fori_loop(0, ROWS // CHUNK, first_norm_rows, (zeros, zeros, zeros))
    give_attended = net.copy(ga.at[:, pl.ds(aligned((1 - core) * 512, 512), 512)], ga_s, twin)
    give_attended.start()
    gct[...] = dot(w_out[...].reshape(D, D), ga[...], ((1,), (1,))).astype(BF)
    back_start, back_wait = swap_copies(
        lambda b: head_tile(gct, b), lambda b: do.at[b], (back_send, back_recv, back_local)
    )
    back_start()

    error = jnp.broadcast_to(jnp.sum(jnp.sum(error, axis=0, keepdims=True), axis=1, keepdims=True), (1, 128))
    lines = [out_sum, gain_one_sum, offset_one_sum, down_sum, gain_two_sum, offset_two_sum]
    lines = [jnp.sum(line, axis=0, keepdims=True) for line in lines]
    for i in range(8):
        columns = slice(128 * i, 128 * (i + 1))
        sums_out[i] = jnp.zeros((SMALLS, 128), F32)
        for row, line in enumerate(lines):
            sums_out[i, row : row + 1, :] = line[:, columns]
        both = jnp.sum(up_sums[i] + up_sums[8 + i], axis=0, keepdims=True)
        for e in range(2):
            sums_out[i, pl.ds(6 + 2 * core + e, 1), :] = both[:, 128 * e : 128 * (e + 1)]
        sums_out[i, 10:11, :] = error

    give_context.wait()
    give_attended.wait()

    def stored(i):
        return pltpu.make_async_copy(stage.at[i % 2], g_ref.at[i // 2, i % 2], local.at[4 + i % 2])

    for i in range(8):
        if i >= 2:
            stored(i - 2).wait()
        tall = slice(128 * i, 128 * (i + 1))
        wide = slice(256 * i, 256 * (i + 1))
        up = turned(h[0, :, tall], gu[0]) + turned(h[1, :, tall], gu[1])
        for k in range(4):
            stage[i % 2, 128 * k : 128 * (k + 1), :] = up[:, 512 * k : 512 * (k + 1)].astype(BF)
        down = turned(act[0, :, wide], gb[0]) + turned(act[1, :, wide], gb[1])
        for k in range(2):
            stage[i % 2, 512 + 256 * k : 768 + 256 * k, :] = down[:, 512 * k : 512 * (k + 1)].astype(BF)
        own_half = ga[:, pl.ds(aligned(core * 512, 512), 512)]
        out = dot(context[tall, :], own_half) + dot(context_s[tall, :], ga_s[...])
        stage[i % 2, 1024:, :] = out.astype(BF)
        stored(i).start()
    stored(6).wait()
    stored(7).wait()
    back_wait()
    wait_all(later)


def middle(blocks, meta, tokens, teacher, flags, smalls, out_all, up_all, down_all, qkv_all):
    shape = jax.ShapeDtypeStruct
    in_vmem = pl.BlockSpec(memory_space=pltpu.VMEM)
    dma = pltpu.SemaphoreType.DMA
    wide = pltpu.VMEM((ROWS, D), F32)
    return pl.pallas_call(
        middle_kernel,
        in_specs=[ANY] + [in_vmem] * 5 + [ANY] * 4,
        out_specs=[in_vmem, in_vmem, ANY, ANY, in_vmem, in_vmem, ANY],
        out_shape=[
            shape((ROWS, D), BF),
            shape((ROWS, D), F32),
            shape((NB, HD, TB), BF),
            shape((4, 2, 1152, 512), BF),
            shape((8, SMALLS, 128), F32),
            shape((8, 128), F32),
            shape(qkv_all.shape, BF),
        ],
        input_output_aliases={9: 6},
        scratch_shapes=[
            pltpu.VMEM((D, ROWS), BF),
            pltpu.VMEM((D, ROWS), BF),
            pltpu.VMEM((8, 128, D), BF),
            pltpu.VMEM((8, 128, 2048), BF),
            pltpu.VMEM((8, 256, D), BF),
            pltpu.VMEM((2, ROWS, D), BF),
            pltpu.VMEM((2, ROWS, 2048), BF),
            pltpu.VMEM((2, ROWS, 2048), F32),
            wide,
            wide,
            wide,
            wide,
            pltpu.VMEM((2, ROWS, D), BF),
            pltpu.VMEM((2, ROWS, 2048), BF),
            pltpu.VMEM((ROWS, D), BF),
            pltpu.VMEM((ROWS, 512), BF),
            wide,
            wide,
            pltpu.VMEM((ROWS, 128), F32),
            wide,
            wide,
            pltpu.VMEM((D, ROWS), BF),
            pltpu.VMEM((2, 1152, 512), BF),
            pltpu.VMEM((8, 128), F32),
            pltpu.VMEM((8, 8, 128), F32),
            pltpu.VMEM((ROWS, 128), F32),
            dma((24,)),
            dma((24,)),
            dma((8,)),
            *swap_sems(),
            *swap_sems(),
        ],
        name="middle",
        compiler_params=pltpu.CompilerParams(
            collective_id=3, has_side_effects=True, vmem_limit_bytes=VMEM_CAP
        ),
    )(blocks, meta, tokens, teacher, flags, smalls, out_all, up_all, down_all, qkv_all)


BACK_KEYS = 512
BACK_STEPS = L // BACK_KEYS
BACK_WIDTH = 1024


def back_kernel(
    qat, ka, va, kt, q8, do, wide, lse, smalls, x_seq, g_ref, a0,
    projected, heads_out, shard_out, smalls_out, qkv_all,
    x_buf, queries, grads, grad_rows, dq, d_ref, mine_ref, parts_ref, sum_ref, heads_buf, small_buf, small_sum, small_all,
    send, recv, local, dk_send, dk_recv, dk_local, dq_send, dq_recv, dq_local, spread_send, spread_recv, *reduce_refs,
):
    x, y, z, core = place()
    shard_at = y * 2 + x // 2
    seq = lax.axis_index("seq")
    mine = seq * 2 + x // 2
    net = (g_ref,) + reduce_refs

    def shard_device(d):
        other = (shard_at + d) % 8
        return other, (other // 2, seq, other % 2)

    load_x = pltpu.make_async_copy(x_seq, x_buf, local.at[0])
    load_x.start()
    greet_all([shard_device(d)[1] for d in range(1, 8)])
    for part in range(3):
        reduce_start(part, net)
    far = Transfers(send, recv)
    small_out = [far.copy(smalls.at[shard_device(d)[0]], small_buf.at[shard_at], shard_device(d)[1]) for d in range(1, 8)]
    start_all(small_out)
    small_buf[shard_at] = smalls[shard_at]
    rows = half_rows(core)
    weights = far.copy(qkv_all.at[:, rows], qkv_all.at[:, rows], sibling())
    weights.start()

    for j in range(L // BACK_WIDTH):
        columns = slice(j * BACK_WIDTH, (j + 1) * BACK_WIDTH)
        grad_t = jnp.concatenate([do[j * (BACK_WIDTH // TB) + i] for i in range(BACK_WIDTH // TB)], axis=1)
        wider = grad_t.astype(F32)
        delta = jnp.sum(wider * wide[:, columns], axis=0, keepdims=True)
        grads[:HD, columns] = grad_t
        grads[HD:, columns] = jnp.concatenate([three_pieces(-delta), jnp.zeros((61, BACK_WIDTH), BF)], axis=0)
        queries[:96, columns] = qat[:96, columns]
        queries[96:, columns] = jnp.concatenate(
            [three_pieces(-lse[:, columns]), jnp.zeros((29, BACK_WIDTH), BF)], axis=0
        )
        grad_rows[columns, :] = wider.T.astype(BF)
    dq[...] = jnp.zeros_like(dq)

    def landing(first, count):
        return projected.at[pl.ds(first, count), pl.ds(aligned(seq * HD, HD), HD), pl.ds(aligned((x // 2) * TB, TB), TB)]

    def block_device(b):
        return (y, b // 2, b % 2)

    def dk_copy(b, recv_at):
        return remote(d_ref.at[b, pl.ds(1, 2)], landing(1, 2), dk_send.at[b], dk_recv.at[recv_at], block_device(b))

    def dq_copy(b, recv_at):
        return remote(d_ref.at[b, pl.ds(0, 1)], landing(0, 1), dq_send.at[b], dq_recv.at[recv_at], block_device(b))

    dk_own = pltpu.make_async_copy(d_ref.at[mine, pl.ds(1, 2)], landing(1, 2), dk_local)
    dq_own = pltpu.make_async_copy(d_ref.at[mine, pl.ds(0, 1)], landing(0, 1), dq_local)

    @pl.loop(0, BACK_STEPS)
    def _(step):
        at = (step + seq) % BACK_STEPS
        keys = pl.ds(aligned(at * BACK_KEYS, BACK_KEYS), BACK_KEYS)
        ka_part, va_part, kt_part = ka[keys, :], va[keys, :], kt[:, keys]
        dk = jnp.zeros((BACK_KEYS, HD), F32)
        dv = jnp.zeros((BACK_KEYS, HD), F32)
        for j in range(L // BACK_WIDTH):
            columns = slice(j * BACK_WIDTH, (j + 1) * BACK_WIDTH)
            probs = jnp.exp(dot(ka_part, queries[:, columns]))
            raw = (probs * dot(va_part, grads[:, columns])).astype(BF)
            dv = dv + dot(probs.astype(BF), grad_rows[columns, :])
            dk = dk + dot(raw, q8[columns, :])
            dq[:, columns] += dot(kt_part, raw)
        dk_t, dv_t = dk.T.astype(BF), dv.T.astype(BF)
        for i in range(BACK_KEYS // TB):
            b = at * (BACK_KEYS // TB) + i
            d_ref[b, 1] = dk_t[:, i * TB : (i + 1) * TB]
            d_ref[b, 2] = dv_t[:, i * TB : (i + 1) * TB]

            @pl.when(b != mine)
            def _():
                dk_copy(b, mine).start()

            @pl.when(b == mine)
            def _():
                dk_own.start()

        @pl.when(step == BACK_STEPS - 3)
        def _():
            reduce_step(0, 1, net)

        @pl.when(step == BACK_STEPS - 2)
        def _():
            reduce_step(0, 2, net)

    for b in range(NB):
        d_ref[b, 0] = (dq[:, b * TB : (b + 1) * TB] * 0.125).astype(BF)

    @pl.loop(1, NB)
    def _(shift):
        dq_copy((mine + shift) % NB, mine).start()

    dq_own.start()
    reduce_step(0, 0, net)
    reduce_step(1, 1, net)
    reduce_step(1, 2, net)
    wait_all(small_out)
    small_sum[...] = jnp.sum(small_buf[...], axis=0)

    load_x.wait()
    left = jnp.concatenate([d_ref[b].reshape(3 * HD, TB) for b in range(NB)], axis=1)
    sums = dot(jnp.ones((8, L), BF), left, ((1,), (1,)))
    gap = jnp.zeros((1, 128 - HD), F32)
    tail = jnp.concatenate(
        [
            jnp.concatenate([sums[:1, :HD], gap], axis=1),
            jnp.concatenate([sums[:1, 2 * HD :], gap], axis=1),
            jnp.zeros((14, 128), F32),
        ],
        axis=0,
    ).astype(BF)
    for i in range(4):
        total = dot(left, x_buf[:, :, 256 * i : 256 * (i + 1)].reshape(L, 256))
        for k in range(2):
            mine_ref[2 * i + k, : 3 * HD, :] = total[:, 128 * k : 128 * (k + 1)].astype(BF)
            mine_ref[2 * i + k, 3 * HD :, :] = tail
    part_out = [far.copy(mine_ref.at[shard_device(d)[0]], parts_ref.at[d], shard_device(d)[1]) for d in range(1, 8)]
    start_all(part_out)

    steps = [spread_steps(part, reduce_refs[6 + part].at[0], (local.at[pl.ds(1, 3)], spread_send, spread_recv), shard_out) for part in range(3)]
    for part in (1, 2, 0):
        if part == 0:
            reduce_step(1, 0, net)
        reduce_step(2, part, net)
        steps[part][0]()
    wait_all(part_out)
    added = mine_ref[shard_at].astype(F32)
    for d in range(1, 8):
        added = added + parts_ref[d].astype(F32)
    sum_ref[...] = added.astype(BF)
    heads_buf[seq // 2, core] = sum_ref[...]
    small_all[seq // 2, core] = small_sum[...]
    head_out = []
    for d in range(1, 8):
        target = (y, (seq + 2 * d) % 16, x // 2)
        head_out.append(far.copy(sum_ref, heads_buf.at[seq // 2, core], target))
        head_out.append(far.copy(small_sum, small_all.at[seq // 2, core], target))
    start_all(head_out)
    for part in (1, 2, 0):
        steps[part][1]()
    wait_all(head_out)
    across = [
        far.copy(heads_buf.at[:, core], heads_buf.at[:, core], sibling()),
        far.copy(small_all.at[:, core], small_all.at[:, core], sibling()),
    ]
    start_all(across)
    for part in (1, 2, 0):
        steps[part][2]()
    shared = far.copy(shard_out.at[core], shard_out.at[core], sibling())
    shared.start()

    @pl.loop(1, NB)
    def _(shift):
        b = (mine + shift) % NB
        dk_copy(b, b).wait()
        dq_copy(b, b).wait()

    dk_own.wait()
    dq_own.wait()
    weights.wait()
    wait_all(across)
    for i in range(8):
        heads_out[2 * i] = heads_buf[i, 0]
        heads_out[2 * i + 1] = heads_buf[i, 1]
    smalls_out[...] = jnp.sum(small_all[...].reshape(16, 16, 128), axis=0)
    shared.wait()


def back(qat, ka, va, kt, q8, do, wide, lse, smalls, x_seq, g, qkv_all):
    shape = jax.ShapeDtypeStruct
    in_vmem = pl.BlockSpec(memory_space=pltpu.VMEM)
    dma = pltpu.SemaphoreType.DMA
    return pl.pallas_call(
        back_kernel,
        in_specs=[in_vmem] * 9 + [ANY] * 3,
        out_specs=[ANY, in_vmem, ANY, in_vmem, ANY],
        out_shape=[
            shape((3, D, 2 * TB), BF),
            shape((H, 208, 128), BF),
            shape((2, 1152, 512), BF),
            shape((16, 128), F32),
            shape(qkv_all.shape, BF),
        ],
        input_output_aliases={11: 4},
        scratch_shapes=[
            pltpu.VMEM((NB, TB, D), BF),
            pltpu.VMEM((128, L), BF),
            pltpu.VMEM((128, L), BF),
            pltpu.VMEM((L, HD), BF),
            pltpu.VMEM((HD, L), F32),
            pltpu.VMEM((NB, 3, HD, TB), BF),
            pltpu.VMEM((8, 208, 128), BF),
            pltpu.VMEM((8, 208, 128), BF),
            pltpu.VMEM((208, 128), BF),
            pltpu.VMEM((8, 2, 208, 128), BF),
            pltpu.VMEM((8, 16, 128), F32),
            pltpu.VMEM((16, 128), F32),
            pltpu.VMEM((8, 2, 16, 128), F32),
            dma((40,)),
            dma((40,)),
            dma((4,)),
            *swap_sems(),
            *swap_sems(),
            dma((3, 8)),
            dma((3, 8)),
            *reduce_scratch(),
        ],
        name="attend_back",
        compiler_params=pltpu.CompilerParams(
            collective_id=4, has_side_effects=True, vmem_limit_bytes=VMEM_CAP
        ),
    )(qat, ka, va, kt, q8, do, wide, lse, smalls, x_seq, g, qkv_all)


def finish_kernel(
    projected, qkv_ref, resid_ref, heads_ref, shard_ref, tokens_ref, grad_qkv, grad_out, grad_up, grad_down
):
    step = pl.program_id(0)
    tokens_ref[...] = resid_ref[...] + dot(projected[...], qkv_ref[...], ((0,), (1,)))
    for c in range(2):
        columns = slice(512 * c, 512 * (c + 1))
        for j in range(2):
            piece = shard_ref[c, pl.ds(aligned(step * 128, 128), 128), 256 * j : 256 * (j + 1)]
            grad_up[:, 512 * j + 256 * c : 512 * j + 256 * (c + 1)] = piece.astype(F32)
        rows = pl.ds(aligned(512 + 256 * c + (step % 2) * 128, 128), 128)
        grad_down[:, columns] = shard_ref[step // 2, rows, :].astype(F32)
        grad_out[:, columns] = shard_ref[c, pl.ds(aligned(1024 + step * 32, 32), 32), :].astype(F32)

    @pl.when(step == 0)
    def _():
        for p in range(3):
            for pair in range(8):
                both = [heads_ref[2 * pair + k, p * HD : (p + 1) * HD, :].astype(F32) for k in range(2)]
                at = p * D + pair * 128
                grad_qkv[:, at : at + 128] = jnp.concatenate(both, axis=0).T


def finish(projected, qkv, resid, heads, shard):
    shape = jax.ShapeDtypeStruct

    def whole(dims):
        return pl.BlockSpec(dims, lambda i: (0,) * len(dims))

    return pl.pallas_call(
        finish_kernel,
        grid=(4,),
        in_specs=[
            whole((3 * D, 2 * TB)),
            pl.BlockSpec((256, 3 * D), lambda i: (i, 0)),
            pl.BlockSpec((2 * TB, 256), lambda i: (0, i)),
            whole((H, 208, 128)),
            whole((2, 1152, 512)),
        ],
        out_specs=[
            pl.BlockSpec((2 * TB, 256), lambda i: (0, i)),
            whole((128, 3 * D)),
            pl.BlockSpec((32, D), lambda i: (i, 0)),
            pl.BlockSpec((128, 1024), lambda i: (0, i)),
            pl.BlockSpec((128, D), lambda i: (i, 0)),
        ],
        out_shape=[
            shape((2 * TB, D), F32),
            shape((128, 3 * D), F32),
            shape((128, D), F32),
            shape((128, FF), F32),
            shape((512, D), F32),
        ],
        name="finish",
        compiler_params=pltpu.CompilerParams(vmem_limit_bytes=VMEM_CAP),
    )(projected, qkv, resid, heads, shard)


def on_device(
    tokens,
    segments,
    valid_flags,
    teacher,
    w_qkv,
    b_query,
    b_value,
    w_out,
    b_out,
    ln1_gain,
    ln1_bias,
    w_up,
    b_up,
    w_down,
    b_down,
    ln2_gain,
    ln2_bias,
):
    seq_local, row_local, _ = tokens.shape
    token_rows = seq_local * row_local
    shard_at = lax.axis_index("dp") * 2 + lax.axis_index("wshard")

    vectors = jnp.stack([b_query, b_value, b_out, ln1_gain, ln1_bias, b_down, ln2_gain, ln2_bias]).astype(F32)
    x_seq, meta_all, heads_all, smalls_all, out_all, up_all, down_all, qkv_all = front(
        tokens, segments, valid_flags, vectors, b_up.reshape(4, 128).astype(F32), w_out, w_up, w_down, w_qkv
    )
    x_seq = x_seq.reshape(NB, TB, D)
    qat, ka, vat, va, kt, q8 = project(x_seq.reshape(L, D), heads_all.reshape(D, 384), smalls_all, meta_all)
    blocks, wide, lse, up_all, down_all, out_all, qkv_all = attend_send(
        qat, ka, vat, (up_all, down_all, out_all, qkv_all)
    )
    states, grad_resid_one, do, g, small_sums, count, qkv_all = middle(
        blocks,
        meta_all,
        tokens.reshape(token_rows, D),
        teacher.reshape(token_rows, D),
        valid_flags,
        smalls_all,
        out_all,
        up_all,
        down_all,
        qkv_all,
    )
    projected, heads_out, shard_out, small_out, qkv_all = back(
        qat, ka, va, kt, q8, do, wide, lse, small_sums, x_seq, g, qkv_all
    )
    grad_tokens, grad_qkv, grad_out, grad_up, grad_down = finish(
        projected.reshape(3 * D, token_rows), qkv_all.reshape(D, 3 * D), grad_resid_one, heads_out, shard_out
    )
    own_heads = lax.dynamic_slice(heads_out, (shard_at * 2, 3 * HD, 0), (2, 2, HD)).astype(F32)
    mean_loss = small_out[10, 0] / (D * count[0, 0])
    return (
        states.reshape(seq_local, row_local, D),
        mean_loss,
        grad_tokens.reshape(seq_local, row_local, D),
        grad_qkv,
        own_heads[:, 0].reshape(128),
        own_heads[:, 1].reshape(128),
        grad_out,
        small_out[0],
        small_out[1],
        small_out[2],
        grad_up,
        small_out[6:10].reshape(512),
        grad_down,
        small_out[3],
        small_out[4],
        small_out[5],
    )


def solution(mesh):
    rows = P("dp", ("seq", "wshard"), None)
    flags = P("dp", ("seq", "wshard"))
    matrix = P(("dp", "wshard"), None)
    vector = P(("dp", "wshard"))
    return jax.shard_map(
        on_device,
        mesh=mesh,
        in_specs=(
            rows,
            flags,
            flags,
            rows,
            matrix,
            vector,
            vector,
            matrix,
            vector,
            vector,
            vector,
            matrix,
            vector,
            matrix,
            vector,
            vector,
            vector,
        ),
        out_specs=(
            rows,
            P(),
            rows,
            matrix,
            vector,
            vector,
            matrix,
            vector,
            vector,
            vector,
            matrix,
            vector,
            matrix,
            vector,
            vector,
            vector,
        ),
        check_vma=False,
    )
```

```python
import functools

import jax
import jax.numpy as jnp
from jax import lax
from jax.experimental import pallas as pl
from jax.experimental.pallas import tpu as pltpu
from jax.sharding import PartitionSpec as P

D = 1024
H = 16
HD = 64
FF = 4096
L = 4096
EPS = 1e-06
F32 = jnp.float32
BF = jnp.bfloat16
MASKED = 1000000000.0
VMEM_CAP = 60 * 1024 * 1024
MESH = pl.DeviceIdType.MESH
ANY = pl.BlockSpec(memory_space=pl.ANY)
TB = 128
NB = L // TB


def dot(first, second, dims=((1,), (0,))):
    return lax.dot_general(first, second, (dims, ((), ())), preferred_element_type=F32)


def three_pieces(row):
    high = row.astype(BF)
    rest = row - high.astype(F32)
    middle = rest.astype(BF)
    lowest = (rest - middle.astype(F32)).astype(BF)
    return jnp.concatenate([high, middle, lowest], axis=0)


def place():
    at = lax.axis_index("seq")
    return (lax.axis_index("wshard") * 2 + (at // 2) % 2, lax.axis_index("dp"), at // 4, at % 2)


def device_at(x, y, z, core):
    return (y, (z * 2 + x % 2) * 2 + core, x // 2)


def along(axis, shift):
    x, y, z, core = place()
    if axis == "x":
        return device_at((x + shift) % 4, y, z, core)
    if axis == "y":
        return device_at(x, (y + shift) % 4, z, core)
    return device_at(x, y, (z + shift) % 4, core)


def sibling():
    x, y, z, core = place()
    return device_at(x, y, z, 1 - core)


def greet(partners):
    barrier = pltpu.get_barrier_semaphore()
    for partner in partners:
        pl.semaphore_signal(barrier, inc=1, device_id=partner, device_id_type=MESH)
    pl.semaphore_wait(barrier, len(partners))


def remote(src, dst, send_sem, recv_sem, target):
    return pltpu.make_async_remote_copy(
        src_ref=src, dst_ref=dst, send_sem=send_sem, recv_sem=recv_sem, device_id=target, device_id_type=MESH
    )


ORDERS = ("yzx", "zxy", "xyz")
PIECE = (64, 32, 48)
FIRST = (0, 512, 768)


def ring_partners():
    return [along(axis, shift) for axis in "xyz" for shift in (1, 2, 3)] + [sibling()]


def reduce_scratch():
    a, b, c = PIECE
    return [
        pltpu.VMEM((4, 2, 8 * a, 512), BF),
        pltpu.VMEM((4, 4, 2, 2 * b, 512), BF),
        pltpu.VMEM((4, 4, 4 * c, 512), BF),
        pltpu.VMEM((4, 2, 2 * a, 512), BF),
        pltpu.VMEM((4, 4, b, 512), BF),
        pltpu.VMEM((4, 4 * c, 512), BF),
        pltpu.VMEM((4, a, 512), BF),
        pltpu.VMEM((4, b, 512), BF),
        pltpu.VMEM((4, c, 512), BF),
        pltpu.SemaphoreType.DMA((3, 3, 3)),
        pltpu.SemaphoreType.DMA((3, 3, 3)),
        pltpu.SemaphoreType.DMA((3,)),
    ]


def aligned(value, unit):
    return pl.multiple_of(value, unit)


def reduce_piece(stage, part, refs, at):
    g_ref = refs[0]
    half, low, n = at // 2, at % 2, PIECE[part]
    if stage == 0:
        first = FIRST[part]
        if part == 0:
            return g_ref.at[at, :, pl.ds(first, 8 * n), :]
        if part == 1:
            return g_ref.at[:, :, pl.ds(aligned(first + at * 2 * n, 16), 2 * n), :]
        return g_ref.at[:, half, pl.ds(aligned(first + low * 4 * n, 16), 4 * n), :]
    held = refs[1 + 3 * (stage - 1) + part]
    if stage == 1:
        if part == 0:
            return held.at[0, :, pl.ds(aligned(at * 2 * n, 16), 2 * n), :]
        if part == 1:
            return held.at[0, :, half, pl.ds(aligned(low * n, 16), n), :]
        return held.at[0, at]
    if part == 0:
        return held.at[0, half, pl.ds(aligned(low * n, 16), n), :]
    if part == 1:
        return held.at[0, at]
    return held.at[0, pl.ds(aligned(at * n, 16), n), :]


def ring_at(axis):
    x, y, z, _ = place()
    return {"x": x, "y": y, "z": z}[axis]


def reduce_copies(stage, part, refs):
    send, recv = refs[10], refs[11]
    axis = ORDERS[part][stage]
    return [
        remote(
            reduce_piece(stage, part, refs, (ring_at(axis) + shift) % 4),
            refs[1 + 3 * stage + part].at[shift],
            send.at[stage, part, shift - 1],
            recv.at[stage, part, shift - 1],
            along(axis, shift),
        )
        for shift in (1, 3, 2)
    ]


def reduce_own(part, refs):
    return pltpu.make_async_copy(
        reduce_piece(0, part, refs, ring_at(ORDERS[part][0])), refs[1 + part].at[0], refs[12].at[part]
    )


def reduce_start(part, refs):
    start_all(reduce_copies(0, part, refs))
    reduce_own(part, refs).start()


def add_four(values):
    total = values[0].astype(F32) + values[1].astype(F32)
    return (total + values[2].astype(F32) + values[3].astype(F32)).astype(BF)


def reduce_step(stage, part, refs):
    a1, b1, c1, a2, b2, c2, a3, b3, c3 = refs[1:10]
    wait_all(reduce_copies(stage, part, refs))
    x, y, z, _ = place()
    n = PIECE[part]
    rest = (1, 2, 3)
    if stage == 0:
        reduce_own(part, refs).wait()

        @pl.loop(0, 16)
        def _(i):
            if part == 0:
                rows = pl.ds(aligned((i % 8) * n, 16), n)
                a1[0, i // 8, rows, :] = add_four([a1[s, i // 8, rows, :] for s in range(4)])
            elif part == 1:
                rows = pl.ds(aligned((i % 2) * n, 16), n)
                b1[0, i // 4, (i // 2) % 2, rows, :] = add_four([b1[s, i // 4, (i // 2) % 2, rows, :] for s in range(4)])
            else:
                rows = pl.ds(aligned((i % 4) * n, 16), n)
                c1[0, i // 4, rows, :] = add_four([c1[s, i // 4, rows, :] for s in range(4)])

    elif stage == 1:

        @pl.loop(0, 4)
        def _(i):
            if part == 0:
                rows = pl.ds(aligned((i % 2) * n, 16), n)
                own = a1[0, i // 2, pl.ds(aligned(z * 2 * n + (i % 2) * n, 16), n), :]
                a2[0, i // 2, rows, :] = add_four([own] + [a2[s, i // 2, rows, :] for s in rest])
            elif part == 1:
                own = b1[0, i, x // 2, pl.ds(aligned((x % 2) * n, 16), n), :]
                b2[0, i] = add_four([own] + [b2[s, i] for s in rest])
            else:
                rows = pl.ds(aligned(i * n, 16), n)
                own = c1[0, y, rows, :]
                c2[0, rows, :] = add_four([own] + [c2[s, rows, :] for s in rest])

    elif part == 0:
        own = a2[0, x // 2, pl.ds(aligned((x % 2) * n, 16), n), :]
        a3[0] = add_four([own] + [a3[s] for s in rest])
    elif part == 1:
        b3[0] = add_four([b2[0, y]] + [b3[s] for s in rest])
    else:
        own = c2[0, pl.ds(aligned(z * n, 16), n), :]
        c3[0] = add_four([own] + [c3[s] for s in rest])
    if stage < 2:
        start_all(reduce_copies(stage + 1, part, refs))


def shard_rows(o_ref, part, x_low, z, core):
    sub = x_low * 4 + z if part == 2 else z * 2 + x_low
    return o_ref.at[core, pl.ds(aligned(FIRST[part] + sub * PIECE[part], 16), PIECE[part]), :]


def spread_steps(part, mine, sems, o_ref):
    local, send, recv = sems
    x, y, z, core = place()
    low = x % 2
    pair = device_at(x // 2 * 2 + 1 - low, y, z, core)
    spot = shard_rows(o_ref, part, low, z, core)
    own = pltpu.make_async_copy(mine, spot, local.at[part])
    first = remote(mine, spot, send.at[part, 0], recv.at[part, 0], pair)
    second = [remote(mine, spot, send.at[part, d], recv.at[part, d], along("z", d)) for d in (1, 3, 2)]
    spot = shard_rows(o_ref, part, 1 - low, z, core)
    third = [remote(spot, spot, send.at[part, 3 + d], recv.at[part, 3 + d], along("z", d)) for d in (1, 3, 2)]

    def begin():
        start_all([own, first] + second)

    def middle():
        first.wait()
        start_all(third)

    def end():
        wait_all([own] + second + third)

    return begin, middle, end


def swap_partner(shift):
    mine = lax.axis_index("seq") * 2 + lax.axis_index("wshard")
    other = (mine + shift) % NB
    return other, (lax.axis_index("dp"), other // 2, other % 2)


def swap_greet():
    barrier = pltpu.get_barrier_semaphore()

    @pl.loop(1, NB)
    def _(shift):
        pl.semaphore_signal(barrier, inc=1, device_id=swap_partner(shift)[1], device_id_type=MESH)

    pl.semaphore_wait(barrier, NB - 1)


def swap_copies(piece_for, landing_from, sems):
    mine = lax.axis_index("seq") * 2 + lax.axis_index("wshard")
    send, recv, local = sems

    def copy(shift):
        other, device = swap_partner(shift)
        return remote(piece_for(other), landing_from(mine), send.at[shift], recv.at[shift], device)

    own = pltpu.make_async_copy(piece_for(mine), landing_from(mine), local)

    def start():
        @pl.loop(1, NB)
        def _(shift):
            copy(shift).start()

        own.start()

    def wait():
        @pl.loop(1, NB)
        def _(shift):
            copy(shift).wait()

        own.wait()

    return start, wait


def swap_sems():
    return [pltpu.SemaphoreType.DMA((NB,)), pltpu.SemaphoreType.DMA((NB,)), pltpu.SemaphoreType.DMA]


def block_of(ref, b):
    return ref.at[b]


def head_tile(ref, b):
    return ref.at[pl.ds(aligned((b // 2) * HD, HD), HD), pl.ds(aligned((b % 2) * TB, TB), TB)]


def head_tile3(ref, b):
    return ref.at[:, pl.ds(aligned((b // 2) * HD, HD), HD), pl.ds(aligned((b % 2) * TB, TB), TB)]


HALVES = ((128, 2048), (256, 1024))


class Transfers:
    def __init__(self, send, recv):
        self.send, self.recv, self.used = send, recv, 0

    def copy(self, src, dst, target):
        made = remote(src, dst, self.send.at[self.used], self.recv.at[self.used], target)
        self.used += 1
        return made


def start_all(copies):
    for copy in copies:
        copy.start()


def wait_all(copies):
    for copy in copies:
        copy.wait()


def unit_rows(matrix, unit, count=1):
    rows = HALVES[matrix][0] // 4
    return pl.ds(unit * rows, count * rows)


def columns_part(matrix, at, parts):
    width = HALVES[matrix][1] // parts
    return pl.ds(aligned(at * width, 128), width)


def half_rows(core, rows=64):
    return pl.ds(aligned(core * rows, rows), rows)


def shard_greet():
    x, y, z, core = place()
    return [device_at(x, (y + d) % 4, z, core) for d in (1, 2, 3)] + [
        device_at(3 - x, (y + d) % 4, z, core) for d in range(4)
    ]


def greet_all(others):
    barrier = pltpu.get_barrier_semaphore()

    @pl.loop(1, NB)
    def _(shift):
        pl.semaphore_signal(barrier, inc=1, device_id=swap_partner(shift)[1], device_id_type=MESH)

    for other in others:
        pl.semaphore_signal(barrier, inc=1, device_id=other, device_id_type=MESH)
    pl.semaphore_wait(barrier, NB - 1 + len(others))


FRONT_COPIES = 144


def front_kernel(
    tokens, segments, flags, vectors, b_up, w_out, w_up, w_down, w_qkv,
    x_seq, meta_out, smalls_out, out_all, up_all, down_all, qkv_all, qat_ref, ka_ref, va_ref, kt_ref, q_ref,
    context, wide_ref, lse_ref,
    vat_ref, blocks, x_buf, tok_buf, out_buf, up_buf, down_buf, qkv_buf, meta, heads, smalls, meta_all, heads_all, smalls_all, w_ref, b_ref,
    send, recv, local, meta_send, meta_recv, meta_local, back_send, back_recv, back_local,
):
    x, y, z, core = place()
    hi, lo = x // 2, x % 2
    mine, across = y * 2 + hi, y * 2 + 1 - hi
    wrap, pair, other_core = device_at(3 - x, y, z, core), device_at(hi * 2 + 1 - lo, y, z, core), sibling()
    shards, wholes = (up_buf.at[core], down_buf), (up_all, down_all)
    rows_out = half_rows(core)
    load_tokens = pltpu.make_async_copy(tokens, tok_buf, local.at[0])
    load_qkv = pltpu.make_async_copy(w_qkv, qkv_buf, local.at[11])
    loads = [
        pltpu.make_async_copy(w_out, out_buf, local.at[9]),
        pltpu.make_async_copy(w_down.at[half_rows(core, 256)], down_buf, local.at[10]),
    ]
    for j in range(8):
        piece = w_up.at[:, pl.ds(aligned(j * 512 + core * 256, 256), 256)]
        loads.append(pltpu.make_async_copy(piece, up_buf.at[core, :, pl.ds(j * 256, 256)], local.at[1 + j]))
    start_all([load_tokens, load_qkv] + loads)
    meta[...] = jnp.zeros_like(meta)
    for s in range(2):
        meta[s, 0:1, :] = segments[s : s + 1, :]
        meta[s, 1:2, :] = flags[s : s + 1, :]
    smalls[...] = jnp.zeros_like(smalls)
    smalls[0:8, :] = vectors[...]
    smalls[8:12, :] = b_up[...]
    greet_all(shard_greet())
    load_tokens.wait()
    net = Transfers(send, recv)
    first, second = pl.ds(0, 64), pl.ds(64, 64)

    def block(at, low, w, rows=slice(None)):
        return x_buf.at[at, low, core, w, rows]

    own = tok_buf.at[hi]
    swap = net.copy(tok_buf.at[1 - hi], block(z, lo, hi), wrap)
    own_z = [net.copy(own, block(z, lo, hi), along("z", d)) for d in (1, 3, 2)]
    own_pair = [net.copy(own.at[rows], block(z, lo, hi, rows), pair) for rows in (first, second)]
    start_all([swap, own_pair[0]] + own_z)
    x_buf[z, lo, core, hi] = tok_buf[hi]
    load_qkv.wait()
    for p in range(3):
        for k, pair_at in ((0, z * 2 + lo), (1, z * 2 + 1 - lo)):
            heads[k, :, 128 * p : 128 * (p + 1)] = qkv_buf[:, pl.ds(aligned(p * D + pair_at * 128, 128), 128)]
    cross_first = [
        net.copy(heads.at[1], heads_all.at[mine], wrap),
        net.copy(smalls, smalls_all.at[mine], wrap),
    ]
    start_all(cross_first)

    def small_y(shard, heads_source, smalls_source):
        copies = []
        for d in (1, 3, 2):
            copies.append(net.copy(heads_source, heads_all.at[shard], along("y", d)))
            copies.append(net.copy(smalls_source, smalls_all.at[shard], along("y", d)))
        return copies

    own_small = small_y(mine, heads.at[0], smalls)
    start_all(own_small)
    heads_all[mine] = heads[0]
    smalls_all[mine] = smalls[...]
    meta_start, meta_wait = swap_copies(
        lambda b: meta.at[b % 2], lambda b: meta_all.at[b], (meta_send, meta_recv, meta_local)
    )
    meta_start()
    wait_all(loads)
    keep = [
        pltpu.make_async_copy(out_buf.at[rows_out], out_all.at[mine, rows_out], local.at[9]),
        pltpu.make_async_copy(qkv_buf, qkv_all.at[mine], local.at[11]),
    ]
    for m in range(2):
        parts = [
            (unit_rows(m, 0), columns_part(m, z, 4)),
            (unit_rows(m, 3), columns_part(m, lo, 2)),
            (unit_rows(m, 1, 2), slice(None)),
        ]
        for k, (rows, columns) in enumerate(parts):
            piece = wholes[m].at[mine, rows, columns]
            keep.append(pltpu.make_async_copy(shards[m].at[rows, columns], piece, local.at[1 + 3 * m + k]))
    start_all(keep)

    def along_y(shard, source, out_source, up_unit):
        copies = []
        for d in (1, 3, 2):
            there = along("y", d)
            copies.append(net.copy(out_source.at[rows_out], out_all.at[shard, rows_out], there))
            for m in range(2):
                parts = [(0, columns_part(m, z, 4)), (3, columns_part(m, lo, 2))]
                for unit, columns in parts + ([(1, slice(None))] if up_unit and m == 0 else []):
                    rows = unit_rows(m, unit)
                    copies.append(net.copy(source(m).at[rows, columns], wholes[m].at[shard, rows, columns], there))
        return copies

    own_y = along_y(mine, lambda m: shards[m], out_buf, True)
    start_all(own_y)
    swap.wait_recv()
    came = block(z, 1 - lo, 1 - hi)
    came_pair = [
        net.copy(block(z, 1 - lo, 1 - hi, rows), block(z, 1 - lo, 1 - hi, rows), pair) for rows in (first, second)
    ]
    came_z = [net.copy(came, came, along("z", d)) for d in (1, 3, 2)]
    start_all([came_pair[0]] + came_z + [own_pair[1], came_pair[1]])
    cross_early, cross_late = [net.copy(out_buf.at[rows_out], out_all.at[mine, rows_out], wrap)], []
    for m in range(2):
        for unit, columns in ((0, columns_part(m, z, 4)), (3, columns_part(m, 1 - lo, 2))):
            rows = unit_rows(m, unit)
            cross_early.append(net.copy(shards[m].at[rows, columns], wholes[m].at[mine, rows, columns], wrap))
        rows = unit_rows(m, 1, 2)
        cross_late.append(net.copy(shards[m].at[rows], wholes[m].at[mine, rows], wrap))
    rows = half_rows(core)
    cross_late.append(net.copy(qkv_buf.at[rows], qkv_all.at[mine, rows], wrap))
    start_all(cross_early)
    pair_late = []

    def forward(got, d, low, w):
        got.wait_recv()
        piece = block((z + 4 - d) % 4, low, w, second)
        pair_late.append(net.copy(piece, piece, pair))
        pair_late[-1].start()

    for i, d in enumerate((1, 3, 2)):
        forward(own_z[i], d, lo, hi)
    for copy in cross_first:
        copy.wait_recv()
    across_small = small_y(across, heads_all.at[across], smalls_all.at[across])
    start_all(across_small)
    half_z = []

    def halves(got, low, w):
        got.wait_recv()
        piece = block(z, low, w, first)
        copies = [net.copy(piece, piece, along("z", d)) for d in (1, 3, 2)]
        start_all(copies)
        half_z.extend(copies)

    halves(own_pair[0], 1 - lo, hi)
    for copy in cross_early:
        copy.wait_recv()
    across_y = along_y(across, lambda m: wholes[m].at[across], out_all.at[across], False)
    start_all(across_y + cross_late)
    for i, d in enumerate((1, 3, 2)):
        forward(came_z[i], d, 1 - lo, 1 - hi)
    halves(came_pair[0], lo, 1 - hi)
    share, rest = [], []
    for low, w in ((lo, hi), (1 - lo, 1 - hi)):
        piece = x_buf.at[:, low, core, w]
        share.append(net.copy(piece, piece, other_core))
    start_all(share)

    for copy in own_small + across_small:
        copy.wait_recv()
    meta_wait()
    at_first = core == 0
    both = heads_all[...].reshape(D, 384)
    parts = [jnp.where(at_first, both[:, 128 * p : 128 * p + HD], both[:, 128 * p + HD : 128 * (p + 1)]) for p in range(3)]
    w_ref[...] = jnp.concatenate(parts, axis=1)
    biases = smalls_all[lax.axis_index("seq") // 2]
    bias = [jnp.where(at_first, biases[k : k + 1, :HD], biases[k : k + 1, HD:]) for k in range(2)]
    b_ref[...] = jnp.broadcast_to(jnp.concatenate([bias[0], jnp.zeros((1, HD), F32), bias[1]], axis=1), (8, 3 * HD))

    def project(low, at_core, w):
        @pl.loop(0, 4)
        def _(at):
            b = at * 8 + low * 4 + at_core * 2 + w
            rows = pl.ds(aligned(b * TB, TB), TB)
            side = dot(x_buf[at, low, at_core, w], w_ref[...]) + b_ref[:1, :]
            q8 = side[:, :HD].astype(BF).astype(F32) * 0.125
            hot = jnp.where(lax.broadcasted_iota(jnp.int32, (32, TB), 0) == meta_all[b, 0:1, :], 1.0, 0.0)
            lane = lax.broadcasted_iota(jnp.int32, (TB, HD), 1)
            ones3 = jnp.where(lane < 3, 1.0, 0.0)
            apart = (hot.T - 1.0) * MASKED
            key = side[:, HD : 2 * HD]
            value = side[:, 2 * HD :]
            q_ref[rows, :] = q8.astype(BF)
            ka_ref[rows, :] = jnp.concatenate([key, apart, ones3[:, :32]], axis=1).astype(BF)
            va_ref[rows, :] = jnp.concatenate([value, ones3], axis=1).astype(BF)
            qat_ref[:, rows] = jnp.concatenate([q8.T, hot, jnp.zeros((32, TB), F32)], axis=0).astype(BF)
            kt_ref[:, rows] = key.T.astype(BF)
            ones_row = jnp.where(lax.broadcasted_iota(jnp.int32, (16, TB), 0) == 0, 1.0, 0.0)
            vat_ref[:, rows] = jnp.concatenate([value.T, ones_row], axis=0).astype(BF)

    project(lo, core, hi)
    project(1 - lo, core, 1 - hi)
    for copy in half_z + [own_pair[1], came_pair[1]] + pair_late:
        copy.wait_recv()
    for low, w in ((1 - lo, hi), (lo, 1 - hi)):
        piece = x_buf.at[:, low, core, w]
        rest.append(net.copy(piece, piece, other_core))
    start_all(rest)
    for copy in share:
        copy.wait_recv()
    project(1 - lo, core, hi)
    project(lo, core, 1 - hi)
    project(lo, 1 - core, hi)
    project(1 - lo, 1 - core, 1 - hi)
    for copy in rest:
        copy.wait_recv()
    store = pltpu.make_async_copy(x_buf, x_seq, local.at[0])
    store.start()
    project(1 - lo, 1 - core, hi)
    project(lo, 1 - core, 1 - hi)
    meta_out[...] = meta_all[...]
    smalls_out[...] = smalls_all[...]

    wait_all(keep)
    for copy in own_y + across_y + cross_late:
        copy.wait_recv()
    later = []
    for m in range(2):
        piece = wholes[m].at[:, unit_rows(m, 3), columns_part(m, lo, 2)]
        later.append(net.copy(piece, piece, pair))
        for d in (1, 3, 2):
            piece = wholes[m].at[:, unit_rows(m, 0), columns_part(m, z, 4)]
            later.append(net.copy(piece, piece, along("z", d)))
    for d in (1, 3, 2):
        for shard, unit, number in ((mine, 2, 1), (across, 1, 2)):
            piece = up_all.at[shard, unit_rows(0, unit, number)]
            later.append(net.copy(piece, piece, along("y", d)))
    piece = out_all.at[:, half_rows(core)]
    later.append(net.copy(piece, piece, other_core))
    later += qkv_along_y(qkv_all, net, 0, 16)
    start_all(later)

    position = lax.axis_index("seq") * 2 + hi

    def result(b, recv_at):
        there = head_tile(context, position)
        return remote(blocks.at[b], there, back_send.at[b], back_recv.at[recv_at], (y, b // 2, b % 2))

    own_result = pltpu.make_async_copy(blocks.at[position], head_tile(context, position), back_local)

    @pl.loop(0, 4)
    def _(step):
        at = (step + z + 1) % 4
        columns = pl.ds(aligned(at * 1024, 1024), 1024)
        queries = qat_ref[:, columns]
        peak = jnp.full((1, 1024), -jnp.inf, F32)
        total = jnp.zeros((80, 1024), F32)
        for j in range(8):
            keys = slice(j * 512, (j + 1) * 512)
            logits = dot(ka_ref[keys, :], queries)
            new_peak = jnp.maximum(peak, jnp.max(logits, axis=0, keepdims=True))
            expos = jnp.exp(logits - new_peak).astype(BF)
            total = total * jnp.exp(peak - new_peak) + dot(vat_ref[:, keys], expos)
            peak = new_peak
        sums = total[HD : HD + 1]
        found = total[:HD] / sums
        wide_ref[:, columns] = found
        lse_ref[:, columns] = peak + jnp.log(sums)
        low = found.astype(BF)
        for j in range(8):
            b = at * 8 + j
            blocks[b] = low[:, j * TB : (j + 1) * TB]

            @pl.when(b != position)
            def _():
                result(b, position).start()

            @pl.when(b == position)
            def _():
                own_result.start()

    store.wait()
    for copy in [swap] + own_pair + own_z + came_pair + came_z + half_z + pair_late + share + rest:
        copy.wait_send()
    for copy in cross_first + cross_early + cross_late + own_small + across_small + own_y + across_y:
        copy.wait_send()
    wait_all(later)

    @pl.loop(1, NB)
    def _(shift):
        b = (position + shift) % NB
        result(b, b).wait()

    own_result.wait()


def front(tokens, segments, flags, vectors, b_up, w_out, w_up, w_down, w_qkv):
    shape = jax.ShapeDtypeStruct
    in_vmem = pl.BlockSpec(memory_space=pltpu.VMEM)
    return pl.pallas_call(
        front_kernel,
        in_specs=[ANY] + [in_vmem] * 4 + [ANY] * 4,
        out_specs=[ANY] + [in_vmem] * 2 + [ANY] * 4 + [in_vmem] * 5 + [ANY] + [in_vmem] * 2,
        out_shape=[
            shape((4, 2, 2, 2, TB, D), BF),
            shape((NB, 8, TB), jnp.int32),
            shape((8, 16, 128), F32),
            shape((8, 128, D), BF),
            shape((8, 128, 2048), BF),
            shape((8, 256, D), BF),
            shape((8, 128, 3 * D), BF),
            shape((128, L), BF),
            shape((L, 128), BF),
            shape((L, 128), BF),
            shape((HD, L), BF),
            shape((L, HD), BF),
            shape((D, 2 * TB), BF),
            shape((HD, L), F32),
            shape((1, L), F32),
        ],
        scratch_shapes=[
            pltpu.VMEM((80, L), BF),
            pltpu.VMEM((NB, HD, TB), BF),
            pltpu.VMEM((4, 2, 2, 2, TB, D), BF),
            pltpu.VMEM((2, TB, D), BF),
            pltpu.VMEM((128, D), BF),
            pltpu.VMEM((2, 128, 2048), BF),
            pltpu.VMEM((256, D), BF),
            pltpu.VMEM((128, 3 * D), BF),
            pltpu.VMEM((2, 8, TB), jnp.int32),
            pltpu.VMEM((2, 128, 384), BF),
            pltpu.VMEM((16, 128), F32),
            pltpu.VMEM((NB, 8, TB), jnp.int32),
            pltpu.VMEM((8, 128, 384), BF),
            pltpu.VMEM((8, 16, 128), F32),
            pltpu.VMEM((D, 3 * HD), BF),
            pltpu.VMEM((8, 3 * HD), F32),
            pltpu.SemaphoreType.DMA((FRONT_COPIES,)),
            pltpu.SemaphoreType.DMA((FRONT_COPIES,)),
            pltpu.SemaphoreType.DMA((12,)),
            *swap_sems(),
            *swap_sems(),
        ],
        name="front",
        compiler_params=pltpu.CompilerParams(
            collective_id=1, has_side_effects=True, vmem_limit_bytes=VMEM_CAP
        ),
    )(tokens, segments, flags, vectors, b_up, w_out, w_up, w_down, w_qkv)


def qkv_along_y(qkv_all, net, first, count):
    _, y, _, core = place()
    copies = []
    for d in (1, 3, 2):
        for w in range(2):
            piece = qkv_all.at[y * 2 + w, pl.ds(aligned(core * 64 + first, 16), count)]
            copies.append(net.copy(piece, piece, along("y", d)))
    return copies


def turned(first, second):
    return dot(first, second, ((0,), (0,)))


def gelu_both(u):
    rate = 0.7978845608028654
    square = u * u
    curve = jnp.tanh(rate * (u + 0.044715 * (square * u)))
    half = 0.5 * (1.0 + curve)
    slope = half + 0.5 * u * (1.0 - curve * curve) * (rate * (1.0 + 0.134145 * square))
    return u * half, slope


def fold(values):
    return jnp.sum(values.reshape(values.shape[0] // 8, 8, values.shape[1]), axis=0)


ROWS = 256
CHUNK = 32
SMALLS = 16


def middle_kernel(
    context_in, meta, tokens, teacher, flags, smalls, out_all, up_all, down_all, a0,
    states, resid_out, do, g_ref, sums_out, count_out, qkv_all,
    context, context_s, w_out, w_up, w_down, h, act, slope, send_one, come_one, send_two, come_two,
    gb, gu, ga, ga_s, normed, hidden, rate, work, resid, gct, stage, count, counts, valid,
    send, recv, local, back_send, back_recv, back_local,
):
    x, y, z, core = place()
    mine = y * 2 + x // 2
    twin = sibling()
    loads = [
        pltpu.make_async_copy(context_in, context, local.at[6]),
        pltpu.make_async_copy(out_all, w_out, local.at[0]),
        pltpu.make_async_copy(up_all, w_up, local.at[1]),
    ]
    ends = [pl.ds(0, 64), pl.ds(192, 64)]
    down_loads = [
        pltpu.make_async_copy(down_all.at[:, rows], w_down.at[:, rows], local.at[2 + 5 * k]) for k, rows in enumerate(ends)
    ]
    inner = [(y * 2 + w, pl.ds(64, 128)) for w in range(2)]
    down_loads += [pltpu.make_async_copy(down_all.at[a], w_down.at[a], local.at[8 + k]) for k, a in enumerate(inner)]
    start_all(loads + down_loads)
    greet_all(shard_greet())
    net = Transfers(send, recv)
    down_y = [net.copy(down_all.at[a], w_down.at[a], along("y", d)) for d in (1, 3, 2) for a in inner]
    start_all(down_y)
    valid_here = jnp.sum(meta[:, 1, :].astype(F32), axis=0, keepdims=True)
    count[...] = jnp.broadcast_to(jnp.sum(valid_here, axis=1, keepdims=True), (8, 128))
    ahead = [net.copy(count, counts.at[mine], target) for target in shard_greet()]
    start_all(ahead)
    own_count = pltpu.make_async_copy(count, counts.at[mine], local.at[3])
    own_count.start()
    for s in range(2):
        column = jnp.broadcast_to(flags[s : s + 1, :].astype(F32), (128, 128)).T
        valid[128 * s : 128 * (s + 1), :] = column

    def vector(row):
        return jnp.concatenate([smalls[i, row : row + 1, :] for i in range(8)], axis=1)

    out_bias, gain_one, offset_one, down_bias, gain_two, offset_two = [vector(row) for row in range(2, 8)]
    zeros = jnp.zeros((8, D), F32)
    wait_all(loads)
    give_context = net.copy(context, context_s, twin)
    give_context.start()
    work[...] = turned(context[...], w_out[...].reshape(D, D))

    @pl.loop(0, ROWS // CHUNK)
    def _(i):
        rows = pl.ds(aligned(i * CHUNK, CHUNK), CHUNK)
        total = tokens[rows, :].astype(F32) + work[rows, :] + out_bias
        centre = total - jnp.mean(total, axis=1, keepdims=True)
        scale = lax.rsqrt(jnp.mean(centre * centre, axis=1, keepdims=True) + EPS)
        unit = centre * scale
        normed[rows, :] = unit
        rate[rows, :] = jnp.broadcast_to(scale, (CHUNK, 128))
        full = unit * gain_one + offset_one
        hidden[rows, :] = full
        h[0, rows, :] = full.astype(BF)

    give_hidden = net.copy(h.at[0], h.at[1], twin)
    give_hidden.start()
    for slot in range(2):
        if slot == 1:
            give_hidden.wait()
        for k in range(8):
            columns = slice(256 * k, 256 * (k + 1))
            bias = jnp.concatenate([smalls[k, pl.ds(8 + 2 * core + e, 1), :] for e in range(2)], axis=1)
            u = dot(h[slot], w_up[:, :, columns].reshape(D, 256)) + bias
            value, incline = gelu_both(u)
            act[slot, :, columns] = value.astype(BF)
            slope[slot, :, columns] = incline
    wait_all(down_loads)
    for copy in down_y:
        copy.wait()
    later = qkv_along_y(qkv_all, net, 16, 48)
    start_all(later)
    send_one[...] = dot(act[1], w_down[...].reshape(2048, D))
    give_one = net.copy(send_one, come_one, twin)
    give_one.start()
    work[...] = dot(act[0], w_down[...].reshape(2048, D))
    give_one.wait()
    wait_all(ahead)
    own_count.wait()
    total_count = jnp.sum(counts[...], axis=0)
    count_out[...] = total_count
    factor = (128 * ROWS) / total_count[:1, :1]

    def loss_rows(i, carried):
        rows = pl.ds(aligned(i * CHUNK, CHUNK), CHUNK)
        total = hidden[rows, :] + (work[rows, :] + come_one[rows, :] + down_bias)
        centre = total - jnp.mean(total, axis=1, keepdims=True)
        scale = lax.rsqrt(jnp.mean(centre * centre, axis=1, keepdims=True) + EPS)
        unit = centre * scale
        final = unit * gain_two + offset_two
        states[rows, :] = final.astype(BF)
        differ = final - teacher[rows, :].astype(F32)
        held = valid[rows, :1] * differ
        grad = factor * held
        weighted = grad * gain_two
        back = weighted - jnp.mean(weighted, axis=1, keepdims=True)
        back = scale * (back - unit * jnp.mean(weighted * unit, axis=1, keepdims=True))
        resid[rows, :] = back
        low = back.astype(BF)
        gb[0, rows, :] = low
        return (
            carried[0] + fold(grad * unit),
            carried[1] + fold(grad),
            carried[2] + fold(low.astype(F32)),
            carried[3] + fold(held * differ),
        )

    gain_two_sum, offset_two_sum, down_sum, error = lax.fori_loop(
        0, ROWS // CHUNK, loss_rows, (zeros, zeros, zeros, zeros)
    )
    give_branch = net.copy(gb.at[0], gb.at[1], twin)
    give_branch.start()
    up_sums = []
    for slot in range(2):
        if slot == 1:
            give_branch.wait()
        for k in range(8):
            columns = slice(256 * k, 256 * (k + 1))
            pulled = dot(gb[slot], w_down[k], ((1,), (1,))) * slope[slot, :, columns]
            low = pulled.astype(BF)
            gu[slot, :, columns] = low
            up_sums.append(fold(low.astype(F32)))
    for i in range(8):
        send_two[:, 128 * i : 128 * (i + 1)] = dot(gu[1], w_up[i], ((1,), (1,)))
    give_two = net.copy(send_two, come_two, twin)
    give_two.start()
    for i in range(8):
        work[:, 128 * i : 128 * (i + 1)] = dot(gu[0], w_up[i], ((1,), (1,)))
    give_two.wait()

    def first_norm_rows(i, carried):
        rows = pl.ds(aligned(i * CHUNK, CHUNK), CHUNK)
        grad = resid[rows, :] + (work[rows, :] + come_two[rows, :])
        unit = normed[rows, :]
        weighted = grad * gain_one
        back = weighted - jnp.mean(weighted, axis=1, keepdims=True)
        back = rate[rows, :1] * (back - unit * jnp.mean(weighted * unit, axis=1, keepdims=True))
        resid_out[rows, :] = back
        low = back.astype(BF)
        ga[rows, :] = low
        return (carried[0] + fold(grad * unit), carried[1] + fold(grad), carried[2] + fold(low.astype(F32)))

    gain_one_sum, offset_one_sum, out_sum = lax.fori_loop(0, ROWS // CHUNK, first_norm_rows, (zeros, zeros, zeros))
    give_attended = net.copy(ga.at[:, pl.ds(aligned((1 - core) * 512, 512), 512)], ga_s, twin)
    give_attended.start()
    gct[...] = dot(w_out[...].reshape(D, D), ga[...], ((1,), (1,))).astype(BF)
    back_start, back_wait = swap_copies(
        lambda b: head_tile(gct, b), lambda b: do.at[b], (back_send, back_recv, back_local)
    )
    back_start()

    error = jnp.broadcast_to(jnp.sum(jnp.sum(error, axis=0, keepdims=True), axis=1, keepdims=True), (1, 128))
    lines = [out_sum, gain_one_sum, offset_one_sum, down_sum, gain_two_sum, offset_two_sum]
    lines = [jnp.sum(line, axis=0, keepdims=True) for line in lines]
    for i in range(8):
        columns = slice(128 * i, 128 * (i + 1))
        sums_out[i] = jnp.zeros((SMALLS, 128), F32)
        for row, line in enumerate(lines):
            sums_out[i, row : row + 1, :] = line[:, columns]
        both = jnp.sum(up_sums[i] + up_sums[8 + i], axis=0, keepdims=True)
        for e in range(2):
            sums_out[i, pl.ds(6 + 2 * core + e, 1), :] = both[:, 128 * e : 128 * (e + 1)]
        sums_out[i, 10:11, :] = error

    give_context.wait()
    give_attended.wait()

    def stored(i):
        return pltpu.make_async_copy(stage.at[i % 2], g_ref.at[i // 2, i % 2], local.at[4 + i % 2])

    for i in range(8):
        if i >= 2:
            stored(i - 2).wait()
        tall = slice(128 * i, 128 * (i + 1))
        wide = slice(256 * i, 256 * (i + 1))
        up = turned(h[0, :, tall], gu[0]) + turned(h[1, :, tall], gu[1])
        for k in range(4):
            stage[i % 2, 128 * k : 128 * (k + 1), :] = up[:, 512 * k : 512 * (k + 1)].astype(BF)
        down = turned(act[0, :, wide], gb[0]) + turned(act[1, :, wide], gb[1])
        for k in range(2):
            stage[i % 2, 512 + 256 * k : 768 + 256 * k, :] = down[:, 512 * k : 512 * (k + 1)].astype(BF)
        own_half = ga[:, pl.ds(aligned(core * 512, 512), 512)]
        out = dot(context[tall, :], own_half) + dot(context_s[tall, :], ga_s[...])
        stage[i % 2, 1024:, :] = out.astype(BF)
        stored(i).start()
    stored(6).wait()
    stored(7).wait()
    back_wait()
    wait_all(later)


def middle(context, meta, tokens, teacher, flags, smalls, out_all, up_all, down_all, qkv_all):
    shape = jax.ShapeDtypeStruct
    in_vmem = pl.BlockSpec(memory_space=pltpu.VMEM)
    dma = pltpu.SemaphoreType.DMA
    wide = pltpu.VMEM((ROWS, D), F32)
    return pl.pallas_call(
        middle_kernel,
        in_specs=[ANY] + [in_vmem] * 5 + [ANY] * 4,
        out_specs=[in_vmem, in_vmem, ANY, ANY, in_vmem, in_vmem, ANY],
        out_shape=[
            shape((ROWS, D), BF),
            shape((ROWS, D), F32),
            shape((NB, HD, TB), BF),
            shape((4, 2, 1152, 512), BF),
            shape((8, SMALLS, 128), F32),
            shape((8, 128), F32),
            shape(qkv_all.shape, BF),
        ],
        input_output_aliases={9: 6},
        scratch_shapes=[
            pltpu.VMEM((D, ROWS), BF),
            pltpu.VMEM((D, ROWS), BF),
            pltpu.VMEM((8, 128, D), BF),
            pltpu.VMEM((8, 128, 2048), BF),
            pltpu.VMEM((8, 256, D), BF),
            pltpu.VMEM((2, ROWS, D), BF),
            pltpu.VMEM((2, ROWS, 2048), BF),
            pltpu.VMEM((2, ROWS, 2048), F32),
            wide,
            wide,
            wide,
            wide,
            pltpu.VMEM((2, ROWS, D), BF),
            pltpu.VMEM((2, ROWS, 2048), BF),
            pltpu.VMEM((ROWS, D), BF),
            pltpu.VMEM((ROWS, 512), BF),
            wide,
            wide,
            pltpu.VMEM((ROWS, 128), F32),
            wide,
            wide,
            pltpu.VMEM((D, ROWS), BF),
            pltpu.VMEM((2, 1152, 512), BF),
            pltpu.VMEM((8, 128), F32),
            pltpu.VMEM((8, 8, 128), F32),
            pltpu.VMEM((ROWS, 128), F32),
            dma((32,)),
            dma((32,)),
            dma((10,)),
            *swap_sems(),
        ],
        name="middle",
        compiler_params=pltpu.CompilerParams(
            collective_id=3, has_side_effects=True, vmem_limit_bytes=VMEM_CAP
        ),
    )(context, meta, tokens, teacher, flags, smalls, out_all, up_all, down_all, qkv_all)


BACK_KEYS = 512
BACK_STEPS = L // BACK_KEYS
BACK_WIDTH = 1024


def back_kernel(
    qat, ka, va, kt, q8, do, wide, lse, smalls, x_seq, g_ref, a0,
    projected, heads_out, shard_out, smalls_out, qkv_all,
    x_buf, queries, grads, grad_rows, dq, d_ref, mine_ref, parts_ref, sum_ref, heads_buf, small_buf, small_sum, small_all,
    send, recv, local, dk_send, dk_recv, dk_local, dq_send, dq_recv, dq_local, spread_send, spread_recv, *reduce_refs,
):
    x, y, z, core = place()
    shard_at = y * 2 + x // 2
    seq = lax.axis_index("seq")
    mine = seq * 2 + x // 2
    net = (g_ref,) + reduce_refs

    def shard_device(d):
        other = (shard_at + d) % 8
        return other, (other // 2, seq, other % 2)

    load_x = pltpu.make_async_copy(x_seq, x_buf, local.at[0])
    load_x.start()
    greet_all([shard_device(d)[1] for d in range(1, 8)])
    for part in range(3):
        reduce_start(part, net)
    far = Transfers(send, recv)
    small_out = [far.copy(smalls.at[shard_device(d)[0]], small_buf.at[shard_at], shard_device(d)[1]) for d in range(1, 8)]
    start_all(small_out)
    small_buf[shard_at] = smalls[shard_at]
    rows = half_rows(core)
    weights = far.copy(qkv_all.at[:, rows], qkv_all.at[:, rows], sibling())
    weights.start()

    for j in range(L // BACK_WIDTH):
        columns = slice(j * BACK_WIDTH, (j + 1) * BACK_WIDTH)
        grad_t = jnp.concatenate([do[j * (BACK_WIDTH // TB) + i] for i in range(BACK_WIDTH // TB)], axis=1)
        wider = grad_t.astype(F32)
        delta = jnp.sum(wider * wide[:, columns], axis=0, keepdims=True)
        grads[:HD, columns] = grad_t
        grads[HD:, columns] = jnp.concatenate([three_pieces(-delta), jnp.zeros((61, BACK_WIDTH), BF)], axis=0)
        queries[:96, columns] = qat[:96, columns]
        queries[96:, columns] = jnp.concatenate(
            [three_pieces(-lse[:, columns]), jnp.zeros((29, BACK_WIDTH), BF)], axis=0
        )
        grad_rows[columns, :] = wider.T.astype(BF)
    dq[...] = jnp.zeros_like(dq)

    def landing(first, count):
        return projected.at[pl.ds(first, count), pl.ds(aligned(seq * HD, HD), HD), pl.ds(aligned((x // 2) * TB, TB), TB)]

    def block_device(b):
        return (y, b // 2, b % 2)

    def dk_copy(b, recv_at):
        return remote(d_ref.at[b, pl.ds(1, 2)], landing(1, 2), dk_send.at[b], dk_recv.at[recv_at], block_device(b))

    def dq_copy(b, recv_at):
        return remote(d_ref.at[b, pl.ds(0, 1)], landing(0, 1), dq_send.at[b], dq_recv.at[recv_at], block_device(b))

    dk_own = pltpu.make_async_copy(d_ref.at[mine, pl.ds(1, 2)], landing(1, 2), dk_local)
    dq_own = pltpu.make_async_copy(d_ref.at[mine, pl.ds(0, 1)], landing(0, 1), dq_local)

    @pl.loop(0, BACK_STEPS)
    def _(step):
        at = (step + 2 * (z + 1)) % BACK_STEPS
        keys = pl.ds(aligned(at * BACK_KEYS, BACK_KEYS), BACK_KEYS)
        ka_part, va_part, kt_part = ka[keys, :], va[keys, :], kt[:, keys]
        dk = jnp.zeros((BACK_KEYS, HD), F32)
        dv = jnp.zeros((BACK_KEYS, HD), F32)
        for j in range(L // BACK_WIDTH):
            columns = slice(j * BACK_WIDTH, (j + 1) * BACK_WIDTH)
            probs = jnp.exp(dot(ka_part, queries[:, columns]))
            raw = (probs * dot(va_part, grads[:, columns])).astype(BF)
            dv = dv + dot(probs.astype(BF), grad_rows[columns, :])
            dk = dk + dot(raw, q8[columns, :])
            dq[:, columns] += dot(kt_part, raw)
        dk_t, dv_t = dk.T.astype(BF), dv.T.astype(BF)
        for i in range(BACK_KEYS // TB):
            b = at * (BACK_KEYS // TB) + i
            d_ref[b, 1] = dk_t[:, i * TB : (i + 1) * TB]
            d_ref[b, 2] = dv_t[:, i * TB : (i + 1) * TB]

            @pl.when(b != mine)
            def _():
                dk_copy(b, mine).start()

            @pl.when(b == mine)
            def _():
                dk_own.start()

        @pl.when(step == BACK_STEPS - 3)
        def _():
            reduce_step(0, 1, net)

        @pl.when(step == BACK_STEPS - 2)
        def _():
            reduce_step(0, 2, net)

    for b in range(NB):
        d_ref[b, 0] = (dq[:, b * TB : (b + 1) * TB] * 0.125).astype(BF)

    @pl.loop(1, NB)
    def _(shift):
        dq_copy((mine + shift) % NB, mine).start()

    dq_own.start()
    reduce_step(0, 0, net)
    reduce_step(1, 1, net)
    reduce_step(1, 2, net)
    wait_all(small_out)
    small_sum[...] = jnp.sum(small_buf[...], axis=0)

    load_x.wait()
    left = jnp.concatenate([d_ref[b].reshape(3 * HD, TB) for b in range(NB)], axis=1)
    sums = dot(jnp.ones((8, L), BF), left, ((1,), (1,)))
    gap = jnp.zeros((1, 128 - HD), F32)
    tail = jnp.concatenate(
        [
            jnp.concatenate([sums[:1, :HD], gap], axis=1),
            jnp.concatenate([sums[:1, 2 * HD :], gap], axis=1),
            jnp.zeros((14, 128), F32),
        ],
        axis=0,
    ).astype(BF)
    for i in range(4):
        total = dot(left, x_buf[:, :, 256 * i : 256 * (i + 1)].reshape(L, 256))
        for k in range(2):
            mine_ref[2 * i + k, : 3 * HD, :] = total[:, 128 * k : 128 * (k + 1)].astype(BF)
            mine_ref[2 * i + k, 3 * HD :, :] = tail
    part_out = [far.copy(mine_ref.at[shard_device(d)[0]], parts_ref.at[d], shard_device(d)[1]) for d in range(1, 8)]
    start_all(part_out)

    steps = [spread_steps(part, reduce_refs[6 + part].at[0], (local.at[pl.ds(1, 3)], spread_send, spread_recv), shard_out) for part in range(3)]
    for part in (1, 2, 0):
        if part == 0:
            reduce_step(1, 0, net)
        reduce_step(2, part, net)
        steps[part][0]()
    wait_all(part_out)
    added = mine_ref[shard_at].astype(F32)
    for d in range(1, 8):
        added = added + parts_ref[d].astype(F32)
    sum_ref[...] = added.astype(BF)
    heads_buf[seq // 2, core] = sum_ref[...]
    small_all[seq // 2, core] = small_sum[...]
    head_out = []
    for d in range(1, 8):
        target = (y, (seq + 2 * d) % 16, x // 2)
        head_out.append(far.copy(sum_ref, heads_buf.at[seq // 2, core], target))
        head_out.append(far.copy(small_sum, small_all.at[seq // 2, core], target))
    start_all(head_out)
    for part in (1, 2, 0):
        steps[part][1]()
    wait_all(head_out)
    across = [
        far.copy(heads_buf.at[:, core], heads_buf.at[:, core], sibling()),
        far.copy(small_all.at[:, core], small_all.at[:, core], sibling()),
    ]
    start_all(across)
    for part in (1, 2, 0):
        steps[part][2]()
    shared = far.copy(shard_out.at[core], shard_out.at[core], sibling())
    shared.start()

    @pl.loop(1, NB)
    def _(shift):
        b = (mine + shift) % NB
        dk_copy(b, b).wait()
        dq_copy(b, b).wait()

    dk_own.wait()
    dq_own.wait()
    weights.wait()
    wait_all(across)
    for i in range(8):
        heads_out[2 * i] = heads_buf[i, 0]
        heads_out[2 * i + 1] = heads_buf[i, 1]
    smalls_out[...] = jnp.sum(small_all[...].reshape(16, 16, 128), axis=0)
    shared.wait()


def back(qat, ka, va, kt, q8, do, wide, lse, smalls, x_seq, g, qkv_all):
    shape = jax.ShapeDtypeStruct
    in_vmem = pl.BlockSpec(memory_space=pltpu.VMEM)
    dma = pltpu.SemaphoreType.DMA
    return pl.pallas_call(
        back_kernel,
        in_specs=[in_vmem] * 9 + [ANY] * 3,
        out_specs=[ANY, in_vmem, ANY, in_vmem, ANY],
        out_shape=[
            shape((3, D, 2 * TB), BF),
            shape((H, 208, 128), BF),
            shape((2, 1152, 512), BF),
            shape((16, 128), F32),
            shape(qkv_all.shape, BF),
        ],
        input_output_aliases={11: 4},
        scratch_shapes=[
            pltpu.VMEM((NB, TB, D), BF),
            pltpu.VMEM((128, L), BF),
            pltpu.VMEM((128, L), BF),
            pltpu.VMEM((L, HD), BF),
            pltpu.VMEM((HD, L), F32),
            pltpu.VMEM((NB, 3, HD, TB), BF),
            pltpu.VMEM((8, 208, 128), BF),
            pltpu.VMEM((8, 208, 128), BF),
            pltpu.VMEM((208, 128), BF),
            pltpu.VMEM((8, 2, 208, 128), BF),
            pltpu.VMEM((8, 16, 128), F32),
            pltpu.VMEM((16, 128), F32),
            pltpu.VMEM((8, 2, 16, 128), F32),
            dma((40,)),
            dma((40,)),
            dma((4,)),
            *swap_sems(),
            *swap_sems(),
            dma((3, 8)),
            dma((3, 8)),
            *reduce_scratch(),
        ],
        name="attend_back",
        compiler_params=pltpu.CompilerParams(
            collective_id=4, has_side_effects=True, vmem_limit_bytes=VMEM_CAP
        ),
    )(qat, ka, va, kt, q8, do, wide, lse, smalls, x_seq, g, qkv_all)


def finish_kernel(
    projected, qkv_ref, resid_ref, heads_ref, shard_ref, tokens_ref, grad_qkv, grad_out, grad_up, grad_down
):
    step = pl.program_id(0)
    tokens_ref[...] = resid_ref[...] + dot(projected[...], qkv_ref[...], ((0,), (1,)))
    for c in range(2):
        columns = slice(512 * c, 512 * (c + 1))
        for j in range(2):
            piece = shard_ref[c, pl.ds(aligned(step * 128, 128), 128), 256 * j : 256 * (j + 1)]
            grad_up[:, 512 * j + 256 * c : 512 * j + 256 * (c + 1)] = piece.astype(F32)
        rows = pl.ds(aligned(512 + 256 * c + (step % 2) * 128, 128), 128)
        grad_down[:, columns] = shard_ref[step // 2, rows, :].astype(F32)
        grad_out[:, columns] = shard_ref[c, pl.ds(aligned(1024 + step * 32, 32), 32), :].astype(F32)

    @pl.when(step == 0)
    def _():
        for p in range(3):
            for pair in range(8):
                both = [heads_ref[2 * pair + k, p * HD : (p + 1) * HD, :].astype(F32) for k in range(2)]
                at = p * D + pair * 128
                grad_qkv[:, at : at + 128] = jnp.concatenate(both, axis=0).T


def finish(projected, qkv, resid, heads, shard):
    shape = jax.ShapeDtypeStruct

    def whole(dims):
        return pl.BlockSpec(dims, lambda i: (0,) * len(dims))

    return pl.pallas_call(
        finish_kernel,
        grid=(4,),
        in_specs=[
            whole((3 * D, 2 * TB)),
            pl.BlockSpec((256, 3 * D), lambda i: (i, 0)),
            pl.BlockSpec((2 * TB, 256), lambda i: (0, i)),
            whole((H, 208, 128)),
            whole((2, 1152, 512)),
        ],
        out_specs=[
            pl.BlockSpec((2 * TB, 256), lambda i: (0, i)),
            whole((128, 3 * D)),
            pl.BlockSpec((32, D), lambda i: (i, 0)),
            pl.BlockSpec((128, 1024), lambda i: (0, i)),
            pl.BlockSpec((128, D), lambda i: (i, 0)),
        ],
        out_shape=[
            shape((2 * TB, D), F32),
            shape((128, 3 * D), F32),
            shape((128, D), F32),
            shape((128, FF), F32),
            shape((512, D), F32),
        ],
        name="finish",
        compiler_params=pltpu.CompilerParams(vmem_limit_bytes=VMEM_CAP),
    )(projected, qkv, resid, heads, shard)


def on_device(
    tokens,
    segments,
    valid_flags,
    teacher,
    w_qkv,
    b_query,
    b_value,
    w_out,
    b_out,
    ln1_gain,
    ln1_bias,
    w_up,
    b_up,
    w_down,
    b_down,
    ln2_gain,
    ln2_bias,
):
    seq_local, row_local, _ = tokens.shape
    token_rows = seq_local * row_local
    shard_at = lax.axis_index("dp") * 2 + lax.axis_index("wshard")

    vectors = jnp.stack([b_query, b_value, b_out, ln1_gain, ln1_bias, b_down, ln2_gain, ln2_bias]).astype(F32)
    (
        x_seq, meta_all, smalls_all, out_all, up_all, down_all, qkv_all, qat, ka, va, kt, q8, context, wide, lse
    ) = front(
        tokens, segments, valid_flags, vectors, b_up.reshape(4, 128).astype(F32), w_out, w_up, w_down, w_qkv
    )
    x_seq = x_seq.reshape(NB, TB, D)
    states, grad_resid_one, do, g, small_sums, count, qkv_all = middle(
        context,
        meta_all,
        tokens.reshape(token_rows, D),
        teacher.reshape(token_rows, D),
        valid_flags,
        smalls_all,
        out_all,
        up_all,
        down_all,
        qkv_all,
    )
    projected, heads_out, shard_out, small_out, qkv_all = back(
        qat, ka, va, kt, q8, do, wide, lse, small_sums, x_seq, g, qkv_all
    )
    grad_tokens, grad_qkv, grad_out, grad_up, grad_down = finish(
        projected.reshape(3 * D, token_rows), qkv_all.reshape(D, 3 * D), grad_resid_one, heads_out, shard_out
    )
    own_heads = lax.dynamic_slice(heads_out, (shard_at * 2, 3 * HD, 0), (2, 2, HD)).astype(F32)
    mean_loss = small_out[10, 0] / (D * count[0, 0])
    return (
        states.reshape(seq_local, row_local, D),
        mean_loss,
        grad_tokens.reshape(seq_local, row_local, D),
        grad_qkv,
        own_heads[:, 0].reshape(128),
        own_heads[:, 1].reshape(128),
        grad_out,
        small_out[0],
        small_out[1],
        small_out[2],
        grad_up,
        small_out[6:10].reshape(512),
        grad_down,
        small_out[3],
        small_out[4],
        small_out[5],
    )


def solution(mesh):
    rows = P("dp", ("seq", "wshard"), None)
    flags = P("dp", ("seq", "wshard"))
    matrix = P(("dp", "wshard"), None)
    vector = P(("dp", "wshard"))
    return jax.shard_map(
        on_device,
        mesh=mesh,
        in_specs=(
            rows,
            flags,
            flags,
            rows,
            matrix,
            vector,
            vector,
            matrix,
            vector,
            vector,
            vector,
            matrix,
            vector,
            matrix,
            vector,
            vector,
            vector,
        ),
        out_specs=(
            rows,
            P(),
            rows,
            matrix,
            vector,
            vector,
            matrix,
            vector,
            vector,
            vector,
            matrix,
            vector,
            matrix,
            vector,
            vector,
            vector,
        ),
        check_vma=False,
    )
```

```python
import functools

import jax
import jax.numpy as jnp
from jax import lax
from jax.experimental import pallas as pl
from jax.experimental.pallas import tpu as pltpu
from jax.sharding import PartitionSpec as P

D = 1024
H = 16
HD = 64
FF = 4096
L = 4096
EPS = 1e-06
F32 = jnp.float32
BF = jnp.bfloat16
MASKED = 1000000000.0
VMEM_CAP = 60 * 1024 * 1024
MESH = pl.DeviceIdType.MESH
ANY = pl.BlockSpec(memory_space=pl.ANY)
TB = 128
NB = L // TB


def dot(first, second, dims=((1,), (0,))):
    return lax.dot_general(first, second, (dims, ((), ())), preferred_element_type=F32)


def three_pieces(row):
    high = row.astype(BF)
    rest = row - high.astype(F32)
    middle = rest.astype(BF)
    lowest = (rest - middle.astype(F32)).astype(BF)
    return jnp.concatenate([high, middle, lowest], axis=0)


def place():
    at = lax.axis_index("seq")
    return (lax.axis_index("wshard") * 2 + (at // 2) % 2, lax.axis_index("dp"), at // 4, at % 2)


def device_at(x, y, z, core):
    return (y, (z * 2 + x % 2) * 2 + core, x // 2)


def along(axis, shift):
    x, y, z, core = place()
    if axis == "x":
        return device_at((x + shift) % 4, y, z, core)
    if axis == "y":
        return device_at(x, (y + shift) % 4, z, core)
    return device_at(x, y, (z + shift) % 4, core)


def sibling():
    x, y, z, core = place()
    return device_at(x, y, z, 1 - core)


def greet(partners):
    barrier = pltpu.get_barrier_semaphore()
    for partner in partners:
        pl.semaphore_signal(barrier, inc=1, device_id=partner, device_id_type=MESH)
    pl.semaphore_wait(barrier, len(partners))


def remote(src, dst, send_sem, recv_sem, target):
    return pltpu.make_async_remote_copy(
        src_ref=src, dst_ref=dst, send_sem=send_sem, recv_sem=recv_sem, device_id=target, device_id_type=MESH
    )


ORDERS = ("yzx", "zxy", "xyz")
PIECE = (64, 32, 48)
FIRST = (0, 512, 768)


def ring_partners():
    return [along(axis, shift) for axis in "xyz" for shift in (1, 2, 3)] + [sibling()]


def reduce_scratch():
    a, b, c = PIECE
    return [
        pltpu.VMEM((4, 2, 8 * a, 512), BF),
        pltpu.VMEM((4, 4, 2, 2 * b, 512), BF),
        pltpu.VMEM((4, 4, 4 * c, 512), BF),
        pltpu.VMEM((4, 2, 2 * a, 512), BF),
        pltpu.VMEM((4, 4, b, 512), BF),
        pltpu.VMEM((4, 4 * c, 512), BF),
        pltpu.VMEM((4, a, 512), BF),
        pltpu.VMEM((4, b, 512), BF),
        pltpu.VMEM((4, c, 512), BF),
        pltpu.SemaphoreType.DMA((3, 3, 3)),
        pltpu.SemaphoreType.DMA((3, 3, 3)),
        pltpu.SemaphoreType.DMA((3,)),
        pltpu.VMEM((2, 8 * a, 512), BF),
        pltpu.SemaphoreType.DMA((6,)),
        pltpu.SemaphoreType.DMA((6,)),
        pltpu.SemaphoreType.DMA((2,)),
    ]


def aligned(value, unit):
    return pl.multiple_of(value, unit)


def reduce_piece(stage, part, refs, at):
    g_ref = refs[0]
    half, low, n = at // 2, at % 2, PIECE[part]
    if stage == 0:
        first = FIRST[part]
        if part == 0:
            return g_ref.at[at, :, pl.ds(first, 8 * n), :]
        if part == 1:
            return g_ref.at[:, :, pl.ds(aligned(first + at * 2 * n, 16), 2 * n), :]
        return g_ref.at[:, half, pl.ds(aligned(first + low * 4 * n, 16), 4 * n), :]
    held = refs[1 + 3 * (stage - 1) + part]
    if stage == 1:
        if part == 0:
            return held.at[0, :, pl.ds(aligned(at * 2 * n, 16), 2 * n), :]
        if part == 1:
            return held.at[0, :, half, pl.ds(aligned(low * n, 16), n), :]
        return held.at[0, at]
    if part == 0:
        return held.at[0, half, pl.ds(aligned(low * n, 16), n), :]
    if part == 1:
        return held.at[0, at]
    return held.at[0, pl.ds(aligned(at * n, 16), n), :]


def ring_at(axis):
    x, y, z, _ = place()
    return {"x": x, "y": y, "z": z}[axis]


def reduce_copies(stage, part, refs):
    send, recv = refs[10], refs[11]
    axis = ORDERS[part][stage]
    return [
        remote(
            reduce_piece(stage, part, refs, (ring_at(axis) + shift) % 4),
            refs[1 + 3 * stage + part].at[shift],
            send.at[stage, part, shift - 1],
            recv.at[stage, part, shift - 1],
            along(axis, shift),
        )
        for shift in (1, 3, 2)
    ]


def reduce_own(part, refs):
    return pltpu.make_async_copy(
        reduce_piece(0, part, refs, ring_at(ORDERS[part][0])), refs[1 + part].at[0], refs[12].at[part]
    )


def reduce_start(part, refs):
    start_all(first_copies(refs)[:4] + first_loads(refs) if part == 0 else reduce_copies(0, part, refs))
    reduce_own(part, refs).start()


def first_copies(refs):
    g_ref, a1, relay, send, recv = refs[0], refs[1], refs[13], refs[14], refs[15]
    _, y, _, _ = place()
    rows = pl.ds(0, 8 * PIECE[0])
    up, down, far = (y + 1) % 4, (y + 3) % 4, (y + 2) % 4
    moves = [
        (g_ref.at[far, 0, rows], a1.at[2, 0], 1),
        (g_ref.at[far, 1, rows], a1.at[2, 1], 3),
        (g_ref.at[up, 1, rows], a1.at[1, 1], 1),
        (g_ref.at[down, 0, rows], a1.at[3, 0], 3),
        (relay.at[0], a1.at[1, 0], 1),
        (relay.at[1], a1.at[3, 1], 3),
    ]
    return [remote(src, dst, send.at[k], recv.at[k], along("y", d)) for k, (src, dst, d) in enumerate(moves)]


def first_loads(refs):
    g_ref, relay, local = refs[0], refs[13], refs[16]
    _, y, _, _ = place()
    rows = pl.ds(0, 8 * PIECE[0])
    return [
        pltpu.make_async_copy(g_ref.at[(y + 1) % 4, 0, rows], relay.at[0], local.at[0]),
        pltpu.make_async_copy(g_ref.at[(y + 3) % 4, 1, rows], relay.at[1], local.at[1]),
    ]


def first_relay(refs):
    a1, relay = refs[1], refs[13]
    copies = first_copies(refs)
    wait_all(first_loads(refs))
    for copy in copies[:2]:
        copy.wait_recv()

    @pl.loop(0, 16)
    def _(i):
        rows = pl.ds(aligned((i % 8) * PIECE[0], 16), PIECE[0])
        half = i // 8
        relay[half, rows, :] = (relay[half, rows, :].astype(F32) + a1[2, half, rows, :].astype(F32)).astype(BF)

    start_all(copies[4:])


def first_end(refs):
    copies = first_copies(refs)
    for copy in copies[:2]:
        copy.wait_send()
    wait_all(copies[2:])


def add_four(values):
    total = values[0].astype(F32) + values[1].astype(F32)
    return (total + values[2].astype(F32) + values[3].astype(F32)).astype(BF)


def reduce_step(stage, part, refs):
    a1, b1, c1, a2, b2, c2, a3, b3, c3 = refs[1:10]
    if stage == 0 and part == 0:
        first_end(refs)
    else:
        wait_all(reduce_copies(stage, part, refs))
    x, y, z, _ = place()
    n = PIECE[part]
    rest = (1, 2, 3)
    if stage == 0:
        reduce_own(part, refs).wait()

        @pl.loop(0, 16)
        def _(i):
            if part == 0:
                rows = pl.ds(aligned((i % 8) * n, 16), n)
                total = a1[0, i // 8, rows, :].astype(F32) + a1[1, i // 8, rows, :].astype(F32)
                a1[0, i // 8, rows, :] = (total + a1[3, i // 8, rows, :].astype(F32)).astype(BF)
            elif part == 1:
                rows = pl.ds(aligned((i % 2) * n, 16), n)
                b1[0, i // 4, (i // 2) % 2, rows, :] = add_four([b1[s, i // 4, (i // 2) % 2, rows, :] for s in range(4)])
            else:
                rows = pl.ds(aligned((i % 4) * n, 16), n)
                c1[0, i // 4, rows, :] = add_four([c1[s, i // 4, rows, :] for s in range(4)])

    elif stage == 1:

        @pl.loop(0, 4)
        def _(i):
            if part == 0:
                rows = pl.ds(aligned((i % 2) * n, 16), n)
                own = a1[0, i // 2, pl.ds(aligned(z * 2 * n + (i % 2) * n, 16), n), :]
                a2[0, i // 2, rows, :] = add_four([own] + [a2[s, i // 2, rows, :] for s in rest])
            elif part == 1:
                own = b1[0, i, x // 2, pl.ds(aligned((x % 2) * n, 16), n), :]
                b2[0, i] = add_four([own] + [b2[s, i] for s in rest])
            else:
                rows = pl.ds(aligned(i * n, 16), n)
                own = c1[0, y, rows, :]
                c2[0, rows, :] = add_four([own] + [c2[s, rows, :] for s in rest])

    elif part == 0:
        own = a2[0, x // 2, pl.ds(aligned((x % 2) * n, 16), n), :]
        a3[0] = add_four([own] + [a3[s] for s in rest])
    elif part == 1:
        b3[0] = add_four([b2[0, y]] + [b3[s] for s in rest])
    else:
        own = c2[0, pl.ds(aligned(z * n, 16), n), :]
        c3[0] = add_four([own] + [c3[s] for s in rest])
    if stage < 2:
        start_all(reduce_copies(stage + 1, part, refs))


def shard_rows(o_ref, part, x_low, z, core):
    sub = x_low * 4 + z if part == 2 else z * 2 + x_low
    return o_ref.at[core, pl.ds(aligned(FIRST[part] + sub * PIECE[part], 16), PIECE[part]), :]


def spread_steps(part, mine, sems, o_ref):
    local, send, recv = sems
    x, y, z, core = place()
    low = x % 2
    pair = device_at(x // 2 * 2 + 1 - low, y, z, core)
    spot = shard_rows(o_ref, part, low, z, core)
    own = pltpu.make_async_copy(mine, spot, local.at[part])
    first = remote(mine, spot, send.at[part, 0], recv.at[part, 0], pair)
    second = [remote(mine, spot, send.at[part, d], recv.at[part, d], along("z", d)) for d in (1, 3, 2)]
    spot = shard_rows(o_ref, part, 1 - low, z, core)
    third = [remote(spot, spot, send.at[part, 3 + d], recv.at[part, 3 + d], along("z", d)) for d in (1, 3, 2)]

    def begin():
        start_all([own, first] + second)

    def middle():
        first.wait()
        start_all(third)

    def end():
        wait_all([own] + second + third)

    return begin, middle, end


def swap_partner(shift):
    mine = lax.axis_index("seq") * 2 + lax.axis_index("wshard")
    other = (mine + shift) % NB
    return other, (lax.axis_index("dp"), other // 2, other % 2)


def swap_greet():
    barrier = pltpu.get_barrier_semaphore()

    @pl.loop(1, NB)
    def _(shift):
        pl.semaphore_signal(barrier, inc=1, device_id=swap_partner(shift)[1], device_id_type=MESH)

    pl.semaphore_wait(barrier, NB - 1)


def swap_copies(piece_for, landing_from, sems):
    mine = lax.axis_index("seq") * 2 + lax.axis_index("wshard")
    send, recv, local = sems

    def copy(shift):
        other, device = swap_partner(shift)
        return remote(piece_for(other), landing_from(mine), send.at[shift], recv.at[shift], device)

    own = pltpu.make_async_copy(piece_for(mine), landing_from(mine), local)

    def start():
        @pl.loop(1, NB)
        def _(shift):
            copy(shift).start()

        own.start()

    def wait():
        @pl.loop(1, NB)
        def _(shift):
            copy(shift).wait()

        own.wait()

    return start, wait


def swap_sems():
    return [pltpu.SemaphoreType.DMA((NB,)), pltpu.SemaphoreType.DMA((NB,)), pltpu.SemaphoreType.DMA]


def block_of(ref, b):
    return ref.at[b]


def head_tile(ref, b):
    return ref.at[pl.ds(aligned((b // 2) * HD, HD), HD), pl.ds(aligned((b % 2) * TB, TB), TB)]


def head_tile3(ref, b):
    return ref.at[:, pl.ds(aligned((b // 2) * HD, HD), HD), pl.ds(aligned((b % 2) * TB, TB), TB)]


HALVES = ((128, 2048), (256, 1024))


class Transfers:
    def __init__(self, send, recv):
        self.send, self.recv, self.used = send, recv, 0

    def copy(self, src, dst, target):
        made = remote(src, dst, self.send.at[self.used], self.recv.at[self.used], target)
        self.used += 1
        return made


def start_all(copies):
    for copy in copies:
        copy.start()


def wait_all(copies):
    for copy in copies:
        copy.wait()


def unit_rows(matrix, unit, count=1):
    rows = HALVES[matrix][0] // 4
    return pl.ds(unit * rows, count * rows)


def columns_part(matrix, at, parts):
    width = HALVES[matrix][1] // parts
    return pl.ds(aligned(at * width, 128), width)


def half_rows(core, rows=64):
    return pl.ds(aligned(core * rows, rows), rows)


def shard_greet():
    x, y, z, core = place()
    return [device_at(x, (y + d) % 4, z, core) for d in (1, 2, 3)] + [
        device_at(3 - x, (y + d) % 4, z, core) for d in range(4)
    ]


def greet_signal(others):
    barrier = pltpu.get_barrier_semaphore()

    @pl.loop(1, NB)
    def _(shift):
        pl.semaphore_signal(barrier, inc=1, device_id=swap_partner(shift)[1], device_id_type=MESH)

    for other in others:
        pl.semaphore_signal(barrier, inc=1, device_id=other, device_id_type=MESH)


def greet_wait(others):
    pl.semaphore_wait(pltpu.get_barrier_semaphore(), NB - 1 + len(others))


FRONT_COPIES = 144


def front_kernel(
    tokens, segments, flags, vectors, b_up, w_out, w_up, w_down, w_qkv,
    x_seq, meta_out, smalls_out, out_all, up_all, down_all, qkv_all, qat_ref, ka_ref, va_ref, kt_ref, q_ref,
    context, wide_ref, lse_ref,
    vat_ref, blocks, x_buf, tok_buf, out_buf, up_buf, down_buf, qkv_buf, meta, heads, smalls, meta_all, heads_all, smalls_all, w_ref, b_ref,
    send, recv, local, meta_send, meta_recv, meta_local, back_send, back_recv, back_local,
):
    x, y, z, core = place()
    hi, lo = x // 2, x % 2
    mine, across = y * 2 + hi, y * 2 + 1 - hi
    wrap, pair, other_core = device_at(3 - x, y, z, core), device_at(hi * 2 + 1 - lo, y, z, core), sibling()
    shards, wholes = (up_buf.at[core], down_buf), (up_all, down_all)
    rows_out = half_rows(core)
    greet_signal(shard_greet())
    load_tokens = pltpu.make_async_copy(tokens, tok_buf, local.at[0])
    load_qkv = pltpu.make_async_copy(w_qkv, qkv_buf, local.at[11])
    loads = [
        pltpu.make_async_copy(w_out, out_buf, local.at[9]),
        pltpu.make_async_copy(w_down.at[half_rows(core, 256)], down_buf, local.at[10]),
    ]
    for j in range(8):
        piece = w_up.at[:, pl.ds(aligned(j * 512 + core * 256, 256), 256)]
        loads.append(pltpu.make_async_copy(piece, up_buf.at[core, :, pl.ds(j * 256, 256)], local.at[1 + j]))
    start_all([load_tokens, load_qkv] + loads)
    meta[...] = jnp.zeros_like(meta)
    for s in range(2):
        meta[s, 0:1, :] = segments[s : s + 1, :]
        meta[s, 1:2, :] = flags[s : s + 1, :]
    smalls[...] = jnp.zeros_like(smalls)
    smalls[0:8, :] = vectors[...]
    smalls[8:12, :] = b_up[...]
    greet_wait(shard_greet())
    load_tokens.wait()
    net = Transfers(send, recv)
    first, second = pl.ds(0, 64), pl.ds(64, 64)

    def block(at, low, w, rows=slice(None)):
        return x_buf.at[at, low, core, w, rows]

    own = tok_buf.at[hi]
    swap = net.copy(tok_buf.at[1 - hi], block(z, lo, hi), wrap)
    own_z = [net.copy(own, block(z, lo, hi), along("z", d)) for d in (1, 3, 2)]
    own_pair = [net.copy(own.at[rows], block(z, lo, hi, rows), pair) for rows in (first, second)]
    start_all([swap, own_pair[0]] + own_z)
    x_buf[z, lo, core, hi] = tok_buf[hi]
    load_qkv.wait()
    for p in range(3):
        for k, pair_at in ((0, z * 2 + lo), (1, z * 2 + 1 - lo)):
            heads[k, :, 128 * p : 128 * (p + 1)] = qkv_buf[:, pl.ds(aligned(p * D + pair_at * 128, 128), 128)]
    cross_first = [
        net.copy(heads.at[1], heads_all.at[mine], wrap),
        net.copy(smalls, smalls_all.at[mine], wrap),
    ]
    start_all(cross_first)

    def small_y(shard, heads_source, smalls_source):
        copies = []
        for d in (1, 3, 2):
            copies.append(net.copy(heads_source, heads_all.at[shard], along("y", d)))
            copies.append(net.copy(smalls_source, smalls_all.at[shard], along("y", d)))
        return copies

    own_small = small_y(mine, heads.at[0], smalls)
    start_all(own_small)
    heads_all[mine] = heads[0]
    smalls_all[mine] = smalls[...]
    meta_start, meta_wait = swap_copies(
        lambda b: meta.at[b % 2], lambda b: meta_all.at[b], (meta_send, meta_recv, meta_local)
    )
    meta_start()
    wait_all(loads)
    keep = [
        pltpu.make_async_copy(out_buf.at[rows_out], out_all.at[mine, rows_out], local.at[9]),
        pltpu.make_async_copy(qkv_buf, qkv_all.at[mine], local.at[11]),
    ]
    for m in range(2):
        parts = [
            (unit_rows(m, 0), columns_part(m, z, 4)),
            (unit_rows(m, 3), columns_part(m, lo, 2)),
            (unit_rows(m, 1, 2), slice(None)),
        ]
        for k, (rows, columns) in enumerate(parts):
            piece = wholes[m].at[mine, rows, columns]
            keep.append(pltpu.make_async_copy(shards[m].at[rows, columns], piece, local.at[1 + 3 * m + k]))
    start_all(keep)

    def along_y(shard, source, out_source, up_unit):
        copies = []
        for d in (1, 3, 2):
            there = along("y", d)
            copies.append(net.copy(out_source.at[rows_out], out_all.at[shard, rows_out], there))
            for m in range(2):
                parts = [(0, columns_part(m, z, 4)), (3, columns_part(m, lo, 2))]
                if up_unit:
                    parts.append((1, slice(None)))
                for unit, columns in parts:
                    rows = unit_rows(m, unit, 2 if m == 1 and unit == 1 else 1)
                    copies.append(net.copy(source(m).at[rows, columns], wholes[m].at[shard, rows, columns], there))
        return copies

    own_y = along_y(mine, lambda m: shards[m], out_buf, True)
    start_all(own_y)
    swap.wait_recv()
    came = block(z, 1 - lo, 1 - hi)
    came_pair = [
        net.copy(block(z, 1 - lo, 1 - hi, rows), block(z, 1 - lo, 1 - hi, rows), pair) for rows in (first, second)
    ]
    came_z = [net.copy(came, came, along("z", d)) for d in (1, 3, 2)]
    start_all([came_pair[0]] + came_z + [own_pair[1], came_pair[1]])
    cross_early, cross_late = [net.copy(out_buf.at[rows_out], out_all.at[mine, rows_out], wrap)], []
    for m in range(2):
        for unit, columns in ((0, columns_part(m, z, 4)), (3, columns_part(m, 1 - lo, 2))):
            rows = unit_rows(m, unit)
            cross_early.append(net.copy(shards[m].at[rows, columns], wholes[m].at[mine, rows, columns], wrap))
    rows = unit_rows(0, 1, 2)
    cross_late.append(net.copy(shards[0].at[rows], up_all.at[mine, rows], wrap))
    rows = half_rows(core)
    cross_late.append(net.copy(qkv_buf.at[rows], qkv_all.at[mine, rows], wrap))
    start_all(cross_early)
    pair_late = []

    def forward(got, d, low, w):
        got.wait_recv()
        piece = block((z + 4 - d) % 4, low, w, second)
        pair_late.append(net.copy(piece, piece, pair))
        pair_late[-1].start()

    for i, d in enumerate((1, 3, 2)):
        forward(own_z[i], d, lo, hi)
    for copy in cross_first:
        copy.wait_recv()
    across_small = small_y(across, heads_all.at[across], smalls_all.at[across])
    start_all(across_small)
    half_z = []

    def halves(got, low, w):
        got.wait_recv()
        piece = block(z, low, w, first)
        copies = [net.copy(piece, piece, along("z", d)) for d in (1, 3, 2)]
        start_all(copies)
        half_z.extend(copies)

    halves(own_pair[0], 1 - lo, hi)
    for copy in cross_early:
        copy.wait_recv()
    across_y = along_y(across, lambda m: wholes[m].at[across], out_all.at[across], False)
    start_all(across_y + cross_late)
    for i, d in enumerate((1, 3, 2)):
        forward(came_z[i], d, 1 - lo, 1 - hi)
    halves(came_pair[0], lo, 1 - hi)
    share, rest = [], []
    for low, w in ((lo, hi), (1 - lo, 1 - hi)):
        piece = x_buf.at[:, low, core, w]
        share.append(net.copy(piece, piece, other_core))
    start_all(share)

    for copy in own_small + across_small:
        copy.wait_recv()
    meta_wait()
    at_first = core == 0
    both = heads_all[...].reshape(D, 384)
    parts = [jnp.where(at_first, both[:, 128 * p : 128 * p + HD], both[:, 128 * p + HD : 128 * (p + 1)]) for p in range(3)]
    w_ref[...] = jnp.concatenate(parts, axis=1)
    biases = smalls_all[lax.axis_index("seq") // 2]
    bias = [jnp.where(at_first, biases[k : k + 1, :HD], biases[k : k + 1, HD:]) for k in range(2)]
    b_ref[...] = jnp.broadcast_to(jnp.concatenate([bias[0], jnp.zeros((1, HD), F32), bias[1]], axis=1), (8, 3 * HD))

    def project(low, at_core, w):
        @pl.loop(0, 4)
        def _(at):
            b = at * 8 + low * 4 + at_core * 2 + w
            rows = pl.ds(aligned(b * TB, TB), TB)
            side = dot(x_buf[at, low, at_core, w], w_ref[...]) + b_ref[:1, :]
            q8 = side[:, :HD].astype(BF).astype(F32) * 0.125
            hot = jnp.where(lax.broadcasted_iota(jnp.int32, (32, TB), 0) == meta_all[b, 0:1, :], 1.0, 0.0)
            lane = lax.broadcasted_iota(jnp.int32, (TB, HD), 1)
            ones3 = jnp.where(lane < 3, 1.0, 0.0)
            apart = (hot.T - 1.0) * MASKED
            key = side[:, HD : 2 * HD]
            value = side[:, 2 * HD :]
            q_ref[rows, :] = q8.astype(BF)
            ka_ref[rows, :] = jnp.concatenate([key, apart, ones3[:, :32]], axis=1).astype(BF)
            va_ref[rows, :] = jnp.concatenate([value, ones3], axis=1).astype(BF)
            qat_ref[:, rows] = jnp.concatenate([q8.T, hot, jnp.zeros((32, TB), F32)], axis=0).astype(BF)
            kt_ref[:, rows] = key.T.astype(BF)
            ones_row = jnp.where(lax.broadcasted_iota(jnp.int32, (16, TB), 0) == 0, 1.0, 0.0)
            vat_ref[:, rows] = jnp.concatenate([value.T, ones_row], axis=0).astype(BF)

    project(lo, core, hi)
    project(1 - lo, core, 1 - hi)
    for copy in half_z + [own_pair[1], came_pair[1]] + pair_late:
        copy.wait_recv()
    for low, w in ((1 - lo, hi), (lo, 1 - hi)):
        piece = x_buf.at[:, low, core, w]
        rest.append(net.copy(piece, piece, other_core))
    start_all(rest)
    for copy in share:
        copy.wait_recv()
    project(1 - lo, core, hi)
    project(lo, core, 1 - hi)
    project(lo, 1 - core, hi)
    project(1 - lo, 1 - core, 1 - hi)
    for copy in rest:
        copy.wait_recv()
    store = pltpu.make_async_copy(x_buf, x_seq, local.at[0])
    store.start()
    project(1 - lo, 1 - core, hi)
    project(lo, 1 - core, 1 - hi)
    meta_out[...] = meta_all[...]
    smalls_out[...] = smalls_all[...]

    wait_all(keep)
    for copy in own_y + across_y + cross_late:
        copy.wait_recv()
    later = []
    for m in range(2):
        piece = wholes[m].at[:, unit_rows(m, 3), columns_part(m, lo, 2)]
        later.append(net.copy(piece, piece, pair))
        for d in (1, 3, 2):
            piece = wholes[m].at[:, unit_rows(m, 0), columns_part(m, z, 4)]
            later.append(net.copy(piece, piece, along("z", d)))
    for d in (1, 3, 2):
        for shard, unit, number in ((mine, 2, 1), (across, 1, 2)):
            piece = up_all.at[shard, unit_rows(0, unit, number)]
            later.append(net.copy(piece, piece, along("y", d)))
    piece = out_all.at[:, half_rows(core)]
    later.append(net.copy(piece, piece, other_core))
    for d in range(4):
        piece = down_all.at[(y + d) % 4 * 2 + hi, unit_rows(1, 1, 2)]
        later.append(net.copy(piece, piece, wrap))
    later += qkv_along_y(qkv_all, net, 0, 16)
    start_all(later)

    position = lax.axis_index("seq") * 2 + hi

    def result(b, recv_at):
        there = head_tile(context, position)
        return remote(blocks.at[b], there, back_send.at[b], back_recv.at[recv_at], (y, b // 2, b % 2))

    own_result = pltpu.make_async_copy(blocks.at[position], head_tile(context, position), back_local)

    @pl.loop(0, 4)
    def _(step):
        at = (step + z + 1) % 4
        columns = pl.ds(aligned(at * 1024, 1024), 1024)
        queries = qat_ref[:, columns]
        peak = jnp.full((1, 1024), -jnp.inf, F32)
        total = jnp.zeros((80, 1024), F32)
        for j in range(8):
            keys = slice(j * 512, (j + 1) * 512)
            logits = dot(ka_ref[keys, :], queries)
            new_peak = jnp.maximum(peak, jnp.max(logits, axis=0, keepdims=True))
            expos = jnp.exp(logits - new_peak).astype(BF)
            total = total * jnp.exp(peak - new_peak) + dot(vat_ref[:, keys], expos)
            peak = new_peak
        sums = total[HD : HD + 1]
        found = total[:HD] / sums
        wide_ref[:, columns] = found
        lse_ref[:, columns] = peak + jnp.log(sums)
        low = found.astype(BF)
        for j in range(8):
            b = at * 8 + j
            blocks[b] = low[:, j * TB : (j + 1) * TB]

            @pl.when(b != position)
            def _():
                result(b, position).start()

            @pl.when(b == position)
            def _():
                own_result.start()

    store.wait()
    for copy in [swap] + own_pair + own_z + came_pair + came_z + half_z + pair_late + share + rest:
        copy.wait_send()
    for copy in cross_first + cross_early + cross_late + own_small + across_small + own_y + across_y:
        copy.wait_send()
    wait_all(later)

    @pl.loop(1, NB)
    def _(shift):
        b = (position + shift) % NB
        result(b, b).wait()

    own_result.wait()


def front(tokens, segments, flags, vectors, b_up, w_out, w_up, w_down, w_qkv):
    shape = jax.ShapeDtypeStruct
    in_vmem = pl.BlockSpec(memory_space=pltpu.VMEM)
    return pl.pallas_call(
        front_kernel,
        in_specs=[ANY] + [in_vmem] * 4 + [ANY] * 4,
        out_specs=[ANY] + [in_vmem] * 2 + [ANY] * 4 + [in_vmem] * 5 + [ANY] + [in_vmem] * 2,
        out_shape=[
            shape((4, 2, 2, 2, TB, D), BF),
            shape((NB, 8, TB), jnp.int32),
            shape((8, 16, 128), F32),
            shape((8, 128, D), BF),
            shape((8, 128, 2048), BF),
            shape((8, 256, D), BF),
            shape((8, 128, 3 * D), BF),
            shape((128, L), BF),
            shape((L, 128), BF),
            shape((L, 128), BF),
            shape((HD, L), BF),
            shape((L, HD), BF),
            shape((D, 2 * TB), BF),
            shape((HD, L), F32),
            shape((1, L), F32),
        ],
        scratch_shapes=[
            pltpu.VMEM((80, L), BF),
            pltpu.VMEM((NB, HD, TB), BF),
            pltpu.VMEM((4, 2, 2, 2, TB, D), BF),
            pltpu.VMEM((2, TB, D), BF),
            pltpu.VMEM((128, D), BF),
            pltpu.VMEM((2, 128, 2048), BF),
            pltpu.VMEM((256, D), BF),
            pltpu.VMEM((128, 3 * D), BF),
            pltpu.VMEM((2, 8, TB), jnp.int32),
            pltpu.VMEM((2, 128, 384), BF),
            pltpu.VMEM((16, 128), F32),
            pltpu.VMEM((NB, 8, TB), jnp.int32),
            pltpu.VMEM((8, 128, 384), BF),
            pltpu.VMEM((8, 16, 128), F32),
            pltpu.VMEM((D, 3 * HD), BF),
            pltpu.VMEM((8, 3 * HD), F32),
            pltpu.SemaphoreType.DMA((FRONT_COPIES,)),
            pltpu.SemaphoreType.DMA((FRONT_COPIES,)),
            pltpu.SemaphoreType.DMA((12,)),
            *swap_sems(),
            *swap_sems(),
        ],
        name="front",
        compiler_params=pltpu.CompilerParams(
            collective_id=1, has_side_effects=True, vmem_limit_bytes=VMEM_CAP
        ),
    )(tokens, segments, flags, vectors, b_up, w_out, w_up, w_down, w_qkv)


def qkv_along_y(qkv_all, net, first, count):
    _, y, _, core = place()
    copies = []
    for d in (1, 3, 2):
        for w in range(2):
            piece = qkv_all.at[y * 2 + w, pl.ds(aligned(core * 64 + first, 16), count)]
            copies.append(net.copy(piece, piece, along("y", d)))
    return copies


def turned(first, second):
    return dot(first, second, ((0,), (0,)))


def gelu_both(u):
    rate = 0.7978845608028654
    square = u * u
    curve = jnp.tanh(rate * (u + 0.044715 * (square * u)))
    half = 0.5 * (1.0 + curve)
    slope = half + 0.5 * u * (1.0 - curve * curve) * (rate * (1.0 + 0.134145 * square))
    return u * half, slope


def fold(values):
    return jnp.sum(values.reshape(values.shape[0] // 8, 8, values.shape[1]), axis=0)


ROWS = 256
CHUNK = 32
SMALLS = 16


def middle_kernel(
    context_in, meta, tokens, teacher, flags, smalls, out_all, up_all, down_all, a0,
    states, resid_out, do, g_ref, sums_out, count_out, qkv_all,
    context, context_s, w_out, w_up, w_down, h, act, slope, send_one, come_one, send_two, come_two,
    gb, gu, ga, ga_s, normed, hidden, rate, work, resid, gct, stage, count, counts, valid,
    send, recv, local, back_send, back_recv, back_local,
):
    x, y, z, core = place()
    mine = y * 2 + x // 2
    twin = sibling()
    loads = [
        pltpu.make_async_copy(context_in, context, local.at[6]),
        pltpu.make_async_copy(out_all, w_out, local.at[0]),
        pltpu.make_async_copy(up_all, w_up, local.at[1]),
    ]
    load_down = pltpu.make_async_copy(down_all, w_down, local.at[2])
    start_all(loads + [load_down])
    greet_signal(shard_greet())
    greet_wait(shard_greet())
    net = Transfers(send, recv)
    later = qkv_along_y(qkv_all, net, 16, 48)
    valid_here = jnp.sum(meta[:, 1, :].astype(F32), axis=0, keepdims=True)
    count[...] = jnp.broadcast_to(jnp.sum(valid_here, axis=1, keepdims=True), (8, 128))
    ahead = [net.copy(count, counts.at[mine], target) for target in shard_greet()]
    start_all(ahead + later)
    own_count = pltpu.make_async_copy(count, counts.at[mine], local.at[3])
    own_count.start()
    for s in range(2):
        column = jnp.broadcast_to(flags[s : s + 1, :].astype(F32), (128, 128)).T
        valid[128 * s : 128 * (s + 1), :] = column

    def vector(row):
        return jnp.concatenate([smalls[i, row : row + 1, :] for i in range(8)], axis=1)

    out_bias, gain_one, offset_one, down_bias, gain_two, offset_two = [vector(row) for row in range(2, 8)]
    zeros = jnp.zeros((8, D), F32)
    wait_all(loads)
    give_context = net.copy(context, context_s, twin)
    give_context.start()
    work[...] = turned(context[...], w_out[...].reshape(D, D))

    @pl.loop(0, ROWS // CHUNK)
    def _(i):
        rows = pl.ds(aligned(i * CHUNK, CHUNK), CHUNK)
        total = tokens[rows, :].astype(F32) + work[rows, :] + out_bias
        centre = total - jnp.mean(total, axis=1, keepdims=True)
        scale = lax.rsqrt(jnp.mean(centre * centre, axis=1, keepdims=True) + EPS)
        unit = centre * scale
        normed[rows, :] = unit
        rate[rows, :] = jnp.broadcast_to(scale, (CHUNK, 128))
        full = unit * gain_one + offset_one
        hidden[rows, :] = full
        h[0, rows, :] = full.astype(BF)

    give_hidden = net.copy(h.at[0], h.at[1], twin)
    give_hidden.start()
    for slot in range(2):
        if slot == 1:
            give_hidden.wait()
        for k in range(8):
            columns = slice(256 * k, 256 * (k + 1))
            bias = jnp.concatenate([smalls[k, pl.ds(8 + 2 * core + e, 1), :] for e in range(2)], axis=1)
            u = dot(h[slot], w_up[:, :, columns].reshape(D, 256)) + bias
            value, incline = gelu_both(u)
            act[slot, :, columns] = value.astype(BF)
            slope[slot, :, columns] = incline
    load_down.wait()
    send_one[...] = dot(act[1], w_down[...].reshape(2048, D))
    give_one = net.copy(send_one, come_one, twin)
    give_one.start()
    work[...] = dot(act[0], w_down[...].reshape(2048, D))
    give_one.wait()
    wait_all(ahead)
    own_count.wait()
    total_count = jnp.sum(counts[...], axis=0)
    count_out[...] = total_count
    factor = (128 * ROWS) / total_count[:1, :1]

    def loss_rows(i, carried):
        rows = pl.ds(aligned(i * CHUNK, CHUNK), CHUNK)
        total = hidden[rows, :] + (work[rows, :] + come_one[rows, :] + down_bias)
        centre = total - jnp.mean(total, axis=1, keepdims=True)
        scale = lax.rsqrt(jnp.mean(centre * centre, axis=1, keepdims=True) + EPS)
        unit = centre * scale
        final = unit * gain_two + offset_two
        states[rows, :] = final.astype(BF)
        differ = final - teacher[rows, :].astype(F32)
        held = valid[rows, :1] * differ
        grad = factor * held
        weighted = grad * gain_two
        back = weighted - jnp.mean(weighted, axis=1, keepdims=True)
        back = scale * (back - unit * jnp.mean(weighted * unit, axis=1, keepdims=True))
        resid[rows, :] = back
        low = back.astype(BF)
        gb[0, rows, :] = low
        return (
            carried[0] + fold(grad * unit),
            carried[1] + fold(grad),
            carried[2] + fold(low.astype(F32)),
            carried[3] + fold(held * differ),
        )

    gain_two_sum, offset_two_sum, down_sum, error = lax.fori_loop(
        0, ROWS // CHUNK, loss_rows, (zeros, zeros, zeros, zeros)
    )
    give_branch = net.copy(gb.at[0], gb.at[1], twin)
    give_branch.start()
    up_sums = []
    for slot in range(2):
        if slot == 1:
            give_branch.wait()
        for k in range(8):
            columns = slice(256 * k, 256 * (k + 1))
            pulled = dot(gb[slot], w_down[k], ((1,), (1,))) * slope[slot, :, columns]
            low = pulled.astype(BF)
            gu[slot, :, columns] = low
            up_sums.append(fold(low.astype(F32)))
    for i in range(8):
        send_two[:, 128 * i : 128 * (i + 1)] = dot(gu[1], w_up[i], ((1,), (1,)))
    give_two = net.copy(send_two, come_two, twin)
    give_two.start()
    for i in range(8):
        work[:, 128 * i : 128 * (i + 1)] = dot(gu[0], w_up[i], ((1,), (1,)))
    give_two.wait()

    def first_norm_rows(i, carried):
        rows = pl.ds(aligned(i * CHUNK, CHUNK), CHUNK)
        grad = resid[rows, :] + (work[rows, :] + come_two[rows, :])
        unit = normed[rows, :]
        weighted = grad * gain_one
        back = weighted - jnp.mean(weighted, axis=1, keepdims=True)
        back = rate[rows, :1] * (back - unit * jnp.mean(weighted * unit, axis=1, keepdims=True))
        resid_out[rows, :] = back
        low = back.astype(BF)
        ga[rows, :] = low
        return (carried[0] + fold(grad * unit), carried[1] + fold(grad), carried[2] + fold(low.astype(F32)))

    gain_one_sum, offset_one_sum, out_sum = lax.fori_loop(0, ROWS // CHUNK, first_norm_rows, (zeros, zeros, zeros))
    give_attended = net.copy(ga.at[:, pl.ds(aligned((1 - core) * 512, 512), 512)], ga_s, twin)
    give_attended.start()
    gct[...] = dot(w_out[...].reshape(D, D), ga[...], ((1,), (1,))).astype(BF)
    back_start, back_wait = swap_copies(
        lambda b: head_tile(gct, b), lambda b: do.at[b], (back_send, back_recv, back_local)
    )
    back_start()

    error = jnp.broadcast_to(jnp.sum(jnp.sum(error, axis=0, keepdims=True), axis=1, keepdims=True), (1, 128))
    lines = [out_sum, gain_one_sum, offset_one_sum, down_sum, gain_two_sum, offset_two_sum]
    lines = [jnp.sum(line, axis=0, keepdims=True) for line in lines]
    for i in range(8):
        columns = slice(128 * i, 128 * (i + 1))
        sums_out[i] = jnp.zeros((SMALLS, 128), F32)
        for row, line in enumerate(lines):
            sums_out[i, row : row + 1, :] = line[:, columns]
        both = jnp.sum(up_sums[i] + up_sums[8 + i], axis=0, keepdims=True)
        for e in range(2):
            sums_out[i, pl.ds(6 + 2 * core + e, 1), :] = both[:, 128 * e : 128 * (e + 1)]
        sums_out[i, 10:11, :] = error

    give_context.wait()
    give_attended.wait()

    def stored(i):
        return pltpu.make_async_copy(stage.at[i % 2], g_ref.at[i // 2, i % 2], local.at[4 + i % 2])

    for i in range(8):
        if i >= 2:
            stored(i - 2).wait()
        tall = slice(128 * i, 128 * (i + 1))
        wide = slice(256 * i, 256 * (i + 1))
        up = turned(h[0, :, tall], gu[0]) + turned(h[1, :, tall], gu[1])
        for k in range(4):
            stage[i % 2, 128 * k : 128 * (k + 1), :] = up[:, 512 * k : 512 * (k + 1)].astype(BF)
        down = turned(act[0, :, wide], gb[0]) + turned(act[1, :, wide], gb[1])
        for k in range(2):
            stage[i % 2, 512 + 256 * k : 768 + 256 * k, :] = down[:, 512 * k : 512 * (k + 1)].astype(BF)
        own_half = ga[:, pl.ds(aligned(core * 512, 512), 512)]
        out = dot(context[tall, :], own_half) + dot(context_s[tall, :], ga_s[...])
        stage[i % 2, 1024:, :] = out.astype(BF)
        stored(i).start()
    stored(6).wait()
    stored(7).wait()
    back_wait()
    wait_all(later)


def middle(context, meta, tokens, teacher, flags, smalls, out_all, up_all, down_all, qkv_all):
    shape = jax.ShapeDtypeStruct
    in_vmem = pl.BlockSpec(memory_space=pltpu.VMEM)
    dma = pltpu.SemaphoreType.DMA
    wide = pltpu.VMEM((ROWS, D), F32)
    return pl.pallas_call(
        middle_kernel,
        in_specs=[ANY] + [in_vmem] * 5 + [ANY] * 4,
        out_specs=[in_vmem, in_vmem, ANY, ANY, in_vmem, in_vmem, ANY],
        out_shape=[
            shape((ROWS, D), BF),
            shape((ROWS, D), F32),
            shape((NB, HD, TB), BF),
            shape((4, 2, 1152, 512), BF),
            shape((8, SMALLS, 128), F32),
            shape((8, 128), F32),
            shape(qkv_all.shape, BF),
        ],
        input_output_aliases={9: 6},
        scratch_shapes=[
            pltpu.VMEM((D, ROWS), BF),
            pltpu.VMEM((D, ROWS), BF),
            pltpu.VMEM((8, 128, D), BF),
            pltpu.VMEM((8, 128, 2048), BF),
            pltpu.VMEM((8, 256, D), BF),
            pltpu.VMEM((2, ROWS, D), BF),
            pltpu.VMEM((2, ROWS, 2048), BF),
            pltpu.VMEM((2, ROWS, 2048), F32),
            wide,
            wide,
            wide,
            wide,
            pltpu.VMEM((2, ROWS, D), BF),
            pltpu.VMEM((2, ROWS, 2048), BF),
            pltpu.VMEM((ROWS, D), BF),
            pltpu.VMEM((ROWS, 512), BF),
            wide,
            wide,
            pltpu.VMEM((ROWS, 128), F32),
            wide,
            wide,
            pltpu.VMEM((D, ROWS), BF),
            pltpu.VMEM((2, 1152, 512), BF),
            pltpu.VMEM((8, 128), F32),
            pltpu.VMEM((8, 8, 128), F32),
            pltpu.VMEM((ROWS, 128), F32),
            dma((32,)),
            dma((32,)),
            dma((10,)),
            *swap_sems(),
        ],
        name="middle",
        compiler_params=pltpu.CompilerParams(
            collective_id=3, has_side_effects=True, vmem_limit_bytes=VMEM_CAP
        ),
    )(context, meta, tokens, teacher, flags, smalls, out_all, up_all, down_all, qkv_all)


BACK_KEYS = 256
BACK_STEPS = L // BACK_KEYS
BACK_WIDTH = 1024


def back_prepare(qat, do, wide, lse, queries, grads, grad_rows):
    for j in range(L // BACK_WIDTH):
        columns = slice(j * BACK_WIDTH, (j + 1) * BACK_WIDTH)
        grad_t = jnp.concatenate([do[j * (BACK_WIDTH // TB) + i] for i in range(BACK_WIDTH // TB)], axis=1)
        wider = grad_t.astype(F32)
        delta = jnp.sum(wider * wide[:, columns], axis=0, keepdims=True)
        grads[:HD, columns] = grad_t
        grads[HD:, columns] = jnp.concatenate([three_pieces(-delta), jnp.zeros((61, BACK_WIDTH), BF)], axis=0)
        queries[:96, columns] = qat[:96, columns]
        queries[96:, columns] = jnp.concatenate(
            [three_pieces(-lse[:, columns]), jnp.zeros((29, BACK_WIDTH), BF)], axis=0
        )
        grad_rows[columns, :] = wider.T.astype(BF)


def back_kernel(
    qat, ka, va, kt, q8, do, wide, lse, smalls, x_seq, g_ref, a0,
    projected, heads_out, shard_out, smalls_out, qkv_all,
    x_buf, queries, grads, grad_rows, dq, d_ref, mine_ref, parts_ref, sum_ref, heads_buf, small_buf, small_sum, small_all,
    send, recv, local, dk_send, dk_recv, dk_local, dq_send, dq_recv, dq_local, spread_send, spread_recv, *reduce_refs,
):
    x, y, z, core = place()
    shard_at = y * 2 + x // 2
    seq = lax.axis_index("seq")
    mine = seq * 2 + x // 2
    net = (g_ref,) + reduce_refs

    def shard_device(d):
        other = (shard_at + d) % 8
        return other, (other // 2, seq, other % 2)

    load_x = pltpu.make_async_copy(x_seq, x_buf, local.at[0])
    load_x.start()
    shard_others = [shard_device(d)[1] for d in range(1, 8)]
    greet_signal(shard_others)
    back_prepare(qat, do, wide, lse, queries, grads, grad_rows)
    dq[...] = jnp.zeros_like(dq)
    greet_wait(shard_others)
    for part in range(3):
        reduce_start(part, net)
    far = Transfers(send, recv)
    small_out = [far.copy(smalls.at[shard_device(d)[0]], small_buf.at[shard_at], shard_device(d)[1]) for d in range(1, 8)]
    start_all(small_out)
    small_buf[shard_at] = smalls[shard_at]
    rows = half_rows(core)
    weights = far.copy(qkv_all.at[:, rows], qkv_all.at[:, rows], sibling())
    weights.start()

    def landing(first, count):
        return projected.at[pl.ds(first, count), pl.ds(aligned(seq * HD, HD), HD), pl.ds(aligned((x // 2) * TB, TB), TB)]

    def block_device(b):
        return (y, b // 2, b % 2)

    def dk_copy(b, recv_at):
        return remote(d_ref.at[b, pl.ds(1, 2)], landing(1, 2), dk_send.at[b], dk_recv.at[recv_at], block_device(b))

    def dq_copy(b, recv_at):
        return remote(d_ref.at[b, pl.ds(0, 1)], landing(0, 1), dq_send.at[b], dq_recv.at[recv_at], block_device(b))

    dk_own = pltpu.make_async_copy(d_ref.at[mine, pl.ds(1, 2)], landing(1, 2), dk_local)
    dq_own = pltpu.make_async_copy(d_ref.at[mine, pl.ds(0, 1)], landing(0, 1), dq_local)

    @pl.loop(0, BACK_STEPS)
    def _(step):
        at = (step + 4 * (z + 1)) % BACK_STEPS
        keys = pl.ds(aligned(at * BACK_KEYS, BACK_KEYS), BACK_KEYS)
        ka_part, va_part, kt_part = ka[keys, :], va[keys, :], kt[:, keys]
        dk = jnp.zeros((BACK_KEYS, HD), F32)
        dv = jnp.zeros((BACK_KEYS, HD), F32)
        for j in range(L // BACK_WIDTH):
            columns = slice(j * BACK_WIDTH, (j + 1) * BACK_WIDTH)
            probs = jnp.exp(dot(ka_part, queries[:, columns]))
            raw = (probs * dot(va_part, grads[:, columns])).astype(BF)
            dv = dv + dot(probs.astype(BF), grad_rows[columns, :])
            dk = dk + dot(raw, q8[columns, :])
            dq[:, columns] += dot(kt_part, raw)
        dk_t, dv_t = dk.T.astype(BF), dv.T.astype(BF)
        for i in range(BACK_KEYS // TB):
            b = at * (BACK_KEYS // TB) + i
            d_ref[b, 1] = dk_t[:, i * TB : (i + 1) * TB]
            d_ref[b, 2] = dv_t[:, i * TB : (i + 1) * TB]

            @pl.when(b != mine)
            def _():
                dk_copy(b, mine).start()

            @pl.when(b == mine)
            def _():
                dk_own.start()

        @pl.when(step == 4)
        def _():
            first_relay(net)

        @pl.when(step == 9)
        def _():
            reduce_step(0, 1, net)

        @pl.when(step == 11)
        def _():
            reduce_step(0, 0, net)

        @pl.when(step == 13)
        def _():
            reduce_step(0, 2, net)
            reduce_step(1, 1, net)

    for b in range(NB):
        d_ref[b, 0] = (dq[:, b * TB : (b + 1) * TB] * 0.125).astype(BF)

    @pl.loop(1, NB)
    def _(shift):
        dq_copy((mine + shift) % NB, mine).start()

    dq_own.start()
    steps = [
        spread_steps(part, reduce_refs[6 + part].at[0], (local.at[pl.ds(1, 3)], spread_send, spread_recv), shard_out)
        for part in range(3)
    ]
    reduce_step(2, 1, net)
    steps[1][0]()
    wait_all(small_out)
    small_sum[...] = jnp.sum(small_buf[...], axis=0)

    load_x.wait()
    left = jnp.concatenate([d_ref[b].reshape(3 * HD, TB) for b in range(NB)], axis=1)
    sums = dot(jnp.ones((8, L), BF), left, ((1,), (1,)))
    gap = jnp.zeros((1, 128 - HD), F32)
    tail = jnp.concatenate(
        [
            jnp.concatenate([sums[:1, :HD], gap], axis=1),
            jnp.concatenate([sums[:1, 2 * HD :], gap], axis=1),
            jnp.zeros((14, 128), F32),
        ],
        axis=0,
    ).astype(BF)
    for i in range(4):
        total = dot(left, x_buf[:, :, 256 * i : 256 * (i + 1)].reshape(L, 256))
        for k in range(2):
            mine_ref[2 * i + k, : 3 * HD, :] = total[:, 128 * k : 128 * (k + 1)].astype(BF)
            mine_ref[2 * i + k, 3 * HD :, :] = tail
    part_out = [far.copy(mine_ref.at[shard_device(d)[0]], parts_ref.at[d], shard_device(d)[1]) for d in range(1, 8)]
    start_all(part_out)

    reduce_step(1, 2, net)
    reduce_step(1, 0, net)
    wait_all(part_out)
    added = mine_ref[shard_at].astype(F32)
    for d in range(1, 8):
        added = added + parts_ref[d].astype(F32)
    sum_ref[...] = added.astype(BF)
    heads_buf[seq // 2, core] = sum_ref[...]
    small_all[seq // 2, core] = small_sum[...]
    head_out = []
    for d in range(1, 8):
        target = (y, (seq + 2 * d) % 16, x // 2)
        head_out.append(far.copy(sum_ref, heads_buf.at[seq // 2, core], target))
        head_out.append(far.copy(small_sum, small_all.at[seq // 2, core], target))
    start_all(head_out)
    for part in (2, 0):
        reduce_step(2, part, net)
        steps[part][0]()
    for part in (1, 2, 0):
        steps[part][1]()
    wait_all(head_out)
    across = [
        far.copy(heads_buf.at[:, core], heads_buf.at[:, core], sibling()),
        far.copy(small_all.at[:, core], small_all.at[:, core], sibling()),
    ]
    start_all(across)
    shared = []
    for part in (1, 2, 0):
        steps[part][2]()
        piece = shard_out.at[core, pl.ds(FIRST[part], 8 * PIECE[part])]
        shared.append(far.copy(piece, piece, sibling()))
        shared[-1].start()

    @pl.loop(1, NB)
    def _(shift):
        b = (mine + shift) % NB
        dk_copy(b, b).wait()
        dq_copy(b, b).wait()

    dk_own.wait()
    dq_own.wait()
    weights.wait()
    wait_all(across)
    for i in range(8):
        heads_out[2 * i] = heads_buf[i, 0]
        heads_out[2 * i + 1] = heads_buf[i, 1]
    smalls_out[...] = jnp.sum(small_all[...].reshape(16, 16, 128), axis=0)
    wait_all(shared)


def back(qat, ka, va, kt, q8, do, wide, lse, smalls, x_seq, g, qkv_all):
    shape = jax.ShapeDtypeStruct
    in_vmem = pl.BlockSpec(memory_space=pltpu.VMEM)
    dma = pltpu.SemaphoreType.DMA
    return pl.pallas_call(
        back_kernel,
        in_specs=[in_vmem] * 9 + [ANY] * 3,
        out_specs=[ANY, in_vmem, ANY, in_vmem, ANY],
        out_shape=[
            shape((3, D, 2 * TB), BF),
            shape((H, 208, 128), BF),
            shape((2, 1152, 512), BF),
            shape((16, 128), F32),
            shape(qkv_all.shape, BF),
        ],
        input_output_aliases={11: 4},
        scratch_shapes=[
            pltpu.VMEM((NB, TB, D), BF),
            pltpu.VMEM((128, L), BF),
            pltpu.VMEM((128, L), BF),
            pltpu.VMEM((L, HD), BF),
            pltpu.VMEM((HD, L), F32),
            pltpu.VMEM((NB, 3, HD, TB), BF),
            pltpu.VMEM((8, 208, 128), BF),
            pltpu.VMEM((8, 208, 128), BF),
            pltpu.VMEM((208, 128), BF),
            pltpu.VMEM((8, 2, 208, 128), BF),
            pltpu.VMEM((8, 16, 128), F32),
            pltpu.VMEM((16, 128), F32),
            pltpu.VMEM((8, 2, 16, 128), F32),
            dma((40,)),
            dma((40,)),
            dma((4,)),
            *swap_sems(),
            *swap_sems(),
            dma((3, 8)),
            dma((3, 8)),
            *reduce_scratch(),
        ],
        name="attend_back",
        compiler_params=pltpu.CompilerParams(
            collective_id=4, has_side_effects=True, vmem_limit_bytes=VMEM_CAP
        ),
    )(qat, ka, va, kt, q8, do, wide, lse, smalls, x_seq, g, qkv_all)


def finish_kernel(
    projected, qkv_ref, resid_ref, heads_ref, shard_ref, tokens_ref, grad_qkv, grad_out, grad_up, grad_down
):
    step = pl.program_id(0)
    tokens_ref[...] = resid_ref[...] + dot(projected[...], qkv_ref[...], ((0,), (1,)))
    for c in range(2):
        columns = slice(512 * c, 512 * (c + 1))
        for j in range(2):
            piece = shard_ref[c, pl.ds(aligned(step * 128, 128), 128), 256 * j : 256 * (j + 1)]
            grad_up[:, 512 * j + 256 * c : 512 * j + 256 * (c + 1)] = piece.astype(F32)
        rows = pl.ds(aligned(512 + 256 * c + (step % 2) * 128, 128), 128)
        grad_down[:, columns] = shard_ref[step // 2, rows, :].astype(F32)
        grad_out[:, columns] = shard_ref[c, pl.ds(aligned(1024 + step * 32, 32), 32), :].astype(F32)

    @pl.when(step == 0)
    def _():
        for p in range(3):
            for pair in range(8):
                both = [heads_ref[2 * pair + k, p * HD : (p + 1) * HD, :].astype(F32) for k in range(2)]
                at = p * D + pair * 128
                grad_qkv[:, at : at + 128] = jnp.concatenate(both, axis=0).T


def finish(projected, qkv, resid, heads, shard):
    shape = jax.ShapeDtypeStruct

    def whole(dims):
        return pl.BlockSpec(dims, lambda i: (0,) * len(dims))

    return pl.pallas_call(
        finish_kernel,
        grid=(4,),
        in_specs=[
            whole((3 * D, 2 * TB)),
            pl.BlockSpec((256, 3 * D), lambda i: (i, 0)),
            pl.BlockSpec((2 * TB, 256), lambda i: (0, i)),
            whole((H, 208, 128)),
            whole((2, 1152, 512)),
        ],
        out_specs=[
            pl.BlockSpec((2 * TB, 256), lambda i: (0, i)),
            whole((128, 3 * D)),
            pl.BlockSpec((32, D), lambda i: (i, 0)),
            pl.BlockSpec((128, 1024), lambda i: (0, i)),
            pl.BlockSpec((128, D), lambda i: (i, 0)),
        ],
        out_shape=[
            shape((2 * TB, D), F32),
            shape((128, 3 * D), F32),
            shape((128, D), F32),
            shape((128, FF), F32),
            shape((512, D), F32),
        ],
        name="finish",
        compiler_params=pltpu.CompilerParams(vmem_limit_bytes=VMEM_CAP),
    )(projected, qkv, resid, heads, shard)


def on_device(
    tokens,
    segments,
    valid_flags,
    teacher,
    w_qkv,
    b_query,
    b_value,
    w_out,
    b_out,
    ln1_gain,
    ln1_bias,
    w_up,
    b_up,
    w_down,
    b_down,
    ln2_gain,
    ln2_bias,
):
    seq_local, row_local, _ = tokens.shape
    token_rows = seq_local * row_local
    shard_at = lax.axis_index("dp") * 2 + lax.axis_index("wshard")

    vectors = jnp.stack([b_query, b_value, b_out, ln1_gain, ln1_bias, b_down, ln2_gain, ln2_bias]).astype(F32)
    (
        x_seq, meta_all, smalls_all, out_all, up_all, down_all, qkv_all, qat, ka, va, kt, q8, context, wide, lse
    ) = front(
        tokens, segments, valid_flags, vectors, b_up.reshape(4, 128).astype(F32), w_out, w_up, w_down, w_qkv
    )
    x_seq = x_seq.reshape(NB, TB, D)
    states, grad_resid_one, do, g, small_sums, count, qkv_all = middle(
        context,
        meta_all,
        tokens.reshape(token_rows, D),
        teacher.reshape(token_rows, D),
        valid_flags,
        smalls_all,
        out_all,
        up_all,
        down_all,
        qkv_all,
    )
    projected, heads_out, shard_out, small_out, qkv_all = back(
        qat, ka, va, kt, q8, do, wide, lse, small_sums, x_seq, g, qkv_all
    )
    grad_tokens, grad_qkv, grad_out, grad_up, grad_down = finish(
        projected.reshape(3 * D, token_rows), qkv_all.reshape(D, 3 * D), grad_resid_one, heads_out, shard_out
    )
    own_heads = lax.dynamic_slice(heads_out, (shard_at * 2, 3 * HD, 0), (2, 2, HD)).astype(F32)
    mean_loss = small_out[10, 0] / (D * count[0, 0])
    return (
        states.reshape(seq_local, row_local, D),
        mean_loss,
        grad_tokens.reshape(seq_local, row_local, D),
        grad_qkv,
        own_heads[:, 0].reshape(128),
        own_heads[:, 1].reshape(128),
        grad_out,
        small_out[0],
        small_out[1],
        small_out[2],
        grad_up,
        small_out[6:10].reshape(512),
        grad_down,
        small_out[3],
        small_out[4],
        small_out[5],
    )


def solution(mesh):
    rows = P("dp", ("seq", "wshard"), None)
    flags = P("dp", ("seq", "wshard"))
    matrix = P(("dp", "wshard"), None)
    vector = P(("dp", "wshard"))
    return jax.shard_map(
        on_device,
        mesh=mesh,
        in_specs=(
            rows,
            flags,
            flags,
            rows,
            matrix,
            vector,
            vector,
            matrix,
            vector,
            vector,
            vector,
            matrix,
            vector,
            matrix,
            vector,
            vector,
            vector,
        ),
        out_specs=(
            rows,
            P(),
            rows,
            matrix,
            vector,
            vector,
            matrix,
            vector,
            vector,
            vector,
            matrix,
            vector,
            matrix,
            vector,
            vector,
            vector,
        ),
        check_vma=False,
    )
```

```python
import functools

import jax
import jax.numpy as jnp
from jax import lax
from jax.experimental import pallas as pl
from jax.experimental.pallas import tpu as pltpu
from jax.sharding import PartitionSpec as P

D = 1024
H = 16
HD = 64
FF = 4096
L = 4096
EPS = 1e-06
F32 = jnp.float32
BF = jnp.bfloat16
MASKED = 1000000000.0
VMEM_CAP = 60 * 1024 * 1024
MESH = pl.DeviceIdType.MESH
ANY = pl.BlockSpec(memory_space=pl.ANY)
TB = 128
NB = L // TB


def dot(first, second, dims=((1,), (0,))):
    return lax.dot_general(first, second, (dims, ((), ())), preferred_element_type=F32)


def three_pieces(row):
    high = row.astype(BF)
    rest = row - high.astype(F32)
    middle = rest.astype(BF)
    lowest = (rest - middle.astype(F32)).astype(BF)
    return jnp.concatenate([high, middle, lowest], axis=0)


def place():
    at = lax.axis_index("seq")
    return (lax.axis_index("wshard") * 2 + (at // 2) % 2, lax.axis_index("dp"), at // 4, at % 2)


def device_at(x, y, z, core):
    return (y, (z * 2 + x % 2) * 2 + core, x // 2)


def along(axis, shift):
    x, y, z, core = place()
    if axis == "x":
        return device_at((x + shift) % 4, y, z, core)
    if axis == "y":
        return device_at(x, (y + shift) % 4, z, core)
    return device_at(x, y, (z + shift) % 4, core)


def sibling():
    x, y, z, core = place()
    return device_at(x, y, z, 1 - core)


def greet(partners):
    barrier = pltpu.get_barrier_semaphore()
    for partner in partners:
        pl.semaphore_signal(barrier, inc=1, device_id=partner, device_id_type=MESH)
    pl.semaphore_wait(barrier, len(partners))


def remote(src, dst, send_sem, recv_sem, target):
    return pltpu.make_async_remote_copy(
        src_ref=src, dst_ref=dst, send_sem=send_sem, recv_sem=recv_sem, device_id=target, device_id_type=MESH
    )


ORDERS = ("yzx", "zxy", "xyz")
PIECE = (64, 32, 48)
FIRST = (0, 512, 768)


def ring_partners():
    return [along(axis, shift) for axis in "xyz" for shift in (1, 2, 3)] + [sibling()]


def reduce_scratch():
    a, b, c = PIECE
    return [
        pltpu.VMEM((4, 2, 8 * a, 512), BF),
        pltpu.VMEM((4, 4, 2, 2 * b, 512), BF),
        pltpu.VMEM((4, 4, 4 * c, 512), BF),
        pltpu.VMEM((4, 2, 2 * a, 512), BF),
        pltpu.VMEM((4, 4, b, 512), BF),
        pltpu.VMEM((4, 4 * c, 512), BF),
        pltpu.VMEM((4, a, 512), BF),
        pltpu.VMEM((4, b, 512), BF),
        pltpu.VMEM((4, c, 512), BF),
        pltpu.SemaphoreType.DMA((3, 3, 3)),
        pltpu.SemaphoreType.DMA((3, 3, 3)),
        pltpu.SemaphoreType.DMA((3,)),
        pltpu.VMEM((2, 8 * a, 512), BF),
        pltpu.SemaphoreType.DMA((6,)),
        pltpu.SemaphoreType.DMA((6,)),
        pltpu.SemaphoreType.DMA((2,)),
    ]


def aligned(value, unit):
    return pl.multiple_of(value, unit)


def reduce_piece(stage, part, refs, at):
    g_ref = refs[0]
    half, low, n = at // 2, at % 2, PIECE[part]
    if stage == 0:
        first = FIRST[part]
        if part == 0:
            return g_ref.at[at, :, pl.ds(first, 8 * n), :]
        if part == 1:
            return g_ref.at[:, :, pl.ds(aligned(first + at * 2 * n, 16), 2 * n), :]
        return g_ref.at[:, half, pl.ds(aligned(first + low * 4 * n, 16), 4 * n), :]
    held = refs[1 + 3 * (stage - 1) + part]
    if stage == 1:
        if part == 0:
            return held.at[0, :, pl.ds(aligned(at * 2 * n, 16), 2 * n), :]
        if part == 1:
            return held.at[0, :, half, pl.ds(aligned(low * n, 16), n), :]
        return held.at[0, at]
    if part == 0:
        return held.at[0, half, pl.ds(aligned(low * n, 16), n), :]
    if part == 1:
        return held.at[0, at]
    return held.at[0, pl.ds(aligned(at * n, 16), n), :]


def ring_at(axis):
    x, y, z, _ = place()
    return {"x": x, "y": y, "z": z}[axis]


def reduce_copies(stage, part, refs):
    send, recv = refs[10], refs[11]
    axis = ORDERS[part][stage]
    return [
        remote(
            reduce_piece(stage, part, refs, (ring_at(axis) + shift) % 4),
            refs[1 + 3 * stage + part].at[shift],
            send.at[stage, part, shift - 1],
            recv.at[stage, part, shift - 1],
            along(axis, shift),
        )
        for shift in (1, 3, 2)
    ]


def reduce_own(part, refs):
    return pltpu.make_async_copy(
        reduce_piece(0, part, refs, ring_at(ORDERS[part][0])), refs[1 + part].at[0], refs[12].at[part]
    )


def reduce_start(part, refs):
    start_all(first_copies(refs)[:4] + first_loads(refs) if part == 0 else reduce_copies(0, part, refs))
    reduce_own(part, refs).start()


def first_copies(refs):
    g_ref, a1, relay, send, recv = refs[0], refs[1], refs[13], refs[14], refs[15]
    _, y, _, _ = place()
    rows = pl.ds(0, 8 * PIECE[0])
    up, down, far = (y + 1) % 4, (y + 3) % 4, (y + 2) % 4
    moves = [
        (g_ref.at[far, 0, rows], a1.at[2, 0], 1),
        (g_ref.at[far, 1, rows], a1.at[2, 1], 3),
        (g_ref.at[up, 1, rows], a1.at[1, 1], 1),
        (g_ref.at[down, 0, rows], a1.at[3, 0], 3),
        (relay.at[0], a1.at[1, 0], 1),
        (relay.at[1], a1.at[3, 1], 3),
    ]
    return [remote(src, dst, send.at[k], recv.at[k], along("y", d)) for k, (src, dst, d) in enumerate(moves)]


def first_loads(refs):
    g_ref, relay, local = refs[0], refs[13], refs[16]
    _, y, _, _ = place()
    rows = pl.ds(0, 8 * PIECE[0])
    return [
        pltpu.make_async_copy(g_ref.at[(y + 1) % 4, 0, rows], relay.at[0], local.at[0]),
        pltpu.make_async_copy(g_ref.at[(y + 3) % 4, 1, rows], relay.at[1], local.at[1]),
    ]


def first_relay(refs):
    a1, relay = refs[1], refs[13]
    copies = first_copies(refs)
    wait_all(first_loads(refs))
    for copy in copies[:2]:
        copy.wait_recv()

    @pl.loop(0, 16)
    def _(i):
        rows = pl.ds(aligned((i % 8) * PIECE[0], 16), PIECE[0])
        half = i // 8
        relay[half, rows, :] = (relay[half, rows, :].astype(F32) + a1[2, half, rows, :].astype(F32)).astype(BF)

    start_all(copies[4:])


def first_end(refs):
    copies = first_copies(refs)
    for copy in copies[:2]:
        copy.wait_send()
    wait_all(copies[2:])


def add_four(values):
    total = values[0].astype(F32) + values[1].astype(F32)
    return (total + values[2].astype(F32) + values[3].astype(F32)).astype(BF)


def reduce_step(stage, part, refs):
    a1, b1, c1, a2, b2, c2, a3, b3, c3 = refs[1:10]
    if stage == 0 and part == 0:
        first_end(refs)
    else:
        wait_all(reduce_copies(stage, part, refs))
    x, y, z, _ = place()
    n = PIECE[part]
    rest = (1, 2, 3)
    if stage == 0:
        reduce_own(part, refs).wait()

        @pl.loop(0, 16)
        def _(i):
            if part == 0:
                rows = pl.ds(aligned((i % 8) * n, 16), n)
                total = a1[0, i // 8, rows, :].astype(F32) + a1[1, i // 8, rows, :].astype(F32)
                a1[0, i // 8, rows, :] = (total + a1[3, i // 8, rows, :].astype(F32)).astype(BF)
            elif part == 1:
                rows = pl.ds(aligned((i % 2) * n, 16), n)
                b1[0, i // 4, (i // 2) % 2, rows, :] = add_four([b1[s, i // 4, (i // 2) % 2, rows, :] for s in range(4)])
            else:
                rows = pl.ds(aligned((i % 4) * n, 16), n)
                c1[0, i // 4, rows, :] = add_four([c1[s, i // 4, rows, :] for s in range(4)])

    elif stage == 1:

        @pl.loop(0, 4)
        def _(i):
            if part == 0:
                rows = pl.ds(aligned((i % 2) * n, 16), n)
                own = a1[0, i // 2, pl.ds(aligned(z * 2 * n + (i % 2) * n, 16), n), :]
                a2[0, i // 2, rows, :] = add_four([own] + [a2[s, i // 2, rows, :] for s in rest])
            elif part == 1:
                own = b1[0, i, x // 2, pl.ds(aligned((x % 2) * n, 16), n), :]
                b2[0, i] = add_four([own] + [b2[s, i] for s in rest])
            else:
                rows = pl.ds(aligned(i * n, 16), n)
                own = c1[0, y, rows, :]
                c2[0, rows, :] = add_four([own] + [c2[s, rows, :] for s in rest])

    elif part == 0:
        own = a2[0, x // 2, pl.ds(aligned((x % 2) * n, 16), n), :]
        a3[0] = add_four([own] + [a3[s] for s in rest])
    elif part == 1:
        b3[0] = add_four([b2[0, y]] + [b3[s] for s in rest])
    else:
        own = c2[0, pl.ds(aligned(z * n, 16), n), :]
        c3[0] = add_four([own] + [c3[s] for s in rest])
    if stage < 2:
        start_all(reduce_copies(stage + 1, part, refs))


def shard_rows(o_ref, part, x_low, z, core):
    sub = x_low * 4 + z if part == 2 else z * 2 + x_low
    return o_ref.at[core, pl.ds(aligned(FIRST[part] + sub * PIECE[part], 16), PIECE[part]), :]


def spread_steps(part, mine, sems, o_ref):
    local, send, recv = sems
    x, y, z, core = place()
    low = x % 2
    pair = device_at(x // 2 * 2 + 1 - low, y, z, core)
    spot = shard_rows(o_ref, part, low, z, core)
    own = pltpu.make_async_copy(mine, spot, local.at[part])
    first = remote(mine, spot, send.at[part, 0], recv.at[part, 0], pair)
    second = [remote(mine, spot, send.at[part, d], recv.at[part, d], along("z", d)) for d in (1, 3, 2)]
    spot = shard_rows(o_ref, part, 1 - low, z, core)
    third = [remote(spot, spot, send.at[part, 3 + d], recv.at[part, 3 + d], along("z", d)) for d in (1, 3, 2)]

    def begin():
        start_all([own, first] + second)

    def middle():
        first.wait()
        start_all(third)

    def end():
        wait_all([own] + second + third)

    return begin, middle, end


def swap_partner(shift):
    mine = lax.axis_index("seq") * 2 + lax.axis_index("wshard")
    other = (mine + shift) % NB
    return other, (lax.axis_index("dp"), other // 2, other % 2)


def swap_greet():
    barrier = pltpu.get_barrier_semaphore()

    @pl.loop(1, NB)
    def _(shift):
        pl.semaphore_signal(barrier, inc=1, device_id=swap_partner(shift)[1], device_id_type=MESH)

    pl.semaphore_wait(barrier, NB - 1)


def swap_copies(piece_for, landing_from, sems):
    mine = lax.axis_index("seq") * 2 + lax.axis_index("wshard")
    send, recv, local = sems

    def copy(shift):
        other, device = swap_partner(shift)
        return remote(piece_for(other), landing_from(mine), send.at[shift], recv.at[shift], device)

    own = pltpu.make_async_copy(piece_for(mine), landing_from(mine), local)

    def start():
        @pl.loop(1, NB)
        def _(shift):
            copy(shift).start()

        own.start()

    def wait():
        @pl.loop(1, NB)
        def _(shift):
            copy(shift).wait()

        own.wait()

    return start, wait


def swap_sems():
    return [pltpu.SemaphoreType.DMA((NB,)), pltpu.SemaphoreType.DMA((NB,)), pltpu.SemaphoreType.DMA]


def block_of(ref, b):
    return ref.at[b]


def head_tile(ref, b):
    return ref.at[pl.ds(aligned((b // 2) * HD, HD), HD), pl.ds(aligned((b % 2) * TB, TB), TB)]


def head_tile3(ref, b):
    return ref.at[:, pl.ds(aligned((b // 2) * HD, HD), HD), pl.ds(aligned((b % 2) * TB, TB), TB)]


HALVES = ((128, 2048), (256, 1024))


class Transfers:
    def __init__(self, send, recv):
        self.send, self.recv, self.used = send, recv, 0

    def copy(self, src, dst, target):
        made = remote(src, dst, self.send.at[self.used], self.recv.at[self.used], target)
        self.used += 1
        return made


def start_all(copies):
    for copy in copies:
        copy.start()


def wait_all(copies):
    for copy in copies:
        copy.wait()


def unit_rows(matrix, unit, count=1):
    rows = HALVES[matrix][0] // 4
    return pl.ds(unit * rows, count * rows)


def columns_part(matrix, at, parts):
    width = HALVES[matrix][1] // parts
    return pl.ds(aligned(at * width, 128), width)


def half_rows(core, rows=64):
    return pl.ds(aligned(core * rows, rows), rows)


def shard_greet():
    x, y, z, core = place()
    return [device_at(x, (y + d) % 4, z, core) for d in (1, 2, 3)] + [
        device_at(3 - x, (y + d) % 4, z, core) for d in range(4)
    ]


def greet_signal(others):
    barrier = pltpu.get_barrier_semaphore()

    @pl.loop(1, NB)
    def _(shift):
        pl.semaphore_signal(barrier, inc=1, device_id=swap_partner(shift)[1], device_id_type=MESH)

    for other in others:
        pl.semaphore_signal(barrier, inc=1, device_id=other, device_id_type=MESH)


def greet_wait(others):
    pl.semaphore_wait(pltpu.get_barrier_semaphore(), NB - 1 + len(others))


FRONT_COPIES = 144


def front_kernel(
    tokens, segments, flags, vectors, b_up, w_out, w_up, w_down, w_qkv,
    x_seq, meta_out, smalls_out, out_all, up_all, down_all, qkv_all, qat_ref, ka_ref, va_ref, kt_ref, q_ref,
    context, wide_ref, lse_ref,
    vat_ref, blocks, x_buf, tok_buf, out_buf, up_buf, down_buf, qkv_buf, meta, heads, smalls, meta_all, heads_all, smalls_all, w_ref, b_ref,
    send, recv, local, meta_send, meta_recv, meta_local, back_send, back_recv, back_local,
):
    x, y, z, core = place()
    hi, lo = x // 2, x % 2
    mine, across = y * 2 + hi, y * 2 + 1 - hi
    wrap, pair, other_core = device_at(3 - x, y, z, core), device_at(hi * 2 + 1 - lo, y, z, core), sibling()
    shards, wholes = (up_buf.at[core], down_buf), (up_all, down_all)
    rows_out = half_rows(core)
    greet_signal(shard_greet())
    load_tokens = pltpu.make_async_copy(tokens, tok_buf, local.at[0])
    load_qkv = pltpu.make_async_copy(w_qkv, qkv_buf, local.at[11])
    loads = [
        pltpu.make_async_copy(w_out, out_buf, local.at[9]),
        pltpu.make_async_copy(w_down.at[half_rows(core, 256)], down_buf, local.at[10]),
    ]
    for j in range(8):
        piece = w_up.at[:, pl.ds(aligned(j * 512 + core * 256, 256), 256)]
        loads.append(pltpu.make_async_copy(piece, up_buf.at[core, :, pl.ds(j * 256, 256)], local.at[1 + j]))
    start_all([load_tokens, load_qkv] + loads)
    meta[...] = jnp.zeros_like(meta)
    for s in range(2):
        meta[s, 0:1, :] = segments[s : s + 1, :]
        meta[s, 1:2, :] = flags[s : s + 1, :]
    smalls[...] = jnp.zeros_like(smalls)
    smalls[0:8, :] = vectors[...]
    smalls[8:12, :] = b_up[...]
    greet_wait(shard_greet())
    load_tokens.wait()
    net = Transfers(send, recv)
    first, second = pl.ds(0, 64), pl.ds(64, 64)

    def block(at, low, w, rows=slice(None)):
        return x_buf.at[at, low, core, w, rows]

    own = tok_buf.at[hi]
    swap = net.copy(tok_buf.at[1 - hi], block(z, lo, hi), wrap)
    own_z = [net.copy(own, block(z, lo, hi), along("z", d)) for d in (1, 3, 2)]
    own_pair = [net.copy(own.at[rows], block(z, lo, hi, rows), pair) for rows in (first, second)]
    start_all([swap, own_pair[0]] + own_z)
    x_buf[z, lo, core, hi] = tok_buf[hi]
    load_qkv.wait()
    for p in range(3):
        for k, pair_at in ((0, z * 2 + lo), (1, z * 2 + 1 - lo)):
            heads[k, :, 128 * p : 128 * (p + 1)] = qkv_buf[:, pl.ds(aligned(p * D + pair_at * 128, 128), 128)]
    cross_first = [
        net.copy(heads.at[1], heads_all.at[mine], wrap),
        net.copy(smalls, smalls_all.at[mine], wrap),
    ]
    start_all(cross_first)

    def small_y(shard, heads_source, smalls_source):
        copies = []
        for d in (1, 3, 2):
            copies.append(net.copy(heads_source, heads_all.at[shard], along("y", d)))
            copies.append(net.copy(smalls_source, smalls_all.at[shard], along("y", d)))
        return copies

    own_small = small_y(mine, heads.at[0], smalls)
    start_all(own_small)
    heads_all[mine] = heads[0]
    smalls_all[mine] = smalls[...]
    meta_start, meta_wait = swap_copies(
        lambda b: meta.at[b % 2], lambda b: meta_all.at[b], (meta_send, meta_recv, meta_local)
    )
    meta_start()
    wait_all(loads)
    keep = [
        pltpu.make_async_copy(out_buf.at[rows_out], out_all.at[mine, rows_out], local.at[9]),
        pltpu.make_async_copy(qkv_buf, qkv_all.at[mine], local.at[11]),
    ]
    for m in range(2):
        parts = [
            (unit_rows(m, 0), columns_part(m, z, 4)),
            (unit_rows(m, 3), columns_part(m, lo, 2)),
            (unit_rows(m, 1, 2), slice(None)),
        ]
        for k, (rows, columns) in enumerate(parts):
            piece = wholes[m].at[mine, rows, columns]
            keep.append(pltpu.make_async_copy(shards[m].at[rows, columns], piece, local.at[1 + 3 * m + k]))
    start_all(keep)

    def along_y(shard, source, out_source, inner):
        copies = []
        for d in (1, 3, 2):
            there = along("y", d)
            copies.append(net.copy(out_source.at[rows_out], out_all.at[shard, rows_out], there))
            for m in range(2):
                parts = [(0, columns_part(m, z, 4)), (3, columns_part(m, lo, 2))]
                for unit, columns in parts + ([(1, slice(None))] if inner else []):
                    rows = unit_rows(m, unit, 2 if unit == 1 else 1)
                    copies.append(net.copy(source(m).at[rows, columns], wholes[m].at[shard, rows, columns], there))
        return copies

    own_y = along_y(mine, lambda m: shards[m], out_buf, True)
    start_all(own_y)
    swap.wait_recv()
    came = block(z, 1 - lo, 1 - hi)
    came_pair = [
        net.copy(block(z, 1 - lo, 1 - hi, rows), block(z, 1 - lo, 1 - hi, rows), pair) for rows in (first, second)
    ]
    came_z = [net.copy(came, came, along("z", d)) for d in (1, 3, 2)]
    start_all([came_pair[0]] + came_z + [own_pair[1], came_pair[1]])
    cross_early, cross_late = [net.copy(out_buf.at[rows_out], out_all.at[mine, rows_out], wrap)], []
    for m in range(2):
        for unit, columns in ((0, columns_part(m, z, 4)), (3, columns_part(m, 1 - lo, 2))):
            rows = unit_rows(m, unit)
            cross_early.append(net.copy(shards[m].at[rows, columns], wholes[m].at[mine, rows, columns], wrap))
    rows = unit_rows(0, 1, 2)
    cross_late.append(net.copy(shards[0].at[rows], up_all.at[mine, rows], wrap))
    rows = half_rows(core)
    cross_late.append(net.copy(qkv_buf.at[rows], qkv_all.at[mine, rows], wrap))
    start_all(cross_early)
    pair_late = []

    def forward(got, d, low, w):
        got.wait_recv()
        piece = block((z + 4 - d) % 4, low, w, second)
        pair_late.append(net.copy(piece, piece, pair))
        pair_late[-1].start()

    for i, d in enumerate((1, 3, 2)):
        forward(own_z[i], d, lo, hi)
    for copy in cross_first:
        copy.wait_recv()
    across_small = small_y(across, heads_all.at[across], smalls_all.at[across])
    start_all(across_small)
    half_z = []

    def halves(got, low, w):
        got.wait_recv()
        piece = block(z, low, w, first)
        copies = [net.copy(piece, piece, along("z", d)) for d in (1, 3, 2)]
        start_all(copies)
        half_z.extend(copies)

    halves(own_pair[0], 1 - lo, hi)
    for copy in cross_early:
        copy.wait_recv()
    across_y = along_y(across, lambda m: wholes[m].at[across], out_all.at[across], False)
    start_all(across_y + cross_late)
    for i, d in enumerate((1, 3, 2)):
        forward(came_z[i], d, 1 - lo, 1 - hi)
    halves(came_pair[0], lo, 1 - hi)
    share, rest = [], []
    for low, w in ((lo, hi), (1 - lo, 1 - hi)):
        piece = x_buf.at[:, low, core, w]
        share.append(net.copy(piece, piece, other_core))
    start_all(share)
    cross_late[0].wait_recv()
    rows = unit_rows(0, 1, 2)
    across_up = [net.copy(up_all.at[across, rows], up_all.at[across, rows], along("y", d)) for d in (1, 3, 2)]
    start_all(across_up)

    for copy in own_small + across_small:
        copy.wait_recv()
    meta_wait()
    at_first = core == 0
    both = heads_all[...].reshape(D, 384)
    parts = [jnp.where(at_first, both[:, 128 * p : 128 * p + HD], both[:, 128 * p + HD : 128 * (p + 1)]) for p in range(3)]
    w_ref[...] = jnp.concatenate(parts, axis=1)
    biases = smalls_all[lax.axis_index("seq") // 2]
    bias = [jnp.where(at_first, biases[k : k + 1, :HD], biases[k : k + 1, HD:]) for k in range(2)]
    b_ref[...] = jnp.broadcast_to(jnp.concatenate([bias[0], jnp.zeros((1, HD), F32), bias[1]], axis=1), (8, 3 * HD))

    def project(low, at_core, w):
        @pl.loop(0, 4)
        def _(at):
            b = at * 8 + low * 4 + at_core * 2 + w
            rows = pl.ds(aligned(b * TB, TB), TB)
            side = dot(x_buf[at, low, at_core, w], w_ref[...]) + b_ref[:1, :]
            q8 = side[:, :HD].astype(BF).astype(F32) * 0.125
            hot = jnp.where(lax.broadcasted_iota(jnp.int32, (32, TB), 0) == meta_all[b, 0:1, :], 1.0, 0.0)
            lane = lax.broadcasted_iota(jnp.int32, (TB, HD), 1)
            ones3 = jnp.where(lane < 3, 1.0, 0.0)
            apart = (hot.T - 1.0) * MASKED
            key = side[:, HD : 2 * HD]
            value = side[:, 2 * HD :]
            q_ref[rows, :] = q8.astype(BF)
            ka_ref[rows, :] = jnp.concatenate([key, apart, ones3[:, :32]], axis=1).astype(BF)
            va_ref[rows, :] = jnp.concatenate([value, ones3], axis=1).astype(BF)
            qat_ref[:, rows] = jnp.concatenate([q8.T, hot, jnp.zeros((32, TB), F32)], axis=0).astype(BF)
            kt_ref[:, rows] = key.T.astype(BF)
            ones_row = jnp.where(lax.broadcasted_iota(jnp.int32, (16, TB), 0) == 0, 1.0, 0.0)
            vat_ref[:, rows] = jnp.concatenate([value.T, ones_row], axis=0).astype(BF)

    project(lo, core, hi)
    project(1 - lo, core, 1 - hi)
    for copy in half_z + [own_pair[1], came_pair[1]] + pair_late:
        copy.wait_recv()
    for low, w in ((1 - lo, hi), (lo, 1 - hi)):
        piece = x_buf.at[:, low, core, w]
        rest.append(net.copy(piece, piece, other_core))
    start_all(rest)
    for copy in share:
        copy.wait_recv()
    project(1 - lo, core, hi)
    project(lo, core, 1 - hi)
    project(lo, 1 - core, hi)
    project(1 - lo, 1 - core, 1 - hi)
    for copy in rest:
        copy.wait_recv()
    store = pltpu.make_async_copy(x_buf, x_seq, local.at[0])
    store.start()
    project(1 - lo, 1 - core, hi)
    project(lo, 1 - core, 1 - hi)
    meta_out[...] = meta_all[...]
    smalls_out[...] = smalls_all[...]

    wait_all(keep)
    for copy in own_y + across_y + cross_late[1:]:
        copy.wait_recv()
    later = []
    for m in range(2):
        piece = wholes[m].at[:, unit_rows(m, 3), columns_part(m, lo, 2)]
        later.append(net.copy(piece, piece, pair))
        for d in (1, 3, 2):
            piece = wholes[m].at[:, unit_rows(m, 0), columns_part(m, z, 4)]
            later.append(net.copy(piece, piece, along("z", d)))
    piece = out_all.at[:, half_rows(core)]
    later.append(net.copy(piece, piece, other_core))
    for d in range(4):
        piece = down_all.at[(y + d) % 4 * 2 + hi, unit_rows(1, 1, 2)]
        later.append(net.copy(piece, piece, wrap))
    start_all(later)

    position = lax.axis_index("seq") * 2 + hi

    def result(b, recv_at):
        there = head_tile(context, position)
        return remote(blocks.at[b], there, back_send.at[b], back_recv.at[recv_at], (y, b // 2, b % 2))

    own_result = pltpu.make_async_copy(blocks.at[position], head_tile(context, position), back_local)

    @pl.loop(0, 4)
    def _(step):
        at = (step + z + 1) % 4
        columns = pl.ds(aligned(at * 1024, 1024), 1024)
        queries = qat_ref[:, columns]
        peak = jnp.full((1, 1024), -jnp.inf, F32)
        total = jnp.zeros((80, 1024), F32)
        for j in range(8):
            keys = slice(j * 512, (j + 1) * 512)
            logits = dot(ka_ref[keys, :], queries)
            new_peak = jnp.maximum(peak, jnp.max(logits, axis=0, keepdims=True))
            expos = jnp.exp(logits - new_peak).astype(BF)
            total = total * jnp.exp(peak - new_peak) + dot(vat_ref[:, keys], expos)
            peak = new_peak
        sums = total[HD : HD + 1]
        found = total[:HD] / sums
        wide_ref[:, columns] = found
        lse_ref[:, columns] = peak + jnp.log(sums)
        low = found.astype(BF)
        for j in range(8):
            b = at * 8 + j
            blocks[b] = low[:, j * TB : (j + 1) * TB]

            @pl.when(b != position)
            def _():
                result(b, position).start()

            @pl.when(b == position)
            def _():
                own_result.start()

    store.wait()
    for copy in [swap] + own_pair + own_z + came_pair + came_z + half_z + pair_late + share + rest:
        copy.wait_send()
    for copy in cross_first + cross_early + cross_late + own_small + across_small + own_y + across_y:
        copy.wait_send()
    wait_all(across_up)
    wait_all(later)

    @pl.loop(1, NB)
    def _(shift):
        b = (position + shift) % NB
        result(b, b).wait()

    own_result.wait()


def front(tokens, segments, flags, vectors, b_up, w_out, w_up, w_down, w_qkv):
    shape = jax.ShapeDtypeStruct
    in_vmem = pl.BlockSpec(memory_space=pltpu.VMEM)
    return pl.pallas_call(
        front_kernel,
        in_specs=[ANY] + [in_vmem] * 4 + [ANY] * 4,
        out_specs=[ANY] + [in_vmem] * 2 + [ANY] * 4 + [in_vmem] * 5 + [ANY] + [in_vmem] * 2,
        out_shape=[
            shape((4, 2, 2, 2, TB, D), BF),
            shape((NB, 8, TB), jnp.int32),
            shape((8, 16, 128), F32),
            shape((8, 128, D), BF),
            shape((8, 128, 2048), BF),
            shape((8, 256, D), BF),
            shape((8, 128, 3 * D), BF),
            shape((128, L), BF),
            shape((L, 128), BF),
            shape((L, 128), BF),
            shape((HD, L), BF),
            shape((L, HD), BF),
            shape((D, 2 * TB), BF),
            shape((HD, L), F32),
            shape((1, L), F32),
        ],
        scratch_shapes=[
            pltpu.VMEM((80, L), BF),
            pltpu.VMEM((NB, HD, TB), BF),
            pltpu.VMEM((4, 2, 2, 2, TB, D), BF),
            pltpu.VMEM((2, TB, D), BF),
            pltpu.VMEM((128, D), BF),
            pltpu.VMEM((2, 128, 2048), BF),
            pltpu.VMEM((256, D), BF),
            pltpu.VMEM((128, 3 * D), BF),
            pltpu.VMEM((2, 8, TB), jnp.int32),
            pltpu.VMEM((2, 128, 384), BF),
            pltpu.VMEM((16, 128), F32),
            pltpu.VMEM((NB, 8, TB), jnp.int32),
            pltpu.VMEM((8, 128, 384), BF),
            pltpu.VMEM((8, 16, 128), F32),
            pltpu.VMEM((D, 3 * HD), BF),
            pltpu.VMEM((8, 3 * HD), F32),
            pltpu.SemaphoreType.DMA((FRONT_COPIES,)),
            pltpu.SemaphoreType.DMA((FRONT_COPIES,)),
            pltpu.SemaphoreType.DMA((12,)),
            *swap_sems(),
            *swap_sems(),
        ],
        name="front",
        compiler_params=pltpu.CompilerParams(
            collective_id=1, has_side_effects=True, vmem_limit_bytes=VMEM_CAP
        ),
    )(tokens, segments, flags, vectors, b_up, w_out, w_up, w_down, w_qkv)


def qkv_along_y(qkv_all, net):
    _, y, _, core = place()
    copies = []
    for d in (1, 3, 2):
        for w in range(2):
            piece = qkv_all.at[y * 2 + w, half_rows(core)]
            copies.append(net.copy(piece, piece, along("y", d)))
    return copies


def turned(first, second):
    return dot(first, second, ((0,), (0,)))


def gelu_both(u):
    rate = 0.7978845608028654
    square = u * u
    curve = jnp.tanh(rate * (u + 0.044715 * (square * u)))
    half = 0.5 * (1.0 + curve)
    slope = half + 0.5 * u * (1.0 - curve * curve) * (rate * (1.0 + 0.134145 * square))
    return u * half, slope


def fold(values):
    return jnp.sum(values.reshape(values.shape[0] // 8, 8, values.shape[1]), axis=0)


ROWS = 256
CHUNK = 32
SMALLS = 16


def middle_kernel(
    context_in, meta, tokens, teacher, flags, smalls, out_all, up_all, down_all, a0,
    states, resid_out, do, g_ref, sums_out, count_out, qkv_all,
    context, context_s, w_out, w_up, w_down, h, act, slope, send_one, come_one, send_two, come_two,
    gb, gu, ga, ga_s, normed, hidden, rate, work, resid, gct, stage, count, counts, valid,
    send, recv, local, back_send, back_recv, back_local,
):
    x, y, z, core = place()
    mine = y * 2 + x // 2
    twin = sibling()
    loads = [
        pltpu.make_async_copy(context_in, context, local.at[6]),
        pltpu.make_async_copy(out_all, w_out, local.at[0]),
        pltpu.make_async_copy(up_all, w_up, local.at[1]),
    ]
    load_down = pltpu.make_async_copy(down_all, w_down, local.at[2])
    start_all(loads + [load_down])
    greet_signal(shard_greet())
    greet_wait(shard_greet())
    net = Transfers(send, recv)
    later = qkv_along_y(qkv_all, net)
    valid_here = jnp.sum(meta[:, 1, :].astype(F32), axis=0, keepdims=True)
    count[...] = jnp.broadcast_to(jnp.sum(valid_here, axis=1, keepdims=True), (8, 128))
    ahead = [net.copy(count, counts.at[mine], target) for target in shard_greet()]
    start_all(ahead + later)
    own_count = pltpu.make_async_copy(count, counts.at[mine], local.at[3])
    own_count.start()
    for s in range(2):
        column = jnp.broadcast_to(flags[s : s + 1, :].astype(F32), (128, 128)).T
        valid[128 * s : 128 * (s + 1), :] = column

    def vector(row):
        return jnp.concatenate([smalls[i, row : row + 1, :] for i in range(8)], axis=1)

    out_bias, gain_one, offset_one, down_bias, gain_two, offset_two = [vector(row) for row in range(2, 8)]
    zeros = jnp.zeros((8, D), F32)
    wait_all(loads)
    give_context = net.copy(context, context_s, twin)
    give_context.start()
    work[...] = turned(context[...], w_out[...].reshape(D, D))

    @pl.loop(0, ROWS // CHUNK)
    def _(i):
        rows = pl.ds(aligned(i * CHUNK, CHUNK), CHUNK)
        total = tokens[rows, :].astype(F32) + work[rows, :] + out_bias
        centre = total - jnp.mean(total, axis=1, keepdims=True)
        scale = lax.rsqrt(jnp.mean(centre * centre, axis=1, keepdims=True) + EPS)
        unit = centre * scale
        normed[rows, :] = unit
        rate[rows, :] = jnp.broadcast_to(scale, (CHUNK, 128))
        full = unit * gain_one + offset_one
        hidden[rows, :] = full
        h[0, rows, :] = full.astype(BF)

    give_hidden = net.copy(h.at[0], h.at[1], twin)
    give_hidden.start()
    for slot in range(2):
        if slot == 1:
            give_hidden.wait()
        for k in range(8):
            columns = slice(256 * k, 256 * (k + 1))
            bias = jnp.concatenate([smalls[k, pl.ds(8 + 2 * core + e, 1), :] for e in range(2)], axis=1)
            u = dot(h[slot], w_up[:, :, columns].reshape(D, 256)) + bias
            value, incline = gelu_both(u)
            act[slot, :, columns] = value.astype(BF)
            slope[slot, :, columns] = incline
    load_down.wait()
    send_one[...] = dot(act[1], w_down[...].reshape(2048, D))
    give_one = net.copy(send_one, come_one, twin)
    give_one.start()
    work[...] = dot(act[0], w_down[...].reshape(2048, D))
    give_one.wait()
    wait_all(ahead)
    own_count.wait()
    total_count = jnp.sum(counts[...], axis=0)
    count_out[...] = total_count
    factor = (128 * ROWS) / total_count[:1, :1]

    def loss_rows(i, carried):
        rows = pl.ds(aligned(i * CHUNK, CHUNK), CHUNK)
        total = hidden[rows, :] + (work[rows, :] + come_one[rows, :] + down_bias)
        centre = total - jnp.mean(total, axis=1, keepdims=True)
        scale = lax.rsqrt(jnp.mean(centre * centre, axis=1, keepdims=True) + EPS)
        unit = centre * scale
        final = unit * gain_two + offset_two
        states[rows, :] = final.astype(BF)
        differ = final - teacher[rows, :].astype(F32)
        held = valid[rows, :1] * differ
        grad = factor * held
        weighted = grad * gain_two
        back = weighted - jnp.mean(weighted, axis=1, keepdims=True)
        back = scale * (back - unit * jnp.mean(weighted * unit, axis=1, keepdims=True))
        resid[rows, :] = back
        low = back.astype(BF)
        gb[0, rows, :] = low
        return (
            carried[0] + fold(grad * unit),
            carried[1] + fold(grad),
            carried[2] + fold(low.astype(F32)),
            carried[3] + fold(held * differ),
        )

    gain_two_sum, offset_two_sum, down_sum, error = lax.fori_loop(
        0, ROWS // CHUNK, loss_rows, (zeros, zeros, zeros, zeros)
    )
    give_branch = net.copy(gb.at[0], gb.at[1], twin)
    give_branch.start()
    up_sums = []
    for slot in range(2):
        if slot == 1:
            give_branch.wait()
        for k in range(8):
            columns = slice(256 * k, 256 * (k + 1))
            pulled = dot(gb[slot], w_down[k], ((1,), (1,))) * slope[slot, :, columns]
            low = pulled.astype(BF)
            gu[slot, :, columns] = low
            up_sums.append(fold(low.astype(F32)))
    for i in range(8):
        send_two[:, 128 * i : 128 * (i + 1)] = dot(gu[1], w_up[i], ((1,), (1,)))
    give_two = net.copy(send_two, come_two, twin)
    give_two.start()
    for i in range(8):
        work[:, 128 * i : 128 * (i + 1)] = dot(gu[0], w_up[i], ((1,), (1,)))
    give_two.wait()

    def first_norm_rows(i, carried):
        rows = pl.ds(aligned(i * CHUNK, CHUNK), CHUNK)
        grad = resid[rows, :] + (work[rows, :] + come_two[rows, :])
        unit = normed[rows, :]
        weighted = grad * gain_one
        back = weighted - jnp.mean(weighted, axis=1, keepdims=True)
        back = rate[rows, :1] * (back - unit * jnp.mean(weighted * unit, axis=1, keepdims=True))
        resid_out[rows, :] = back
        low = back.astype(BF)
        ga[rows, :] = low
        return (carried[0] + fold(grad * unit), carried[1] + fold(grad), carried[2] + fold(low.astype(F32)))

    gain_one_sum, offset_one_sum, out_sum = lax.fori_loop(0, ROWS // CHUNK, first_norm_rows, (zeros, zeros, zeros))
    give_attended = net.copy(ga.at[:, pl.ds(aligned((1 - core) * 512, 512), 512)], ga_s, twin)
    give_attended.start()
    gct[...] = dot(w_out[...].reshape(D, D), ga[...], ((1,), (1,))).astype(BF)
    back_start, back_wait = swap_copies(
        lambda b: head_tile(gct, b), lambda b: do.at[b], (back_send, back_recv, back_local)
    )
    back_start()

    error = jnp.broadcast_to(jnp.sum(jnp.sum(error, axis=0, keepdims=True), axis=1, keepdims=True), (1, 128))
    lines = [out_sum, gain_one_sum, offset_one_sum, down_sum, gain_two_sum, offset_two_sum]
    lines = [jnp.sum(line, axis=0, keepdims=True) for line in lines]
    for i in range(8):
        columns = slice(128 * i, 128 * (i + 1))
        sums_out[i] = jnp.zeros((SMALLS, 128), F32)
        for row, line in enumerate(lines):
            sums_out[i, row : row + 1, :] = line[:, columns]
        both = jnp.sum(up_sums[i] + up_sums[8 + i], axis=0, keepdims=True)
        for e in range(2):
            sums_out[i, pl.ds(6 + 2 * core + e, 1), :] = both[:, 128 * e : 128 * (e + 1)]
        sums_out[i, 10:11, :] = error

    give_context.wait()
    give_attended.wait()

    def stored(i):
        return pltpu.make_async_copy(stage.at[i % 2], g_ref.at[i // 2, i % 2], local.at[4 + i % 2])

    for i in range(8):
        if i >= 2:
            stored(i - 2).wait()
        tall = slice(128 * i, 128 * (i + 1))
        wide = slice(256 * i, 256 * (i + 1))
        up = turned(h[0, :, tall], gu[0]) + turned(h[1, :, tall], gu[1])
        for k in range(4):
            stage[i % 2, 128 * k : 128 * (k + 1), :] = up[:, 512 * k : 512 * (k + 1)].astype(BF)
        down = turned(act[0, :, wide], gb[0]) + turned(act[1, :, wide], gb[1])
        for k in range(2):
            stage[i % 2, 512 + 256 * k : 768 + 256 * k, :] = down[:, 512 * k : 512 * (k + 1)].astype(BF)
        own_half = ga[:, pl.ds(aligned(core * 512, 512), 512)]
        out = dot(context[tall, :], own_half) + dot(context_s[tall, :], ga_s[...])
        stage[i % 2, 1024:, :] = out.astype(BF)
        stored(i).start()
    stored(6).wait()
    stored(7).wait()
    back_wait()
    wait_all(later)


def middle(context, meta, tokens, teacher, flags, smalls, out_all, up_all, down_all, qkv_all):
    shape = jax.ShapeDtypeStruct
    in_vmem = pl.BlockSpec(memory_space=pltpu.VMEM)
    dma = pltpu.SemaphoreType.DMA
    wide = pltpu.VMEM((ROWS, D), F32)
    return pl.pallas_call(
        middle_kernel,
        in_specs=[ANY] + [in_vmem] * 5 + [ANY] * 4,
        out_specs=[in_vmem, in_vmem, ANY, ANY, in_vmem, in_vmem, ANY],
        out_shape=[
            shape((ROWS, D), BF),
            shape((ROWS, D), F32),
            shape((NB, HD, TB), BF),
            shape((4, 2, 1152, 512), BF),
            shape((8, SMALLS, 128), F32),
            shape((8, 128), F32),
            shape(qkv_all.shape, BF),
        ],
        input_output_aliases={9: 6},
        scratch_shapes=[
            pltpu.VMEM((D, ROWS), BF),
            pltpu.VMEM((D, ROWS), BF),
            pltpu.VMEM((8, 128, D), BF),
            pltpu.VMEM((8, 128, 2048), BF),
            pltpu.VMEM((8, 256, D), BF),
            pltpu.VMEM((2, ROWS, D), BF),
            pltpu.VMEM((2, ROWS, 2048), BF),
            pltpu.VMEM((2, ROWS, 2048), F32),
            wide,
            wide,
            wide,
            wide,
            pltpu.VMEM((2, ROWS, D), BF),
            pltpu.VMEM((2, ROWS, 2048), BF),
            pltpu.VMEM((ROWS, D), BF),
            pltpu.VMEM((ROWS, 512), BF),
            wide,
            wide,
            pltpu.VMEM((ROWS, 128), F32),
            wide,
            wide,
            pltpu.VMEM((D, ROWS), BF),
            pltpu.VMEM((2, 1152, 512), BF),
            pltpu.VMEM((8, 128), F32),
            pltpu.VMEM((8, 8, 128), F32),
            pltpu.VMEM((ROWS, 128), F32),
            dma((32,)),
            dma((32,)),
            dma((10,)),
            *swap_sems(),
        ],
        name="middle",
        compiler_params=pltpu.CompilerParams(
            collective_id=3, has_side_effects=True, vmem_limit_bytes=VMEM_CAP
        ),
    )(context, meta, tokens, teacher, flags, smalls, out_all, up_all, down_all, qkv_all)


BACK_KEYS = 256
BACK_STEPS = L // BACK_KEYS
BACK_WIDTH = 1024


def back_prepare(qat, do, wide, lse, queries, grads, grad_rows):
    for j in range(L // BACK_WIDTH):
        columns = slice(j * BACK_WIDTH, (j + 1) * BACK_WIDTH)
        grad_t = jnp.concatenate([do[j * (BACK_WIDTH // TB) + i] for i in range(BACK_WIDTH // TB)], axis=1)
        wider = grad_t.astype(F32)
        delta = jnp.sum(wider * wide[:, columns], axis=0, keepdims=True)
        grads[:HD, columns] = grad_t
        grads[HD:, columns] = jnp.concatenate([three_pieces(-delta), jnp.zeros((61, BACK_WIDTH), BF)], axis=0)
        queries[:96, columns] = qat[:96, columns]
        queries[96:, columns] = jnp.concatenate(
            [three_pieces(-lse[:, columns]), jnp.zeros((29, BACK_WIDTH), BF)], axis=0
        )
        grad_rows[columns, :] = wider.T.astype(BF)


def back_kernel(
    qat, ka, va, kt, q8, do, wide, lse, smalls, x_seq, g_ref, a0,
    projected, heads_out, shard_out, smalls_out, qkv_all,
    x_buf, queries, grads, grad_rows, dq, d_ref, mine_ref, parts_ref, sum_ref, heads_buf, small_buf, small_sum, small_all,
    send, recv, local, dk_send, dk_recv, dk_local, dq_send, dq_recv, dq_local, spread_send, spread_recv, *reduce_refs,
):
    x, y, z, core = place()
    shard_at = y * 2 + x // 2
    seq = lax.axis_index("seq")
    mine = seq * 2 + x // 2
    net = (g_ref,) + reduce_refs

    def shard_device(d):
        other = (shard_at + d) % 8
        return other, (other // 2, seq, other % 2)

    load_x = pltpu.make_async_copy(x_seq, x_buf, local.at[0])
    load_x.start()
    shard_others = [shard_device(d)[1] for d in range(1, 8)]
    greet_signal(shard_others)
    back_prepare(qat, do, wide, lse, queries, grads, grad_rows)
    dq[...] = jnp.zeros_like(dq)
    greet_wait(shard_others)
    for part in range(3):
        reduce_start(part, net)
    far = Transfers(send, recv)
    small_out = [far.copy(smalls.at[shard_device(d)[0]], small_buf.at[shard_at], shard_device(d)[1]) for d in range(1, 8)]
    start_all(small_out)
    small_buf[shard_at] = smalls[shard_at]
    rows = half_rows(core)
    weights = far.copy(qkv_all.at[:, rows], qkv_all.at[:, rows], sibling())
    weights.start()

    def landing(first, count):
        return projected.at[pl.ds(first, count), pl.ds(aligned(seq * HD, HD), HD), pl.ds(aligned((x // 2) * TB, TB), TB)]

    def block_device(b):
        return (y, b // 2, b % 2)

    def dk_copy(b, recv_at):
        return remote(d_ref.at[b, pl.ds(1, 2)], landing(1, 2), dk_send.at[b], dk_recv.at[recv_at], block_device(b))

    def dq_copy(b, recv_at):
        return remote(d_ref.at[b, pl.ds(0, 1)], landing(0, 1), dq_send.at[b], dq_recv.at[recv_at], block_device(b))

    dk_own = pltpu.make_async_copy(d_ref.at[mine, pl.ds(1, 2)], landing(1, 2), dk_local)
    dq_own = pltpu.make_async_copy(d_ref.at[mine, pl.ds(0, 1)], landing(0, 1), dq_local)

    @pl.loop(0, BACK_STEPS)
    def _(step):
        at = (step + 4 * (z + 1)) % BACK_STEPS
        keys = pl.ds(aligned(at * BACK_KEYS, BACK_KEYS), BACK_KEYS)
        ka_part, va_part, kt_part = ka[keys, :], va[keys, :], kt[:, keys]
        dk = jnp.zeros((BACK_KEYS, HD), F32)
        dv = jnp.zeros((BACK_KEYS, HD), F32)
        for j in range(L // BACK_WIDTH):
            columns = slice(j * BACK_WIDTH, (j + 1) * BACK_WIDTH)
            probs = jnp.exp(dot(ka_part, queries[:, columns]))
            raw = (probs * dot(va_part, grads[:, columns])).astype(BF)
            dv = dv + dot(probs.astype(BF), grad_rows[columns, :])
            dk = dk + dot(raw, q8[columns, :])
            dq[:, columns] += dot(kt_part, raw)
        dk_t, dv_t = dk.T.astype(BF), dv.T.astype(BF)
        for i in range(BACK_KEYS // TB):
            b = at * (BACK_KEYS // TB) + i
            d_ref[b, 1] = dk_t[:, i * TB : (i + 1) * TB]
            d_ref[b, 2] = dv_t[:, i * TB : (i + 1) * TB]

            @pl.when(b != mine)
            def _():
                dk_copy(b, mine).start()

            @pl.when(b == mine)
            def _():
                dk_own.start()

        @pl.when(step == 4)
        def _():
            first_relay(net)

        @pl.when(step == 9)
        def _():
            reduce_step(0, 1, net)

        @pl.when(step == 11)
        def _():
            reduce_step(0, 0, net)

        @pl.when(step == 13)
        def _():
            reduce_step(0, 2, net)
            reduce_step(1, 1, net)

    reduce_step(1, 0, net)
    reduce_step(1, 2, net)
    steps = [
        spread_steps(part, reduce_refs[6 + part].at[0], (local.at[pl.ds(1, 3)], spread_send, spread_recv), shard_out)
        for part in range(3)
    ]
    reduce_step(2, 1, net)
    steps[1][0]()
    for b in range(NB):
        d_ref[b, 0] = (dq[:, b * TB : (b + 1) * TB] * 0.125).astype(BF)

    load_x.wait()
    left = jnp.concatenate([d_ref[b].reshape(3 * HD, TB) for b in range(NB)], axis=1)
    sums = dot(jnp.ones((8, L), BF), left, ((1,), (1,)))
    gap = jnp.zeros((1, 128 - HD), F32)
    tail = jnp.concatenate(
        [
            jnp.concatenate([sums[:1, :HD], gap], axis=1),
            jnp.concatenate([sums[:1, 2 * HD :], gap], axis=1),
            jnp.zeros((14, 128), F32),
        ],
        axis=0,
    ).astype(BF)
    for i in range(4):
        total = dot(left, x_buf[:, :, 256 * i : 256 * (i + 1)].reshape(L, 256))
        for k in range(2):
            mine_ref[2 * i + k, : 3 * HD, :] = total[:, 128 * k : 128 * (k + 1)].astype(BF)
            mine_ref[2 * i + k, 3 * HD :, :] = tail
    part_out = [far.copy(mine_ref.at[shard_device(d)[0]], parts_ref.at[d], shard_device(d)[1]) for d in range(1, 8)]
    start_all(part_out)

    @pl.loop(1, NB)
    def _(shift):
        dq_copy((mine + shift) % NB, mine).start()

    dq_own.start()
    for part in (2, 0):
        reduce_step(2, part, net)
        steps[part][0]()
    wait_all(small_out)
    small_sum[...] = jnp.sum(small_buf[...], axis=0)
    wait_all(part_out)
    added = mine_ref[shard_at].astype(F32)
    for d in range(1, 8):
        added = added + parts_ref[d].astype(F32)
    sum_ref[...] = added.astype(BF)
    heads_buf[seq // 2, core] = sum_ref[...]
    small_all[seq // 2, core] = small_sum[...]
    head_out = []
    for d in range(1, 8):
        target = (y, (seq + 2 * d) % 16, x // 2)
        head_out.append(far.copy(sum_ref, heads_buf.at[seq // 2, core], target))
        head_out.append(far.copy(small_sum, small_all.at[seq // 2, core], target))
    start_all(head_out)
    for part in (1, 2, 0):
        steps[part][1]()
    wait_all(head_out)
    across = [
        far.copy(heads_buf.at[:, core], heads_buf.at[:, core], sibling()),
        far.copy(small_all.at[:, core], small_all.at[:, core], sibling()),
    ]
    start_all(across)
    shared = []
    for part in (1, 2, 0):
        steps[part][2]()
        piece = shard_out.at[core, pl.ds(FIRST[part], 8 * PIECE[part])]
        shared.append(far.copy(piece, piece, sibling()))
        shared[-1].start()

    @pl.loop(1, NB)
    def _(shift):
        b = (mine + shift) % NB
        dk_copy(b, b).wait()
        dq_copy(b, b).wait()

    dk_own.wait()
    dq_own.wait()
    weights.wait()
    wait_all(across)
    for i in range(8):
        heads_out[2 * i] = heads_buf[i, 0]
        heads_out[2 * i + 1] = heads_buf[i, 1]
    smalls_out[...] = jnp.sum(small_all[...].reshape(16, 16, 128), axis=0)
    wait_all(shared)


def back(qat, ka, va, kt, q8, do, wide, lse, smalls, x_seq, g, qkv_all):
    shape = jax.ShapeDtypeStruct
    in_vmem = pl.BlockSpec(memory_space=pltpu.VMEM)
    dma = pltpu.SemaphoreType.DMA
    return pl.pallas_call(
        back_kernel,
        in_specs=[in_vmem] * 9 + [ANY] * 3,
        out_specs=[ANY, in_vmem, ANY, in_vmem, ANY],
        out_shape=[
            shape((3, D, 2 * TB), BF),
            shape((H, 208, 128), BF),
            shape((2, 1152, 512), BF),
            shape((16, 128), F32),
            shape(qkv_all.shape, BF),
        ],
        input_output_aliases={11: 4},
        scratch_shapes=[
            pltpu.VMEM((NB, TB, D), BF),
            pltpu.VMEM((128, L), BF),
            pltpu.VMEM((128, L), BF),
            pltpu.VMEM((L, HD), BF),
            pltpu.VMEM((HD, L), F32),
            pltpu.VMEM((NB, 3, HD, TB), BF),
            pltpu.VMEM((8, 208, 128), BF),
            pltpu.VMEM((8, 208, 128), BF),
            pltpu.VMEM((208, 128), BF),
            pltpu.VMEM((8, 2, 208, 128), BF),
            pltpu.VMEM((8, 16, 128), F32),
            pltpu.VMEM((16, 128), F32),
            pltpu.VMEM((8, 2, 16, 128), F32),
            dma((40,)),
            dma((40,)),
            dma((4,)),
            *swap_sems(),
            *swap_sems(),
            dma((3, 8)),
            dma((3, 8)),
            *reduce_scratch(),
        ],
        name="attend_back",
        compiler_params=pltpu.CompilerParams(
            collective_id=4, has_side_effects=True, vmem_limit_bytes=VMEM_CAP
        ),
    )(qat, ka, va, kt, q8, do, wide, lse, smalls, x_seq, g, qkv_all)


def finish_kernel(
    projected, qkv_ref, resid_ref, heads_ref, shard_ref, tokens_ref, grad_qkv, grad_out, grad_up, grad_down
):
    step = pl.program_id(0)
    tokens_ref[...] = resid_ref[...] + dot(projected[...], qkv_ref[...], ((0,), (1,)))
    for c in range(2):
        columns = slice(512 * c, 512 * (c + 1))
        for j in range(2):
            piece = shard_ref[c, pl.ds(aligned(step * 128, 128), 128), 256 * j : 256 * (j + 1)]
            grad_up[:, 512 * j + 256 * c : 512 * j + 256 * (c + 1)] = piece.astype(F32)
        rows = pl.ds(aligned(512 + 256 * c + (step % 2) * 128, 128), 128)
        grad_down[:, columns] = shard_ref[step // 2, rows, :].astype(F32)
        grad_out[:, columns] = shard_ref[c, pl.ds(aligned(1024 + step * 32, 32), 32), :].astype(F32)

    @pl.when(step == 0)
    def _():
        for p in range(3):
            for pair in range(8):
                both = [heads_ref[2 * pair + k, p * HD : (p + 1) * HD, :].astype(F32) for k in range(2)]
                at = p * D + pair * 128
                grad_qkv[:, at : at + 128] = jnp.concatenate(both, axis=0).T


def finish(projected, qkv, resid, heads, shard):
    shape = jax.ShapeDtypeStruct

    def whole(dims):
        return pl.BlockSpec(dims, lambda i: (0,) * len(dims))

    return pl.pallas_call(
        finish_kernel,
        grid=(4,),
        in_specs=[
            whole((3 * D, 2 * TB)),
            pl.BlockSpec((256, 3 * D), lambda i: (i, 0)),
            pl.BlockSpec((2 * TB, 256), lambda i: (0, i)),
            whole((H, 208, 128)),
            whole((2, 1152, 512)),
        ],
        out_specs=[
            pl.BlockSpec((2 * TB, 256), lambda i: (0, i)),
            whole((128, 3 * D)),
            pl.BlockSpec((32, D), lambda i: (i, 0)),
            pl.BlockSpec((128, 1024), lambda i: (0, i)),
            pl.BlockSpec((128, D), lambda i: (i, 0)),
        ],
        out_shape=[
            shape((2 * TB, D), F32),
            shape((128, 3 * D), F32),
            shape((128, D), F32),
            shape((128, FF), F32),
            shape((512, D), F32),
        ],
        name="finish",
        compiler_params=pltpu.CompilerParams(vmem_limit_bytes=VMEM_CAP),
    )(projected, qkv, resid, heads, shard)


def on_device(
    tokens,
    segments,
    valid_flags,
    teacher,
    w_qkv,
    b_query,
    b_value,
    w_out,
    b_out,
    ln1_gain,
    ln1_bias,
    w_up,
    b_up,
    w_down,
    b_down,
    ln2_gain,
    ln2_bias,
):
    seq_local, row_local, _ = tokens.shape
    token_rows = seq_local * row_local
    shard_at = lax.axis_index("dp") * 2 + lax.axis_index("wshard")

    vectors = jnp.stack([b_query, b_value, b_out, ln1_gain, ln1_bias, b_down, ln2_gain, ln2_bias]).astype(F32)
    (
        x_seq, meta_all, smalls_all, out_all, up_all, down_all, qkv_all, qat, ka, va, kt, q8, context, wide, lse
    ) = front(
        tokens, segments, valid_flags, vectors, b_up.reshape(4, 128).astype(F32), w_out, w_up, w_down, w_qkv
    )
    x_seq = x_seq.reshape(NB, TB, D)
    states, grad_resid_one, do, g, small_sums, count, qkv_all = middle(
        context,
        meta_all,
        tokens.reshape(token_rows, D),
        teacher.reshape(token_rows, D),
        valid_flags,
        smalls_all,
        out_all,
        up_all,
        down_all,
        qkv_all,
    )
    projected, heads_out, shard_out, small_out, qkv_all = back(
        qat, ka, va, kt, q8, do, wide, lse, small_sums, x_seq, g, qkv_all
    )
    grad_tokens, grad_qkv, grad_out, grad_up, grad_down = finish(
        projected.reshape(3 * D, token_rows), qkv_all.reshape(D, 3 * D), grad_resid_one, heads_out, shard_out
    )
    own_heads = lax.dynamic_slice(heads_out, (shard_at * 2, 3 * HD, 0), (2, 2, HD)).astype(F32)
    mean_loss = small_out[10, 0] / (D * count[0, 0])
    return (
        states.reshape(seq_local, row_local, D),
        mean_loss,
        grad_tokens.reshape(seq_local, row_local, D),
        grad_qkv,
        own_heads[:, 0].reshape(128),
        own_heads[:, 1].reshape(128),
        grad_out,
        small_out[0],
        small_out[1],
        small_out[2],
        grad_up,
        small_out[6:10].reshape(512),
        grad_down,
        small_out[3],
        small_out[4],
        small_out[5],
    )


def solution(mesh):
    rows = P("dp", ("seq", "wshard"), None)
    flags = P("dp", ("seq", "wshard"))
    matrix = P(("dp", "wshard"), None)
    vector = P(("dp", "wshard"))
    return jax.shard_map(
        on_device,
        mesh=mesh,
        in_specs=(
            rows,
            flags,
            flags,
            rows,
            matrix,
            vector,
            vector,
            matrix,
            vector,
            vector,
            vector,
            matrix,
            vector,
            matrix,
            vector,
            vector,
            vector,
        ),
        out_specs=(
            rows,
            P(),
            rows,
            matrix,
            vector,
            vector,
            matrix,
            vector,
            vector,
            vector,
            matrix,
            vector,
            matrix,
            vector,
            vector,
            vector,
        ),
        check_vma=False,
    )
```

```python
import functools

import jax
import jax.numpy as jnp
from jax import lax
from jax.experimental import pallas as pl
from jax.experimental.pallas import tpu as pltpu
from jax.sharding import PartitionSpec as P

D = 1024
H = 16
HD = 64
FF = 4096
L = 4096
EPS = 1e-06
F32 = jnp.float32
BF = jnp.bfloat16
MASKED = 1000000000.0
VMEM_CAP = 60 * 1024 * 1024
MESH = pl.DeviceIdType.MESH
ANY = pl.BlockSpec(memory_space=pl.ANY)
TB = 128
NB = L // TB


def dot(first, second, dims=((1,), (0,))):
    return lax.dot_general(first, second, (dims, ((), ())), preferred_element_type=F32)


def three_pieces(row):
    high = row.astype(BF)
    rest = row - high.astype(F32)
    middle = rest.astype(BF)
    lowest = (rest - middle.astype(F32)).astype(BF)
    return jnp.concatenate([high, middle, lowest], axis=0)


def place():
    at = lax.axis_index("seq")
    return (lax.axis_index("wshard") * 2 + (at // 2) % 2, lax.axis_index("dp"), at // 4, at % 2)


def device_at(x, y, z, core):
    return (y, (z * 2 + x % 2) * 2 + core, x // 2)


def along(axis, shift):
    x, y, z, core = place()
    if axis == "x":
        return device_at((x + shift) % 4, y, z, core)
    if axis == "y":
        return device_at(x, (y + shift) % 4, z, core)
    return device_at(x, y, (z + shift) % 4, core)


def sibling():
    x, y, z, core = place()
    return device_at(x, y, z, 1 - core)


def greet(partners):
    barrier = pltpu.get_barrier_semaphore()
    for partner in partners:
        pl.semaphore_signal(barrier, inc=1, device_id=partner, device_id_type=MESH)
    pl.semaphore_wait(barrier, len(partners))


def remote(src, dst, send_sem, recv_sem, target):
    return pltpu.make_async_remote_copy(
        src_ref=src, dst_ref=dst, send_sem=send_sem, recv_sem=recv_sem, device_id=target, device_id_type=MESH
    )


ORDERS = ("yzx", "zxy", "xyz")
PIECE = (64, 32, 48)
FIRST = (0, 512, 768)


def ring_partners():
    return [along(axis, shift) for axis in "xyz" for shift in (1, 2, 3)] + [sibling()]


def reduce_scratch():
    a, b, c = PIECE
    return [
        pltpu.VMEM((4, 2, 8 * a, 512), BF),
        pltpu.VMEM((4, 4, 2, 2 * b, 512), BF),
        pltpu.VMEM((4, 4, 4 * c, 512), BF),
        pltpu.VMEM((4, 2, 2 * a, 512), BF),
        pltpu.VMEM((4, 4, b, 512), BF),
        pltpu.VMEM((4, 4 * c, 512), BF),
        pltpu.VMEM((4, a, 512), BF),
        pltpu.VMEM((4, b, 512), BF),
        pltpu.VMEM((4, c, 512), BF),
        pltpu.SemaphoreType.DMA((3, 3, 3)),
        pltpu.SemaphoreType.DMA((3, 3, 3)),
        pltpu.SemaphoreType.DMA((3,)),
        pltpu.VMEM((2, 8 * a, 512), BF),
        pltpu.SemaphoreType.DMA((6,)),
        pltpu.SemaphoreType.DMA((6,)),
        pltpu.SemaphoreType.DMA((2,)),
    ]


def aligned(value, unit):
    return pl.multiple_of(value, unit)


def reduce_piece(stage, part, refs, at):
    g_ref = refs[0]
    half, low, n = at // 2, at % 2, PIECE[part]
    if stage == 0:
        first = FIRST[part]
        if part == 0:
            return g_ref.at[at, :, pl.ds(first, 8 * n), :]
        if part == 1:
            return g_ref.at[:, :, pl.ds(aligned(first + at * 2 * n, 16), 2 * n), :]
        return g_ref.at[:, half, pl.ds(aligned(first + low * 4 * n, 16), 4 * n), :]
    held = refs[1 + 3 * (stage - 1) + part]
    if stage == 1:
        if part == 0:
            return held.at[0, :, pl.ds(aligned(at * 2 * n, 16), 2 * n), :]
        if part == 1:
            return held.at[0, :, half, pl.ds(aligned(low * n, 16), n), :]
        return held.at[0, at]
    if part == 0:
        return held.at[0, half, pl.ds(aligned(low * n, 16), n), :]
    if part == 1:
        return held.at[0, at]
    return held.at[0, pl.ds(aligned(at * n, 16), n), :]


def ring_at(axis):
    x, y, z, _ = place()
    return {"x": x, "y": y, "z": z}[axis]


def reduce_copies(stage, part, refs):
    send, recv = refs[10], refs[11]
    axis = ORDERS[part][stage]
    return [
        remote(
            reduce_piece(stage, part, refs, (ring_at(axis) + shift) % 4),
            refs[1 + 3 * stage + part].at[shift],
            send.at[stage, part, shift - 1],
            recv.at[stage, part, shift - 1],
            along(axis, shift),
        )
        for shift in (1, 3, 2)
    ]


def reduce_own(part, refs):
    return pltpu.make_async_copy(
        reduce_piece(0, part, refs, ring_at(ORDERS[part][0])), refs[1 + part].at[0], refs[12].at[part]
    )


def reduce_start(part, refs):
    start_all(first_copies(refs)[:4] + first_loads(refs) if part == 0 else reduce_copies(0, part, refs))
    reduce_own(part, refs).start()


def first_copies(refs):
    g_ref, a1, relay, send, recv = refs[0], refs[1], refs[13], refs[14], refs[15]
    _, y, _, _ = place()
    rows = pl.ds(0, 8 * PIECE[0])
    up, down, far = (y + 1) % 4, (y + 3) % 4, (y + 2) % 4
    moves = [
        (g_ref.at[far, 0, rows], a1.at[2, 0], 1),
        (g_ref.at[far, 1, rows], a1.at[2, 1], 3),
        (g_ref.at[up, 1, rows], a1.at[1, 1], 1),
        (g_ref.at[down, 0, rows], a1.at[3, 0], 3),
        (relay.at[0], a1.at[1, 0], 1),
        (relay.at[1], a1.at[3, 1], 3),
    ]
    return [remote(src, dst, send.at[k], recv.at[k], along("y", d)) for k, (src, dst, d) in enumerate(moves)]


def first_loads(refs):
    g_ref, relay, local = refs[0], refs[13], refs[16]
    _, y, _, _ = place()
    rows = pl.ds(0, 8 * PIECE[0])
    return [
        pltpu.make_async_copy(g_ref.at[(y + 1) % 4, 0, rows], relay.at[0], local.at[0]),
        pltpu.make_async_copy(g_ref.at[(y + 3) % 4, 1, rows], relay.at[1], local.at[1]),
    ]


def first_relay(refs):
    a1, relay = refs[1], refs[13]
    copies = first_copies(refs)
    wait_all(first_loads(refs))
    for copy in copies[:2]:
        copy.wait_recv()

    @pl.loop(0, 16)
    def _(i):
        rows = pl.ds(aligned((i % 8) * PIECE[0], 16), PIECE[0])
        half = i // 8
        relay[half, rows, :] = (relay[half, rows, :].astype(F32) + a1[2, half, rows, :].astype(F32)).astype(BF)

    start_all(copies[4:])


def first_end(refs):
    copies = first_copies(refs)
    for copy in copies[:2]:
        copy.wait_send()
    wait_all(copies[2:])


def add_four(values):
    total = values[0].astype(F32) + values[1].astype(F32)
    return (total + values[2].astype(F32) + values[3].astype(F32)).astype(BF)


def reduce_step(stage, part, refs):
    a1, b1, c1, a2, b2, c2, a3, b3, c3 = refs[1:10]
    if stage == 0 and part == 0:
        first_end(refs)
    else:
        wait_all(reduce_copies(stage, part, refs))
    x, y, z, _ = place()
    n = PIECE[part]
    rest = (1, 2, 3)
    if stage == 0:
        reduce_own(part, refs).wait()

        @pl.loop(0, 16)
        def _(i):
            if part == 0:
                rows = pl.ds(aligned((i % 8) * n, 16), n)
                total = a1[0, i // 8, rows, :].astype(F32) + a1[1, i // 8, rows, :].astype(F32)
                a1[0, i // 8, rows, :] = (total + a1[3, i // 8, rows, :].astype(F32)).astype(BF)
            elif part == 1:
                rows = pl.ds(aligned((i % 2) * n, 16), n)
                b1[0, i // 4, (i // 2) % 2, rows, :] = add_four([b1[s, i // 4, (i // 2) % 2, rows, :] for s in range(4)])
            else:
                rows = pl.ds(aligned((i % 4) * n, 16), n)
                c1[0, i // 4, rows, :] = add_four([c1[s, i // 4, rows, :] for s in range(4)])

    elif stage == 1:

        @pl.loop(0, 4)
        def _(i):
            if part == 0:
                rows = pl.ds(aligned((i % 2) * n, 16), n)
                own = a1[0, i // 2, pl.ds(aligned(z * 2 * n + (i % 2) * n, 16), n), :]
                a2[0, i // 2, rows, :] = add_four([own] + [a2[s, i // 2, rows, :] for s in rest])
            elif part == 1:
                own = b1[0, i, x // 2, pl.ds(aligned((x % 2) * n, 16), n), :]
                b2[0, i] = add_four([own] + [b2[s, i] for s in rest])
            else:
                rows = pl.ds(aligned(i * n, 16), n)
                own = c1[0, y, rows, :]
                c2[0, rows, :] = add_four([own] + [c2[s, rows, :] for s in rest])

    elif part == 0:
        own = a2[0, x // 2, pl.ds(aligned((x % 2) * n, 16), n), :]
        a3[0] = add_four([own] + [a3[s] for s in rest])
    elif part == 1:
        b3[0] = add_four([b2[0, y]] + [b3[s] for s in rest])
    else:
        own = c2[0, pl.ds(aligned(z * n, 16), n), :]
        c3[0] = add_four([own] + [c3[s] for s in rest])
    if stage < 2:
        start_all(reduce_copies(stage + 1, part, refs))


def shard_rows(o_ref, part, x_low, z, core):
    sub = x_low * 4 + z if part == 2 else z * 2 + x_low
    return o_ref.at[core, pl.ds(aligned(FIRST[part] + sub * PIECE[part], 16), PIECE[part]), :]


def spread_steps(part, mine, sems, o_ref):
    local, send, recv = sems
    x, y, z, core = place()
    low = x % 2
    pair = device_at(x // 2 * 2 + 1 - low, y, z, core)
    spot = shard_rows(o_ref, part, low, z, core)
    own = pltpu.make_async_copy(mine, spot, local.at[part])
    first = remote(mine, spot, send.at[part, 0], recv.at[part, 0], pair)
    second = [remote(mine, spot, send.at[part, d], recv.at[part, d], along("z", d)) for d in (1, 3, 2)]
    spot = shard_rows(o_ref, part, 1 - low, z, core)
    third = [remote(spot, spot, send.at[part, 3 + d], recv.at[part, 3 + d], along("z", d)) for d in (1, 3, 2)]

    def begin():
        start_all([own, first] + second)

    def middle():
        first.wait()
        start_all(third)

    def end():
        wait_all([own] + second + third)

    return begin, middle, end


def swap_partner(shift):
    mine = lax.axis_index("seq") * 2 + lax.axis_index("wshard")
    other = (mine + shift) % NB
    return other, (lax.axis_index("dp"), other // 2, other % 2)


def swap_greet():
    barrier = pltpu.get_barrier_semaphore()

    @pl.loop(1, NB)
    def _(shift):
        pl.semaphore_signal(barrier, inc=1, device_id=swap_partner(shift)[1], device_id_type=MESH)

    pl.semaphore_wait(barrier, NB - 1)


def swap_copies(piece_for, landing_from, sems):
    mine = lax.axis_index("seq") * 2 + lax.axis_index("wshard")
    send, recv, local = sems

    def copy(shift):
        other, device = swap_partner(shift)
        return remote(piece_for(other), landing_from(mine), send.at[shift], recv.at[shift], device)

    own = pltpu.make_async_copy(piece_for(mine), landing_from(mine), local)

    def start():
        @pl.loop(1, NB)
        def _(shift):
            copy(shift).start()

        own.start()

    def wait():
        @pl.loop(1, NB)
        def _(shift):
            copy(shift).wait()

        own.wait()

    return start, wait


def swap_sems():
    return [pltpu.SemaphoreType.DMA((NB,)), pltpu.SemaphoreType.DMA((NB,)), pltpu.SemaphoreType.DMA]


def block_of(ref, b):
    return ref.at[b]


def head_tile(ref, b):
    return ref.at[pl.ds(aligned((b // 2) * HD, HD), HD), pl.ds(aligned((b % 2) * TB, TB), TB)]


def head_tile3(ref, b):
    return ref.at[:, pl.ds(aligned((b // 2) * HD, HD), HD), pl.ds(aligned((b % 2) * TB, TB), TB)]


HALVES = ((128, 2048), (256, 1024))


class Transfers:
    def __init__(self, send, recv):
        self.send, self.recv, self.used = send, recv, 0

    def copy(self, src, dst, target):
        made = remote(src, dst, self.send.at[self.used], self.recv.at[self.used], target)
        self.used += 1
        return made


def start_all(copies):
    for copy in copies:
        copy.start()


def wait_all(copies):
    for copy in copies:
        copy.wait()


def unit_rows(matrix, unit, count=1):
    rows = HALVES[matrix][0] // 4
    return pl.ds(unit * rows, count * rows)


def columns_part(matrix, at, parts):
    width = HALVES[matrix][1] // parts
    return pl.ds(aligned(at * width, 128), width)


def half_rows(core, rows=64):
    return pl.ds(aligned(core * rows, rows), rows)


def shard_greet():
    x, y, z, core = place()
    return [device_at(x, (y + d) % 4, z, core) for d in (1, 2, 3)] + [
        device_at(3 - x, (y + d) % 4, z, core) for d in range(4)
    ]


def greet_signal(others):
    barrier = pltpu.get_barrier_semaphore()

    @pl.loop(1, NB)
    def _(shift):
        pl.semaphore_signal(barrier, inc=1, device_id=swap_partner(shift)[1], device_id_type=MESH)

    for other in others:
        pl.semaphore_signal(barrier, inc=1, device_id=other, device_id_type=MESH)


def greet_wait(others):
    pl.semaphore_wait(pltpu.get_barrier_semaphore(), NB - 1 + len(others))


FRONT_COPIES = 144


def front_kernel(
    tokens, segments, flags, vectors, b_up, w_out, w_up, w_down, w_qkv,
    x_seq, meta_out, smalls_out, out_all, up_all, down_all, qkv_all, qat_ref, ka_ref, va_ref, kt_ref, q_ref,
    context, wide_ref, lse_ref,
    vat_ref, blocks, x_buf, tok_buf, out_buf, up_buf, down_buf, qkv_buf, meta, heads, smalls, meta_all, heads_all, smalls_all, w_ref, b_ref,
    send, recv, local, meta_send, meta_recv, meta_local, back_send, back_recv, back_local,
):
    x, y, z, core = place()
    hi, lo = x // 2, x % 2
    mine, across = y * 2 + hi, y * 2 + 1 - hi
    wrap, pair, other_core = device_at(3 - x, y, z, core), device_at(hi * 2 + 1 - lo, y, z, core), sibling()
    shards, wholes = (up_buf.at[core], down_buf), (up_all, down_all)
    rows_out = half_rows(core)
    greet_signal(shard_greet())
    load_tokens = pltpu.make_async_copy(tokens, tok_buf, local.at[0])
    load_qkv = pltpu.make_async_copy(w_qkv, qkv_buf, local.at[11])
    loads = [
        pltpu.make_async_copy(w_out, out_buf, local.at[9]),
        pltpu.make_async_copy(w_down.at[half_rows(core, 256)], down_buf, local.at[10]),
    ]
    for j in range(8):
        piece = w_up.at[:, pl.ds(aligned(j * 512 + core * 256, 256), 256)]
        loads.append(pltpu.make_async_copy(piece, up_buf.at[core, :, pl.ds(j * 256, 256)], local.at[1 + j]))
    start_all([load_tokens, load_qkv] + loads)
    meta[...] = jnp.zeros_like(meta)
    for s in range(2):
        meta[s, 0:1, :] = segments[s : s + 1, :]
        meta[s, 1:2, :] = flags[s : s + 1, :]
    smalls[...] = jnp.zeros_like(smalls)
    smalls[0:8, :] = vectors[...]
    smalls[8:12, :] = b_up[...]
    greet_wait(shard_greet())
    load_tokens.wait()
    net = Transfers(send, recv)
    first, second = pl.ds(0, 64), pl.ds(64, 64)

    def block(at, low, w, rows=slice(None)):
        return x_buf.at[at, low, core, w, rows]

    own = tok_buf.at[hi]
    swap = net.copy(tok_buf.at[1 - hi], block(z, lo, hi), wrap)
    own_z = [net.copy(own, block(z, lo, hi), along("z", d)) for d in (1, 3, 2)]
    own_pair = [net.copy(own.at[rows], block(z, lo, hi, rows), pair) for rows in (first, second)]
    start_all([swap, own_pair[0]] + own_z)
    x_buf[z, lo, core, hi] = tok_buf[hi]
    load_qkv.wait()
    for p in range(3):
        for k, pair_at in ((0, z * 2 + lo), (1, z * 2 + 1 - lo)):
            heads[k, :, 128 * p : 128 * (p + 1)] = qkv_buf[:, pl.ds(aligned(p * D + pair_at * 128, 128), 128)]
    cross_first = [
        net.copy(heads.at[1], heads_all.at[mine], wrap),
        net.copy(smalls, smalls_all.at[mine], wrap),
    ]
    start_all(cross_first)
    wait_all(loads)
    cross_early, cross_late = [net.copy(out_buf.at[rows_out], out_all.at[mine, rows_out], wrap)], []
    for m in range(2):
        for unit, columns in ((0, columns_part(m, z, 4)), (3, columns_part(m, 1 - lo, 2))):
            rows = unit_rows(m, unit)
            cross_early.append(net.copy(shards[m].at[rows, columns], wholes[m].at[mine, rows, columns], wrap))

    def small_y(shard, heads_source, smalls_source):
        copies = []
        for d in (1, 3, 2):
            copies.append(net.copy(heads_source, heads_all.at[shard], along("y", d)))
            copies.append(net.copy(smalls_source, smalls_all.at[shard], along("y", d)))
        return copies

    own_small = small_y(mine, heads.at[0], smalls)
    start_all(own_small + cross_early)
    heads_all[mine] = heads[0]
    smalls_all[mine] = smalls[...]
    meta_start, meta_wait = swap_copies(
        lambda b: meta.at[b % 2], lambda b: meta_all.at[b], (meta_send, meta_recv, meta_local)
    )
    meta_start()
    keep = [
        pltpu.make_async_copy(out_buf.at[rows_out], out_all.at[mine, rows_out], local.at[9]),
        pltpu.make_async_copy(qkv_buf, qkv_all.at[mine], local.at[11]),
    ]
    for m in range(2):
        parts = [
            (unit_rows(m, 0), columns_part(m, z, 4)),
            (unit_rows(m, 3), columns_part(m, lo, 2)),
            (unit_rows(m, 1, 2), slice(None)),
        ]
        for k, (rows, columns) in enumerate(parts):
            piece = wholes[m].at[mine, rows, columns]
            keep.append(pltpu.make_async_copy(shards[m].at[rows, columns], piece, local.at[1 + 3 * m + k]))
    start_all(keep)

    def outer_y(shard, source, out_source):
        copies = []
        for d in (1, 3, 2):
            there = along("y", d)
            copies.append(net.copy(out_source.at[rows_out], out_all.at[shard, rows_out], there))
            for m in range(2):
                for unit, columns in ((0, columns_part(m, z, 4)), (3, columns_part(m, lo, 2))):
                    rows = unit_rows(m, unit)
                    copies.append(net.copy(source(m).at[rows, columns], wholes[m].at[shard, rows, columns], there))
        return copies

    def inner_y(m, shard, source):
        rows = unit_rows(m, 1, 2)
        return [net.copy(source.at[rows], wholes[m].at[shard, rows], along("y", d)) for d in (1, 3, 2)]

    swap.wait_recv()
    came = block(z, 1 - lo, 1 - hi)
    came_pair = [
        net.copy(block(z, 1 - lo, 1 - hi, rows), block(z, 1 - lo, 1 - hi, rows), pair) for rows in (first, second)
    ]
    came_z = [net.copy(came, came, along("z", d)) for d in (1, 3, 2)]
    start_all([came_pair[0]] + came_z + [own_pair[1], came_pair[1]])
    for copy in cross_first:
        copy.wait_recv()
    across_small = small_y(across, heads_all.at[across], smalls_all.at[across])
    own_y = outer_y(mine, lambda m: shards[m], out_buf)
    start_all(across_small + own_y)
    pair_late = []

    def forward(got, d, low, w):
        got.wait_recv()
        piece = block((z + 4 - d) % 4, low, w, second)
        pair_late.append(net.copy(piece, piece, pair))
        pair_late[-1].start()

    for i, d in enumerate((1, 3, 2)):
        forward(own_z[i], d, lo, hi)
    half_z = []

    def halves(got, low, w):
        got.wait_recv()
        piece = block(z, low, w, first)
        copies = [net.copy(piece, piece, along("z", d)) for d in (1, 3, 2)]
        start_all(copies)
        half_z.extend(copies)

    halves(own_pair[0], 1 - lo, hi)
    for copy in cross_early:
        copy.wait_recv()
    across_y = outer_y(across, lambda m: wholes[m].at[across], out_all.at[across])
    inner_down = inner_y(1, mine, down_buf)
    inner_up = inner_y(0, mine, up_buf.at[core])
    rows = unit_rows(0, 1, 2)
    cross_late.append(net.copy(up_buf.at[core, rows], up_all.at[mine, rows], wrap))
    rows = half_rows(core)
    cross_late.append(net.copy(qkv_buf.at[rows], qkv_all.at[mine, rows], wrap))
    start_all(across_y + cross_late + inner_down + inner_up)
    for i, d in enumerate((1, 3, 2)):
        forward(came_z[i], d, 1 - lo, 1 - hi)
    halves(came_pair[0], lo, 1 - hi)
    share, rest = [], []
    for low, w in ((lo, hi), (1 - lo, 1 - hi)):
        piece = x_buf.at[:, low, core, w]
        share.append(net.copy(piece, piece, other_core))
    start_all(share)
    cross_late[0].wait_recv()
    across_up = inner_y(0, across, up_all.at[across])
    start_all(across_up)

    for copy in own_small + across_small:
        copy.wait_recv()
    meta_wait()
    at_first = core == 0
    both = heads_all[...].reshape(D, 384)
    parts = [jnp.where(at_first, both[:, 128 * p : 128 * p + HD], both[:, 128 * p + HD : 128 * (p + 1)]) for p in range(3)]
    w_ref[...] = jnp.concatenate(parts, axis=1)
    biases = smalls_all[lax.axis_index("seq") // 2]
    bias = [jnp.where(at_first, biases[k : k + 1, :HD], biases[k : k + 1, HD:]) for k in range(2)]
    b_ref[...] = jnp.broadcast_to(jnp.concatenate([bias[0], jnp.zeros((1, HD), F32), bias[1]], axis=1), (8, 3 * HD))

    def project(low, at_core, w):
        @pl.loop(0, 4)
        def _(at):
            b = at * 8 + low * 4 + at_core * 2 + w
            rows = pl.ds(aligned(b * TB, TB), TB)
            side = dot(x_buf[at, low, at_core, w], w_ref[...]) + b_ref[:1, :]
            q8 = side[:, :HD].astype(BF).astype(F32) * 0.125
            hot = jnp.where(lax.broadcasted_iota(jnp.int32, (32, TB), 0) == meta_all[b, 0:1, :], 1.0, 0.0)
            lane = lax.broadcasted_iota(jnp.int32, (TB, HD), 1)
            ones3 = jnp.where(lane < 3, 1.0, 0.0)
            apart = (hot.T - 1.0) * MASKED
            key = side[:, HD : 2 * HD]
            value = side[:, 2 * HD :]
            q_ref[rows, :] = q8.astype(BF)
            ka_ref[rows, :] = jnp.concatenate([key, apart, ones3[:, :32]], axis=1).astype(BF)
            va_ref[rows, :] = jnp.concatenate([value, ones3], axis=1).astype(BF)
            qat_ref[:, rows] = jnp.concatenate([q8.T, hot, jnp.zeros((32, TB), F32)], axis=0).astype(BF)
            kt_ref[:, rows] = key.T.astype(BF)
            ones_row = jnp.where(lax.broadcasted_iota(jnp.int32, (16, TB), 0) == 0, 1.0, 0.0)
            vat_ref[:, rows] = jnp.concatenate([value.T, ones_row], axis=0).astype(BF)

    project(lo, core, hi)
    project(1 - lo, core, 1 - hi)
    for copy in half_z + [own_pair[1], came_pair[1]] + pair_late:
        copy.wait_recv()
    for low, w in ((1 - lo, hi), (lo, 1 - hi)):
        piece = x_buf.at[:, low, core, w]
        rest.append(net.copy(piece, piece, other_core))
    start_all(rest)
    for copy in share:
        copy.wait_recv()
    project(1 - lo, core, hi)
    project(lo, core, 1 - hi)
    project(lo, 1 - core, hi)
    project(1 - lo, 1 - core, 1 - hi)
    for copy in rest:
        copy.wait_recv()
    store = pltpu.make_async_copy(x_buf, x_seq, local.at[0])
    store.start()
    project(1 - lo, 1 - core, hi)
    project(lo, 1 - core, 1 - hi)
    meta_out[...] = meta_all[...]
    smalls_out[...] = smalls_all[...]

    wait_all(keep)
    for copy in own_y + across_y:
        copy.wait_recv()
    later, inner_wrap = [], []
    for m in range(2):
        piece = wholes[m].at[:, unit_rows(m, 3), columns_part(m, lo, 2)]
        later.append(net.copy(piece, piece, pair))
        for d in (1, 3, 2):
            piece = wholes[m].at[:, unit_rows(m, 0), columns_part(m, z, 4)]
            later.append(net.copy(piece, piece, along("z", d)))
    piece = out_all.at[:, half_rows(core)]
    later.append(net.copy(piece, piece, other_core))
    for d in range(4):
        piece = down_all.at[(y + d) % 4 * 2 + hi, unit_rows(1, 1, 2)]
        inner_wrap.append(net.copy(piece, piece, wrap))
    start_all(later)

    position = lax.axis_index("seq") * 2 + hi

    def result(b, recv_at):
        there = head_tile(context, position)
        return remote(blocks.at[b], there, back_send.at[b], back_recv.at[recv_at], (y, b // 2, b % 2))

    own_result = pltpu.make_async_copy(blocks.at[position], head_tile(context, position), back_local)

    @pl.loop(0, 4)
    def _(step):
        at = (step + z + 1) % 4
        columns = pl.ds(aligned(at * 1024, 1024), 1024)
        queries = qat_ref[:, columns]
        peak = jnp.full((1, 1024), -jnp.inf, F32)
        total = jnp.zeros((80, 1024), F32)
        for j in range(8):
            keys = slice(j * 512, (j + 1) * 512)
            logits = dot(ka_ref[keys, :], queries)
            new_peak = jnp.maximum(peak, jnp.max(logits, axis=0, keepdims=True))
            expos = jnp.exp(logits - new_peak).astype(BF)
            total = total * jnp.exp(peak - new_peak) + dot(vat_ref[:, keys], expos)
            peak = new_peak
        sums = total[HD : HD + 1]
        found = total[:HD] / sums
        wide_ref[:, columns] = found
        lse_ref[:, columns] = peak + jnp.log(sums)
        low = found.astype(BF)
        for j in range(8):
            b = at * 8 + j
            blocks[b] = low[:, j * TB : (j + 1) * TB]

            @pl.when(b != position)
            def _():
                result(b, position).start()

            @pl.when(b == position)
            def _():
                own_result.start()

        @pl.when(step == 0)
        def _():
            for copy in inner_down:
                copy.wait_recv()
            start_all(inner_wrap)

    store.wait()
    for copy in [swap] + own_pair + own_z + came_pair + came_z + half_z + pair_late + share + rest:
        copy.wait_send()
    for copy in cross_first + cross_early + cross_late + own_small + across_small + own_y + across_y + inner_down:
        copy.wait_send()
    for copy in cross_late[1:]:
        copy.wait_recv()
    wait_all(inner_up + across_up + later + inner_wrap)

    @pl.loop(1, NB)
    def _(shift):
        b = (position + shift) % NB
        result(b, b).wait()

    own_result.wait()


def front(tokens, segments, flags, vectors, b_up, w_out, w_up, w_down, w_qkv):
    shape = jax.ShapeDtypeStruct
    in_vmem = pl.BlockSpec(memory_space=pltpu.VMEM)
    return pl.pallas_call(
        front_kernel,
        in_specs=[ANY] + [in_vmem] * 4 + [ANY] * 4,
        out_specs=[ANY] + [in_vmem] * 2 + [ANY] * 4 + [in_vmem] * 5 + [ANY] + [in_vmem] * 2,
        out_shape=[
            shape((4, 2, 2, 2, TB, D), BF),
            shape((NB, 8, TB), jnp.int32),
            shape((8, 16, 128), F32),
            shape((8, 128, D), BF),
            shape((8, 128, 2048), BF),
            shape((8, 256, D), BF),
            shape((8, 128, 3 * D), BF),
            shape((128, L), BF),
            shape((L, 128), BF),
            shape((L, 128), BF),
            shape((HD, L), BF),
            shape((L, HD), BF),
            shape((D, 2 * TB), BF),
            shape((HD, L), F32),
            shape((1, L), F32),
        ],
        scratch_shapes=[
            pltpu.VMEM((80, L), BF),
            pltpu.VMEM((NB, HD, TB), BF),
            pltpu.VMEM((4, 2, 2, 2, TB, D), BF),
            pltpu.VMEM((2, TB, D), BF),
            pltpu.VMEM((128, D), BF),
            pltpu.VMEM((2, 128, 2048), BF),
            pltpu.VMEM((256, D), BF),
            pltpu.VMEM((128, 3 * D), BF),
            pltpu.VMEM((2, 8, TB), jnp.int32),
            pltpu.VMEM((2, 128, 384), BF),
            pltpu.VMEM((16, 128), F32),
            pltpu.VMEM((NB, 8, TB), jnp.int32),
            pltpu.VMEM((8, 128, 384), BF),
            pltpu.VMEM((8, 16, 128), F32),
            pltpu.VMEM((D, 3 * HD), BF),
            pltpu.VMEM((8, 3 * HD), F32),
            pltpu.SemaphoreType.DMA((FRONT_COPIES,)),
            pltpu.SemaphoreType.DMA((FRONT_COPIES,)),
            pltpu.SemaphoreType.DMA((12,)),
            *swap_sems(),
            *swap_sems(),
        ],
        name="front",
        compiler_params=pltpu.CompilerParams(
            collective_id=1, has_side_effects=True, vmem_limit_bytes=VMEM_CAP
        ),
    )(tokens, segments, flags, vectors, b_up, w_out, w_up, w_down, w_qkv)


def qkv_along_y(qkv_all, net):
    _, y, _, core = place()
    copies = []
    for d in (1, 3, 2):
        for w in range(2):
            piece = qkv_all.at[y * 2 + w, half_rows(core)]
            copies.append(net.copy(piece, piece, along("y", d)))
    return copies


def turned(first, second):
    return dot(first, second, ((0,), (0,)))


def gelu_both(u):
    rate = 0.7978845608028654
    square = u * u
    curve = jnp.tanh(rate * (u + 0.044715 * (square * u)))
    half = 0.5 * (1.0 + curve)
    slope = half + 0.5 * u * (1.0 - curve * curve) * (rate * (1.0 + 0.134145 * square))
    return u * half, slope


def fold(values):
    return jnp.sum(values.reshape(values.shape[0] // 8, 8, values.shape[1]), axis=0)


ROWS = 256
CHUNK = 32
SMALLS = 16


def middle_kernel(
    context_in, meta, tokens, teacher, flags, smalls, out_all, up_all, down_all, a0,
    states, resid_out, do, g_ref, sums_out, count_out, qkv_all,
    context, context_s, w_out, w_up, w_down, h, act, slope, send_one, come_one, send_two, come_two,
    gb, gu, ga, ga_s, normed, hidden, rate, work, resid, gct, stage, count, counts, valid,
    send, recv, local, back_send, back_recv, back_local,
):
    x, y, z, core = place()
    mine = y * 2 + x // 2
    twin = sibling()
    loads = [
        pltpu.make_async_copy(context_in, context, local.at[6]),
        pltpu.make_async_copy(out_all, w_out, local.at[0]),
        pltpu.make_async_copy(up_all, w_up, local.at[1]),
    ]
    load_down = pltpu.make_async_copy(down_all, w_down, local.at[2])
    start_all(loads + [load_down])
    greet_signal(shard_greet())
    greet_wait(shard_greet())
    net = Transfers(send, recv)
    later = qkv_along_y(qkv_all, net)
    valid_here = jnp.sum(meta[:, 1, :].astype(F32), axis=0, keepdims=True)
    count[...] = jnp.broadcast_to(jnp.sum(valid_here, axis=1, keepdims=True), (8, 128))
    ahead = [net.copy(count, counts.at[mine], target) for target in shard_greet()]
    start_all(ahead + later)
    own_count = pltpu.make_async_copy(count, counts.at[mine], local.at[3])
    own_count.start()
    for s in range(2):
        column = jnp.broadcast_to(flags[s : s + 1, :].astype(F32), (128, 128)).T
        valid[128 * s : 128 * (s + 1), :] = column

    def vector(row):
        return jnp.concatenate([smalls[i, row : row + 1, :] for i in range(8)], axis=1)

    out_bias, gain_one, offset_one, down_bias, gain_two, offset_two = [vector(row) for row in range(2, 8)]
    zeros = jnp.zeros((8, D), F32)
    wait_all(loads)
    give_context = net.copy(context, context_s, twin)
    give_context.start()
    work[...] = turned(context[...], w_out[...].reshape(D, D))

    @pl.loop(0, ROWS // CHUNK)
    def _(i):
        rows = pl.ds(aligned(i * CHUNK, CHUNK), CHUNK)
        total = tokens[rows, :].astype(F32) + work[rows, :] + out_bias
        centre = total - jnp.mean(total, axis=1, keepdims=True)
        scale = lax.rsqrt(jnp.mean(centre * centre, axis=1, keepdims=True) + EPS)
        unit = centre * scale
        normed[rows, :] = unit
        rate[rows, :] = jnp.broadcast_to(scale, (CHUNK, 128))
        full = unit * gain_one + offset_one
        hidden[rows, :] = full
        h[0, rows, :] = full.astype(BF)

    give_hidden = net.copy(h.at[0], h.at[1], twin)
    give_hidden.start()
    for slot in range(2):
        if slot == 1:
            give_hidden.wait()
        for k in range(8):
            columns = slice(256 * k, 256 * (k + 1))
            bias = jnp.concatenate([smalls[k, pl.ds(8 + 2 * core + e, 1), :] for e in range(2)], axis=1)
            u = dot(h[slot], w_up[:, :, columns].reshape(D, 256)) + bias
            value, incline = gelu_both(u)
            act[slot, :, columns] = value.astype(BF)
            slope[slot, :, columns] = incline
    load_down.wait()
    send_one[...] = dot(act[1], w_down[...].reshape(2048, D))
    give_one = net.copy(send_one, come_one, twin)
    give_one.start()
    work[...] = dot(act[0], w_down[...].reshape(2048, D))
    give_one.wait()
    wait_all(ahead)
    own_count.wait()
    total_count = jnp.sum(counts[...], axis=0)
    count_out[...] = total_count
    factor = (128 * ROWS) / total_count[:1, :1]

    def loss_rows(i, carried):
        rows = pl.ds(aligned(i * CHUNK, CHUNK), CHUNK)
        total = hidden[rows, :] + (work[rows, :] + come_one[rows, :] + down_bias)
        centre = total - jnp.mean(total, axis=1, keepdims=True)
        scale = lax.rsqrt(jnp.mean(centre * centre, axis=1, keepdims=True) + EPS)
        unit = centre * scale
        final = unit * gain_two + offset_two
        states[rows, :] = final.astype(BF)
        differ = final - teacher[rows, :].astype(F32)
        held = valid[rows, :1] * differ
        grad = factor * held
        weighted = grad * gain_two
        back = weighted - jnp.mean(weighted, axis=1, keepdims=True)
        back = scale * (back - unit * jnp.mean(weighted * unit, axis=1, keepdims=True))
        resid[rows, :] = back
        low = back.astype(BF)
        gb[0, rows, :] = low
        return (
            carried[0] + fold(grad * unit),
            carried[1] + fold(grad),
            carried[2] + fold(low.astype(F32)),
            carried[3] + fold(held * differ),
        )

    gain_two_sum, offset_two_sum, down_sum, error = lax.fori_loop(
        0, ROWS // CHUNK, loss_rows, (zeros, zeros, zeros, zeros)
    )
    give_branch = net.copy(gb.at[0], gb.at[1], twin)
    give_branch.start()
    up_sums = []
    for slot in range(2):
        if slot == 1:
            give_branch.wait()
        for k in range(8):
            columns = slice(256 * k, 256 * (k + 1))
            pulled = dot(gb[slot], w_down[k], ((1,), (1,))) * slope[slot, :, columns]
            low = pulled.astype(BF)
            gu[slot, :, columns] = low
            up_sums.append(fold(low.astype(F32)))
    for i in range(8):
        send_two[:, 128 * i : 128 * (i + 1)] = dot(gu[1], w_up[i], ((1,), (1,)))
    give_two = net.copy(send_two, come_two, twin)
    give_two.start()
    for i in range(8):
        work[:, 128 * i : 128 * (i + 1)] = dot(gu[0], w_up[i], ((1,), (1,)))
    give_two.wait()

    def first_norm_rows(i, carried):
        rows = pl.ds(aligned(i * CHUNK, CHUNK), CHUNK)
        grad = resid[rows, :] + (work[rows, :] + come_two[rows, :])
        unit = normed[rows, :]
        weighted = grad * gain_one
        back = weighted - jnp.mean(weighted, axis=1, keepdims=True)
        back = rate[rows, :1] * (back - unit * jnp.mean(weighted * unit, axis=1, keepdims=True))
        resid_out[rows, :] = back
        low = back.astype(BF)
        ga[rows, :] = low
        return (carried[0] + fold(grad * unit), carried[1] + fold(grad), carried[2] + fold(low.astype(F32)))

    gain_one_sum, offset_one_sum, out_sum = lax.fori_loop(0, ROWS // CHUNK, first_norm_rows, (zeros, zeros, zeros))
    give_attended = net.copy(ga.at[:, pl.ds(aligned((1 - core) * 512, 512), 512)], ga_s, twin)
    give_attended.start()
    gct[...] = dot(w_out[...].reshape(D, D), ga[...], ((1,), (1,))).astype(BF)
    back_start, back_wait = swap_copies(
        lambda b: head_tile(gct, b), lambda b: do.at[b], (back_send, back_recv, back_local)
    )
    back_start()

    error = jnp.broadcast_to(jnp.sum(jnp.sum(error, axis=0, keepdims=True), axis=1, keepdims=True), (1, 128))
    lines = [out_sum, gain_one_sum, offset_one_sum, down_sum, gain_two_sum, offset_two_sum]
    lines = [jnp.sum(line, axis=0, keepdims=True) for line in lines]
    for i in range(8):
        columns = slice(128 * i, 128 * (i + 1))
        sums_out[i] = jnp.zeros((SMALLS, 128), F32)
        for row, line in enumerate(lines):
            sums_out[i, row : row + 1, :] = line[:, columns]
        both = jnp.sum(up_sums[i] + up_sums[8 + i], axis=0, keepdims=True)
        for e in range(2):
            sums_out[i, pl.ds(6 + 2 * core + e, 1), :] = both[:, 128 * e : 128 * (e + 1)]
        sums_out[i, 10:11, :] = error

    give_context.wait()
    give_attended.wait()

    def stored(i):
        return pltpu.make_async_copy(stage.at[i % 2], g_ref.at[i // 2, i % 2], local.at[4 + i % 2])

    for i in range(8):
        if i >= 2:
            stored(i - 2).wait()
        tall = slice(128 * i, 128 * (i + 1))
        wide = slice(256 * i, 256 * (i + 1))
        up = turned(h[0, :, tall], gu[0]) + turned(h[1, :, tall], gu[1])
        for k in range(4):
            stage[i % 2, 128 * k : 128 * (k + 1), :] = up[:, 512 * k : 512 * (k + 1)].astype(BF)
        down = turned(act[0, :, wide], gb[0]) + turned(act[1, :, wide], gb[1])
        for k in range(2):
            stage[i % 2, 512 + 256 * k : 768 + 256 * k, :] = down[:, 512 * k : 512 * (k + 1)].astype(BF)
        own_half = ga[:, pl.ds(aligned(core * 512, 512), 512)]
        out = dot(context[tall, :], own_half) + dot(context_s[tall, :], ga_s[...])
        stage[i % 2, 1024:, :] = out.astype(BF)
        stored(i).start()
    stored(6).wait()
    stored(7).wait()
    back_wait()
    wait_all(later)


def middle(context, meta, tokens, teacher, flags, smalls, out_all, up_all, down_all, qkv_all):
    shape = jax.ShapeDtypeStruct
    in_vmem = pl.BlockSpec(memory_space=pltpu.VMEM)
    dma = pltpu.SemaphoreType.DMA
    wide = pltpu.VMEM((ROWS, D), F32)
    return pl.pallas_call(
        middle_kernel,
        in_specs=[ANY] + [in_vmem] * 5 + [ANY] * 4,
        out_specs=[in_vmem, in_vmem, ANY, ANY, in_vmem, in_vmem, ANY],
        out_shape=[
            shape((ROWS, D), BF),
            shape((ROWS, D), F32),
            shape((NB, HD, TB), BF),
            shape((4, 2, 1152, 512), BF),
            shape((8, SMALLS, 128), F32),
            shape((8, 128), F32),
            shape(qkv_all.shape, BF),
        ],
        input_output_aliases={9: 6},
        scratch_shapes=[
            pltpu.VMEM((D, ROWS), BF),
            pltpu.VMEM((D, ROWS), BF),
            pltpu.VMEM((8, 128, D), BF),
            pltpu.VMEM((8, 128, 2048), BF),
            pltpu.VMEM((8, 256, D), BF),
            pltpu.VMEM((2, ROWS, D), BF),
            pltpu.VMEM((2, ROWS, 2048), BF),
            pltpu.VMEM((2, ROWS, 2048), F32),
            wide,
            wide,
            wide,
            wide,
            pltpu.VMEM((2, ROWS, D), BF),
            pltpu.VMEM((2, ROWS, 2048), BF),
            pltpu.VMEM((ROWS, D), BF),
            pltpu.VMEM((ROWS, 512), BF),
            wide,
            wide,
            pltpu.VMEM((ROWS, 128), F32),
            wide,
            wide,
            pltpu.VMEM((D, ROWS), BF),
            pltpu.VMEM((2, 1152, 512), BF),
            pltpu.VMEM((8, 128), F32),
            pltpu.VMEM((8, 8, 128), F32),
            pltpu.VMEM((ROWS, 128), F32),
            dma((32,)),
            dma((32,)),
            dma((10,)),
            *swap_sems(),
        ],
        name="middle",
        compiler_params=pltpu.CompilerParams(
            collective_id=3, has_side_effects=True, vmem_limit_bytes=VMEM_CAP
        ),
    )(context, meta, tokens, teacher, flags, smalls, out_all, up_all, down_all, qkv_all)


BACK_KEYS = 256
BACK_STEPS = L // BACK_KEYS
BACK_WIDTH = 1024


def back_prepare(qat, do, wide, lse, queries, grads, grad_rows):
    for j in range(L // BACK_WIDTH):
        columns = slice(j * BACK_WIDTH, (j + 1) * BACK_WIDTH)
        grad_t = jnp.concatenate([do[j * (BACK_WIDTH // TB) + i] for i in range(BACK_WIDTH // TB)], axis=1)
        wider = grad_t.astype(F32)
        delta = jnp.sum(wider * wide[:, columns], axis=0, keepdims=True)
        grads[:HD, columns] = grad_t
        grads[HD:, columns] = jnp.concatenate([three_pieces(-delta), jnp.zeros((61, BACK_WIDTH), BF)], axis=0)
        queries[:96, columns] = qat[:96, columns]
        queries[96:, columns] = jnp.concatenate(
            [three_pieces(-lse[:, columns]), jnp.zeros((29, BACK_WIDTH), BF)], axis=0
        )
        grad_rows[columns, :] = wider.T.astype(BF)


def back_kernel(
    qat, ka, va, kt, q8, do, wide, lse, smalls, x_seq, g_ref, a0,
    projected, heads_out, shard_out, smalls_out, qkv_all,
    x_buf, queries, grads, grad_rows, dq, d_ref, mine_ref, parts_ref, sum_ref, heads_buf, small_buf, small_sum, small_all,
    send, recv, local, dk_send, dk_recv, dk_local, dq_send, dq_recv, dq_local, spread_send, spread_recv, *reduce_refs,
):
    x, y, z, core = place()
    shard_at = y * 2 + x // 2
    seq = lax.axis_index("seq")
    mine = seq * 2 + x // 2
    net = (g_ref,) + reduce_refs

    def shard_device(d):
        other = (shard_at + d) % 8
        return other, (other // 2, seq, other % 2)

    load_x = pltpu.make_async_copy(x_seq, x_buf, local.at[0])
    load_x.start()
    shard_others = [shard_device(d)[1] for d in range(1, 8)]
    greet_signal(shard_others)
    back_prepare(qat, do, wide, lse, queries, grads, grad_rows)
    dq[...] = jnp.zeros_like(dq)
    greet_wait(shard_others)
    for part in range(3):
        reduce_start(part, net)
    far = Transfers(send, recv)
    small_out = [far.copy(smalls.at[shard_device(d)[0]], small_buf.at[shard_at], shard_device(d)[1]) for d in range(1, 8)]
    start_all(small_out)
    small_buf[shard_at] = smalls[shard_at]
    rows = half_rows(core)
    weights = far.copy(qkv_all.at[:, rows], qkv_all.at[:, rows], sibling())
    weights.start()

    def landing(first, count):
        return projected.at[pl.ds(first, count), pl.ds(aligned(seq * HD, HD), HD), pl.ds(aligned((x // 2) * TB, TB), TB)]

    def block_device(b):
        return (y, b // 2, b % 2)

    def dk_copy(b, recv_at):
        return remote(d_ref.at[b, pl.ds(1, 2)], landing(1, 2), dk_send.at[b], dk_recv.at[recv_at], block_device(b))

    def dq_copy(b, recv_at):
        return remote(d_ref.at[b, pl.ds(0, 1)], landing(0, 1), dq_send.at[b], dq_recv.at[recv_at], block_device(b))

    dk_own = pltpu.make_async_copy(d_ref.at[mine, pl.ds(1, 2)], landing(1, 2), dk_local)
    dq_own = pltpu.make_async_copy(d_ref.at[mine, pl.ds(0, 1)], landing(0, 1), dq_local)

    @pl.loop(0, BACK_STEPS)
    def _(step):
        at = (step + 4 * (z + 1)) % BACK_STEPS
        keys = pl.ds(aligned(at * BACK_KEYS, BACK_KEYS), BACK_KEYS)
        ka_part, va_part, kt_part = ka[keys, :], va[keys, :], kt[:, keys]
        dk = jnp.zeros((BACK_KEYS, HD), F32)
        dv = jnp.zeros((BACK_KEYS, HD), F32)
        for j in range(L // BACK_WIDTH):
            columns = slice(j * BACK_WIDTH, (j + 1) * BACK_WIDTH)
            probs = jnp.exp(dot(ka_part, queries[:, columns]))
            raw = (probs * dot(va_part, grads[:, columns])).astype(BF)
            dv = dv + dot(probs.astype(BF), grad_rows[columns, :])
            dk = dk + dot(raw, q8[columns, :])
            dq[:, columns] += dot(kt_part, raw)
        dk_t, dv_t = dk.T.astype(BF), dv.T.astype(BF)
        for i in range(BACK_KEYS // TB):
            b = at * (BACK_KEYS // TB) + i
            d_ref[b, 1] = dk_t[:, i * TB : (i + 1) * TB]
            d_ref[b, 2] = dv_t[:, i * TB : (i + 1) * TB]

            @pl.when(b != mine)
            def _():
                dk_copy(b, mine).start()

            @pl.when(b == mine)
            def _():
                dk_own.start()

        @pl.when(step == 4)
        def _():
            first_relay(net)

        @pl.when(step == 9)
        def _():
            reduce_step(0, 1, net)

        @pl.when(step == 11)
        def _():
            reduce_step(0, 0, net)

        @pl.when(step == 13)
        def _():
            reduce_step(0, 2, net)
            reduce_step(1, 1, net)

    for b in range(NB):
        d_ref[b, 0] = (dq[:, b * TB : (b + 1) * TB] * 0.125).astype(BF)

    load_x.wait()
    left = jnp.concatenate([d_ref[b].reshape(3 * HD, TB) for b in range(NB)], axis=1)
    sums = dot(jnp.ones((8, L), BF), left, ((1,), (1,)))
    gap = jnp.zeros((1, 128 - HD), F32)
    tail = jnp.concatenate(
        [
            jnp.concatenate([sums[:1, :HD], gap], axis=1),
            jnp.concatenate([sums[:1, 2 * HD :], gap], axis=1),
            jnp.zeros((14, 128), F32),
        ],
        axis=0,
    ).astype(BF)
    for i in range(4):
        total = dot(left, x_buf[:, :, 256 * i : 256 * (i + 1)].reshape(L, 256))
        for k in range(2):
            mine_ref[2 * i + k, : 3 * HD, :] = total[:, 128 * k : 128 * (k + 1)].astype(BF)
            mine_ref[2 * i + k, 3 * HD :, :] = tail
    part_out = [far.copy(mine_ref.at[shard_device(d)[0]], parts_ref.at[d], shard_device(d)[1]) for d in range(1, 8)]
    start_all(part_out)

    @pl.loop(1, NB)
    def _(shift):
        dq_copy((mine + shift) % NB, mine).start()

    dq_own.start()
    steps = [
        spread_steps(part, reduce_refs[6 + part].at[0], (local.at[pl.ds(1, 3)], spread_send, spread_recv), shard_out)
        for part in range(3)
    ]
    reduce_step(1, 0, net)
    reduce_step(1, 2, net)
    reduce_step(2, 1, net)
    steps[1][0]()
    wait_all(small_out)
    small_sum[...] = jnp.sum(small_buf[...], axis=0)
    wait_all(part_out)
    added = mine_ref[shard_at].astype(F32)
    for d in range(1, 8):
        added = added + parts_ref[d].astype(F32)
    sum_ref[...] = added.astype(BF)
    heads_buf[seq // 2, core] = sum_ref[...]
    small_all[seq // 2, core] = small_sum[...]
    head_out = []
    for d in range(1, 8):
        target = (y, (seq + 2 * d) % 16, x // 2)
        head_out.append(far.copy(sum_ref, heads_buf.at[seq // 2, core], target))
        head_out.append(far.copy(small_sum, small_all.at[seq // 2, core], target))
    start_all(head_out)
    for part in (2, 0):
        reduce_step(2, part, net)
        steps[part][0]()
    for part in (1, 2, 0):
        steps[part][1]()
    wait_all(head_out)
    across = [
        far.copy(heads_buf.at[:, core], heads_buf.at[:, core], sibling()),
        far.copy(small_all.at[:, core], small_all.at[:, core], sibling()),
    ]
    start_all(across)
    shared = []
    for part in (1, 2, 0):
        steps[part][2]()
        piece = shard_out.at[core, pl.ds(FIRST[part], 8 * PIECE[part])]
        shared.append(far.copy(piece, piece, sibling()))
        shared[-1].start()

    @pl.loop(1, NB)
    def _(shift):
        b = (mine + shift) % NB
        dk_copy(b, b).wait()
        dq_copy(b, b).wait()

    dk_own.wait()
    dq_own.wait()
    weights.wait()
    wait_all(across)
    for i in range(8):
        heads_out[2 * i] = heads_buf[i, 0]
        heads_out[2 * i + 1] = heads_buf[i, 1]
    smalls_out[...] = jnp.sum(small_all[...].reshape(16, 16, 128), axis=0)
    wait_all(shared)


def back(qat, ka, va, kt, q8, do, wide, lse, smalls, x_seq, g, qkv_all):
    shape = jax.ShapeDtypeStruct
    in_vmem = pl.BlockSpec(memory_space=pltpu.VMEM)
    dma = pltpu.SemaphoreType.DMA
    return pl.pallas_call(
        back_kernel,
        in_specs=[in_vmem] * 9 + [ANY] * 3,
        out_specs=[ANY, in_vmem, ANY, in_vmem, ANY],
        out_shape=[
            shape((3, D, 2 * TB), BF),
            shape((H, 208, 128), BF),
            shape((2, 1152, 512), BF),
            shape((16, 128), F32),
            shape(qkv_all.shape, BF),
        ],
        input_output_aliases={11: 4},
        scratch_shapes=[
            pltpu.VMEM((NB, TB, D), BF),
            pltpu.VMEM((128, L), BF),
            pltpu.VMEM((128, L), BF),
            pltpu.VMEM((L, HD), BF),
            pltpu.VMEM((HD, L), F32),
            pltpu.VMEM((NB, 3, HD, TB), BF),
            pltpu.VMEM((8, 208, 128), BF),
            pltpu.VMEM((8, 208, 128), BF),
            pltpu.VMEM((208, 128), BF),
            pltpu.VMEM((8, 2, 208, 128), BF),
            pltpu.VMEM((8, 16, 128), F32),
            pltpu.VMEM((16, 128), F32),
            pltpu.VMEM((8, 2, 16, 128), F32),
            dma((40,)),
            dma((40,)),
            dma((4,)),
            *swap_sems(),
            *swap_sems(),
            dma((3, 8)),
            dma((3, 8)),
            *reduce_scratch(),
        ],
        name="attend_back",
        compiler_params=pltpu.CompilerParams(
            collective_id=4, has_side_effects=True, vmem_limit_bytes=VMEM_CAP
        ),
    )(qat, ka, va, kt, q8, do, wide, lse, smalls, x_seq, g, qkv_all)


def finish_kernel(
    projected, qkv_ref, resid_ref, heads_ref, shard_ref, smalls_ref, count_ref, states_ref,
    tokens_ref, grad_qkv, grad_out, grad_up, grad_down, states_out, loss_ref,
    q_bias, v_bias, o_bias, gain_one, bias_one, d_bias, gain_two, bias_two, u_bias,
    sides,
):
    step = pl.program_id(0)

    @pl.when(step == 0)
    def _():
        sides[...] = projected[...].astype(F32).T.astype(BF)
        x, y, _, _ = place()
        shard_at = y * 2 + x // 2
        for row, out in enumerate((q_bias, v_bias)):
            both = [heads_ref[shard_at * 2 + k, 3 * HD + row, :HD].astype(F32) for k in range(2)]
            out[...] = jnp.concatenate(both)
        for row, out in enumerate((o_bias, gain_one, bias_one, d_bias, gain_two, bias_two)):
            out[...] = smalls_ref[row, :]
        u_bias[...] = jnp.concatenate([smalls_ref[6 + k, :] for k in range(4)])
        loss_ref[...] = smalls_ref[10:11, :1] / (D * count_ref[:1, :1])
        for p in range(3):
            for pair in range(8):
                both = [heads_ref[2 * pair + k, p * HD : (p + 1) * HD, :].astype(F32) for k in range(2)]
                at = p * D + pair * 128
                grad_qkv[:, at : at + 128] = jnp.concatenate(both, axis=0).T

    states_out[...] = states_ref[...]
    tokens_ref[...] = resid_ref[...] + dot(sides[...], qkv_ref[...], ((1,), (1,)))
    for c in range(2):
        columns = slice(512 * c, 512 * (c + 1))
        for j in range(2):
            piece = shard_ref[c, pl.ds(aligned(step * 128, 128), 128), 256 * j : 256 * (j + 1)]
            grad_up[:, 512 * j + 256 * c : 512 * j + 256 * (c + 1)] = piece.astype(F32)
        rows = pl.ds(aligned(512 + 256 * c + (step % 2) * 128, 128), 128)
        grad_down[:, columns] = shard_ref[step // 2, rows, :].astype(F32)
        grad_out[:, columns] = shard_ref[c, pl.ds(aligned(1024 + step * 32, 32), 32), :].astype(F32)


def finish(projected, qkv, resid, heads, shard, smalls, count, states):
    shape = jax.ShapeDtypeStruct

    def whole(*dims):
        return pl.BlockSpec(dims, lambda i: (0,) * len(dims))

    part = pl.BlockSpec((2 * TB, 256), lambda i: (0, i))
    return pl.pallas_call(
        finish_kernel,
        grid=(4,),
        in_specs=[
            whole(3 * D, 2 * TB),
            pl.BlockSpec((256, 3 * D), lambda i: (i, 0)),
            part,
            whole(H, 208, 128),
            whole(2, 1152, 512),
            whole(16, 128),
            whole(8, 128),
            part,
        ],
        out_specs=[
            part,
            whole(128, 3 * D),
            pl.BlockSpec((32, D), lambda i: (i, 0)),
            pl.BlockSpec((128, 1024), lambda i: (0, i)),
            pl.BlockSpec((128, D), lambda i: (i, 0)),
            part,
            whole(1, 1),
        ]
        + [whole(128)] * 8
        + [whole(512)],
        out_shape=[
            shape((2 * TB, D), F32),
            shape((128, 3 * D), F32),
            shape((128, D), F32),
            shape((128, FF), F32),
            shape((512, D), F32),
            shape((2 * TB, D), BF),
            shape((1, 1), F32),
        ]
        + [shape((128,), F32)] * 8
        + [shape((512,), F32)],
        scratch_shapes=[pltpu.VMEM((2 * TB, 3 * D), BF)],
        name="finish",
        compiler_params=pltpu.CompilerParams(vmem_limit_bytes=VMEM_CAP),
    )(projected, qkv, resid, heads, shard, smalls, count, states)


def on_device(
    tokens,
    segments,
    valid_flags,
    teacher,
    w_qkv,
    b_query,
    b_value,
    w_out,
    b_out,
    ln1_gain,
    ln1_bias,
    w_up,
    b_up,
    w_down,
    b_down,
    ln2_gain,
    ln2_bias,
):
    seq_local, row_local, _ = tokens.shape
    token_rows = seq_local * row_local

    vectors = jnp.stack([b_query, b_value, b_out, ln1_gain, ln1_bias, b_down, ln2_gain, ln2_bias]).astype(F32)
    (
        x_seq, meta_all, smalls_all, out_all, up_all, down_all, qkv_all, qat, ka, va, kt, q8, context, wide, lse
    ) = front(
        tokens, segments, valid_flags, vectors, b_up.reshape(4, 128).astype(F32), w_out, w_up, w_down, w_qkv
    )
    x_seq = x_seq.reshape(NB, TB, D)
    states, grad_resid_one, do, g, small_sums, count, qkv_all = middle(
        context,
        meta_all,
        tokens.reshape(token_rows, D),
        teacher.reshape(token_rows, D),
        valid_flags,
        smalls_all,
        out_all,
        up_all,
        down_all,
        qkv_all,
    )
    projected, heads_out, shard_out, small_out, qkv_all = back(
        qat, ka, va, kt, q8, do, wide, lse, small_sums, x_seq, g, qkv_all
    )
    (
        grad_tokens, grad_qkv, grad_out, grad_up, grad_down, states, mean_loss,
        q_bias, v_bias, o_bias, gain_one, bias_one, d_bias, gain_two, bias_two, u_bias,
    ) = finish(
        projected.reshape(3 * D, token_rows), qkv_all.reshape(D, 3 * D), grad_resid_one, heads_out, shard_out, small_out,
        count, states,
    )
    return (
        states.reshape(seq_local, row_local, D),
        mean_loss.reshape(()),
        grad_tokens.reshape(seq_local, row_local, D),
        grad_qkv,
        q_bias,
        v_bias,
        grad_out,
        o_bias,
        gain_one,
        bias_one,
        grad_up,
        u_bias,
        grad_down,
        d_bias,
        gain_two,
        bias_two,
    )


def solution(mesh):
    rows = P("dp", ("seq", "wshard"), None)
    flags = P("dp", ("seq", "wshard"))
    matrix = P(("dp", "wshard"), None)
    vector = P(("dp", "wshard"))
    return jax.shard_map(
        on_device,
        mesh=mesh,
        in_specs=(
            rows,
            flags,
            flags,
            rows,
            matrix,
            vector,
            vector,
            matrix,
            vector,
            vector,
            vector,
            matrix,
            vector,
            matrix,
            vector,
            vector,
            vector,
        ),
        out_specs=(
            rows,
            P(),
            rows,
            matrix,
            vector,
            vector,
            matrix,
            vector,
            vector,
            vector,
            matrix,
            vector,
            matrix,
            vector,
            vector,
            vector,
        ),
        check_vma=False,
    )
```

```python
import functools

import jax
import jax.numpy as jnp
from jax import lax
from jax.experimental import pallas as pl
from jax.experimental.pallas import tpu as pltpu
from jax.sharding import PartitionSpec as P

D = 1024
H = 16
HD = 64
FF = 4096
L = 4096
EPS = 1e-06
F32 = jnp.float32
BF = jnp.bfloat16
MASKED = 1000000000.0
VMEM_CAP = 60 * 1024 * 1024
MESH = pl.DeviceIdType.MESH
ANY = pl.BlockSpec(memory_space=pl.ANY)
TB = 128
NB = L // TB


def dot(first, second, dims=((1,), (0,))):
    return lax.dot_general(first, second, (dims, ((), ())), preferred_element_type=F32)


def three_pieces(row):
    high = row.astype(BF)
    rest = row - high.astype(F32)
    middle = rest.astype(BF)
    lowest = (rest - middle.astype(F32)).astype(BF)
    return jnp.concatenate([high, middle, lowest], axis=0)


def place():
    at = lax.axis_index("seq")
    return (lax.axis_index("wshard") * 2 + (at // 2) % 2, lax.axis_index("dp"), at // 4, at % 2)


def device_at(x, y, z, core):
    return (y, (z * 2 + x % 2) * 2 + core, x // 2)


def along(axis, shift):
    x, y, z, core = place()
    if axis == "x":
        return device_at((x + shift) % 4, y, z, core)
    if axis == "y":
        return device_at(x, (y + shift) % 4, z, core)
    return device_at(x, y, (z + shift) % 4, core)


def sibling():
    x, y, z, core = place()
    return device_at(x, y, z, 1 - core)


def greet(partners):
    barrier = pltpu.get_barrier_semaphore()
    for partner in partners:
        pl.semaphore_signal(barrier, inc=1, device_id=partner, device_id_type=MESH)
    pl.semaphore_wait(barrier, len(partners))


def remote(src, dst, send_sem, recv_sem, target):
    return pltpu.make_async_remote_copy(
        src_ref=src, dst_ref=dst, send_sem=send_sem, recv_sem=recv_sem, device_id=target, device_id_type=MESH
    )


ORDERS = ("yzx", "zxy", "xyz")
PIECE = (64, 32, 48)
FIRST = (0, 512, 768)


def ring_partners():
    return [along(axis, shift) for axis in "xyz" for shift in (1, 2, 3)] + [sibling()]


def reduce_scratch():
    a, b, c = PIECE
    return [
        pltpu.VMEM((4, 2, 8 * a, 512), BF),
        pltpu.VMEM((4, 4, 2, 2 * b, 512), BF),
        pltpu.VMEM((4, 4, 4 * c, 512), BF),
        pltpu.VMEM((4, 2, 2 * a, 512), BF),
        pltpu.VMEM((4, 4, b, 512), BF),
        pltpu.VMEM((4, 4 * c, 512), BF),
        pltpu.VMEM((4, a, 512), BF),
        pltpu.VMEM((4, b, 512), BF),
        pltpu.VMEM((4, c, 512), BF),
        pltpu.SemaphoreType.DMA((3, 3, 3)),
        pltpu.SemaphoreType.DMA((3, 3, 3)),
        pltpu.SemaphoreType.DMA((3,)),
        pltpu.VMEM((2, 8 * a, 512), BF),
        pltpu.SemaphoreType.DMA((6,)),
        pltpu.SemaphoreType.DMA((6,)),
        pltpu.SemaphoreType.DMA((2,)),
    ]


def aligned(value, unit):
    return pl.multiple_of(value, unit)


def reduce_piece(stage, part, refs, at):
    g_ref = refs[0]
    half, low, n = at // 2, at % 2, PIECE[part]
    if stage == 0:
        first = FIRST[part]
        if part == 0:
            return g_ref.at[at, :, pl.ds(first, 8 * n), :]
        if part == 1:
            return g_ref.at[:, :, pl.ds(aligned(first + at * 2 * n, 16), 2 * n), :]
        return g_ref.at[:, half, pl.ds(aligned(first + low * 4 * n, 16), 4 * n), :]
    held = refs[1 + 3 * (stage - 1) + part]
    if stage == 1:
        if part == 0:
            return held.at[0, :, pl.ds(aligned(at * 2 * n, 16), 2 * n), :]
        if part == 1:
            return held.at[0, :, half, pl.ds(aligned(low * n, 16), n), :]
        return held.at[0, at]
    if part == 0:
        return held.at[0, half, pl.ds(aligned(low * n, 16), n), :]
    if part == 1:
        return held.at[0, at]
    return held.at[0, pl.ds(aligned(at * n, 16), n), :]


def ring_at(axis):
    x, y, z, _ = place()
    return {"x": x, "y": y, "z": z}[axis]


def reduce_copies(stage, part, refs):
    send, recv = refs[10], refs[11]
    axis = ORDERS[part][stage]
    return [
        remote(
            reduce_piece(stage, part, refs, (ring_at(axis) + shift) % 4),
            refs[1 + 3 * stage + part].at[shift],
            send.at[stage, part, shift - 1],
            recv.at[stage, part, shift - 1],
            along(axis, shift),
        )
        for shift in (1, 3, 2)
    ]


def reduce_own(part, refs):
    return pltpu.make_async_copy(
        reduce_piece(0, part, refs, ring_at(ORDERS[part][0])), refs[1 + part].at[0], refs[12].at[part]
    )


def reduce_start(part, refs):
    start_all(first_copies(refs)[:4] + first_loads(refs) if part == 0 else reduce_copies(0, part, refs))
    reduce_own(part, refs).start()


def first_copies(refs):
    g_ref, a1, relay, send, recv = refs[0], refs[1], refs[13], refs[14], refs[15]
    _, y, _, _ = place()
    rows = pl.ds(0, 8 * PIECE[0])
    up, down, far = (y + 1) % 4, (y + 3) % 4, (y + 2) % 4
    moves = [
        (g_ref.at[far, 0, rows], a1.at[2, 0], 1),
        (g_ref.at[far, 1, rows], a1.at[2, 1], 3),
        (g_ref.at[up, 1, rows], a1.at[1, 1], 1),
        (g_ref.at[down, 0, rows], a1.at[3, 0], 3),
        (relay.at[0], a1.at[1, 0], 1),
        (relay.at[1], a1.at[3, 1], 3),
    ]
    return [remote(src, dst, send.at[k], recv.at[k], along("y", d)) for k, (src, dst, d) in enumerate(moves)]


def first_loads(refs):
    g_ref, relay, local = refs[0], refs[13], refs[16]
    _, y, _, _ = place()
    rows = pl.ds(0, 8 * PIECE[0])
    return [
        pltpu.make_async_copy(g_ref.at[(y + 1) % 4, 0, rows], relay.at[0], local.at[0]),
        pltpu.make_async_copy(g_ref.at[(y + 3) % 4, 1, rows], relay.at[1], local.at[1]),
    ]


def first_relay(refs):
    a1, relay = refs[1], refs[13]
    copies = first_copies(refs)
    wait_all(first_loads(refs))
    for copy in copies[:2]:
        copy.wait_recv()

    @pl.loop(0, 16)
    def _(i):
        rows = pl.ds(aligned((i % 8) * PIECE[0], 16), PIECE[0])
        half = i // 8
        relay[half, rows, :] = (relay[half, rows, :].astype(F32) + a1[2, half, rows, :].astype(F32)).astype(BF)

    start_all(copies[4:])


def first_end(refs):
    copies = first_copies(refs)
    for copy in copies[:2]:
        copy.wait_send()
    wait_all(copies[2:])


def add_four(values):
    total = values[0].astype(F32) + values[1].astype(F32)
    return (total + values[2].astype(F32) + values[3].astype(F32)).astype(BF)


def reduce_step(stage, part, refs):
    a1, b1, c1, a2, b2, c2, a3, b3, c3 = refs[1:10]
    if stage == 0 and part == 0:
        first_end(refs)
    else:
        wait_all(reduce_copies(stage, part, refs))
    x, y, z, _ = place()
    n = PIECE[part]
    rest = (1, 2, 3)
    if stage == 0:
        reduce_own(part, refs).wait()

        @pl.loop(0, 16)
        def _(i):
            if part == 0:
                rows = pl.ds(aligned((i % 8) * n, 16), n)
                total = a1[0, i // 8, rows, :].astype(F32) + a1[1, i // 8, rows, :].astype(F32)
                a1[0, i // 8, rows, :] = (total + a1[3, i // 8, rows, :].astype(F32)).astype(BF)
            elif part == 1:
                rows = pl.ds(aligned((i % 2) * n, 16), n)
                b1[0, i // 4, (i // 2) % 2, rows, :] = add_four([b1[s, i // 4, (i // 2) % 2, rows, :] for s in range(4)])
            else:
                rows = pl.ds(aligned((i % 4) * n, 16), n)
                c1[0, i // 4, rows, :] = add_four([c1[s, i // 4, rows, :] for s in range(4)])

    elif stage == 1:

        @pl.loop(0, 4)
        def _(i):
            if part == 0:
                rows = pl.ds(aligned((i % 2) * n, 16), n)
                own = a1[0, i // 2, pl.ds(aligned(z * 2 * n + (i % 2) * n, 16), n), :]
                a2[0, i // 2, rows, :] = add_four([own] + [a2[s, i // 2, rows, :] for s in rest])
            elif part == 1:
                own = b1[0, i, x // 2, pl.ds(aligned((x % 2) * n, 16), n), :]
                b2[0, i] = add_four([own] + [b2[s, i] for s in rest])
            else:
                rows = pl.ds(aligned(i * n, 16), n)
                own = c1[0, y, rows, :]
                c2[0, rows, :] = add_four([own] + [c2[s, rows, :] for s in rest])

    elif part == 0:
        own = a2[0, x // 2, pl.ds(aligned((x % 2) * n, 16), n), :]
        a3[0] = add_four([own] + [a3[s] for s in rest])
    elif part == 1:
        b3[0] = add_four([b2[0, y]] + [b3[s] for s in rest])
    else:
        own = c2[0, pl.ds(aligned(z * n, 16), n), :]
        c3[0] = add_four([own] + [c3[s] for s in rest])
    if stage < 2:
        start_all(reduce_copies(stage + 1, part, refs))


def shard_rows(o_ref, part, x_low, z, core):
    sub = x_low * 4 + z if part == 2 else z * 2 + x_low
    return o_ref.at[core, pl.ds(aligned(FIRST[part] + sub * PIECE[part], 16), PIECE[part]), :]


def spread_steps(part, mine, sems, o_ref):
    local, send, recv = sems
    x, y, z, core = place()
    low = x % 2
    pair = device_at(x // 2 * 2 + 1 - low, y, z, core)
    spot = shard_rows(o_ref, part, low, z, core)
    own = pltpu.make_async_copy(mine, spot, local.at[part])
    first = remote(mine, spot, send.at[part, 0], recv.at[part, 0], pair)
    second = [remote(mine, spot, send.at[part, d], recv.at[part, d], along("z", d)) for d in (1, 3, 2)]
    spot = shard_rows(o_ref, part, 1 - low, z, core)
    third = [remote(spot, spot, send.at[part, 3 + d], recv.at[part, 3 + d], along("z", d)) for d in (1, 3, 2)]

    def begin():
        start_all([own, first] + second)

    def middle():
        first.wait()
        start_all(third)

    def end():
        wait_all([own] + second + third)

    return begin, middle, end


def swap_partner(shift):
    mine = lax.axis_index("seq") * 2 + lax.axis_index("wshard")
    other = (mine + shift) % NB
    return other, (lax.axis_index("dp"), other // 2, other % 2)


def swap_greet():
    barrier = pltpu.get_barrier_semaphore()

    @pl.loop(1, NB)
    def _(shift):
        pl.semaphore_signal(barrier, inc=1, device_id=swap_partner(shift)[1], device_id_type=MESH)

    pl.semaphore_wait(barrier, NB - 1)


def swap_copies(piece_for, landing_from, sems):
    mine = lax.axis_index("seq") * 2 + lax.axis_index("wshard")
    send, recv, local = sems

    def copy(shift):
        other, device = swap_partner(shift)
        return remote(piece_for(other), landing_from(mine), send.at[shift], recv.at[shift], device)

    own = pltpu.make_async_copy(piece_for(mine), landing_from(mine), local)

    def start():
        @pl.loop(1, NB)
        def _(shift):
            copy(shift).start()

        own.start()

    def wait():
        @pl.loop(1, NB)
        def _(shift):
            copy(shift).wait()

        own.wait()

    return start, wait


def swap_sems():
    return [pltpu.SemaphoreType.DMA((NB,)), pltpu.SemaphoreType.DMA((NB,)), pltpu.SemaphoreType.DMA]


def block_of(ref, b):
    return ref.at[b]


def head_tile(ref, b):
    return ref.at[pl.ds(aligned((b // 2) * HD, HD), HD), pl.ds(aligned((b % 2) * TB, TB), TB)]


def head_tile3(ref, b):
    return ref.at[:, pl.ds(aligned((b // 2) * HD, HD), HD), pl.ds(aligned((b % 2) * TB, TB), TB)]


HALVES = ((128, 2048), (256, 1024))


class Transfers:
    def __init__(self, send, recv):
        self.send, self.recv, self.used = send, recv, 0

    def copy(self, src, dst, target):
        made = remote(src, dst, self.send.at[self.used], self.recv.at[self.used], target)
        self.used += 1
        return made


def start_all(copies):
    for copy in copies:
        copy.start()


def wait_all(copies):
    for copy in copies:
        copy.wait()


def unit_rows(matrix, unit, count=1):
    rows = HALVES[matrix][0] // 4
    return pl.ds(unit * rows, count * rows)


def columns_part(matrix, at, parts):
    width = HALVES[matrix][1] // parts
    return pl.ds(aligned(at * width, 128), width)


def half_rows(core, rows=64):
    return pl.ds(aligned(core * rows, rows), rows)


def shard_greet():
    x, y, z, core = place()
    return [device_at(x, (y + d) % 4, z, core) for d in (1, 2, 3)] + [
        device_at(3 - x, (y + d) % 4, z, core) for d in range(4)
    ]


def greet_signal(others):
    barrier = pltpu.get_barrier_semaphore()

    @pl.loop(1, NB)
    def _(shift):
        pl.semaphore_signal(barrier, inc=1, device_id=swap_partner(shift)[1], device_id_type=MESH)

    for other in others:
        pl.semaphore_signal(barrier, inc=1, device_id=other, device_id_type=MESH)


def greet_wait(others):
    pl.semaphore_wait(pltpu.get_barrier_semaphore(), NB - 1 + len(others))


FRONT_COPIES = 144


def front_kernel(
    tokens, segments, flags, vectors, b_up, w_out, w_up, w_down, w_qkv,
    x_seq, meta_out, smalls_out, out_all, up_all, down_all, qkv_all, qat_ref, ka_ref, va_ref, kt_ref, q_ref,
    context, wide_ref, lse_ref,
    vat_ref, blocks, give, got, x_buf, tok_buf, out_buf, up_buf, down_buf, qkv_buf, meta, heads, smalls, meta_all, heads_all, smalls_all, w_ref, b_ref,
    send, recv, local, meta_send, meta_recv, meta_local, back_send, back_recv, back_local,
):
    x, y, z, core = place()
    hi, lo = x // 2, x % 2
    mine, across = y * 2 + hi, y * 2 + 1 - hi
    wrap, pair, other_core = device_at(3 - x, y, z, core), device_at(hi * 2 + 1 - lo, y, z, core), sibling()
    shards, wholes = (up_buf.at[core], down_buf), (up_all, down_all)
    rows_out = half_rows(core)
    greet_signal(shard_greet())
    load_tokens = pltpu.make_async_copy(tokens, tok_buf, local.at[0])
    load_qkv = pltpu.make_async_copy(w_qkv, qkv_buf, local.at[11])
    loads = [
        pltpu.make_async_copy(w_out, out_buf, local.at[9]),
        pltpu.make_async_copy(w_down.at[half_rows(core, 256)], down_buf, local.at[10]),
    ]
    for j in range(8):
        piece = w_up.at[:, pl.ds(aligned(j * 512 + core * 256, 256), 256)]
        loads.append(pltpu.make_async_copy(piece, up_buf.at[core, :, pl.ds(j * 256, 256)], local.at[1 + j]))
    start_all([load_tokens, load_qkv] + loads)
    meta[...] = jnp.zeros_like(meta)
    for s in range(2):
        meta[s, 0:1, :] = segments[s : s + 1, :]
        meta[s, 1:2, :] = flags[s : s + 1, :]
    smalls[...] = jnp.zeros_like(smalls)
    smalls[0:8, :] = vectors[...]
    smalls[8:12, :] = b_up[...]
    greet_wait(shard_greet())
    load_tokens.wait()
    net = Transfers(send, recv)
    first, second = pl.ds(0, 64), pl.ds(64, 64)

    def block(at, low, w, rows=slice(None)):
        return x_buf.at[at, low, core, w, rows]

    own = tok_buf.at[hi]
    swap = net.copy(tok_buf.at[1 - hi], block(z, lo, hi), wrap)
    own_z = [net.copy(own, block(z, lo, hi), along("z", d)) for d in (1, 3, 2)]
    own_pair = [net.copy(own.at[rows], block(z, lo, hi, rows), pair) for rows in (first, second)]
    start_all([swap, own_pair[0]] + own_z)
    x_buf[z, lo, core, hi] = tok_buf[hi]
    load_qkv.wait()
    for p in range(3):
        for k, pair_at in ((0, z * 2 + lo), (1, z * 2 + 1 - lo)):
            heads[k, :, 128 * p : 128 * (p + 1)] = qkv_buf[:, pl.ds(aligned(p * D + pair_at * 128, 128), 128)]
    cross_first = [
        net.copy(heads.at[1], heads_all.at[mine], wrap),
        net.copy(smalls, smalls_all.at[mine], wrap),
    ]
    start_all(cross_first)
    wait_all(loads)
    cross_early, cross_late = [net.copy(out_buf.at[rows_out], out_all.at[mine, rows_out], wrap)], []
    for m in range(2):
        for unit, columns in ((0, columns_part(m, z, 4)), (3, columns_part(m, 1 - lo, 2))):
            rows = unit_rows(m, unit)
            cross_early.append(net.copy(shards[m].at[rows, columns], wholes[m].at[mine, rows, columns], wrap))

    def small_y(shard, heads_source, smalls_source):
        copies = []
        for d in (1, 3, 2):
            copies.append(net.copy(heads_source, heads_all.at[shard], along("y", d)))
            copies.append(net.copy(smalls_source, smalls_all.at[shard], along("y", d)))
        return copies

    own_small = small_y(mine, heads.at[0], smalls)
    start_all(own_small + cross_early)
    heads_all[mine] = heads[0]
    smalls_all[mine] = smalls[...]
    meta_start, meta_wait = swap_copies(
        lambda b: meta.at[b % 2], lambda b: meta_all.at[b], (meta_send, meta_recv, meta_local)
    )
    meta_start()
    keep = [
        pltpu.make_async_copy(out_buf.at[rows_out], out_all.at[mine, rows_out], local.at[9]),
        pltpu.make_async_copy(qkv_buf, qkv_all.at[mine], local.at[11]),
    ]
    for m in range(2):
        parts = [
            (unit_rows(m, 0), columns_part(m, z, 4)),
            (unit_rows(m, 3), columns_part(m, lo, 2)),
            (unit_rows(m, 1, 2), slice(None)),
        ]
        for k, (rows, columns) in enumerate(parts):
            piece = wholes[m].at[mine, rows, columns]
            keep.append(pltpu.make_async_copy(shards[m].at[rows, columns], piece, local.at[1 + 3 * m + k]))
    start_all(keep)

    def outer_y(shard, source, out_source):
        copies = []
        for d in (1, 3, 2):
            there = along("y", d)
            copies.append(net.copy(out_source.at[rows_out], out_all.at[shard, rows_out], there))
            for m in range(2):
                for unit, columns in ((0, columns_part(m, z, 4)), (3, columns_part(m, lo, 2))):
                    rows = unit_rows(m, unit)
                    copies.append(net.copy(source(m).at[rows, columns], wholes[m].at[shard, rows, columns], there))
        return copies

    def inner_y(m, shard, source):
        rows = unit_rows(m, 1, 2)
        return [net.copy(source.at[rows], wholes[m].at[shard, rows], along("y", d)) for d in (1, 3)]

    def relay_y(m, w):
        copies = []
        for unit, d in ((1, 1), (2, 3)):
            piece = wholes[m].at[(y + 4 - d) % 4 * 2 + w, unit_rows(m, unit)]
            copies.append(net.copy(piece, piece, along("y", d)))
        return copies

    swap.wait_recv()
    came = block(z, 1 - lo, 1 - hi)
    came_pair = [
        net.copy(block(z, 1 - lo, 1 - hi, rows), block(z, 1 - lo, 1 - hi, rows), pair) for rows in (first, second)
    ]
    came_z = [net.copy(came, came, along("z", d)) for d in (1, 3, 2)]
    start_all([came_pair[0]] + came_z + [own_pair[1], came_pair[1]])
    for copy in cross_first:
        copy.wait_recv()
    across_small = small_y(across, heads_all.at[across], smalls_all.at[across])
    own_y = outer_y(mine, lambda m: shards[m], out_buf)
    start_all(across_small + own_y)
    pair_late = []

    def forward(got, d, low, w):
        got.wait_recv()
        piece = block((z + 4 - d) % 4, low, w, second)
        pair_late.append(net.copy(piece, piece, pair))
        pair_late[-1].start()

    for i, d in enumerate((1, 3, 2)):
        forward(own_z[i], d, lo, hi)
    half_z = []

    def halves(got, low, w):
        got.wait_recv()
        piece = block(z, low, w, first)
        copies = [net.copy(piece, piece, along("z", d)) for d in (1, 3, 2)]
        start_all(copies)
        half_z.extend(copies)

    halves(own_pair[0], 1 - lo, hi)
    for copy in cross_early:
        copy.wait_recv()
    across_y = outer_y(across, lambda m: wholes[m].at[across], out_all.at[across])
    inner_down = inner_y(1, mine, down_buf)
    inner_up = inner_y(0, mine, up_buf.at[core])
    rows = unit_rows(0, 1, 2)
    cross_late.append(net.copy(up_buf.at[core, rows], up_all.at[mine, rows], wrap))
    rows = half_rows(core)
    cross_late.append(net.copy(qkv_buf.at[rows], qkv_all.at[mine, rows], wrap))
    start_all(across_y + cross_late + inner_down + inner_up)
    for i, d in enumerate((1, 3, 2)):
        forward(came_z[i], d, 1 - lo, 1 - hi)
    halves(came_pair[0], lo, 1 - hi)
    cross_late[0].wait_recv()
    across_up = inner_y(0, across, up_all.at[across])
    start_all(across_up)

    for copy in own_small + across_small:
        copy.wait_recv()
    meta_wait()
    at_first = core == 0
    both = heads_all[...].reshape(D, 384)
    biases = smalls_all[lax.axis_index("seq") // 2]
    gap = jnp.zeros((1, HD), F32)
    wide_gap = jnp.zeros((D, HD), BF)
    columns, lines = [], []
    for own_head in (True, False):
        chosen = at_first if own_head else jnp.logical_not(at_first)
        for p in range(3):
            columns.append(jnp.where(chosen, both[:, 128 * p : 128 * p + HD], both[:, 128 * p + HD : 128 * (p + 1)]))
        bias = [jnp.where(chosen, biases[k : k + 1, :HD], biases[k : k + 1, HD:]) for k in range(2)]
        columns.append(wide_gap)
        lines += [bias[0], gap, bias[1], gap]
    w_ref[...] = jnp.concatenate(columns, axis=1)
    b_ref[...] = jnp.broadcast_to(jnp.concatenate(lines, axis=1), (8, 512))

    def forms(b, low):
        rows = pl.ds(aligned(b * TB, TB), TB)
        side = low.astype(F32)
        q8, key, value = side[:, :HD] * 0.125, side[:, HD : 2 * HD], side[:, 2 * HD : 3 * HD]
        hot = jnp.where(lax.broadcasted_iota(jnp.int32, (32, TB), 0) == meta_all[b, 0:1, :], 1.0, 0.0)
        lane = lax.broadcasted_iota(jnp.int32, (TB, HD), 1)
        ones3 = jnp.where(lane < 3, 1.0, 0.0)
        apart = (hot.T - 1.0) * MASKED
        q_ref[rows, :] = q8.astype(BF)
        ka_ref[rows, :] = jnp.concatenate([key, apart, ones3[:, :32]], axis=1).astype(BF)
        va_ref[rows, :] = jnp.concatenate([value, ones3], axis=1).astype(BF)
        qat_ref[:, rows] = jnp.concatenate([q8.T, hot, jnp.zeros((32, TB), F32)], axis=0).astype(BF)
        kt_ref[:, rows] = key.T.astype(BF)
        ones_row = jnp.where(lax.broadcasted_iota(jnp.int32, (16, TB), 0) == 0, 1.0, 0.0)
        vat_ref[:, rows] = jnp.concatenate([value.T, ones_row], axis=0).astype(BF)

    given = []

    def project(low, w):

        @pl.loop(0, 4)
        def _(at):
            side = dot(x_buf[at, low, core, w], w_ref[...]) + b_ref[:1, :]
            rounded = side.astype(BF)
            give[low, w, at] = rounded[:, 256:]
            forms(at * 8 + low * 4 + core * 2 + w, rounded[:, :256])

        given.append(net.copy(give.at[low, w], got.at[low, w], other_core))
        given[-1].start()

    def take(copy, low, w):
        copy.wait_recv()

        @pl.loop(0, 4)
        def _(at):
            forms(at * 8 + low * 4 + (1 - core) * 2 + w, got[low, w, at])

    project(lo, hi)
    project(1 - lo, 1 - hi)
    for copy in half_z + [own_pair[1], came_pair[1]] + pair_late:
        copy.wait_recv()
    project(1 - lo, hi)
    project(lo, 1 - hi)
    piece = x_buf.at[:, :, core]
    share = net.copy(piece, piece, other_core)
    share.start()
    take(given[0], lo, hi)
    take(given[1], 1 - lo, 1 - hi)
    take(given[2], 1 - lo, hi)
    take(given[3], lo, 1 - hi)
    store = pltpu.make_async_copy(x_buf, x_seq, local.at[0])
    meta_out[...] = meta_all[...]
    smalls_out[...] = smalls_all[...]

    wait_all(keep)
    for copy in own_y + across_y:
        copy.wait_recv()
    for copy in inner_down:
        copy.wait_recv()
    relay_down, relay_up = relay_y(1, hi), relay_y(0, hi) + relay_y(0, 1 - hi)
    start_all(relay_down)
    later, inner_wrap = [], []
    for m in range(2):
        piece = wholes[m].at[:, unit_rows(m, 3), columns_part(m, lo, 2)]
        later.append(net.copy(piece, piece, pair))
        for d in (1, 3, 2):
            piece = wholes[m].at[:, unit_rows(m, 0), columns_part(m, z, 4)]
            later.append(net.copy(piece, piece, along("z", d)))
    piece = out_all.at[:, half_rows(core)]
    later.append(net.copy(piece, piece, other_core))
    for d in range(4):
        piece = down_all.at[(y + d) % 4 * 2 + hi, unit_rows(1, 1, 2)]
        inner_wrap.append(net.copy(piece, piece, wrap))
    start_all(later)

    position = lax.axis_index("seq") * 2 + hi

    def result(b, recv_at):
        there = head_tile(context, position)
        return remote(blocks.at[b], there, back_send.at[b], back_recv.at[recv_at], (y, b // 2, b % 2))

    own_result = pltpu.make_async_copy(blocks.at[position], head_tile(context, position), back_local)

    @pl.loop(0, 4)
    def _(step):
        at = (step + z + 1) % 4
        columns = pl.ds(aligned(at * 1024, 1024), 1024)
        queries = qat_ref[:, columns]
        peak = jnp.full((1, 1024), -jnp.inf, F32)
        total = jnp.zeros((80, 1024), F32)
        for j in range(8):
            keys = slice(j * 512, (j + 1) * 512)
            logits = dot(ka_ref[keys, :], queries)
            new_peak = jnp.maximum(peak, jnp.max(logits, axis=0, keepdims=True))
            expos = jnp.exp(logits - new_peak).astype(BF)
            total = total * jnp.exp(peak - new_peak) + dot(vat_ref[:, keys], expos)
            peak = new_peak
        sums = total[HD : HD + 1]
        found = total[:HD] / sums
        wide_ref[:, columns] = found
        lse_ref[:, columns] = peak + jnp.log(sums)
        low = found.astype(BF)
        for j in range(8):
            b = at * 8 + j
            blocks[b] = low[:, j * TB : (j + 1) * TB]

            @pl.when(b != position)
            def _():
                result(b, position).start()

            @pl.when(b == position)
            def _():
                own_result.start()

        @pl.when(step == 0)
        def _():
            for copy in relay_down + inner_up + across_up:
                copy.wait_recv()
            start_all(inner_wrap + relay_up)

        @pl.when(step == 2)
        def _():
            share.wait_recv()
            store.start()

    store.wait()
    for copy in [swap] + own_pair + own_z + came_pair + came_z + half_z + pair_late + [share] + given:
        copy.wait_send()
    for copy in cross_first + cross_early + cross_late + own_small + across_small + own_y + across_y + inner_down:
        copy.wait_send()
    for copy in inner_up + across_up + relay_down:
        copy.wait_send()
    for copy in cross_late[1:]:
        copy.wait_recv()
    wait_all(relay_up + later + inner_wrap)

    @pl.loop(1, NB)
    def _(shift):
        b = (position + shift) % NB
        result(b, b).wait()

    own_result.wait()


def front(tokens, segments, flags, vectors, b_up, w_out, w_up, w_down, w_qkv):
    shape = jax.ShapeDtypeStruct
    in_vmem = pl.BlockSpec(memory_space=pltpu.VMEM)
    return pl.pallas_call(
        front_kernel,
        in_specs=[ANY] + [in_vmem] * 4 + [ANY] * 4,
        out_specs=[ANY] + [in_vmem] * 2 + [ANY] * 4 + [in_vmem] * 5 + [ANY] + [in_vmem] * 2,
        out_shape=[
            shape((4, 2, 2, 2, TB, D), BF),
            shape((NB, 8, TB), jnp.int32),
            shape((8, 16, 128), F32),
            shape((8, 128, D), BF),
            shape((8, 128, 2048), BF),
            shape((8, 256, D), BF),
            shape((8, 128, 3 * D), BF),
            shape((128, L), BF),
            shape((L, 128), BF),
            shape((L, 128), BF),
            shape((HD, L), BF),
            shape((L, HD), BF),
            shape((D, 2 * TB), BF),
            shape((HD, L), F32),
            shape((1, L), F32),
        ],
        scratch_shapes=[
            pltpu.VMEM((80, L), BF),
            pltpu.VMEM((NB, HD, TB), BF),
            pltpu.VMEM((2, 2, 4, TB, 256), BF),
            pltpu.VMEM((2, 2, 4, TB, 256), BF),
            pltpu.VMEM((4, 2, 2, 2, TB, D), BF),
            pltpu.VMEM((2, TB, D), BF),
            pltpu.VMEM((128, D), BF),
            pltpu.VMEM((2, 128, 2048), BF),
            pltpu.VMEM((256, D), BF),
            pltpu.VMEM((128, 3 * D), BF),
            pltpu.VMEM((2, 8, TB), jnp.int32),
            pltpu.VMEM((2, 128, 384), BF),
            pltpu.VMEM((16, 128), F32),
            pltpu.VMEM((NB, 8, TB), jnp.int32),
            pltpu.VMEM((8, 128, 384), BF),
            pltpu.VMEM((8, 16, 128), F32),
            pltpu.VMEM((D, 512), BF),
            pltpu.VMEM((8, 512), F32),
            pltpu.SemaphoreType.DMA((FRONT_COPIES,)),
            pltpu.SemaphoreType.DMA((FRONT_COPIES,)),
            pltpu.SemaphoreType.DMA((12,)),
            *swap_sems(),
            *swap_sems(),
        ],
        name="front",
        compiler_params=pltpu.CompilerParams(
            collective_id=1, has_side_effects=True, vmem_limit_bytes=VMEM_CAP
        ),
    )(tokens, segments, flags, vectors, b_up, w_out, w_up, w_down, w_qkv)


def qkv_along_y(qkv_all, net):
    _, y, _, core = place()
    copies = []
    for d in (1, 3, 2):
        for w in range(2):
            piece = qkv_all.at[y * 2 + w, half_rows(core)]
            copies.append(net.copy(piece, piece, along("y", d)))
    return copies


def turned(first, second):
    return dot(first, second, ((0,), (0,)))


def gelu_both(u):
    rate = 0.7978845608028654
    square = u * u
    curve = jnp.tanh(rate * (u + 0.044715 * (square * u)))
    half = 0.5 * (1.0 + curve)
    slope = half + 0.5 * u * (1.0 - curve * curve) * (rate * (1.0 + 0.134145 * square))
    return u * half, slope


def fold(values):
    return jnp.sum(values.reshape(values.shape[0] // 8, 8, values.shape[1]), axis=0)


ROWS = 256
CHUNK = 32
SMALLS = 16


def middle_kernel(
    context_in, meta, tokens, teacher, flags, smalls, out_all, up_all, down_all, a0,
    states, resid_out, do, g_ref, sums_out, count_out, qkv_all,
    context, context_s, w_out, w_up, w_down, h, act, slope, send_one, come_one, send_two, come_two,
    gb, gu, ga, ga_s, normed, hidden, rate, work, resid, gct, stage, count, counts, valid,
    send, recv, local, back_send, back_recv, back_local,
):
    x, y, z, core = place()
    mine = y * 2 + x // 2
    twin = sibling()
    loads = [
        pltpu.make_async_copy(context_in, context, local.at[6]),
        pltpu.make_async_copy(out_all, w_out, local.at[0]),
        pltpu.make_async_copy(up_all, w_up, local.at[1]),
    ]
    load_down = pltpu.make_async_copy(down_all, w_down, local.at[2])
    start_all(loads + [load_down])
    greet_signal(shard_greet())
    greet_wait(shard_greet())
    net = Transfers(send, recv)
    later = qkv_along_y(qkv_all, net)
    valid_here = jnp.sum(meta[:, 1, :].astype(F32), axis=0, keepdims=True)
    count[...] = jnp.broadcast_to(jnp.sum(valid_here, axis=1, keepdims=True), (8, 128))
    ahead = [net.copy(count, counts.at[mine], target) for target in shard_greet()]
    start_all(ahead + later)
    own_count = pltpu.make_async_copy(count, counts.at[mine], local.at[3])
    own_count.start()
    for s in range(2):
        column = jnp.broadcast_to(flags[s : s + 1, :].astype(F32), (128, 128)).T
        valid[128 * s : 128 * (s + 1), :] = column

    def vector(row):
        return jnp.concatenate([smalls[i, row : row + 1, :] for i in range(8)], axis=1)

    out_bias, gain_one, offset_one, down_bias, gain_two, offset_two = [vector(row) for row in range(2, 8)]
    zeros = jnp.zeros((8, D), F32)
    wait_all(loads)
    give_context = net.copy(context, context_s, twin)
    give_context.start()
    work[...] = turned(context[...], w_out[...].reshape(D, D))

    @pl.loop(0, ROWS // CHUNK)
    def _(i):
        rows = pl.ds(aligned(i * CHUNK, CHUNK), CHUNK)
        total = tokens[rows, :].astype(F32) + work[rows, :] + out_bias
        centre = total - jnp.mean(total, axis=1, keepdims=True)
        scale = lax.rsqrt(jnp.mean(centre * centre, axis=1, keepdims=True) + EPS)
        unit = centre * scale
        normed[rows, :] = unit
        rate[rows, :] = jnp.broadcast_to(scale, (CHUNK, 128))
        full = unit * gain_one + offset_one
        hidden[rows, :] = full
        h[0, rows, :] = full.astype(BF)

    give_hidden = net.copy(h.at[0], h.at[1], twin)
    give_hidden.start()
    for slot in range(2):
        if slot == 1:
            give_hidden.wait()
        for k in range(8):
            columns = slice(256 * k, 256 * (k + 1))
            bias = jnp.concatenate([smalls[k, pl.ds(8 + 2 * core + e, 1), :] for e in range(2)], axis=1)
            u = dot(h[slot], w_up[:, :, columns].reshape(D, 256)) + bias
            value, incline = gelu_both(u)
            act[slot, :, columns] = value.astype(BF)
            slope[slot, :, columns] = incline
    load_down.wait()
    send_one[...] = dot(act[1], w_down[...].reshape(2048, D))
    give_one = net.copy(send_one, come_one, twin)
    give_one.start()
    work[...] = dot(act[0], w_down[...].reshape(2048, D))
    give_one.wait()
    wait_all(ahead)
    own_count.wait()
    total_count = jnp.sum(counts[...], axis=0)
    count_out[...] = total_count
    factor = (128 * ROWS) / total_count[:1, :1]

    def loss_rows(i, carried):
        rows = pl.ds(aligned(i * CHUNK, CHUNK), CHUNK)
        total = hidden[rows, :] + (work[rows, :] + come_one[rows, :] + down_bias)
        centre = total - jnp.mean(total, axis=1, keepdims=True)
        scale = lax.rsqrt(jnp.mean(centre * centre, axis=1, keepdims=True) + EPS)
        unit = centre * scale
        final = unit * gain_two + offset_two
        states[rows, :] = final.astype(BF)
        differ = final - teacher[rows, :].astype(F32)
        held = valid[rows, :1] * differ
        grad = factor * held
        weighted = grad * gain_two
        back = weighted - jnp.mean(weighted, axis=1, keepdims=True)
        back = scale * (back - unit * jnp.mean(weighted * unit, axis=1, keepdims=True))
        resid[rows, :] = back
        low = back.astype(BF)
        gb[0, rows, :] = low
        return (
            carried[0] + fold(grad * unit),
            carried[1] + fold(grad),
            carried[2] + fold(low.astype(F32)),
            carried[3] + fold(held * differ),
        )

    gain_two_sum, offset_two_sum, down_sum, error = lax.fori_loop(
        0, ROWS // CHUNK, loss_rows, (zeros, zeros, zeros, zeros)
    )
    give_branch = net.copy(gb.at[0], gb.at[1], twin)
    give_branch.start()
    up_sums = []
    for slot in range(2):
        if slot == 1:
            give_branch.wait()
        for k in range(8):
            columns = slice(256 * k, 256 * (k + 1))
            pulled = dot(gb[slot], w_down[k], ((1,), (1,))) * slope[slot, :, columns]
            low = pulled.astype(BF)
            gu[slot, :, columns] = low
            up_sums.append(fold(low.astype(F32)))
    for i in range(8):
        send_two[:, 128 * i : 128 * (i + 1)] = dot(gu[1], w_up[i], ((1,), (1,)))
    give_two = net.copy(send_two, come_two, twin)
    give_two.start()
    for i in range(8):
        work[:, 128 * i : 128 * (i + 1)] = dot(gu[0], w_up[i], ((1,), (1,)))
    give_two.wait()

    def first_norm_rows(i, carried):
        rows = pl.ds(aligned(i * CHUNK, CHUNK), CHUNK)
        grad = resid[rows, :] + (work[rows, :] + come_two[rows, :])
        unit = normed[rows, :]
        weighted = grad * gain_one
        back = weighted - jnp.mean(weighted, axis=1, keepdims=True)
        back = rate[rows, :1] * (back - unit * jnp.mean(weighted * unit, axis=1, keepdims=True))
        resid_out[rows, :] = back
        low = back.astype(BF)
        ga[rows, :] = low
        return (carried[0] + fold(grad * unit), carried[1] + fold(grad), carried[2] + fold(low.astype(F32)))

    gain_one_sum, offset_one_sum, out_sum = lax.fori_loop(0, ROWS // CHUNK, first_norm_rows, (zeros, zeros, zeros))
    give_attended = net.copy(ga.at[:, pl.ds(aligned((1 - core) * 512, 512), 512)], ga_s, twin)
    give_attended.start()
    gct[...] = dot(w_out[...].reshape(D, D), ga[...], ((1,), (1,))).astype(BF)
    back_start, back_wait = swap_copies(
        lambda b: head_tile(gct, b), lambda b: do.at[b], (back_send, back_recv, back_local)
    )
    back_start()

    error = jnp.broadcast_to(jnp.sum(jnp.sum(error, axis=0, keepdims=True), axis=1, keepdims=True), (1, 128))
    lines = [out_sum, gain_one_sum, offset_one_sum, down_sum, gain_two_sum, offset_two_sum]
    lines = [jnp.sum(line, axis=0, keepdims=True) for line in lines]
    for i in range(8):
        columns = slice(128 * i, 128 * (i + 1))
        sums_out[i] = jnp.zeros((SMALLS, 128), F32)
        for row, line in enumerate(lines):
            sums_out[i, row : row + 1, :] = line[:, columns]
        both = jnp.sum(up_sums[i] + up_sums[8 + i], axis=0, keepdims=True)
        for e in range(2):
            sums_out[i, pl.ds(6 + 2 * core + e, 1), :] = both[:, 128 * e : 128 * (e + 1)]
        sums_out[i, 10:11, :] = error

    give_context.wait()
    give_attended.wait()

    def stored(i):
        return pltpu.make_async_copy(stage.at[i % 2], g_ref.at[i // 2, i % 2], local.at[4 + i % 2])

    for i in range(8):
        if i >= 2:
            stored(i - 2).wait()
        tall = slice(128 * i, 128 * (i + 1))
        wide = slice(256 * i, 256 * (i + 1))
        up = turned(h[0, :, tall], gu[0]) + turned(h[1, :, tall], gu[1])
        for k in range(4):
            stage[i % 2, 128 * k : 128 * (k + 1), :] = up[:, 512 * k : 512 * (k + 1)].astype(BF)
        down = turned(act[0, :, wide], gb[0]) + turned(act[1, :, wide], gb[1])
        for k in range(2):
            stage[i % 2, 512 + 256 * k : 768 + 256 * k, :] = down[:, 512 * k : 512 * (k + 1)].astype(BF)
        own_half = ga[:, pl.ds(aligned(core * 512, 512), 512)]
        out = dot(context[tall, :], own_half) + dot(context_s[tall, :], ga_s[...])
        stage[i % 2, 1024:, :] = out.astype(BF)
        stored(i).start()
    stored(6).wait()
    stored(7).wait()
    back_wait()
    wait_all(later)


def middle(context, meta, tokens, teacher, flags, smalls, out_all, up_all, down_all, qkv_all):
    shape = jax.ShapeDtypeStruct
    in_vmem = pl.BlockSpec(memory_space=pltpu.VMEM)
    dma = pltpu.SemaphoreType.DMA
    wide = pltpu.VMEM((ROWS, D), F32)
    return pl.pallas_call(
        middle_kernel,
        in_specs=[ANY] + [in_vmem] * 5 + [ANY] * 4,
        out_specs=[in_vmem, in_vmem, ANY, ANY, in_vmem, in_vmem, ANY],
        out_shape=[
            shape((ROWS, D), BF),
            shape((ROWS, D), F32),
            shape((NB, HD, TB), BF),
            shape((4, 2, 1152, 512), BF),
            shape((8, SMALLS, 128), F32),
            shape((8, 128), F32),
            shape(qkv_all.shape, BF),
        ],
        input_output_aliases={9: 6},
        scratch_shapes=[
            pltpu.VMEM((D, ROWS), BF),
            pltpu.VMEM((D, ROWS), BF),
            pltpu.VMEM((8, 128, D), BF),
            pltpu.VMEM((8, 128, 2048), BF),
            pltpu.VMEM((8, 256, D), BF),
            pltpu.VMEM((2, ROWS, D), BF),
            pltpu.VMEM((2, ROWS, 2048), BF),
            pltpu.VMEM((2, ROWS, 2048), F32),
            wide,
            wide,
            wide,
            wide,
            pltpu.VMEM((2, ROWS, D), BF),
            pltpu.VMEM((2, ROWS, 2048), BF),
            pltpu.VMEM((ROWS, D), BF),
            pltpu.VMEM((ROWS, 512), BF),
            wide,
            wide,
            pltpu.VMEM((ROWS, 128), F32),
            wide,
            wide,
            pltpu.VMEM((D, ROWS), BF),
            pltpu.VMEM((2, 1152, 512), BF),
            pltpu.VMEM((8, 128), F32),
            pltpu.VMEM((8, 8, 128), F32),
            pltpu.VMEM((ROWS, 128), F32),
            dma((32,)),
            dma((32,)),
            dma((10,)),
            *swap_sems(),
        ],
        name="middle",
        compiler_params=pltpu.CompilerParams(
            collective_id=3, has_side_effects=True, vmem_limit_bytes=VMEM_CAP
        ),
    )(context, meta, tokens, teacher, flags, smalls, out_all, up_all, down_all, qkv_all)


BACK_KEYS = 256
BACK_STEPS = L // BACK_KEYS
BACK_WIDTH = 1024


def back_prepare(qat, do, wide, lse, queries, grads, grad_rows):
    for j in range(L // BACK_WIDTH):
        columns = slice(j * BACK_WIDTH, (j + 1) * BACK_WIDTH)
        grad_t = jnp.concatenate([do[j * (BACK_WIDTH // TB) + i] for i in range(BACK_WIDTH // TB)], axis=1)
        wider = grad_t.astype(F32)
        delta = jnp.sum(wider * wide[:, columns], axis=0, keepdims=True)
        grads[:HD, columns] = grad_t
        grads[HD:, columns] = jnp.concatenate([three_pieces(-delta), jnp.zeros((61, BACK_WIDTH), BF)], axis=0)
        queries[:96, columns] = qat[:96, columns]
        queries[96:, columns] = jnp.concatenate(
            [three_pieces(-lse[:, columns]), jnp.zeros((29, BACK_WIDTH), BF)], axis=0
        )
        grad_rows[columns, :] = wider.T.astype(BF)


def back_kernel(
    qat, ka, va, kt, q8, do, wide, lse, smalls, x_seq, g_ref, a0,
    projected, heads_out, shard_out, smalls_out, qkv_all,
    x_buf, queries, grads, grad_rows, dq, d_ref, mine_ref, parts_ref, sum_ref, heads_buf, small_buf, small_sum, small_all,
    send, recv, local, dk_send, dk_recv, dk_local, dq_send, dq_recv, dq_local, spread_send, spread_recv, *reduce_refs,
):
    x, y, z, core = place()
    shard_at = y * 2 + x // 2
    seq = lax.axis_index("seq")
    mine = seq * 2 + x // 2
    net = (g_ref,) + reduce_refs

    def shard_device(d):
        other = (shard_at + d) % 8
        return other, (other // 2, seq, other % 2)

    load_x = pltpu.make_async_copy(x_seq, x_buf, local.at[0])
    load_x.start()
    shard_others = [shard_device(d)[1] for d in range(1, 8)]
    greet_signal(shard_others)
    back_prepare(qat, do, wide, lse, queries, grads, grad_rows)
    dq[...] = jnp.zeros_like(dq)
    greet_wait(shard_others)
    for part in range(3):
        reduce_start(part, net)
    far = Transfers(send, recv)
    small_out = [far.copy(smalls.at[shard_device(d)[0]], small_buf.at[shard_at], shard_device(d)[1]) for d in range(1, 8)]
    start_all(small_out)
    small_buf[shard_at] = smalls[shard_at]
    rows = half_rows(core)
    weights = far.copy(qkv_all.at[:, rows], qkv_all.at[:, rows], sibling())
    weights.start()

    def landing(first, count):
        return projected.at[pl.ds(first, count), pl.ds(aligned(seq * HD, HD), HD), pl.ds(aligned((x // 2) * TB, TB), TB)]

    def block_device(b):
        return (y, b // 2, b % 2)

    def dk_copy(b, recv_at):
        return remote(d_ref.at[b, pl.ds(1, 2)], landing(1, 2), dk_send.at[b], dk_recv.at[recv_at], block_device(b))

    def dq_copy(b, recv_at):
        return remote(d_ref.at[b, pl.ds(0, 1)], landing(0, 1), dq_send.at[b], dq_recv.at[recv_at], block_device(b))

    dk_own = pltpu.make_async_copy(d_ref.at[mine, pl.ds(1, 2)], landing(1, 2), dk_local)
    dq_own = pltpu.make_async_copy(d_ref.at[mine, pl.ds(0, 1)], landing(0, 1), dq_local)

    @pl.loop(0, BACK_STEPS)
    def _(step):
        at = (step + 4 * (z + 1)) % BACK_STEPS
        keys = pl.ds(aligned(at * BACK_KEYS, BACK_KEYS), BACK_KEYS)
        ka_part, va_part, kt_part = ka[keys, :], va[keys, :], kt[:, keys]
        dk = jnp.zeros((BACK_KEYS, HD), F32)
        dv = jnp.zeros((BACK_KEYS, HD), F32)
        for j in range(L // BACK_WIDTH):
            columns = slice(j * BACK_WIDTH, (j + 1) * BACK_WIDTH)
            probs = jnp.exp(dot(ka_part, queries[:, columns]))
            raw = (probs * dot(va_part, grads[:, columns])).astype(BF)
            dv = dv + dot(probs.astype(BF), grad_rows[columns, :])
            dk = dk + dot(raw, q8[columns, :])
            dq[:, columns] += dot(kt_part, raw)
        dk_t, dv_t = dk.T.astype(BF), dv.T.astype(BF)
        for i in range(BACK_KEYS // TB):
            b = at * (BACK_KEYS // TB) + i
            d_ref[b, 1] = dk_t[:, i * TB : (i + 1) * TB]
            d_ref[b, 2] = dv_t[:, i * TB : (i + 1) * TB]

            @pl.when(b != mine)
            def _():
                dk_copy(b, mine).start()

            @pl.when(b == mine)
            def _():
                dk_own.start()

        @pl.when(step == 4)
        def _():
            first_relay(net)

        @pl.when(step == 9)
        def _():
            reduce_step(0, 1, net)

        @pl.when(step == 11)
        def _():
            reduce_step(0, 0, net)

        @pl.when(step == 13)
        def _():
            reduce_step(0, 2, net)
            reduce_step(1, 1, net)

    for b in range(NB):
        d_ref[b, 0] = (dq[:, b * TB : (b + 1) * TB] * 0.125).astype(BF)

    load_x.wait()
    left = jnp.concatenate([d_ref[b].reshape(3 * HD, TB) for b in range(NB)], axis=1)
    sums = dot(jnp.ones((8, L), BF), left, ((1,), (1,)))
    gap = jnp.zeros((1, 128 - HD), F32)
    tail = jnp.concatenate(
        [
            jnp.concatenate([sums[:1, :HD], gap], axis=1),
            jnp.concatenate([sums[:1, 2 * HD :], gap], axis=1),
            jnp.zeros((14, 128), F32),
        ],
        axis=0,
    ).astype(BF)
    for i in range(4):
        total = dot(left, x_buf[:, :, 256 * i : 256 * (i + 1)].reshape(L, 256))
        for k in range(2):
            mine_ref[2 * i + k, : 3 * HD, :] = total[:, 128 * k : 128 * (k + 1)].astype(BF)
            mine_ref[2 * i + k, 3 * HD :, :] = tail
    part_out = [far.copy(mine_ref.at[shard_device(d)[0]], parts_ref.at[d], shard_device(d)[1]) for d in range(1, 8)]
    start_all(part_out)

    steps = [
        spread_steps(part, reduce_refs[6 + part].at[0], (local.at[pl.ds(1, 3)], spread_send, spread_recv), shard_out)
        for part in range(3)
    ]
    reduce_step(1, 0, net)
    reduce_step(1, 2, net)
    reduce_step(2, 1, net)
    steps[1][0]()
    wait_all(small_out)
    small_sum[...] = jnp.sum(small_buf[...], axis=0)
    wait_all(part_out)
    added = mine_ref[shard_at].astype(F32)
    for d in range(1, 8):
        added = added + parts_ref[d].astype(F32)
    sum_ref[...] = added.astype(BF)
    heads_buf[seq // 2, core] = sum_ref[...]
    small_all[seq // 2, core] = small_sum[...]
    head_out = []
    for d in range(1, 8):
        target = (y, (seq + 2 * d) % 16, x // 2)
        head_out.append(far.copy(sum_ref, heads_buf.at[seq // 2, core], target))
        head_out.append(far.copy(small_sum, small_all.at[seq // 2, core], target))
    start_all(head_out)
    for part in (2, 0):
        reduce_step(2, part, net)
        steps[part][0]()

    @pl.loop(1, NB)
    def _(shift):
        dq_copy((mine + shift) % NB, mine).start()

    dq_own.start()
    for part in (1, 2, 0):
        steps[part][1]()
    wait_all(head_out)
    across = [
        far.copy(heads_buf.at[:, core], heads_buf.at[:, core], sibling()),
        far.copy(small_all.at[:, core], small_all.at[:, core], sibling()),
    ]
    start_all(across)
    shared = []
    for part in (1, 2, 0):
        steps[part][2]()
        piece = shard_out.at[core, pl.ds(FIRST[part], 8 * PIECE[part])]
        shared.append(far.copy(piece, piece, sibling()))
        shared[-1].start()

    @pl.loop(1, NB)
    def _(shift):
        b = (mine + shift) % NB
        dk_copy(b, b).wait()
        dq_copy(b, b).wait()

    dk_own.wait()
    dq_own.wait()
    weights.wait()
    wait_all(across)
    for i in range(8):
        heads_out[2 * i] = heads_buf[i, 0]
        heads_out[2 * i + 1] = heads_buf[i, 1]
    smalls_out[...] = jnp.sum(small_all[...].reshape(16, 16, 128), axis=0)
    wait_all(shared)


def back(qat, ka, va, kt, q8, do, wide, lse, smalls, x_seq, g, qkv_all):
    shape = jax.ShapeDtypeStruct
    in_vmem = pl.BlockSpec(memory_space=pltpu.VMEM)
    dma = pltpu.SemaphoreType.DMA
    return pl.pallas_call(
        back_kernel,
        in_specs=[in_vmem] * 9 + [ANY] * 3,
        out_specs=[ANY, in_vmem, ANY, in_vmem, ANY],
        out_shape=[
            shape((3, D, 2 * TB), BF),
            shape((H, 208, 128), BF),
            shape((2, 1152, 512), BF),
            shape((16, 128), F32),
            shape(qkv_all.shape, BF),
        ],
        input_output_aliases={11: 4},
        scratch_shapes=[
            pltpu.VMEM((NB, TB, D), BF),
            pltpu.VMEM((128, L), BF),
            pltpu.VMEM((128, L), BF),
            pltpu.VMEM((L, HD), BF),
            pltpu.VMEM((HD, L), F32),
            pltpu.VMEM((NB, 3, HD, TB), BF),
            pltpu.VMEM((8, 208, 128), BF),
            pltpu.VMEM((8, 208, 128), BF),
            pltpu.VMEM((208, 128), BF),
            pltpu.VMEM((8, 2, 208, 128), BF),
            pltpu.VMEM((8, 16, 128), F32),
            pltpu.VMEM((16, 128), F32),
            pltpu.VMEM((8, 2, 16, 128), F32),
            dma((40,)),
            dma((40,)),
            dma((4,)),
            *swap_sems(),
            *swap_sems(),
            dma((3, 8)),
            dma((3, 8)),
            *reduce_scratch(),
        ],
        name="attend_back",
        compiler_params=pltpu.CompilerParams(
            collective_id=4, has_side_effects=True, vmem_limit_bytes=VMEM_CAP
        ),
    )(qat, ka, va, kt, q8, do, wide, lse, smalls, x_seq, g, qkv_all)


def finish_kernel(
    projected, qkv_ref, resid_ref, heads_ref, shard_ref, smalls_ref, count_ref, states_ref,
    tokens_ref, grad_qkv, grad_out, grad_up, grad_down, states_out, loss_ref,
    q_bias, v_bias, o_bias, gain_one, bias_one, d_bias, gain_two, bias_two, u_bias,
    sides,
):
    step = pl.program_id(0)

    @pl.when(step == 0)
    def _():
        sides[...] = projected[...].astype(F32).T.astype(BF)
        x, y, _, _ = place()
        shard_at = y * 2 + x // 2
        for row, out in enumerate((q_bias, v_bias)):
            both = [heads_ref[shard_at * 2 + k, 3 * HD + row, :HD].astype(F32) for k in range(2)]
            out[...] = jnp.concatenate(both)
        for row, out in enumerate((o_bias, gain_one, bias_one, d_bias, gain_two, bias_two)):
            out[...] = smalls_ref[row, :]
        u_bias[...] = jnp.concatenate([smalls_ref[6 + k, :] for k in range(4)])
        loss_ref[...] = smalls_ref[10:11, :1] / (D * count_ref[:1, :1])
        for p in range(3):
            for pair in range(8):
                both = [heads_ref[2 * pair + k, p * HD : (p + 1) * HD, :].astype(F32) for k in range(2)]
                at = p * D + pair * 128
                grad_qkv[:, at : at + 128] = jnp.concatenate(both, axis=0).T

    states_out[...] = states_ref[...]
    tokens_ref[...] = resid_ref[...] + dot(sides[...], qkv_ref[...], ((1,), (1,)))
    for c in range(2):
        columns = slice(512 * c, 512 * (c + 1))
        for j in range(2):
            piece = shard_ref[c, pl.ds(aligned(step * 128, 128), 128), 256 * j : 256 * (j + 1)]
            grad_up[:, 512 * j + 256 * c : 512 * j + 256 * (c + 1)] = piece.astype(F32)
        rows = pl.ds(aligned(512 + 256 * c + (step % 2) * 128, 128), 128)
        grad_down[:, columns] = shard_ref[step // 2, rows, :].astype(F32)
        grad_out[:, columns] = shard_ref[c, pl.ds(aligned(1024 + step * 32, 32), 32), :].astype(F32)


def finish(projected, qkv, resid, heads, shard, smalls, count, states):
    shape = jax.ShapeDtypeStruct

    def whole(*dims):
        return pl.BlockSpec(dims, lambda i: (0,) * len(dims))

    part = pl.BlockSpec((2 * TB, 256), lambda i: (0, i))
    return pl.pallas_call(
        finish_kernel,
        grid=(4,),
        in_specs=[
            whole(3 * D, 2 * TB),
            pl.BlockSpec((256, 3 * D), lambda i: (i, 0)),
            part,
            whole(H, 208, 128),
            whole(2, 1152, 512),
            whole(16, 128),
            whole(8, 128),
            part,
        ],
        out_specs=[
            part,
            whole(128, 3 * D),
            pl.BlockSpec((32, D), lambda i: (i, 0)),
            pl.BlockSpec((128, 1024), lambda i: (0, i)),
            pl.BlockSpec((128, D), lambda i: (i, 0)),
            part,
            whole(1, 1),
        ]
        + [whole(128)] * 8
        + [whole(512)],
        out_shape=[
            shape((2 * TB, D), F32),
            shape((128, 3 * D), F32),
            shape((128, D), F32),
            shape((128, FF), F32),
            shape((512, D), F32),
            shape((2 * TB, D), BF),
            shape((1, 1), F32),
        ]
        + [shape((128,), F32)] * 8
        + [shape((512,), F32)],
        scratch_shapes=[pltpu.VMEM((2 * TB, 3 * D), BF)],
        name="finish",
        compiler_params=pltpu.CompilerParams(vmem_limit_bytes=VMEM_CAP),
    )(projected, qkv, resid, heads, shard, smalls, count, states)


def on_device(
    tokens,
    segments,
    valid_flags,
    teacher,
    w_qkv,
    b_query,
    b_value,
    w_out,
    b_out,
    ln1_gain,
    ln1_bias,
    w_up,
    b_up,
    w_down,
    b_down,
    ln2_gain,
    ln2_bias,
):
    seq_local, row_local, _ = tokens.shape
    token_rows = seq_local * row_local

    vectors = jnp.stack([b_query, b_value, b_out, ln1_gain, ln1_bias, b_down, ln2_gain, ln2_bias]).astype(F32)
    (
        x_seq, meta_all, smalls_all, out_all, up_all, down_all, qkv_all, qat, ka, va, kt, q8, context, wide, lse
    ) = front(
        tokens, segments, valid_flags, vectors, b_up.reshape(4, 128).astype(F32), w_out, w_up, w_down, w_qkv
    )
    x_seq = x_seq.reshape(NB, TB, D)
    states, grad_resid_one, do, g, small_sums, count, qkv_all = middle(
        context,
        meta_all,
        tokens.reshape(token_rows, D),
        teacher.reshape(token_rows, D),
        valid_flags,
        smalls_all,
        out_all,
        up_all,
        down_all,
        qkv_all,
    )
    projected, heads_out, shard_out, small_out, qkv_all = back(
        qat, ka, va, kt, q8, do, wide, lse, small_sums, x_seq, g, qkv_all
    )
    (
        grad_tokens, grad_qkv, grad_out, grad_up, grad_down, states, mean_loss,
        q_bias, v_bias, o_bias, gain_one, bias_one, d_bias, gain_two, bias_two, u_bias,
    ) = finish(
        projected.reshape(3 * D, token_rows), qkv_all.reshape(D, 3 * D), grad_resid_one, heads_out, shard_out, small_out,
        count, states,
    )
    return (
        states.reshape(seq_local, row_local, D),
        mean_loss.reshape(()),
        grad_tokens.reshape(seq_local, row_local, D),
        grad_qkv,
        q_bias,
        v_bias,
        grad_out,
        o_bias,
        gain_one,
        bias_one,
        grad_up,
        u_bias,
        grad_down,
        d_bias,
        gain_two,
        bias_two,
    )


def solution(mesh):
    rows = P("dp", ("seq", "wshard"), None)
    flags = P("dp", ("seq", "wshard"))
    matrix = P(("dp", "wshard"), None)
    vector = P(("dp", "wshard"))
    return jax.shard_map(
        on_device,
        mesh=mesh,
        in_specs=(
            rows,
            flags,
            flags,
            rows,
            matrix,
            vector,
            vector,
            matrix,
            vector,
            vector,
            vector,
            matrix,
            vector,
            matrix,
            vector,
            vector,
            vector,
        ),
        out_specs=(
            rows,
            P(),
            rows,
            matrix,
            vector,
            vector,
            matrix,
            vector,
            vector,
            vector,
            matrix,
            vector,
            matrix,
            vector,
            vector,
            vector,
        ),
        check_vma=False,
    )
```

```python
import functools

import jax
import jax.numpy as jnp
from jax import lax
from jax.experimental import pallas as pl
from jax.experimental.pallas import tpu as pltpu
from jax.sharding import PartitionSpec as P

D = 1024
H = 16
HD = 64
FF = 4096
L = 4096
EPS = 1e-06
F32 = jnp.float32
BF = jnp.bfloat16
MASKED = 1000000000.0
VMEM_CAP = 60 * 1024 * 1024
MESH = pl.DeviceIdType.MESH
ANY = pl.BlockSpec(memory_space=pl.ANY)
TB = 128
NB = L // TB


def dot(first, second, dims=((1,), (0,))):
    return lax.dot_general(first, second, (dims, ((), ())), preferred_element_type=F32)


def three_pieces(row):
    high = row.astype(BF)
    rest = row - high.astype(F32)
    middle = rest.astype(BF)
    lowest = (rest - middle.astype(F32)).astype(BF)
    return jnp.concatenate([high, middle, lowest], axis=0)


def place():
    at = lax.axis_index("seq")
    return (lax.axis_index("wshard") * 2 + (at // 2) % 2, lax.axis_index("dp"), at // 4, at % 2)


def device_at(x, y, z, core):
    return (y, (z * 2 + x % 2) * 2 + core, x // 2)


def along(axis, shift):
    x, y, z, core = place()
    if axis == "x":
        return device_at((x + shift) % 4, y, z, core)
    if axis == "y":
        return device_at(x, (y + shift) % 4, z, core)
    return device_at(x, y, (z + shift) % 4, core)


def sibling():
    x, y, z, core = place()
    return device_at(x, y, z, 1 - core)


def greet(partners):
    barrier = pltpu.get_barrier_semaphore()
    for partner in partners:
        pl.semaphore_signal(barrier, inc=1, device_id=partner, device_id_type=MESH)
    pl.semaphore_wait(barrier, len(partners))


def remote(src, dst, send_sem, recv_sem, target):
    return pltpu.make_async_remote_copy(
        src_ref=src, dst_ref=dst, send_sem=send_sem, recv_sem=recv_sem, device_id=target, device_id_type=MESH
    )


ORDERS = ("yzx", "zxy", "xyz")
PIECE = (64, 32, 48)
FIRST = (0, 512, 768)


def ring_partners():
    return [along(axis, shift) for axis in "xyz" for shift in (1, 2, 3)] + [sibling()]


def reduce_scratch():
    a, b, c = PIECE
    return [
        pltpu.VMEM((4, 2, 8 * a, 512), BF),
        pltpu.VMEM((4, 4, 2, 2 * b, 512), BF),
        pltpu.VMEM((4, 4, 4 * c, 512), BF),
        pltpu.VMEM((4, 2, 2 * a, 512), BF),
        pltpu.VMEM((4, 4, b, 512), BF),
        pltpu.VMEM((4, 4 * c, 512), BF),
        pltpu.VMEM((4, a, 512), BF),
        pltpu.VMEM((4, b, 512), BF),
        pltpu.VMEM((4, c, 512), BF),
        pltpu.SemaphoreType.DMA((3, 3, 3)),
        pltpu.SemaphoreType.DMA((3, 3, 3)),
        pltpu.SemaphoreType.DMA((3, 2)),
        pltpu.VMEM((2, 8 * a, 512), BF),
        pltpu.VMEM((2, 2, 2, 2 * b, 512), BF),
        pltpu.VMEM((2, 2, 4 * c, 512), BF),
        pltpu.SemaphoreType.DMA((3, 6)),
        pltpu.SemaphoreType.DMA((3, 6)),
        pltpu.SemaphoreType.DMA((3, 2)),
    ]


def aligned(value, unit):
    return pl.multiple_of(value, unit)


def reduce_piece(stage, part, refs, at):
    half, low, n = at // 2, at % 2, PIECE[part]
    held = refs[1 + 3 * (stage - 1) + part]
    if stage == 1:
        if part == 0:
            return held.at[0, :, pl.ds(aligned(at * 2 * n, 16), 2 * n), :]
        if part == 1:
            return held.at[0, :, half, pl.ds(aligned(low * n, 16), n), :]
        return held.at[0, at]
    if part == 0:
        return held.at[0, half, pl.ds(aligned(low * n, 16), n), :]
    if part == 1:
        return held.at[0, at]
    return held.at[0, pl.ds(aligned(at * n, 16), n), :]


def ring_at(axis):
    x, y, z, _ = place()
    return {"x": x, "y": y, "z": z}[axis]


def reduce_copies(stage, part, refs):
    send, recv = refs[10], refs[11]
    axis = ORDERS[part][stage]
    return [
        remote(
            reduce_piece(stage, part, refs, (ring_at(axis) + shift) % 4),
            refs[1 + 3 * stage + part].at[shift],
            send.at[stage, part, shift - 1],
            recv.at[stage, part, shift - 1],
            along(axis, shift),
        )
        for shift in (1, 3, 2)
    ]


def first_piece(part, refs, at, half):
    g_ref, n, first = refs[0], PIECE[part], FIRST[part]
    if part == 0:
        return g_ref.at[at, half, pl.ds(0, 8 * n)]
    if part == 1:
        return g_ref.at[pl.ds(2 * half, 2), :, pl.ds(aligned(first + at * 2 * n, 16), 2 * n)]
    return g_ref.at[pl.ds(2 * half, 2), at // 2, pl.ds(aligned(first + at % 2 * 4 * n, 16), 4 * n)]


def first_landing(part, refs, slot, half):
    held = refs[1 + part]
    return held.at[slot, half] if part == 0 else held.at[slot, pl.ds(2 * half, 2)]


def first_copies(part, refs):
    relay, send, recv = refs[13 + part], refs[16], refs[17]
    axis = ORDERS[part][0]
    at = ring_at(axis)
    up, down, far = (at + 1) % 4, (at + 3) % 4, (at + 2) % 4
    moves = [
        (first_piece(part, refs, far, 0), 2, 0, 1),
        (first_piece(part, refs, far, 1), 2, 1, 3),
        (first_piece(part, refs, up, 1), 1, 1, 1),
        (first_piece(part, refs, down, 0), 3, 0, 3),
        (relay.at[0], 1, 0, 1),
        (relay.at[1], 3, 1, 3),
    ]
    return [
        remote(src, first_landing(part, refs, slot, half), send.at[part, k], recv.at[part, k], along(axis, d))
        for k, (src, slot, half, d) in enumerate(moves)
    ]


def first_loads(part, refs):
    relay, local = refs[13 + part], refs[18]
    at = ring_at(ORDERS[part][0])
    return [
        pltpu.make_async_copy(first_piece(part, refs, (at + 1) % 4, 0), relay.at[0], local.at[part, 0]),
        pltpu.make_async_copy(first_piece(part, refs, (at + 3) % 4, 1), relay.at[1], local.at[part, 1]),
    ]


def first_own(part, refs):
    at = ring_at(ORDERS[part][0])
    return [
        pltpu.make_async_copy(first_piece(part, refs, at, h), first_landing(part, refs, 0, h), refs[12].at[part, h])
        for h in range(2)
    ]


def reduce_start(part, refs):
    start_all(first_copies(part, refs)[:4] + first_loads(part, refs) + first_own(part, refs))


def add_two(first, second):
    return (first.astype(F32) + second.astype(F32)).astype(BF)


def first_relay(part, refs):
    held, relay, n = refs[1 + part], refs[13 + part], PIECE[part]
    copies = first_copies(part, refs)
    wait_all(first_loads(part, refs))
    for copy in copies[:2]:
        copy.wait_recv()

    @pl.loop(0, 8 if part == 1 else 16)
    def _(i):
        if part == 0:
            rows = pl.ds(aligned(i % 8 * n, 16), n)
            relay[i // 8, rows, :] = add_two(relay[i // 8, rows, :], held[2, i // 8, rows, :])
        elif part == 1:
            half, k, e = i // 4, i // 2 % 2, i % 2
            relay[half, k, e] = add_two(relay[half, k, e], held[2, 2 * half + k, e])
        else:
            half, k, rows = i // 8, i // 4 % 2, pl.ds(aligned(i % 4 * n, 16), n)
            relay[half, k, rows, :] = add_two(relay[half, k, rows, :], held[2, 2 * half + k, rows, :])

    start_all(copies[4:])


def first_end(part, refs):
    copies = first_copies(part, refs)
    for copy in copies[:2]:
        copy.wait_send()
    wait_all(copies[2:] + first_own(part, refs))


def add_three(values):
    return (values[0].astype(F32) + values[1].astype(F32) + values[2].astype(F32)).astype(BF)


def add_four(values):
    total = values[0].astype(F32) + values[1].astype(F32)
    return (total + values[2].astype(F32) + values[3].astype(F32)).astype(BF)


def reduce_step(stage, part, refs):
    a1, b1, c1, a2, b2, c2, a3, b3, c3 = refs[1:10]
    if stage == 0:
        first_end(part, refs)
    else:
        wait_all(reduce_copies(stage, part, refs))
    x, y, z, _ = place()
    n = PIECE[part]
    rest = (1, 2, 3)
    near = (0, 1, 3)
    if stage == 0:

        @pl.loop(0, 16)
        def _(i):
            if part == 0:
                rows = pl.ds(aligned((i % 8) * n, 16), n)
                a1[0, i // 8, rows, :] = add_three([a1[s, i // 8, rows, :] for s in near])
            elif part == 1:
                rows = pl.ds(aligned((i % 2) * n, 16), n)
                b1[0, i // 4, (i // 2) % 2, rows, :] = add_three([b1[s, i // 4, (i // 2) % 2, rows, :] for s in near])
            else:
                rows = pl.ds(aligned((i % 4) * n, 16), n)
                c1[0, i // 4, rows, :] = add_three([c1[s, i // 4, rows, :] for s in near])

    elif stage == 1:

        @pl.loop(0, 4)
        def _(i):
            if part == 0:
                rows = pl.ds(aligned((i % 2) * n, 16), n)
                own = a1[0, i // 2, pl.ds(aligned(z * 2 * n + (i % 2) * n, 16), n), :]
                a2[0, i // 2, rows, :] = add_four([own] + [a2[s, i // 2, rows, :] for s in rest])
            elif part == 1:
                own = b1[0, i, x // 2, pl.ds(aligned((x % 2) * n, 16), n), :]
                b2[0, i] = add_four([own] + [b2[s, i] for s in rest])
            else:
                rows = pl.ds(aligned(i * n, 16), n)
                own = c1[0, y, rows, :]
                c2[0, rows, :] = add_four([own] + [c2[s, rows, :] for s in rest])

    elif part == 0:
        own = a2[0, x // 2, pl.ds(aligned((x % 2) * n, 16), n), :]
        a3[0] = add_four([own] + [a3[s] for s in rest])
    elif part == 1:
        b3[0] = add_four([b2[0, y]] + [b3[s] for s in rest])
    else:
        own = c2[0, pl.ds(aligned(z * n, 16), n), :]
        c3[0] = add_four([own] + [c3[s] for s in rest])
    if stage < 2:
        start_all(reduce_copies(stage + 1, part, refs))


def shard_rows(o_ref, part, x_low, z, core):
    sub = x_low * 4 + z if part == 2 else z * 2 + x_low
    return o_ref.at[core, pl.ds(aligned(FIRST[part] + sub * PIECE[part], 16), PIECE[part]), :]


def spread_steps(part, mine, sems, o_ref):
    local, send, recv = sems
    x, y, z, core = place()
    low = x % 2
    pair = device_at(x // 2 * 2 + 1 - low, y, z, core)
    spot = shard_rows(o_ref, part, low, z, core)
    own = pltpu.make_async_copy(mine, spot, local.at[part])
    first = remote(mine, spot, send.at[part, 0], recv.at[part, 0], pair)
    second = [remote(mine, spot, send.at[part, d], recv.at[part, d], along("z", d)) for d in (1, 3, 2)]
    spot = shard_rows(o_ref, part, 1 - low, z, core)
    third = [remote(spot, spot, send.at[part, 3 + d], recv.at[part, 3 + d], along("z", d)) for d in (1, 3, 2)]

    def begin():
        start_all([own, first] + second)

    def middle():
        first.wait()
        start_all(third)

    def end():
        wait_all([own] + second + third)

    return begin, middle, end


def swap_partner(shift):
    mine = lax.axis_index("seq") * 2 + lax.axis_index("wshard")
    other = (mine + shift) % NB
    return other, (lax.axis_index("dp"), other // 2, other % 2)


def swap_greet():
    barrier = pltpu.get_barrier_semaphore()

    @pl.loop(1, NB)
    def _(shift):
        pl.semaphore_signal(barrier, inc=1, device_id=swap_partner(shift)[1], device_id_type=MESH)

    pl.semaphore_wait(barrier, NB - 1)


def swap_copies(piece_for, landing_from, sems):
    mine = lax.axis_index("seq") * 2 + lax.axis_index("wshard")
    send, recv, local = sems

    def copy(shift):
        other, device = swap_partner(shift)
        return remote(piece_for(other), landing_from(mine), send.at[shift], recv.at[shift], device)

    own = pltpu.make_async_copy(piece_for(mine), landing_from(mine), local)

    def start():
        @pl.loop(1, NB)
        def _(shift):
            copy(shift).start()

        own.start()

    def wait():
        @pl.loop(1, NB)
        def _(shift):
            copy(shift).wait()

        own.wait()

    return start, wait


def swap_sems():
    return [pltpu.SemaphoreType.DMA((NB,)), pltpu.SemaphoreType.DMA((NB,)), pltpu.SemaphoreType.DMA]


def block_of(ref, b):
    return ref.at[b]


def head_tile(ref, b):
    return ref.at[pl.ds(aligned((b // 2) * HD, HD), HD), pl.ds(aligned((b % 2) * TB, TB), TB)]


def head_tile3(ref, b):
    return ref.at[:, pl.ds(aligned((b // 2) * HD, HD), HD), pl.ds(aligned((b % 2) * TB, TB), TB)]


HALVES = ((128, 2048), (256, 1024))


class Transfers:
    def __init__(self, send, recv):
        self.send, self.recv, self.used = send, recv, 0

    def copy(self, src, dst, target):
        made = remote(src, dst, self.send.at[self.used], self.recv.at[self.used], target)
        self.used += 1
        return made


def start_all(copies):
    for copy in copies:
        copy.start()


def wait_all(copies):
    for copy in copies:
        copy.wait()


def unit_rows(matrix, unit, count=1):
    rows = HALVES[matrix][0] // 4
    return pl.ds(unit * rows, count * rows)


def columns_part(matrix, at, parts):
    width = HALVES[matrix][1] // parts
    return pl.ds(aligned(at * width, 128), width)


def half_rows(core, rows=64):
    return pl.ds(aligned(core * rows, rows), rows)


def shard_greet():
    x, y, z, core = place()
    return [device_at(x, (y + d) % 4, z, core) for d in (1, 2, 3)] + [
        device_at(3 - x, (y + d) % 4, z, core) for d in range(4)
    ]


def greet_signal(others):
    barrier = pltpu.get_barrier_semaphore()

    @pl.loop(1, NB)
    def _(shift):
        pl.semaphore_signal(barrier, inc=1, device_id=swap_partner(shift)[1], device_id_type=MESH)

    for other in others:
        pl.semaphore_signal(barrier, inc=1, device_id=other, device_id_type=MESH)


def greet_wait(others):
    pl.semaphore_wait(pltpu.get_barrier_semaphore(), NB - 1 + len(others))


FRONT_COPIES = 144


def front_kernel(
    tokens, segments, flags, vectors, b_up, w_out, w_up, w_down, w_qkv,
    x_seq, meta_out, smalls_out, out_all, up_all, down_all, qkv_all, qat_ref, ka_ref, va_ref, kt_ref, q_ref,
    context, wide_ref, lse_ref,
    vat_ref, blocks, x_buf, tok_buf, out_buf, up_buf, down_buf, qkv_buf, meta, heads, smalls, meta_all, heads_all, smalls_all, w_ref, b_ref,
    send, recv, local, meta_send, meta_recv, meta_local, back_send, back_recv, back_local,
):
    x, y, z, core = place()
    hi, lo = x // 2, x % 2
    mine, across = y * 2 + hi, y * 2 + 1 - hi
    wrap, pair, other_core = device_at(3 - x, y, z, core), device_at(hi * 2 + 1 - lo, y, z, core), sibling()
    shards, wholes = (up_buf.at[core], down_buf), (up_all, down_all)
    rows_out = half_rows(core)
    greet_signal(shard_greet())
    load_tokens = pltpu.make_async_copy(tokens, tok_buf, local.at[0])
    load_qkv = pltpu.make_async_copy(w_qkv, qkv_buf, local.at[11])
    loads = [
        pltpu.make_async_copy(w_out, out_buf, local.at[9]),
        pltpu.make_async_copy(w_down.at[half_rows(core, 256)], down_buf, local.at[10]),
    ]
    for j in range(8):
        piece = w_up.at[:, pl.ds(aligned(j * 512 + core * 256, 256), 256)]
        loads.append(pltpu.make_async_copy(piece, up_buf.at[core, :, pl.ds(j * 256, 256)], local.at[1 + j]))
    start_all([load_tokens, load_qkv] + loads)
    meta[...] = jnp.zeros_like(meta)
    for s in range(2):
        meta[s, 0:1, :] = segments[s : s + 1, :]
        meta[s, 1:2, :] = flags[s : s + 1, :]
    smalls[...] = jnp.zeros_like(smalls)
    smalls[0:8, :] = vectors[...]
    smalls[8:12, :] = b_up[...]
    greet_wait(shard_greet())
    load_tokens.wait()
    net = Transfers(send, recv)
    first, second = pl.ds(0, 64), pl.ds(64, 64)

    def block(at, low, w, rows=slice(None)):
        return x_buf.at[at, low, core, w, rows]

    own = tok_buf.at[hi]
    swap = net.copy(tok_buf.at[1 - hi], block(z, lo, hi), wrap)
    own_z = [net.copy(own, block(z, lo, hi), along("z", d)) for d in (1, 3, 2)]
    own_pair = [net.copy(own.at[rows], block(z, lo, hi, rows), pair) for rows in (first, second)]
    start_all([swap, own_pair[0]] + own_z)
    x_buf[z, lo, core, hi] = tok_buf[hi]
    load_qkv.wait()
    for p in range(3):
        for k, pair_at in ((0, z * 2 + lo), (1, z * 2 + 1 - lo)):
            heads[k, :, 128 * p : 128 * (p + 1)] = qkv_buf[:, pl.ds(aligned(p * D + pair_at * 128, 128), 128)]
    cross_first = [
        net.copy(heads.at[1], heads_all.at[mine], wrap),
        net.copy(smalls, smalls_all.at[mine], wrap),
    ]
    start_all(cross_first)
    wait_all(loads)
    cross_early, cross_late = [], []
    for m in range(2):
        for unit, columns in ((0, columns_part(m, z, 4)), (3, columns_part(m, 1 - lo, 2))):
            rows = unit_rows(m, unit)
            cross_early.append(net.copy(shards[m].at[rows, columns], wholes[m].at[mine, rows, columns], wrap))

    def small_y(shard, heads_source, smalls_source):
        copies = []
        for d in (1, 3, 2):
            copies.append(net.copy(heads_source, heads_all.at[shard], along("y", d)))
            copies.append(net.copy(smalls_source, smalls_all.at[shard], along("y", d)))
        return copies

    own_small = small_y(mine, heads.at[0], smalls)
    start_all(own_small + cross_early)
    heads_all[mine] = heads[0]
    smalls_all[mine] = smalls[...]
    meta_start, meta_wait = swap_copies(
        lambda b: meta.at[b % 2], lambda b: meta_all.at[b], (meta_send, meta_recv, meta_local)
    )
    meta_start()
    keep = [
        pltpu.make_async_copy(out_buf.at[rows_out], out_all.at[mine, rows_out], local.at[9]),
        pltpu.make_async_copy(qkv_buf, qkv_all.at[mine], local.at[11]),
    ]
    for m in range(2):
        parts = [
            (unit_rows(m, 0), columns_part(m, z, 4)),
            (unit_rows(m, 3), columns_part(m, lo, 2)),
            (unit_rows(m, 1, 2), slice(None)),
        ]
        for k, (rows, columns) in enumerate(parts):
            piece = wholes[m].at[mine, rows, columns]
            keep.append(pltpu.make_async_copy(shards[m].at[rows, columns], piece, local.at[1 + 3 * m + k]))
    start_all(keep)

    def outer_y(shard, source):
        copies = []
        for d in (1, 3, 2):
            there = along("y", d)
            for m in range(2):
                for unit, columns in ((0, columns_part(m, z, 4)), (3, columns_part(m, lo, 2))):
                    rows = unit_rows(m, unit)
                    copies.append(net.copy(source(m).at[rows, columns], wholes[m].at[shard, rows, columns], there))
        return copies

    def inner_y(m, shard, source, shifts):
        rows = unit_rows(m, 1, 2)
        return [net.copy(source.at[rows], wholes[m].at[shard, rows], along("y", d)) for d in shifts]

    def out_y(shard, source):
        return [net.copy(source.at[rows_out], out_all.at[shard, rows_out], along("y", d)) for d in (1, 3, 2)]

    def relay_y(m, w):
        copies = []
        for unit, d in ((1, 1), (2, 3)):
            piece = wholes[m].at[(y + 4 - d) % 4 * 2 + w, unit_rows(m, unit)]
            copies.append(net.copy(piece, piece, along("y", d)))
        return copies

    swap.wait_recv()
    came = block(z, 1 - lo, 1 - hi)
    came_pair = [
        net.copy(block(z, 1 - lo, 1 - hi, rows), block(z, 1 - lo, 1 - hi, rows), pair) for rows in (first, second)
    ]
    came_z = [net.copy(came, came, along("z", d)) for d in (1, 3, 2)]
    start_all([came_pair[0]] + came_z + [own_pair[1], came_pair[1]])
    for copy in cross_first:
        copy.wait_recv()
    across_small = small_y(across, heads_all.at[across], smalls_all.at[across])
    own_y = outer_y(mine, lambda m: shards[m])
    start_all(across_small + own_y)
    pair_late = []

    def forward(got, d, low, w):
        got.wait_recv()
        piece = block((z + 4 - d) % 4, low, w, second)
        pair_late.append(net.copy(piece, piece, pair))
        pair_late[-1].start()

    for i, d in enumerate((1, 3, 2)):
        forward(own_z[i], d, lo, hi)
    half_z = []

    def halves(got, low, w):
        got.wait_recv()
        piece = block(z, low, w, first)
        copies = [net.copy(piece, piece, along("z", d)) for d in (1, 3, 2)]
        start_all(copies)
        half_z.extend(copies)

    halves(own_pair[0], 1 - lo, hi)
    for copy in cross_early:
        copy.wait_recv()
    across_y = outer_y(across, lambda m: wholes[m].at[across])
    inner_down = inner_y(1, mine, down_buf, (1, 3, 2))
    out_own = out_y(mine, out_buf)
    inner_up = inner_y(0, mine, up_buf.at[core], (1, 3))
    cross_late.append(net.copy(out_buf.at[rows_out], out_all.at[mine, rows_out], wrap))
    rows = unit_rows(0, 1, 2)
    cross_late.append(net.copy(up_buf.at[core, rows], up_all.at[mine, rows], wrap))
    rows = half_rows(core)
    cross_late.append(net.copy(qkv_buf.at[rows], qkv_all.at[mine, rows], wrap))
    start_all(across_y + cross_late + inner_down + out_own + inner_up)
    for i, d in enumerate((1, 3, 2)):
        forward(came_z[i], d, 1 - lo, 1 - hi)
    halves(came_pair[0], lo, 1 - hi)
    share, rest = [], []
    for low, w in ((lo, hi), (1 - lo, 1 - hi)):
        piece = x_buf.at[:, low, core, w]
        share.append(net.copy(piece, piece, other_core))
    start_all(share)
    for copy in cross_late[:2]:
        copy.wait_recv()
    out_across = out_y(across, out_all.at[across])
    across_up = inner_y(0, across, up_all.at[across], (1, 3))
    start_all(out_across + across_up)

    for copy in own_small + across_small:
        copy.wait_recv()
    meta_wait()
    at_first = core == 0
    both = heads_all[...].reshape(D, 384)
    parts = [jnp.where(at_first, both[:, 128 * p : 128 * p + HD], both[:, 128 * p + HD : 128 * (p + 1)]) for p in range(3)]
    w_ref[...] = jnp.concatenate(parts, axis=1)
    biases = smalls_all[lax.axis_index("seq") // 2]
    bias = [jnp.where(at_first, biases[k : k + 1, :HD], biases[k : k + 1, HD:]) for k in range(2)]
    b_ref[...] = jnp.broadcast_to(jnp.concatenate([bias[0], jnp.zeros((1, HD), F32), bias[1]], axis=1), (8, 3 * HD))

    def project(low, at_core, w):
        sides = dot(x_buf[:, low, at_core, w].reshape(4 * TB, D), w_ref[...]) + b_ref[:1, :]
        for at in range(4):
            b = at * 8 + low * 4 + at_core * 2 + w
            rows = pl.ds(aligned(b * TB, TB), TB)
            side = sides[at * TB : (at + 1) * TB]
            q8 = side[:, :HD].astype(BF).astype(F32) * 0.125
            hot = jnp.where(lax.broadcasted_iota(jnp.int32, (32, TB), 0) == meta_all[b, 0:1, :], 1.0, 0.0)
            lane = lax.broadcasted_iota(jnp.int32, (TB, HD), 1)
            ones3 = jnp.where(lane < 3, 1.0, 0.0)
            apart = (hot.T - 1.0) * MASKED
            key = side[:, HD : 2 * HD]
            value = side[:, 2 * HD :]
            q_ref[rows, :] = q8.astype(BF)
            ka_ref[rows, :] = jnp.concatenate([key, apart, ones3[:, :32]], axis=1).astype(BF)
            va_ref[rows, :] = jnp.concatenate([value, ones3], axis=1).astype(BF)
            qat_ref[:, rows] = jnp.concatenate([q8.T, hot, jnp.zeros((32, TB), F32)], axis=0).astype(BF)
            kt_ref[:, rows] = key.T.astype(BF)
            ones_row = jnp.where(lax.broadcasted_iota(jnp.int32, (16, TB), 0) == 0, 1.0, 0.0)
            vat_ref[:, rows] = jnp.concatenate([value.T, ones_row], axis=0).astype(BF)

    project(lo, core, hi)
    project(1 - lo, core, 1 - hi)
    for copy in half_z + [own_pair[1], came_pair[1]] + pair_late:
        copy.wait_recv()
    for low, w in ((1 - lo, hi), (lo, 1 - hi)):
        piece = x_buf.at[:, low, core, w]
        rest.append(net.copy(piece, piece, other_core))
    start_all(rest)
    for copy in share:
        copy.wait_recv()
    project(1 - lo, core, hi)
    project(lo, core, 1 - hi)
    project(lo, 1 - core, hi)
    project(1 - lo, 1 - core, 1 - hi)
    for copy in rest:
        copy.wait_recv()
    store = pltpu.make_async_copy(x_buf, x_seq, local.at[0])
    store.start()
    project(1 - lo, 1 - core, hi)
    project(lo, 1 - core, 1 - hi)
    meta_out[...] = meta_all[...]
    smalls_out[...] = smalls_all[...]

    wait_all(keep)
    for copy in own_y + across_y:
        copy.wait_recv()
    later, inner_wrap = [], []
    for m in range(2):
        piece = wholes[m].at[:, unit_rows(m, 3), columns_part(m, lo, 2)]
        later.append(net.copy(piece, piece, pair))
        for d in (1, 3, 2):
            piece = wholes[m].at[:, unit_rows(m, 0), columns_part(m, z, 4)]
            later.append(net.copy(piece, piece, along("z", d)))
    for d in range(4):
        piece = down_all.at[(y + d) % 4 * 2 + hi, unit_rows(1, 1, 2)]
        inner_wrap.append(net.copy(piece, piece, wrap))
    piece = out_all.at[:, half_rows(core)]
    share_out = net.copy(piece, piece, other_core)
    relay_up = relay_y(0, hi) + relay_y(0, 1 - hi)
    start_all(later)

    position = lax.axis_index("seq") * 2 + hi

    def result(b, recv_at):
        there = head_tile(context, position)
        return remote(blocks.at[b], there, back_send.at[b], back_recv.at[recv_at], (y, b // 2, b % 2))

    own_result = pltpu.make_async_copy(blocks.at[position], head_tile(context, position), back_local)

    @pl.loop(0, 4)
    def _(step):
        at = (step + z + 1) % 4
        columns = pl.ds(aligned(at * 1024, 1024), 1024)
        queries = qat_ref[:, columns]
        peak = jnp.full((1, 1024), -jnp.inf, F32)
        total = jnp.zeros((80, 1024), F32)
        for j in range(8):
            keys = slice(j * 512, (j + 1) * 512)
            logits = dot(ka_ref[keys, :], queries)
            new_peak = jnp.maximum(peak, jnp.max(logits, axis=0, keepdims=True))
            expos = jnp.exp(logits - new_peak).astype(BF)
            total = total * jnp.exp(peak - new_peak) + dot(vat_ref[:, keys], expos)
            peak = new_peak
        sums = total[HD : HD + 1]
        found = total[:HD] / sums
        wide_ref[:, columns] = found
        lse_ref[:, columns] = peak + jnp.log(sums)
        low = found.astype(BF)
        for j in range(8):
            b = at * 8 + j
            blocks[b] = low[:, j * TB : (j + 1) * TB]

            @pl.when(b != position)
            def _():
                result(b, position).start()

            @pl.when(b == position)
            def _():
                own_result.start()

        @pl.when(step == 0)
        def _():
            for copy in inner_down:
                copy.wait_recv()
            start_all(inner_wrap)

        @pl.when(step == 2)
        def _():
            for copy in out_own + out_across + inner_up + across_up:
                copy.wait_recv()
            start_all([share_out] + relay_up)

    store.wait()
    for copy in [swap] + own_pair + own_z + came_pair + came_z + half_z + pair_late + share + rest:
        copy.wait_send()
    for copy in cross_first + cross_early + cross_late + own_small + across_small + own_y + across_y + inner_down:
        copy.wait_send()
    for copy in out_own + out_across + inner_up + across_up:
        copy.wait_send()
    cross_late[2].wait_recv()
    wait_all([share_out] + relay_up + later + inner_wrap)

    @pl.loop(1, NB)
    def _(shift):
        b = (position + shift) % NB
        result(b, b).wait()

    own_result.wait()


def front(tokens, segments, flags, vectors, b_up, w_out, w_up, w_down, w_qkv):
    shape = jax.ShapeDtypeStruct
    in_vmem = pl.BlockSpec(memory_space=pltpu.VMEM)
    return pl.pallas_call(
        front_kernel,
        in_specs=[ANY] + [in_vmem] * 4 + [ANY] * 4,
        out_specs=[ANY] + [in_vmem] * 2 + [ANY] * 4 + [in_vmem] * 5 + [ANY] + [in_vmem] * 2,
        out_shape=[
            shape((4, 2, 2, 2, TB, D), BF),
            shape((NB, 8, TB), jnp.int32),
            shape((8, 16, 128), F32),
            shape((8, 128, D), BF),
            shape((8, 128, 2048), BF),
            shape((8, 256, D), BF),
            shape((8, 128, 3 * D), BF),
            shape((128, L), BF),
            shape((L, 128), BF),
            shape((L, 128), BF),
            shape((HD, L), BF),
            shape((L, HD), BF),
            shape((D, 2 * TB), BF),
            shape((HD, L), F32),
            shape((1, L), F32),
        ],
        scratch_shapes=[
            pltpu.VMEM((80, L), BF),
            pltpu.VMEM((NB, HD, TB), BF),
            pltpu.VMEM((4, 2, 2, 2, TB, D), BF),
            pltpu.VMEM((2, TB, D), BF),
            pltpu.VMEM((128, D), BF),
            pltpu.VMEM((2, 128, 2048), BF),
            pltpu.VMEM((256, D), BF),
            pltpu.VMEM((128, 3 * D), BF),
            pltpu.VMEM((2, 8, TB), jnp.int32),
            pltpu.VMEM((2, 128, 384), BF),
            pltpu.VMEM((16, 128), F32),
            pltpu.VMEM((NB, 8, TB), jnp.int32),
            pltpu.VMEM((8, 128, 384), BF),
            pltpu.VMEM((8, 16, 128), F32),
            pltpu.VMEM((D, 3 * HD), BF),
            pltpu.VMEM((8, 3 * HD), F32),
            pltpu.SemaphoreType.DMA((FRONT_COPIES,)),
            pltpu.SemaphoreType.DMA((FRONT_COPIES,)),
            pltpu.SemaphoreType.DMA((12,)),
            *swap_sems(),
            *swap_sems(),
        ],
        name="front",
        compiler_params=pltpu.CompilerParams(
            collective_id=1, has_side_effects=True, vmem_limit_bytes=VMEM_CAP
        ),
    )(tokens, segments, flags, vectors, b_up, w_out, w_up, w_down, w_qkv)


def qkv_along_y(qkv_all, net):
    _, y, _, core = place()
    copies = []
    for d in (1, 3, 2):
        for w in range(2):
            piece = qkv_all.at[y * 2 + w, half_rows(core)]
            copies.append(net.copy(piece, piece, along("y", d)))
    return copies


def turned(first, second):
    return dot(first, second, ((0,), (0,)))


def gelu_both(u):
    rate = 0.7978845608028654
    square = u * u
    curve = jnp.tanh(rate * (u + 0.044715 * (square * u)))
    half = 0.5 * (1.0 + curve)
    slope = half + 0.5 * u * (1.0 - curve * curve) * (rate * (1.0 + 0.134145 * square))
    return u * half, slope


def fold(values):
    return jnp.sum(values.reshape(values.shape[0] // 8, 8, values.shape[1]), axis=0)


ROWS = 256
CHUNK = 32
SMALLS = 16


def middle_kernel(
    context_in, meta, tokens, teacher, flags, smalls, out_all, up_all, down_all, a0,
    states, resid_out, do, g_ref, sums_out, count_out, qkv_all,
    context, context_s, w_out, w_up, w_down, h, act, slope, send_one, come_one, send_two, come_two,
    gb, gu, ga, ga_s, normed, hidden, rate, work, resid, gct, stage, count, counts, valid,
    send, recv, local, back_send, back_recv, back_local,
):
    x, y, z, core = place()
    mine = y * 2 + x // 2
    twin = sibling()
    loads = [
        pltpu.make_async_copy(context_in, context, local.at[6]),
        pltpu.make_async_copy(out_all, w_out, local.at[0]),
        pltpu.make_async_copy(up_all, w_up, local.at[1]),
    ]
    load_down = pltpu.make_async_copy(down_all, w_down, local.at[2])
    start_all(loads + [load_down])
    greet_signal(shard_greet())
    greet_wait(shard_greet())
    net = Transfers(send, recv)
    later = qkv_along_y(qkv_all, net)
    valid_here = jnp.sum(meta[:, 1, :].astype(F32), axis=0, keepdims=True)
    count[...] = jnp.broadcast_to(jnp.sum(valid_here, axis=1, keepdims=True), (8, 128))
    ahead = [net.copy(count, counts.at[mine], target) for target in shard_greet()]
    start_all(ahead + later)
    own_count = pltpu.make_async_copy(count, counts.at[mine], local.at[3])
    own_count.start()
    for s in range(2):
        column = jnp.broadcast_to(flags[s : s + 1, :].astype(F32), (128, 128)).T
        valid[128 * s : 128 * (s + 1), :] = column

    def vector(row):
        return jnp.concatenate([smalls[i, row : row + 1, :] for i in range(8)], axis=1)

    out_bias, gain_one, offset_one, down_bias, gain_two, offset_two = [vector(row) for row in range(2, 8)]
    zeros = jnp.zeros((8, D), F32)
    wait_all(loads)
    give_context = net.copy(context, context_s, twin)
    give_context.start()
    work[...] = turned(context[...], w_out[...].reshape(D, D))

    @pl.loop(0, ROWS // CHUNK)
    def _(i):
        rows = pl.ds(aligned(i * CHUNK, CHUNK), CHUNK)
        total = tokens[rows, :].astype(F32) + work[rows, :] + out_bias
        centre = total - jnp.mean(total, axis=1, keepdims=True)
        scale = lax.rsqrt(jnp.mean(centre * centre, axis=1, keepdims=True) + EPS)
        unit = centre * scale
        normed[rows, :] = unit
        rate[rows, :] = jnp.broadcast_to(scale, (CHUNK, 128))
        full = unit * gain_one + offset_one
        hidden[rows, :] = full
        h[0, rows, :] = full.astype(BF)

    give_hidden = net.copy(h.at[0], h.at[1], twin)
    give_hidden.start()
    for slot in range(2):
        if slot == 1:
            give_hidden.wait()
        for k in range(8):
            columns = slice(256 * k, 256 * (k + 1))
            bias = jnp.concatenate([smalls[k, pl.ds(8 + 2 * core + e, 1), :] for e in range(2)], axis=1)
            u = dot(h[slot], w_up[:, :, columns].reshape(D, 256)) + bias
            value, incline = gelu_both(u)
            act[slot, :, columns] = value.astype(BF)
            slope[slot, :, columns] = incline
    load_down.wait()
    send_one[...] = dot(act[1], w_down[...].reshape(2048, D))
    give_one = net.copy(send_one, come_one, twin)
    give_one.start()
    work[...] = dot(act[0], w_down[...].reshape(2048, D))
    give_one.wait()
    wait_all(ahead)
    own_count.wait()
    total_count = jnp.sum(counts[...], axis=0)
    count_out[...] = total_count
    factor = (128 * ROWS) / total_count[:1, :1]

    def loss_rows(i, carried):
        rows = pl.ds(aligned(i * CHUNK, CHUNK), CHUNK)
        total = hidden[rows, :] + (work[rows, :] + come_one[rows, :] + down_bias)
        centre = total - jnp.mean(total, axis=1, keepdims=True)
        scale = lax.rsqrt(jnp.mean(centre * centre, axis=1, keepdims=True) + EPS)
        unit = centre * scale
        final = unit * gain_two + offset_two
        states[rows, :] = final.astype(BF)
        differ = final - teacher[rows, :].astype(F32)
        held = valid[rows, :1] * differ
        grad = factor * held
        weighted = grad * gain_two
        back = weighted - jnp.mean(weighted, axis=1, keepdims=True)
        back = scale * (back - unit * jnp.mean(weighted * unit, axis=1, keepdims=True))
        resid[rows, :] = back
        low = back.astype(BF)
        gb[0, rows, :] = low
        return (
            carried[0] + fold(grad * unit),
            carried[1] + fold(grad),
            carried[2] + fold(low.astype(F32)),
            carried[3] + fold(held * differ),
        )

    gain_two_sum, offset_two_sum, down_sum, error = lax.fori_loop(
        0, ROWS // CHUNK, loss_rows, (zeros, zeros, zeros, zeros)
    )
    give_branch = net.copy(gb.at[0], gb.at[1], twin)
    give_branch.start()
    up_sums = []
    for slot in range(2):
        if slot == 1:
            give_branch.wait()
        for k in range(8):
            columns = slice(256 * k, 256 * (k + 1))
            pulled = dot(gb[slot], w_down[k], ((1,), (1,))) * slope[slot, :, columns]
            low = pulled.astype(BF)
            gu[slot, :, columns] = low
            up_sums.append(fold(low.astype(F32)))
    for i in range(8):
        send_two[:, 128 * i : 128 * (i + 1)] = dot(gu[1], w_up[i], ((1,), (1,)))
    give_two = net.copy(send_two, come_two, twin)
    give_two.start()
    for i in range(8):
        work[:, 128 * i : 128 * (i + 1)] = dot(gu[0], w_up[i], ((1,), (1,)))
    give_two.wait()

    def first_norm_rows(i, carried):
        rows = pl.ds(aligned(i * CHUNK, CHUNK), CHUNK)
        grad = resid[rows, :] + (work[rows, :] + come_two[rows, :])
        unit = normed[rows, :]
        weighted = grad * gain_one
        back = weighted - jnp.mean(weighted, axis=1, keepdims=True)
        back = rate[rows, :1] * (back - unit * jnp.mean(weighted * unit, axis=1, keepdims=True))
        resid_out[rows, :] = back
        low = back.astype(BF)
        ga[rows, :] = low
        return (carried[0] + fold(grad * unit), carried[1] + fold(grad), carried[2] + fold(low.astype(F32)))

    gain_one_sum, offset_one_sum, out_sum = lax.fori_loop(0, ROWS // CHUNK, first_norm_rows, (zeros, zeros, zeros))
    give_attended = net.copy(ga.at[:, pl.ds(aligned((1 - core) * 512, 512), 512)], ga_s, twin)
    give_attended.start()
    gct[...] = dot(w_out[...].reshape(D, D), ga[...], ((1,), (1,))).astype(BF)
    back_start, back_wait = swap_copies(
        lambda b: head_tile(gct, b), lambda b: do.at[b], (back_send, back_recv, back_local)
    )
    back_start()

    error = jnp.broadcast_to(jnp.sum(jnp.sum(error, axis=0, keepdims=True), axis=1, keepdims=True), (1, 128))
    lines = [out_sum, gain_one_sum, offset_one_sum, down_sum, gain_two_sum, offset_two_sum]
    lines = [jnp.sum(line, axis=0, keepdims=True) for line in lines]
    for i in range(8):
        columns = slice(128 * i, 128 * (i + 1))
        sums_out[i] = jnp.zeros((SMALLS, 128), F32)
        for row, line in enumerate(lines):
            sums_out[i, row : row + 1, :] = line[:, columns]
        both = jnp.sum(up_sums[i] + up_sums[8 + i], axis=0, keepdims=True)
        for e in range(2):
            sums_out[i, pl.ds(6 + 2 * core + e, 1), :] = both[:, 128 * e : 128 * (e + 1)]
        sums_out[i, 10:11, :] = error

    give_context.wait()
    give_attended.wait()

    def stored(i):
        return pltpu.make_async_copy(stage.at[i % 2], g_ref.at[i // 2, i % 2], local.at[4 + i % 2])

    for i in range(8):
        if i >= 2:
            stored(i - 2).wait()
        tall = slice(128 * i, 128 * (i + 1))
        wide = slice(256 * i, 256 * (i + 1))
        up = turned(h[0, :, tall], gu[0]) + turned(h[1, :, tall], gu[1])
        for k in range(4):
            stage[i % 2, 128 * k : 128 * (k + 1), :] = up[:, 512 * k : 512 * (k + 1)].astype(BF)
        down = turned(act[0, :, wide], gb[0]) + turned(act[1, :, wide], gb[1])
        for k in range(2):
            stage[i % 2, 512 + 256 * k : 768 + 256 * k, :] = down[:, 512 * k : 512 * (k + 1)].astype(BF)
        own_half = ga[:, pl.ds(aligned(core * 512, 512), 512)]
        out = dot(context[tall, :], own_half) + dot(context_s[tall, :], ga_s[...])
        stage[i % 2, 1024:, :] = out.astype(BF)
        stored(i).start()
    stored(6).wait()
    stored(7).wait()
    back_wait()
    wait_all(later)


def middle(context, meta, tokens, teacher, flags, smalls, out_all, up_all, down_all, qkv_all):
    shape = jax.ShapeDtypeStruct
    in_vmem = pl.BlockSpec(memory_space=pltpu.VMEM)
    dma = pltpu.SemaphoreType.DMA
    wide = pltpu.VMEM((ROWS, D), F32)
    return pl.pallas_call(
        middle_kernel,
        in_specs=[ANY] + [in_vmem] * 5 + [ANY] * 4,
        out_specs=[in_vmem, in_vmem, ANY, ANY, in_vmem, in_vmem, ANY],
        out_shape=[
            shape((ROWS, D), BF),
            shape((ROWS, D), F32),
            shape((NB, HD, TB), BF),
            shape((4, 2, 1152, 512), BF),
            shape((8, SMALLS, 128), F32),
            shape((8, 128), F32),
            shape(qkv_all.shape, BF),
        ],
        input_output_aliases={9: 6},
        scratch_shapes=[
            pltpu.VMEM((D, ROWS), BF),
            pltpu.VMEM((D, ROWS), BF),
            pltpu.VMEM((8, 128, D), BF),
            pltpu.VMEM((8, 128, 2048), BF),
            pltpu.VMEM((8, 256, D), BF),
            pltpu.VMEM((2, ROWS, D), BF),
            pltpu.VMEM((2, ROWS, 2048), BF),
            pltpu.VMEM((2, ROWS, 2048), F32),
            wide,
            wide,
            wide,
            wide,
            pltpu.VMEM((2, ROWS, D), BF),
            pltpu.VMEM((2, ROWS, 2048), BF),
            pltpu.VMEM((ROWS, D), BF),
            pltpu.VMEM((ROWS, 512), BF),
            wide,
            wide,
            pltpu.VMEM((ROWS, 128), F32),
            wide,
            wide,
            pltpu.VMEM((D, ROWS), BF),
            pltpu.VMEM((2, 1152, 512), BF),
            pltpu.VMEM((8, 128), F32),
            pltpu.VMEM((8, 8, 128), F32),
            pltpu.VMEM((ROWS, 128), F32),
            dma((32,)),
            dma((32,)),
            dma((10,)),
            *swap_sems(),
        ],
        name="middle",
        compiler_params=pltpu.CompilerParams(
            collective_id=3, has_side_effects=True, vmem_limit_bytes=VMEM_CAP
        ),
    )(context, meta, tokens, teacher, flags, smalls, out_all, up_all, down_all, qkv_all)


BACK_KEYS = 256
BACK_STEPS = L // BACK_KEYS
BACK_WIDTH = 1024


def back_prepare(qat, do, wide, lse, queries, grads, grad_rows):
    for j in range(L // BACK_WIDTH):
        columns = slice(j * BACK_WIDTH, (j + 1) * BACK_WIDTH)
        grad_t = jnp.concatenate([do[j * (BACK_WIDTH // TB) + i] for i in range(BACK_WIDTH // TB)], axis=1)
        wider = grad_t.astype(F32)
        delta = jnp.sum(wider * wide[:, columns], axis=0, keepdims=True)
        grads[:HD, columns] = grad_t
        grads[HD:, columns] = jnp.concatenate([three_pieces(-delta), jnp.zeros((61, BACK_WIDTH), BF)], axis=0)
        queries[:96, columns] = qat[:96, columns]
        queries[96:, columns] = jnp.concatenate(
            [three_pieces(-lse[:, columns]), jnp.zeros((29, BACK_WIDTH), BF)], axis=0
        )
        grad_rows[columns, :] = wider.T.astype(BF)


def back_kernel(
    qat_in, ka_in, va_in, kt_in, q8_in, do_in, wide_in, lse, smalls, x_seq, g_ref, a0,
    projected, heads_out, shard_out, smalls_out, qkv_all,
    qat, ka, va, kt, q8, do, wide, input_sems,
    x_buf, queries, grads, grad_rows, dq, d_ref, mine_ref, parts_ref, sum_ref, heads_buf, small_buf, small_sum, small_all,
    send, recv, local, dk_send, dk_recv, dk_local, dq_send, dq_recv, dq_local, spread_send, spread_recv, *reduce_refs,
):
    x, y, z, core = place()
    shard_at = y * 2 + x // 2
    seq = lax.axis_index("seq")
    mine = seq * 2 + x // 2
    net = (g_ref,) + reduce_refs

    def shard_device(d):
        other = (shard_at + d) % 8
        return other, (other // 2, seq, other % 2)

    load_x = pltpu.make_async_copy(x_seq, x_buf, local.at[0])
    held = (qat, do, wide, ka, va, kt, q8)
    loads = [
        pltpu.make_async_copy(src, dst, input_sems.at[k])
        for k, (src, dst) in enumerate(zip((qat_in, do_in, wide_in, ka_in, va_in, kt_in, q8_in), held))
    ]
    shard_others = [shard_device(d)[1] for d in range(1, 8)]
    greet_signal(shard_others)
    start_all(loads)
    dq[...] = jnp.zeros_like(dq)
    greet_wait(shard_others)
    for part in range(3):
        reduce_start(part, net)
    wait_all(loads)
    load_x.start()
    back_prepare(qat, do, wide, lse, queries, grads, grad_rows)
    far = Transfers(send, recv)
    small_out = [far.copy(smalls.at[shard_device(d)[0]], small_buf.at[shard_at], shard_device(d)[1]) for d in range(1, 8)]
    start_all(small_out)
    small_buf[shard_at] = smalls[shard_at]
    rows = half_rows(core)
    weights = far.copy(qkv_all.at[:, rows], qkv_all.at[:, rows], sibling())
    weights.start()

    def landing(first, count):
        return projected.at[pl.ds(first, count), pl.ds(aligned(seq * HD, HD), HD), pl.ds(aligned((x // 2) * TB, TB), TB)]

    def block_device(b):
        return (y, b // 2, b % 2)

    def dk_copy(b, recv_at):
        return remote(d_ref.at[b, pl.ds(1, 2)], landing(1, 2), dk_send.at[b], dk_recv.at[recv_at], block_device(b))

    def dq_copy(b, recv_at):
        return remote(d_ref.at[b, pl.ds(0, 1)], landing(0, 1), dq_send.at[b], dq_recv.at[recv_at], block_device(b))

    dk_own = pltpu.make_async_copy(d_ref.at[mine, pl.ds(1, 2)], landing(1, 2), dk_local)
    dq_own = pltpu.make_async_copy(d_ref.at[mine, pl.ds(0, 1)], landing(0, 1), dq_local)

    steps = [
        spread_steps(part, reduce_refs[6 + part].at[0], (local.at[pl.ds(1, 3)], spread_send, spread_recv), shard_out)
        for part in range(3)
    ]

    @pl.loop(0, BACK_STEPS)
    def _(step):
        at = (step + seq) % BACK_STEPS
        keys = pl.ds(aligned(at * BACK_KEYS, BACK_KEYS), BACK_KEYS)
        ka_part, va_part, kt_part = ka[keys, :], va[keys, :], kt[:, keys]
        dk = jnp.zeros((BACK_KEYS, HD), F32)
        dv = jnp.zeros((BACK_KEYS, HD), F32)
        for j in range(L // BACK_WIDTH):
            columns = slice(j * BACK_WIDTH, (j + 1) * BACK_WIDTH)
            probs = jnp.exp(dot(ka_part, queries[:, columns]))
            raw = (probs * dot(va_part, grads[:, columns])).astype(BF)
            dv = dv + dot(probs.astype(BF), grad_rows[columns, :])
            dk = dk + dot(raw, q8[columns, :])
            dq[:, columns] += dot(kt_part, raw)
        dk_t, dv_t = dk.T.astype(BF), dv.T.astype(BF)
        for i in range(BACK_KEYS // TB):
            b = at * (BACK_KEYS // TB) + i
            d_ref[b, 1] = dk_t[:, i * TB : (i + 1) * TB]
            d_ref[b, 2] = dv_t[:, i * TB : (i + 1) * TB]

            @pl.when(b != mine)
            def _():
                dk_copy(b, mine).start()

            @pl.when(b == mine)
            def _():
                dk_own.start()

        @pl.when(step == 3)
        def _():
            for part in (1, 2, 0):
                first_relay(part, net)

        @pl.when(step == 8)
        def _():
            reduce_step(0, 1, net)

        @pl.when(step == 9)
        def _():
            reduce_step(0, 2, net)

        @pl.when(step == 10)
        def _():
            reduce_step(0, 0, net)

        @pl.when(step == 12)
        def _():
            reduce_step(1, 1, net)

        @pl.when(step == 14)
        def _():
            reduce_step(1, 2, net)
            reduce_step(2, 1, net)
            steps[1][0]()

    reduce_step(1, 0, net)
    for b in range(NB):
        d_ref[b, 0] = (dq[:, b * TB : (b + 1) * TB] * 0.125).astype(BF)

    load_x.wait()
    left = jnp.concatenate([d_ref[b].reshape(3 * HD, TB) for b in range(NB)], axis=1)
    sums = dot(jnp.ones((8, L), BF), left, ((1,), (1,)))
    gap = jnp.zeros((1, 128 - HD), F32)
    tail = jnp.concatenate(
        [
            jnp.concatenate([sums[:1, :HD], gap], axis=1),
            jnp.concatenate([sums[:1, 2 * HD :], gap], axis=1),
            jnp.zeros((14, 128), F32),
        ],
        axis=0,
    ).astype(BF)
    for i in range(4):
        total = dot(left, x_buf[:, :, 256 * i : 256 * (i + 1)].reshape(L, 256))
        for k in range(2):
            mine_ref[2 * i + k, : 3 * HD, :] = total[:, 128 * k : 128 * (k + 1)].astype(BF)
            mine_ref[2 * i + k, 3 * HD :, :] = tail
    part_out = [far.copy(mine_ref.at[shard_device(d)[0]], parts_ref.at[d], shard_device(d)[1]) for d in range(1, 8)]
    start_all(part_out)
    for part in (2, 0):
        reduce_step(2, part, net)
        steps[part][0]()

    @pl.loop(1, NB)
    def _(shift):
        dq_copy((mine + shift) % NB, mine).start()

    dq_own.start()
    wait_all(small_out)
    small_sum[...] = jnp.sum(small_buf[...], axis=0)
    wait_all(part_out)
    added = mine_ref[shard_at].astype(F32)
    for d in range(1, 8):
        added = added + parts_ref[d].astype(F32)
    sum_ref[...] = added.astype(BF)
    heads_buf[seq // 2, core] = sum_ref[...]
    small_all[seq // 2, core] = small_sum[...]
    head_out = []
    for d in range(1, 8):
        target = (y, (seq + 2 * d) % 16, x // 2)
        head_out.append(far.copy(sum_ref, heads_buf.at[seq // 2, core], target))
        head_out.append(far.copy(small_sum, small_all.at[seq // 2, core], target))
    start_all(head_out)
    for part in (1, 2, 0):
        steps[part][1]()
    wait_all(head_out)
    across = [
        far.copy(heads_buf.at[:, core], heads_buf.at[:, core], sibling()),
        far.copy(small_all.at[:, core], small_all.at[:, core], sibling()),
    ]
    start_all(across)
    shared = []
    for part in (1, 2, 0):
        steps[part][2]()
        piece = shard_out.at[core, pl.ds(FIRST[part], 8 * PIECE[part])]
        shared.append(far.copy(piece, piece, sibling()))
        shared[-1].start()

    @pl.loop(1, NB)
    def _(shift):
        b = (mine + shift) % NB
        dk_copy(b, b).wait()
        dq_copy(b, b).wait()

    dk_own.wait()
    dq_own.wait()
    weights.wait()
    wait_all(across)
    for i in range(8):
        heads_out[2 * i] = heads_buf[i, 0]
        heads_out[2 * i + 1] = heads_buf[i, 1]
    smalls_out[...] = jnp.sum(small_all[...].reshape(16, 16, 128), axis=0)
    wait_all(shared)


def back(qat, ka, va, kt, q8, do, wide, lse, smalls, x_seq, g, qkv_all):
    shape = jax.ShapeDtypeStruct
    in_vmem = pl.BlockSpec(memory_space=pltpu.VMEM)
    dma = pltpu.SemaphoreType.DMA
    return pl.pallas_call(
        back_kernel,
        in_specs=[ANY] * 7 + [in_vmem] * 2 + [ANY] * 3,
        out_specs=[ANY, in_vmem, ANY, in_vmem, ANY],
        out_shape=[
            shape((3, D, 2 * TB), BF),
            shape((H, 208, 128), BF),
            shape((2, 1152, 512), BF),
            shape((16, 128), F32),
            shape(qkv_all.shape, BF),
        ],
        input_output_aliases={11: 4},
        scratch_shapes=[
            pltpu.VMEM((128, L), BF),
            pltpu.VMEM((L, 128), BF),
            pltpu.VMEM((L, 128), BF),
            pltpu.VMEM((HD, L), BF),
            pltpu.VMEM((L, HD), BF),
            pltpu.VMEM((NB, HD, TB), BF),
            pltpu.VMEM((HD, L), F32),
            dma((7,)),
            pltpu.VMEM((NB, TB, D), BF),
            pltpu.VMEM((128, L), BF),
            pltpu.VMEM((128, L), BF),
            pltpu.VMEM((L, HD), BF),
            pltpu.VMEM((HD, L), F32),
            pltpu.VMEM((NB, 3, HD, TB), BF),
            pltpu.VMEM((8, 208, 128), BF),
            pltpu.VMEM((8, 208, 128), BF),
            pltpu.VMEM((208, 128), BF),
            pltpu.VMEM((8, 2, 208, 128), BF),
            pltpu.VMEM((8, 16, 128), F32),
            pltpu.VMEM((16, 128), F32),
            pltpu.VMEM((8, 2, 16, 128), F32),
            dma((40,)),
            dma((40,)),
            dma((4,)),
            *swap_sems(),
            *swap_sems(),
            dma((3, 8)),
            dma((3, 8)),
            *reduce_scratch(),
        ],
        name="attend_back",
        compiler_params=pltpu.CompilerParams(
            collective_id=4, has_side_effects=True, vmem_limit_bytes=VMEM_CAP
        ),
    )(qat, ka, va, kt, q8, do, wide, lse, smalls, x_seq, g, qkv_all)


def finish_kernel(
    projected, qkv_ref, resid_ref, heads_ref, shard_ref, smalls_ref, count_ref, states_ref,
    tokens_ref, grad_qkv, grad_out, grad_up, grad_down, states_out, loss_ref,
    q_bias, v_bias, o_bias, gain_one, bias_one, d_bias, gain_two, bias_two, u_bias,
    sides,
):
    step = pl.program_id(0)

    @pl.when(step == 0)
    def _():
        sides[...] = projected[...].astype(F32).T.astype(BF)
        x, y, _, _ = place()
        shard_at = y * 2 + x // 2
        for row, out in enumerate((q_bias, v_bias)):
            both = [heads_ref[shard_at * 2 + k, 3 * HD + row, :HD].astype(F32) for k in range(2)]
            out[...] = jnp.concatenate(both)
        for row, out in enumerate((o_bias, gain_one, bias_one, d_bias, gain_two, bias_two)):
            out[...] = smalls_ref[row, :]
        u_bias[...] = jnp.concatenate([smalls_ref[6 + k, :] for k in range(4)])
        loss_ref[...] = smalls_ref[10:11, :1] / (D * count_ref[:1, :1])
        for p in range(3):
            for pair in range(8):
                both = [heads_ref[2 * pair + k, p * HD : (p + 1) * HD, :].astype(F32) for k in range(2)]
                at = p * D + pair * 128
                grad_qkv[:, at : at + 128] = jnp.concatenate(both, axis=0).T

    states_out[...] = states_ref[...]
    tokens_ref[...] = resid_ref[...] + dot(sides[...], qkv_ref[...], ((1,), (1,)))
    for c in range(2):
        columns = slice(512 * c, 512 * (c + 1))
        for j in range(2):
            piece = shard_ref[c, pl.ds(aligned(step * 128, 128), 128), 256 * j : 256 * (j + 1)]
            grad_up[:, 512 * j + 256 * c : 512 * j + 256 * (c + 1)] = piece.astype(F32)
        rows = pl.ds(aligned(512 + 256 * c + (step % 2) * 128, 128), 128)
        grad_down[:, columns] = shard_ref[step // 2, rows, :].astype(F32)
        grad_out[:, columns] = shard_ref[c, pl.ds(aligned(1024 + step * 32, 32), 32), :].astype(F32)


def finish(projected, qkv, resid, heads, shard, smalls, count, states):
    shape = jax.ShapeDtypeStruct

    def whole(*dims):
        return pl.BlockSpec(dims, lambda i: (0,) * len(dims))

    part = pl.BlockSpec((2 * TB, 256), lambda i: (0, i))
    return pl.pallas_call(
        finish_kernel,
        grid=(4,),
        in_specs=[
            whole(3 * D, 2 * TB),
            pl.BlockSpec((256, 3 * D), lambda i: (i, 0)),
            part,
            whole(H, 208, 128),
            whole(2, 1152, 512),
            whole(16, 128),
            whole(8, 128),
            part,
        ],
        out_specs=[
            part,
            whole(128, 3 * D),
            pl.BlockSpec((32, D), lambda i: (i, 0)),
            pl.BlockSpec((128, 1024), lambda i: (0, i)),
            pl.BlockSpec((128, D), lambda i: (i, 0)),
            part,
            whole(1, 1),
        ]
        + [whole(128)] * 8
        + [whole(512)],
        out_shape=[
            shape((2 * TB, D), F32),
            shape((128, 3 * D), F32),
            shape((128, D), F32),
            shape((128, FF), F32),
            shape((512, D), F32),
            shape((2 * TB, D), BF),
            shape((1, 1), F32),
        ]
        + [shape((128,), F32)] * 8
        + [shape((512,), F32)],
        scratch_shapes=[pltpu.VMEM((2 * TB, 3 * D), BF)],
        name="finish",
        compiler_params=pltpu.CompilerParams(vmem_limit_bytes=VMEM_CAP),
    )(projected, qkv, resid, heads, shard, smalls, count, states)


def on_device(
    tokens,
    segments,
    valid_flags,
    teacher,
    w_qkv,
    b_query,
    b_value,
    w_out,
    b_out,
    ln1_gain,
    ln1_bias,
    w_up,
    b_up,
    w_down,
    b_down,
    ln2_gain,
    ln2_bias,
):
    seq_local, row_local, _ = tokens.shape
    token_rows = seq_local * row_local

    vectors = jnp.stack([b_query, b_value, b_out, ln1_gain, ln1_bias, b_down, ln2_gain, ln2_bias]).astype(F32)
    (
        x_seq, meta_all, smalls_all, out_all, up_all, down_all, qkv_all, qat, ka, va, kt, q8, context, wide, lse
    ) = front(
        tokens, segments, valid_flags, vectors, b_up.reshape(4, 128).astype(F32), w_out, w_up, w_down, w_qkv
    )
    x_seq = x_seq.reshape(NB, TB, D)
    states, grad_resid_one, do, g, small_sums, count, qkv_all = middle(
        context,
        meta_all,
        tokens.reshape(token_rows, D),
        teacher.reshape(token_rows, D),
        valid_flags,
        smalls_all,
        out_all,
        up_all,
        down_all,
        qkv_all,
    )
    projected, heads_out, shard_out, small_out, qkv_all = back(
        qat, ka, va, kt, q8, do, wide, lse, small_sums, x_seq, g, qkv_all
    )
    (
        grad_tokens, grad_qkv, grad_out, grad_up, grad_down, states, mean_loss,
        q_bias, v_bias, o_bias, gain_one, bias_one, d_bias, gain_two, bias_two, u_bias,
    ) = finish(
        projected.reshape(3 * D, token_rows), qkv_all.reshape(D, 3 * D), grad_resid_one, heads_out, shard_out, small_out,
        count, states,
    )
    return (
        states.reshape(seq_local, row_local, D),
        mean_loss.reshape(()),
        grad_tokens.reshape(seq_local, row_local, D),
        grad_qkv,
        q_bias,
        v_bias,
        grad_out,
        o_bias,
        gain_one,
        bias_one,
        grad_up,
        u_bias,
        grad_down,
        d_bias,
        gain_two,
        bias_two,
    )


def solution(mesh):
    rows = P("dp", ("seq", "wshard"), None)
    flags = P("dp", ("seq", "wshard"))
    matrix = P(("dp", "wshard"), None)
    vector = P(("dp", "wshard"))
    return jax.shard_map(
        on_device,
        mesh=mesh,
        in_specs=(
            rows,
            flags,
            flags,
            rows,
            matrix,
            vector,
            vector,
            matrix,
            vector,
            vector,
            vector,
            matrix,
            vector,
            matrix,
            vector,
            vector,
            vector,
        ),
        out_specs=(
            rows,
            P(),
            rows,
            matrix,
            vector,
            vector,
            matrix,
            vector,
            vector,
            vector,
            matrix,
            vector,
            matrix,
            vector,
            vector,
            vector,
        ),
        check_vma=False,
    )
```

```python
import functools

import jax
import jax.numpy as jnp
from jax import lax
from jax.experimental import pallas as pl
from jax.experimental.pallas import tpu as pltpu
from jax.sharding import PartitionSpec as P

D = 1024
H = 16
HD = 64
FF = 4096
L = 4096
EPS = 1e-06
F32 = jnp.float32
BF = jnp.bfloat16
MASKED = 1000000000.0
VMEM_CAP = 60 * 1024 * 1024
MESH = pl.DeviceIdType.MESH
ANY = pl.BlockSpec(memory_space=pl.ANY)
TB = 128
NB = L // TB


def dot(first, second, dims=((1,), (0,))):
    return lax.dot_general(first, second, (dims, ((), ())), preferred_element_type=F32)


def three_pieces(row):
    high = row.astype(BF)
    rest = row - high.astype(F32)
    middle = rest.astype(BF)
    lowest = (rest - middle.astype(F32)).astype(BF)
    return jnp.concatenate([high, middle, lowest], axis=0)


def place():
    at = lax.axis_index("seq")
    return (lax.axis_index("wshard") * 2 + (at // 2) % 2, lax.axis_index("dp"), at // 4, at % 2)


def device_at(x, y, z, core):
    return (y, (z * 2 + x % 2) * 2 + core, x // 2)


def along(axis, shift):
    x, y, z, core = place()
    if axis == "x":
        return device_at((x + shift) % 4, y, z, core)
    if axis == "y":
        return device_at(x, (y + shift) % 4, z, core)
    return device_at(x, y, (z + shift) % 4, core)


def sibling():
    x, y, z, core = place()
    return device_at(x, y, z, 1 - core)


def greet(partners):
    barrier = pltpu.get_barrier_semaphore()
    for partner in partners:
        pl.semaphore_signal(barrier, inc=1, device_id=partner, device_id_type=MESH)
    pl.semaphore_wait(barrier, len(partners))


def remote(src, dst, send_sem, recv_sem, target):
    return pltpu.make_async_remote_copy(
        src_ref=src, dst_ref=dst, send_sem=send_sem, recv_sem=recv_sem, device_id=target, device_id_type=MESH
    )


ORDERS = ("yzx", "zxy", "xyz")
PIECE = (48, 48, 48)
FIRST = (0, 384, 768)


def ring_partners():
    return [along(axis, shift) for axis in "xyz" for shift in (1, 2, 3)] + [sibling()]


def reduce_scratch():
    a, b, c = PIECE
    return [
        pltpu.VMEM((4, 2, 8 * a, 512), BF),
        pltpu.VMEM((4, 4, 2, 2 * b, 512), BF),
        pltpu.VMEM((4, 4, 4 * c, 512), BF),
        pltpu.VMEM((4, 2, 2 * a, 512), BF),
        pltpu.VMEM((4, 4, b, 512), BF),
        pltpu.VMEM((4, 4 * c, 512), BF),
        pltpu.VMEM((4, a, 512), BF),
        pltpu.VMEM((4, b, 512), BF),
        pltpu.VMEM((4, c, 512), BF),
        pltpu.SemaphoreType.DMA((3, 3, 3)),
        pltpu.SemaphoreType.DMA((3, 3, 3)),
        pltpu.SemaphoreType.DMA((3, 2)),
        pltpu.VMEM((2, 8 * a, 512), BF),
        pltpu.VMEM((2, 2, 2, 2 * b, 512), BF),
        pltpu.VMEM((2, 2, 4 * c, 512), BF),
        pltpu.SemaphoreType.DMA((3, 6)),
        pltpu.SemaphoreType.DMA((3, 6)),
        pltpu.SemaphoreType.DMA((3, 2)),
    ]


def aligned(value, unit):
    return pl.multiple_of(value, unit)


def reduce_piece(stage, part, refs, at):
    half, low, n = at // 2, at % 2, PIECE[part]
    held = refs[1 + 3 * (stage - 1) + part]
    if stage == 1:
        if part == 0:
            return held.at[0, :, pl.ds(aligned(at * 2 * n, 16), 2 * n), :]
        if part == 1:
            return held.at[0, :, half, pl.ds(aligned(low * n, 16), n), :]
        return held.at[0, at]
    if part == 0:
        return held.at[0, half, pl.ds(aligned(low * n, 16), n), :]
    if part == 1:
        return held.at[0, at]
    return held.at[0, pl.ds(aligned(at * n, 16), n), :]


def ring_at(axis):
    x, y, z, _ = place()
    return {"x": x, "y": y, "z": z}[axis]


def reduce_copies(stage, part, refs):
    send, recv = refs[10], refs[11]
    axis = ORDERS[part][stage]
    return [
        remote(
            reduce_piece(stage, part, refs, (ring_at(axis) + shift) % 4),
            refs[1 + 3 * stage + part].at[shift],
            send.at[stage, part, shift - 1],
            recv.at[stage, part, shift - 1],
            along(axis, shift),
        )
        for shift in (1, 3, 2)
    ]


def first_piece(part, refs, at, half):
    g_ref, n, first = refs[0], PIECE[part], FIRST[part]
    if part == 0:
        return g_ref.at[at, half, pl.ds(0, 8 * n)]
    if part == 1:
        return g_ref.at[pl.ds(2 * half, 2), :, pl.ds(aligned(first + at * 2 * n, 16), 2 * n)]
    return g_ref.at[pl.ds(2 * half, 2), at // 2, pl.ds(aligned(first + at % 2 * 4 * n, 16), 4 * n)]


def first_landing(part, refs, slot, half):
    held = refs[1 + part]
    return held.at[slot, half] if part == 0 else held.at[slot, pl.ds(2 * half, 2)]


def first_copies(part, refs):
    relay, send, recv = refs[13 + part], refs[16], refs[17]
    axis = ORDERS[part][0]
    at = ring_at(axis)
    up, down, far = (at + 1) % 4, (at + 3) % 4, (at + 2) % 4
    moves = [
        (first_piece(part, refs, far, 0), 2, 0, 1),
        (first_piece(part, refs, far, 1), 2, 1, 3),
        (first_piece(part, refs, up, 1), 1, 1, 1),
        (first_piece(part, refs, down, 0), 3, 0, 3),
        (relay.at[0], 1, 0, 1),
        (relay.at[1], 3, 1, 3),
    ]
    return [
        remote(src, first_landing(part, refs, slot, half), send.at[part, k], recv.at[part, k], along(axis, d))
        for k, (src, slot, half, d) in enumerate(moves)
    ]


def first_loads(part, refs):
    relay, local = refs[13 + part], refs[18]
    at = ring_at(ORDERS[part][0])
    return [
        pltpu.make_async_copy(first_piece(part, refs, (at + 1) % 4, 0), relay.at[0], local.at[part, 0]),
        pltpu.make_async_copy(first_piece(part, refs, (at + 3) % 4, 1), relay.at[1], local.at[part, 1]),
    ]


def first_own(part, refs):
    at = ring_at(ORDERS[part][0])
    return [
        pltpu.make_async_copy(first_piece(part, refs, at, h), first_landing(part, refs, 0, h), refs[12].at[part, h])
        for h in range(2)
    ]


def reduce_start(part, refs):
    start_all(first_copies(part, refs)[:4] + first_loads(part, refs) + first_own(part, refs))


def add_two(first, second):
    return (first.astype(F32) + second.astype(F32)).astype(BF)


def first_relay(part, refs):
    held, relay, n = refs[1 + part], refs[13 + part], PIECE[part]
    copies = first_copies(part, refs)
    wait_all(first_loads(part, refs))
    for copy in copies[:2]:
        copy.wait_recv()

    @pl.loop(0, 8 if part == 1 else 16)
    def _(i):
        if part == 0:
            rows = pl.ds(aligned(i % 8 * n, 16), n)
            relay[i // 8, rows, :] = add_two(relay[i // 8, rows, :], held[2, i // 8, rows, :])
        elif part == 1:
            half, k, e = i // 4, i // 2 % 2, i % 2
            relay[half, k, e] = add_two(relay[half, k, e], held[2, 2 * half + k, e])
        else:
            half, k, rows = i // 8, i // 4 % 2, pl.ds(aligned(i % 4 * n, 16), n)
            relay[half, k, rows, :] = add_two(relay[half, k, rows, :], held[2, 2 * half + k, rows, :])

    start_all(copies[4:])


def first_end(part, refs):
    copies = first_copies(part, refs)
    for copy in copies[:2]:
        copy.wait_send()
    wait_all(copies[2:] + first_own(part, refs))


def add_three(values):
    return (values[0].astype(F32) + values[1].astype(F32) + values[2].astype(F32)).astype(BF)


def add_four(values):
    total = values[0].astype(F32) + values[1].astype(F32)
    return (total + values[2].astype(F32) + values[3].astype(F32)).astype(BF)


def reduce_step(stage, part, refs):
    a1, b1, c1, a2, b2, c2, a3, b3, c3 = refs[1:10]
    if stage == 0:
        first_end(part, refs)
    else:
        wait_all(reduce_copies(stage, part, refs))
    x, y, z, _ = place()
    n = PIECE[part]
    rest = (1, 2, 3)
    near = (0, 1, 3)
    if stage == 0:

        @pl.loop(0, 16)
        def _(i):
            if part == 0:
                rows = pl.ds(aligned((i % 8) * n, 16), n)
                a1[0, i // 8, rows, :] = add_three([a1[s, i // 8, rows, :] for s in near])
            elif part == 1:
                rows = pl.ds(aligned((i % 2) * n, 16), n)
                b1[0, i // 4, (i // 2) % 2, rows, :] = add_three([b1[s, i // 4, (i // 2) % 2, rows, :] for s in near])
            else:
                rows = pl.ds(aligned((i % 4) * n, 16), n)
                c1[0, i // 4, rows, :] = add_three([c1[s, i // 4, rows, :] for s in near])

    elif stage == 1:

        @pl.loop(0, 4)
        def _(i):
            if part == 0:
                rows = pl.ds(aligned((i % 2) * n, 16), n)
                own = a1[0, i // 2, pl.ds(aligned(z * 2 * n + (i % 2) * n, 16), n), :]
                a2[0, i // 2, rows, :] = add_four([own] + [a2[s, i // 2, rows, :] for s in rest])
            elif part == 1:
                own = b1[0, i, x // 2, pl.ds(aligned((x % 2) * n, 16), n), :]
                b2[0, i] = add_four([own] + [b2[s, i] for s in rest])
            else:
                rows = pl.ds(aligned(i * n, 16), n)
                own = c1[0, y, rows, :]
                c2[0, rows, :] = add_four([own] + [c2[s, rows, :] for s in rest])

    elif part == 0:
        own = a2[0, x // 2, pl.ds(aligned((x % 2) * n, 16), n), :]
        a3[0] = add_four([own] + [a3[s] for s in rest])
    elif part == 1:
        b3[0] = add_four([b2[0, y]] + [b3[s] for s in rest])
    else:
        own = c2[0, pl.ds(aligned(z * n, 16), n), :]
        c3[0] = add_four([own] + [c3[s] for s in rest])
    if stage < 2:
        start_all(reduce_copies(stage + 1, part, refs))


def shard_rows(o_ref, part, x_low, z, core):
    sub = x_low * 4 + z if part == 2 else z * 2 + x_low
    return o_ref.at[core, pl.ds(aligned(FIRST[part] + sub * PIECE[part], 16), PIECE[part]), :]


def spread_steps(part, mine, sems, o_ref):
    local, send, recv = sems
    x, y, z, core = place()
    low = x % 2
    pair = device_at(x // 2 * 2 + 1 - low, y, z, core)
    spot = shard_rows(o_ref, part, low, z, core)
    own = pltpu.make_async_copy(mine, spot, local.at[part])
    first = remote(mine, spot, send.at[part, 0], recv.at[part, 0], pair)
    second = [remote(mine, spot, send.at[part, d], recv.at[part, d], along("z", d)) for d in (1, 3, 2)]
    spot = shard_rows(o_ref, part, 1 - low, z, core)
    third = [remote(spot, spot, send.at[part, 3 + d], recv.at[part, 3 + d], along("z", d)) for d in (1, 3, 2)]

    def begin():
        start_all([own, first] + second)

    def middle():
        first.wait()
        start_all(third)

    def end():
        wait_all([own] + second + third)

    return begin, middle, end


def swap_partner(shift):
    mine = lax.axis_index("seq") * 2 + lax.axis_index("wshard")
    other = (mine + shift) % NB
    return other, (lax.axis_index("dp"), other // 2, other % 2)


def swap_greet():
    barrier = pltpu.get_barrier_semaphore()

    @pl.loop(1, NB)
    def _(shift):
        pl.semaphore_signal(barrier, inc=1, device_id=swap_partner(shift)[1], device_id_type=MESH)

    pl.semaphore_wait(barrier, NB - 1)


def swap_copies(piece_for, landing_from, sems):
    mine = lax.axis_index("seq") * 2 + lax.axis_index("wshard")
    send, recv, local = sems

    def copy(shift):
        other, device = swap_partner(shift)
        return remote(piece_for(other), landing_from(mine), send.at[shift], recv.at[shift], device)

    own = pltpu.make_async_copy(piece_for(mine), landing_from(mine), local)

    def start():
        @pl.loop(1, NB)
        def _(shift):
            copy(shift).start()

        own.start()

    def wait():
        @pl.loop(1, NB)
        def _(shift):
            copy(shift).wait()

        own.wait()

    return start, wait


def swap_sems():
    return [pltpu.SemaphoreType.DMA((NB,)), pltpu.SemaphoreType.DMA((NB,)), pltpu.SemaphoreType.DMA]


def block_of(ref, b):
    return ref.at[b]


def head_tile(ref, b):
    return ref.at[pl.ds(aligned((b // 2) * HD, HD), HD), pl.ds(aligned((b % 2) * TB, TB), TB)]


def head_tile3(ref, b):
    return ref.at[:, pl.ds(aligned((b // 2) * HD, HD), HD), pl.ds(aligned((b % 2) * TB, TB), TB)]


HALVES = ((128, 2048), (256, 1024))


class Transfers:
    def __init__(self, send, recv):
        self.send, self.recv, self.used = send, recv, 0

    def copy(self, src, dst, target):
        made = remote(src, dst, self.send.at[self.used], self.recv.at[self.used], target)
        self.used += 1
        return made


def start_all(copies):
    for copy in copies:
        copy.start()


def wait_all(copies):
    for copy in copies:
        copy.wait()


def unit_rows(matrix, unit, count=1):
    rows = HALVES[matrix][0] // 4
    return pl.ds(unit * rows, count * rows)


def columns_part(matrix, at, parts):
    width = HALVES[matrix][1] // parts
    return pl.ds(aligned(at * width, 128), width)


def half_rows(core, rows=64):
    return pl.ds(aligned(core * rows, rows), rows)


def shard_greet():
    x, y, z, core = place()
    return [device_at(x, (y + d) % 4, z, core) for d in (1, 2, 3)] + [
        device_at(3 - x, (y + d) % 4, z, core) for d in range(4)
    ]


def greet_signal(others):
    barrier = pltpu.get_barrier_semaphore()

    @pl.loop(1, NB)
    def _(shift):
        pl.semaphore_signal(barrier, inc=1, device_id=swap_partner(shift)[1], device_id_type=MESH)

    for other in others:
        pl.semaphore_signal(barrier, inc=1, device_id=other, device_id_type=MESH)


def greet_wait(others):
    pl.semaphore_wait(pltpu.get_barrier_semaphore(), NB - 1 + len(others))


FRONT_COPIES = 144


def front_kernel(
    tokens, segments, flags, b_query, b_value, b_out, gain_one, bias_one, b_down, gain_two, bias_two, b_up,
    w_out, w_up, w_down, w_qkv,
    x_seq, meta_out, smalls_out, out_all, up_all, down_all, qkv_all, qat_ref, ka_ref, va_ref, kt_ref, q_ref,
    context, wide_ref, lse_ref,
    vat_ref, blocks, x_buf, tok_buf, out_buf, up_buf, down_buf, qkv_buf, meta, heads, smalls, meta_all, heads_all, smalls_all, w_ref, b_ref,
    send, recv, local, meta_send, meta_recv, meta_local, back_send, back_recv, back_local,
):
    x, y, z, core = place()
    hi, lo = x // 2, x % 2
    mine, across = y * 2 + hi, y * 2 + 1 - hi
    wrap, pair, other_core = device_at(3 - x, y, z, core), device_at(hi * 2 + 1 - lo, y, z, core), sibling()
    shards, wholes = (up_buf.at[core], down_buf), (up_all, down_all)
    rows_out = half_rows(core)
    greet_signal(shard_greet())
    load_tokens = pltpu.make_async_copy(tokens, tok_buf, local.at[0])
    load_qkv = pltpu.make_async_copy(w_qkv, qkv_buf, local.at[11])
    loads = [
        pltpu.make_async_copy(w_out, out_buf, local.at[9]),
        pltpu.make_async_copy(w_down.at[half_rows(core, 256)], down_buf, local.at[10]),
    ]
    for j in range(8):
        piece = w_up.at[:, pl.ds(aligned(j * 512 + core * 256, 256), 256)]
        loads.append(pltpu.make_async_copy(piece, up_buf.at[core, :, pl.ds(j * 256, 256)], local.at[1 + j]))
    start_all([load_tokens, load_qkv] + loads)
    meta[...] = jnp.zeros_like(meta)
    for s in range(2):
        meta[s, 0:1, :] = segments[s : s + 1, :]
        meta[s, 1:2, :] = flags[s : s + 1, :]
    smalls[...] = jnp.zeros_like(smalls)
    for k, vector in enumerate((b_query, b_value, b_out, gain_one, bias_one, b_down, gain_two, bias_two)):
        smalls[k : k + 1, :] = vector[...].astype(F32)
    for k in range(4):
        smalls[8 + k, :] = b_up[128 * k : 128 * (k + 1)].astype(F32)
    greet_wait(shard_greet())
    load_tokens.wait()
    net = Transfers(send, recv)
    first, second = pl.ds(0, 64), pl.ds(64, 64)

    def block(at, low, w, rows=slice(None)):
        return x_buf.at[at, low, core, w, rows]

    own = tok_buf.at[hi]
    swap = net.copy(tok_buf.at[1 - hi], block(z, lo, hi), wrap)
    own_z = [net.copy(own, block(z, lo, hi), along("z", d)) for d in (1, 3, 2)]
    own_pair = [net.copy(own.at[rows], block(z, lo, hi, rows), pair) for rows in (first, second)]
    start_all([swap, own_pair[0]] + own_z)
    x_buf[z, lo, core, hi] = tok_buf[hi]
    load_qkv.wait()
    for p in range(3):
        for k, pair_at in ((0, z * 2 + lo), (1, z * 2 + 1 - lo)):
            heads[k, :, 128 * p : 128 * (p + 1)] = qkv_buf[:, pl.ds(aligned(p * D + pair_at * 128, 128), 128)]
    cross_first = [
        net.copy(heads.at[1], heads_all.at[mine], wrap),
        net.copy(smalls, smalls_all.at[mine], wrap),
    ]
    start_all(cross_first)
    wait_all(loads)
    cross_early, cross_late = [], []
    for m in range(2):
        for unit, columns in ((0, columns_part(m, z, 4)), (3, columns_part(m, 1 - lo, 2))):
            rows = unit_rows(m, unit)
            cross_early.append(net.copy(shards[m].at[rows, columns], wholes[m].at[mine, rows, columns], wrap))

    def small_y(shard, heads_source, smalls_source):
        copies = []
        for d in (1, 3, 2):
            copies.append(net.copy(heads_source, heads_all.at[shard], along("y", d)))
            copies.append(net.copy(smalls_source, smalls_all.at[shard], along("y", d)))
        return copies

    own_small = small_y(mine, heads.at[0], smalls)
    start_all(own_small + cross_early)
    heads_all[mine] = heads[0]
    smalls_all[mine] = smalls[...]
    meta_start, meta_wait = swap_copies(
        lambda b: meta.at[b % 2], lambda b: meta_all.at[b], (meta_send, meta_recv, meta_local)
    )
    meta_start()
    keep = [
        pltpu.make_async_copy(out_buf.at[rows_out], out_all.at[mine, rows_out], local.at[9]),
        pltpu.make_async_copy(qkv_buf, qkv_all.at[mine], local.at[11]),
    ]
    for m in range(2):
        parts = [
            (unit_rows(m, 0), columns_part(m, z, 4)),
            (unit_rows(m, 3), columns_part(m, lo, 2)),
            (unit_rows(m, 1, 2), slice(None)),
        ]
        for k, (rows, columns) in enumerate(parts):
            piece = wholes[m].at[mine, rows, columns]
            keep.append(pltpu.make_async_copy(shards[m].at[rows, columns], piece, local.at[1 + 3 * m + k]))
    start_all(keep)

    def outer_y(shard, source):
        copies = []
        for d in (1, 3, 2):
            there = along("y", d)
            for m in range(2):
                for unit, columns in ((0, columns_part(m, z, 4)), (3, columns_part(m, lo, 2))):
                    rows = unit_rows(m, unit)
                    copies.append(net.copy(source(m).at[rows, columns], wholes[m].at[shard, rows, columns], there))
        return copies

    def inner_y(m, shard, source, shifts):
        rows = unit_rows(m, 1, 2)
        return [net.copy(source.at[rows], wholes[m].at[shard, rows], along("y", d)) for d in shifts]

    def out_y(shard, source):
        return [net.copy(source.at[rows_out], out_all.at[shard, rows_out], along("y", d)) for d in (1, 3, 2)]

    def relay_y(m, w):
        copies = []
        for unit, d in ((1, 1), (2, 3)):
            piece = wholes[m].at[(y + 4 - d) % 4 * 2 + w, unit_rows(m, unit)]
            copies.append(net.copy(piece, piece, along("y", d)))
        return copies

    swap.wait_recv()
    came = block(z, 1 - lo, 1 - hi)
    came_pair = [
        net.copy(block(z, 1 - lo, 1 - hi, rows), block(z, 1 - lo, 1 - hi, rows), pair) for rows in (first, second)
    ]
    came_z = [net.copy(came, came, along("z", d)) for d in (1, 3, 2)]
    start_all([came_pair[0]] + came_z + [own_pair[1], came_pair[1]])
    for copy in cross_first:
        copy.wait_recv()
    across_small = small_y(across, heads_all.at[across], smalls_all.at[across])
    own_y = outer_y(mine, lambda m: shards[m])
    start_all(across_small + own_y)
    pair_late = []

    def forward(got, d, low, w):
        got.wait_recv()
        piece = block((z + 4 - d) % 4, low, w, second)
        pair_late.append(net.copy(piece, piece, pair))
        pair_late[-1].start()

    for i, d in enumerate((1, 3, 2)):
        forward(own_z[i], d, lo, hi)
    half_z = []

    def halves(got, low, w):
        got.wait_recv()
        piece = block(z, low, w, first)
        copies = [net.copy(piece, piece, along("z", d)) for d in (1, 3, 2)]
        start_all(copies)
        half_z.extend(copies)

    halves(own_pair[0], 1 - lo, hi)
    for copy in cross_early:
        copy.wait_recv()
    across_y = outer_y(across, lambda m: wholes[m].at[across])
    inner_down = inner_y(1, mine, down_buf, (1, 3, 2))
    out_own = out_y(mine, out_buf)
    inner_up = inner_y(0, mine, up_buf.at[core], (1, 3))
    cross_late.append(net.copy(out_buf.at[rows_out], out_all.at[mine, rows_out], wrap))
    rows = unit_rows(0, 1, 2)
    cross_late.append(net.copy(up_buf.at[core, rows], up_all.at[mine, rows], wrap))
    rows = half_rows(core)
    cross_late.append(net.copy(qkv_buf.at[rows], qkv_all.at[mine, rows], wrap))
    start_all(across_y + cross_late + inner_down + out_own + inner_up)
    for i, d in enumerate((1, 3, 2)):
        forward(came_z[i], d, 1 - lo, 1 - hi)
    halves(came_pair[0], lo, 1 - hi)
    share, rest = [], []
    for low, w in ((lo, hi), (1 - lo, 1 - hi)):
        piece = x_buf.at[:, low, core, w]
        share.append(net.copy(piece, piece, other_core))
    start_all(share)
    for copy in cross_late[:2]:
        copy.wait_recv()
    out_across = out_y(across, out_all.at[across])
    across_up = inner_y(0, across, up_all.at[across], (1, 3))
    start_all(out_across + across_up)

    for copy in own_small + across_small:
        copy.wait_recv()
    meta_wait()
    at_first = core == 0
    both = heads_all[...].reshape(D, 384)
    parts = [jnp.where(at_first, both[:, 128 * p : 128 * p + HD], both[:, 128 * p + HD : 128 * (p + 1)]) for p in range(3)]
    w_ref[...] = jnp.concatenate(parts, axis=1)
    biases = smalls_all[lax.axis_index("seq") // 2]
    bias = [jnp.where(at_first, biases[k : k + 1, :HD], biases[k : k + 1, HD:]) for k in range(2)]
    b_ref[...] = jnp.broadcast_to(jnp.concatenate([bias[0], jnp.zeros((1, HD), F32), bias[1]], axis=1), (8, 3 * HD))

    def project(low, at_core, w):
        sides = dot(x_buf[:, low, at_core, w].reshape(4 * TB, D), w_ref[...]) + b_ref[:1, :]
        for at in range(4):
            b = at * 8 + low * 4 + at_core * 2 + w
            rows = pl.ds(aligned(b * TB, TB), TB)
            side = sides[at * TB : (at + 1) * TB]
            q8 = side[:, :HD].astype(BF).astype(F32) * 0.125
            hot = jnp.where(lax.broadcasted_iota(jnp.int32, (32, TB), 0) == meta_all[b, 0:1, :], 1.0, 0.0)
            lane = lax.broadcasted_iota(jnp.int32, (TB, HD), 1)
            ones3 = jnp.where(lane < 3, 1.0, 0.0)
            apart = (hot.T - 1.0) * MASKED
            key = side[:, HD : 2 * HD]
            value = side[:, 2 * HD :]
            q_ref[rows, :] = q8.astype(BF)
            ka_ref[rows, :] = jnp.concatenate([key, apart, ones3[:, :32]], axis=1).astype(BF)
            va_ref[rows, :] = jnp.concatenate([value, ones3], axis=1).astype(BF)
            qat_ref[:, rows] = jnp.concatenate([q8.T, hot, jnp.zeros((32, TB), F32)], axis=0).astype(BF)
            kt_ref[:, rows] = key.T.astype(BF)
            ones_row = jnp.where(lax.broadcasted_iota(jnp.int32, (16, TB), 0) == 0, 1.0, 0.0)
            vat_ref[:, rows] = jnp.concatenate([value.T, ones_row], axis=0).astype(BF)

    project(lo, core, hi)
    project(1 - lo, core, 1 - hi)
    for copy in half_z + [own_pair[1], came_pair[1]] + pair_late:
        copy.wait_recv()
    for low, w in ((1 - lo, hi), (lo, 1 - hi)):
        piece = x_buf.at[:, low, core, w]
        rest.append(net.copy(piece, piece, other_core))
    start_all(rest)
    for copy in share:
        copy.wait_recv()
    project(1 - lo, core, hi)
    project(lo, core, 1 - hi)
    project(lo, 1 - core, hi)
    project(1 - lo, 1 - core, 1 - hi)
    for copy in rest:
        copy.wait_recv()
    store = pltpu.make_async_copy(x_buf, x_seq, local.at[0])
    store.start()
    project(1 - lo, 1 - core, hi)
    project(lo, 1 - core, 1 - hi)
    meta_out[...] = meta_all[...]
    smalls_out[...] = smalls_all[...]

    wait_all(keep)
    for copy in own_y + across_y:
        copy.wait_recv()
    later, inner_wrap = [], []
    for m in range(2):
        piece = wholes[m].at[:, unit_rows(m, 3), columns_part(m, lo, 2)]
        later.append(net.copy(piece, piece, pair))
        for d in (1, 3, 2):
            piece = wholes[m].at[:, unit_rows(m, 0), columns_part(m, z, 4)]
            later.append(net.copy(piece, piece, along("z", d)))
    for d in range(4):
        piece = down_all.at[(y + d) % 4 * 2 + hi, unit_rows(1, 1, 2)]
        inner_wrap.append(net.copy(piece, piece, wrap))
    piece = out_all.at[:, half_rows(core)]
    share_out = net.copy(piece, piece, other_core)
    relay_up = relay_y(0, hi) + relay_y(0, 1 - hi)
    start_all(later)

    position = lax.axis_index("seq") * 2 + hi

    def result(b, recv_at):
        there = head_tile(context, position)
        return remote(blocks.at[b], there, back_send.at[b], back_recv.at[recv_at], (y, b // 2, b % 2))

    own_result = pltpu.make_async_copy(blocks.at[position], head_tile(context, position), back_local)

    @pl.loop(0, 4)
    def _(step):
        at = (step + z + 1) % 4
        columns = pl.ds(aligned(at * 1024, 1024), 1024)
        queries = qat_ref[:, columns]
        peak = jnp.full((1, 1024), -jnp.inf, F32)
        total = jnp.zeros((80, 1024), F32)
        for j in range(8):
            keys = slice(j * 512, (j + 1) * 512)
            logits = dot(ka_ref[keys, :], queries)
            new_peak = jnp.maximum(peak, jnp.max(logits, axis=0, keepdims=True))
            expos = jnp.exp(logits - new_peak).astype(BF)
            total = total * jnp.exp(peak - new_peak) + dot(vat_ref[:, keys], expos)
            peak = new_peak
        sums = total[HD : HD + 1]
        found = total[:HD] / sums
        wide_ref[:, columns] = found
        lse_ref[:, columns] = peak + jnp.log(sums)
        low = found.astype(BF)
        for j in range(8):
            b = at * 8 + j
            blocks[b] = low[:, j * TB : (j + 1) * TB]

            @pl.when(b != position)
            def _():
                result(b, position).start()

            @pl.when(b == position)
            def _():
                own_result.start()

        @pl.when(step == 0)
        def _():
            for copy in inner_down:
                copy.wait_recv()
            start_all(inner_wrap)

        @pl.when(step == 2)
        def _():
            for copy in out_own + out_across + inner_up + across_up:
                copy.wait_recv()
            start_all([share_out] + relay_up)

    store.wait()
    for copy in [swap] + own_pair + own_z + came_pair + came_z + half_z + pair_late + share + rest:
        copy.wait_send()
    for copy in cross_first + cross_early + cross_late + own_small + across_small + own_y + across_y + inner_down:
        copy.wait_send()
    for copy in out_own + out_across + inner_up + across_up:
        copy.wait_send()
    cross_late[2].wait_recv()
    wait_all([share_out] + relay_up + later + inner_wrap)

    @pl.loop(1, NB)
    def _(shift):
        b = (position + shift) % NB
        result(b, b).wait()

    own_result.wait()


def front(tokens, segments, flags, vectors, w_out, w_up, w_down, w_qkv):
    shape = jax.ShapeDtypeStruct
    in_vmem = pl.BlockSpec(memory_space=pltpu.VMEM)
    return pl.pallas_call(
        front_kernel,
        in_specs=[ANY] + [in_vmem] * 11 + [ANY] * 4,
        out_specs=[ANY] + [in_vmem] * 2 + [ANY] * 4 + [in_vmem] * 5 + [ANY] + [in_vmem] * 2,
        out_shape=[
            shape((4, 2, 2, 2, TB, D), BF),
            shape((NB, 8, TB), jnp.int32),
            shape((8, 16, 128), F32),
            shape((8, 128, D), BF),
            shape((8, 128, 2048), BF),
            shape((8, 256, D), BF),
            shape((8, 128, 3 * D), BF),
            shape((128, L), BF),
            shape((L, 128), BF),
            shape((L, 128), BF),
            shape((HD, L), BF),
            shape((L, HD), BF),
            shape((D, 2 * TB), BF),
            shape((HD, L), F32),
            shape((1, L), F32),
        ],
        scratch_shapes=[
            pltpu.VMEM((80, L), BF),
            pltpu.VMEM((NB, HD, TB), BF),
            pltpu.VMEM((4, 2, 2, 2, TB, D), BF),
            pltpu.VMEM((2, TB, D), BF),
            pltpu.VMEM((128, D), BF),
            pltpu.VMEM((2, 128, 2048), BF),
            pltpu.VMEM((256, D), BF),
            pltpu.VMEM((128, 3 * D), BF),
            pltpu.VMEM((2, 8, TB), jnp.int32),
            pltpu.VMEM((2, 128, 384), BF),
            pltpu.VMEM((16, 128), F32),
            pltpu.VMEM((NB, 8, TB), jnp.int32),
            pltpu.VMEM((8, 128, 384), BF),
            pltpu.VMEM((8, 16, 128), F32),
            pltpu.VMEM((D, 3 * HD), BF),
            pltpu.VMEM((8, 3 * HD), F32),
            pltpu.SemaphoreType.DMA((FRONT_COPIES,)),
            pltpu.SemaphoreType.DMA((FRONT_COPIES,)),
            pltpu.SemaphoreType.DMA((12,)),
            *swap_sems(),
            *swap_sems(),
        ],
        name="front",
        compiler_params=pltpu.CompilerParams(
            collective_id=1, has_side_effects=True, vmem_limit_bytes=VMEM_CAP
        ),
    )(tokens, segments, flags, *vectors, w_out, w_up, w_down, w_qkv)


def qkv_along_y(qkv_all, net):
    _, y, _, core = place()
    copies = []
    for d in (1, 3, 2):
        for w in range(2):
            piece = qkv_all.at[y * 2 + w, half_rows(core)]
            copies.append(net.copy(piece, piece, along("y", d)))
    return copies


def turned(first, second):
    return dot(first, second, ((0,), (0,)))


def gelu_both(u):
    rate = 0.7978845608028654
    square = u * u
    curve = jnp.tanh(rate * (u + 0.044715 * (square * u)))
    half = 0.5 * (1.0 + curve)
    slope = half + 0.5 * u * (1.0 - curve * curve) * (rate * (1.0 + 0.134145 * square))
    return u * half, slope


def fold(values):
    return jnp.sum(values.reshape(values.shape[0] // 8, 8, values.shape[1]), axis=0)


ROWS = 256
CHUNK = 32
SMALLS = 16


def middle_kernel(
    context_in, meta, tokens, teacher, flags, smalls, out_all, up_all, down_all, a0,
    states, resid_out, do, g_ref, sums_out, count_out, qkv_all,
    context, context_s, w_out, w_up, w_down, h, act, slope, send_one, come_one, send_two, come_two,
    gb, gu, ga, ga_s, normed, hidden, rate, work, resid, gct, stage, count, counts, valid,
    send, recv, local, back_send, back_recv, back_local,
):
    x, y, z, core = place()
    mine = y * 2 + x // 2
    twin = sibling()
    loads = [
        pltpu.make_async_copy(context_in, context, local.at[6]),
        pltpu.make_async_copy(out_all, w_out, local.at[0]),
        pltpu.make_async_copy(up_all, w_up, local.at[1]),
    ]
    load_down = pltpu.make_async_copy(down_all, w_down, local.at[2])
    start_all(loads + [load_down])
    greet_signal(shard_greet())
    greet_wait(shard_greet())
    net = Transfers(send, recv)
    later = qkv_along_y(qkv_all, net)
    valid_here = jnp.sum(meta[:, 1, :].astype(F32), axis=0, keepdims=True)
    count[...] = jnp.broadcast_to(jnp.sum(valid_here, axis=1, keepdims=True), (8, 128))
    ahead = [net.copy(count, counts.at[mine], target) for target in shard_greet()]
    start_all(ahead + later)
    own_count = pltpu.make_async_copy(count, counts.at[mine], local.at[3])
    own_count.start()
    for s in range(2):
        column = jnp.broadcast_to(flags[s : s + 1, :].astype(F32), (128, 128)).T
        valid[128 * s : 128 * (s + 1), :] = column

    def vector(row):
        return jnp.concatenate([smalls[i, row : row + 1, :] for i in range(8)], axis=1)

    out_bias, gain_one, offset_one, down_bias, gain_two, offset_two = [vector(row) for row in range(2, 8)]
    zeros = jnp.zeros((8, D), F32)
    wait_all(loads)
    give_context = net.copy(context, context_s, twin)
    give_context.start()
    work[...] = turned(context[...], w_out[...].reshape(D, D))

    @pl.loop(0, ROWS // CHUNK)
    def _(i):
        rows = pl.ds(aligned(i * CHUNK, CHUNK), CHUNK)
        total = tokens[rows, :].astype(F32) + work[rows, :] + out_bias
        centre = total - jnp.mean(total, axis=1, keepdims=True)
        scale = lax.rsqrt(jnp.mean(centre * centre, axis=1, keepdims=True) + EPS)
        unit = centre * scale
        normed[rows, :] = unit
        rate[rows, :] = jnp.broadcast_to(scale, (CHUNK, 128))
        full = unit * gain_one + offset_one
        hidden[rows, :] = full
        h[0, rows, :] = full.astype(BF)

    give_hidden = net.copy(h.at[0], h.at[1], twin)
    give_hidden.start()
    for slot in range(2):
        if slot == 1:
            give_hidden.wait()
        for k in range(8):
            columns = slice(256 * k, 256 * (k + 1))
            bias = jnp.concatenate([smalls[k, pl.ds(8 + 2 * core + e, 1), :] for e in range(2)], axis=1)
            u = dot(h[slot], w_up[:, :, columns].reshape(D, 256)) + bias
            value, incline = gelu_both(u)
            act[slot, :, columns] = value.astype(BF)
            slope[slot, :, columns] = incline
    load_down.wait()
    send_one[...] = dot(act[1], w_down[...].reshape(2048, D))
    give_one = net.copy(send_one, come_one, twin)
    give_one.start()
    work[...] = dot(act[0], w_down[...].reshape(2048, D))
    give_one.wait()
    wait_all(ahead)
    own_count.wait()
    total_count = jnp.sum(counts[...], axis=0)
    count_out[...] = total_count
    factor = (128 * ROWS) / total_count[:1, :1]

    def loss_rows(i, carried):
        rows = pl.ds(aligned(i * CHUNK, CHUNK), CHUNK)
        total = hidden[rows, :] + (work[rows, :] + come_one[rows, :] + down_bias)
        centre = total - jnp.mean(total, axis=1, keepdims=True)
        scale = lax.rsqrt(jnp.mean(centre * centre, axis=1, keepdims=True) + EPS)
        unit = centre * scale
        final = unit * gain_two + offset_two
        states[rows, :] = final.astype(BF)
        differ = final - teacher[rows, :].astype(F32)
        held = valid[rows, :1] * differ
        grad = factor * held
        weighted = grad * gain_two
        back = weighted - jnp.mean(weighted, axis=1, keepdims=True)
        back = scale * (back - unit * jnp.mean(weighted * unit, axis=1, keepdims=True))
        resid[rows, :] = back
        low = back.astype(BF)
        gb[0, rows, :] = low
        return (
            carried[0] + fold(grad * unit),
            carried[1] + fold(grad),
            carried[2] + fold(low.astype(F32)),
            carried[3] + fold(held * differ),
        )

    gain_two_sum, offset_two_sum, down_sum, error = lax.fori_loop(
        0, ROWS // CHUNK, loss_rows, (zeros, zeros, zeros, zeros)
    )
    give_branch = net.copy(gb.at[0], gb.at[1], twin)
    give_branch.start()
    up_sums = []
    for slot in range(2):
        if slot == 1:
            give_branch.wait()
        for k in range(8):
            columns = slice(256 * k, 256 * (k + 1))
            pulled = dot(gb[slot], w_down[k], ((1,), (1,))) * slope[slot, :, columns]
            low = pulled.astype(BF)
            gu[slot, :, columns] = low
            up_sums.append(fold(low.astype(F32)))
    for i in range(8):
        send_two[:, 128 * i : 128 * (i + 1)] = dot(gu[1], w_up[i], ((1,), (1,)))
    give_two = net.copy(send_two, come_two, twin)
    give_two.start()
    for i in range(8):
        work[:, 128 * i : 128 * (i + 1)] = dot(gu[0], w_up[i], ((1,), (1,)))
    give_two.wait()

    def first_norm_rows(i, carried):
        rows = pl.ds(aligned(i * CHUNK, CHUNK), CHUNK)
        grad = resid[rows, :] + (work[rows, :] + come_two[rows, :])
        unit = normed[rows, :]
        weighted = grad * gain_one
        back = weighted - jnp.mean(weighted, axis=1, keepdims=True)
        back = rate[rows, :1] * (back - unit * jnp.mean(weighted * unit, axis=1, keepdims=True))
        resid_out[rows, :] = back
        low = back.astype(BF)
        ga[rows, :] = low
        return (carried[0] + fold(grad * unit), carried[1] + fold(grad), carried[2] + fold(low.astype(F32)))

    gain_one_sum, offset_one_sum, out_sum = lax.fori_loop(0, ROWS // CHUNK, first_norm_rows, (zeros, zeros, zeros))
    give_attended = net.copy(ga.at[:, pl.ds(aligned((1 - core) * 512, 512), 512)], ga_s, twin)
    give_attended.start()
    gct[...] = dot(w_out[...].reshape(D, D), ga[...], ((1,), (1,))).astype(BF)
    back_start, back_wait = swap_copies(
        lambda b: head_tile(gct, b), lambda b: do.at[b], (back_send, back_recv, back_local)
    )
    back_start()

    error = jnp.broadcast_to(jnp.sum(jnp.sum(error, axis=0, keepdims=True), axis=1, keepdims=True), (1, 128))
    lines = [out_sum, gain_one_sum, offset_one_sum, down_sum, gain_two_sum, offset_two_sum]
    lines = [jnp.sum(line, axis=0, keepdims=True) for line in lines]
    for i in range(8):
        columns = slice(128 * i, 128 * (i + 1))
        sums_out[i] = jnp.zeros((SMALLS, 128), F32)
        for row, line in enumerate(lines):
            sums_out[i, row : row + 1, :] = line[:, columns]
        both = jnp.sum(up_sums[i] + up_sums[8 + i], axis=0, keepdims=True)
        for e in range(2):
            sums_out[i, pl.ds(6 + 2 * core + e, 1), :] = both[:, 128 * e : 128 * (e + 1)]
        sums_out[i, 10:11, :] = error

    give_context.wait()
    give_attended.wait()

    def stored(i):
        return pltpu.make_async_copy(stage.at[i % 2], g_ref.at[i // 2, i % 2], local.at[4 + i % 2])

    for i in range(8):
        if i >= 2:
            stored(i - 2).wait()
        tall = slice(128 * i, 128 * (i + 1))
        wide = slice(256 * i, 256 * (i + 1))
        up = turned(h[0, :, tall], gu[0]) + turned(h[1, :, tall], gu[1])
        for k in range(4):
            stage[i % 2, 128 * k : 128 * (k + 1), :] = up[:, 512 * k : 512 * (k + 1)].astype(BF)
        down = turned(act[0, :, wide], gb[0]) + turned(act[1, :, wide], gb[1])
        for k in range(2):
            stage[i % 2, 512 + 256 * k : 768 + 256 * k, :] = down[:, 512 * k : 512 * (k + 1)].astype(BF)
        own_half = ga[:, pl.ds(aligned(core * 512, 512), 512)]
        out = dot(context[tall, :], own_half) + dot(context_s[tall, :], ga_s[...])
        stage[i % 2, 1024:, :] = out.astype(BF)
        stored(i).start()
    stored(6).wait()
    stored(7).wait()
    back_wait()
    wait_all(later)


def middle(context, meta, tokens, teacher, flags, smalls, out_all, up_all, down_all, qkv_all):
    shape = jax.ShapeDtypeStruct
    in_vmem = pl.BlockSpec(memory_space=pltpu.VMEM)
    dma = pltpu.SemaphoreType.DMA
    wide = pltpu.VMEM((ROWS, D), F32)
    return pl.pallas_call(
        middle_kernel,
        in_specs=[ANY] + [in_vmem] * 5 + [ANY] * 4,
        out_specs=[in_vmem, in_vmem, ANY, ANY, in_vmem, in_vmem, ANY],
        out_shape=[
            shape((ROWS, D), BF),
            shape((ROWS, D), F32),
            shape((NB, HD, TB), BF),
            shape((4, 2, 1152, 512), BF),
            shape((8, SMALLS, 128), F32),
            shape((8, 128), F32),
            shape(qkv_all.shape, BF),
        ],
        input_output_aliases={9: 6},
        scratch_shapes=[
            pltpu.VMEM((D, ROWS), BF),
            pltpu.VMEM((D, ROWS), BF),
            pltpu.VMEM((8, 128, D), BF),
            pltpu.VMEM((8, 128, 2048), BF),
            pltpu.VMEM((8, 256, D), BF),
            pltpu.VMEM((2, ROWS, D), BF),
            pltpu.VMEM((2, ROWS, 2048), BF),
            pltpu.VMEM((2, ROWS, 2048), F32),
            wide,
            wide,
            wide,
            wide,
            pltpu.VMEM((2, ROWS, D), BF),
            pltpu.VMEM((2, ROWS, 2048), BF),
            pltpu.VMEM((ROWS, D), BF),
            pltpu.VMEM((ROWS, 512), BF),
            wide,
            wide,
            pltpu.VMEM((ROWS, 128), F32),
            wide,
            wide,
            pltpu.VMEM((D, ROWS), BF),
            pltpu.VMEM((2, 1152, 512), BF),
            pltpu.VMEM((8, 128), F32),
            pltpu.VMEM((8, 8, 128), F32),
            pltpu.VMEM((ROWS, 128), F32),
            dma((32,)),
            dma((32,)),
            dma((10,)),
            *swap_sems(),
        ],
        name="middle",
        compiler_params=pltpu.CompilerParams(
            collective_id=3, has_side_effects=True, vmem_limit_bytes=VMEM_CAP
        ),
    )(context, meta, tokens, teacher, flags, smalls, out_all, up_all, down_all, qkv_all)


BACK_KEYS = 256
BACK_STEPS = L // BACK_KEYS
BACK_WIDTH = 1024


def back_prepare(qat, do, wide, lse, queries, grads, grad_rows):
    for j in range(L // BACK_WIDTH):
        columns = slice(j * BACK_WIDTH, (j + 1) * BACK_WIDTH)
        grad_t = jnp.concatenate([do[j * (BACK_WIDTH // TB) + i] for i in range(BACK_WIDTH // TB)], axis=1)
        wider = grad_t.astype(F32)
        delta = jnp.sum(wider * wide[:, columns], axis=0, keepdims=True)
        grads[:HD, columns] = grad_t
        grads[HD:, columns] = jnp.concatenate([three_pieces(-delta), jnp.zeros((61, BACK_WIDTH), BF)], axis=0)
        queries[:96, columns] = qat[:96, columns]
        queries[96:, columns] = jnp.concatenate(
            [three_pieces(-lse[:, columns]), jnp.zeros((29, BACK_WIDTH), BF)], axis=0
        )
        grad_rows[columns, :] = wider.T.astype(BF)


def back_kernel(
    qat_in, ka_in, va_in, kt_in, q8_in, do_in, wide_in, lse, smalls, x_seq, g_ref, a0,
    projected, heads_out, shard_out, smalls_out, qkv_all,
    qat, ka, va, kt, q8, do, wide, input_sems,
    x_buf, queries, grads, grad_rows, dq, d_ref, mine_ref, parts_ref, sum_ref, heads_buf, small_buf, small_sum, small_all,
    send, recv, local, dk_send, dk_recv, dk_local, dq_send, dq_recv, dq_local, spread_send, spread_recv, *reduce_refs,
):
    x, y, z, core = place()
    shard_at = y * 2 + x // 2
    seq = lax.axis_index("seq")
    mine = seq * 2 + x // 2
    net = (g_ref,) + reduce_refs

    def shard_device(d):
        other = (shard_at + d) % 8
        return other, (other // 2, seq, other % 2)

    load_x = pltpu.make_async_copy(x_seq, x_buf, local.at[0])
    held = (qat, do, wide, ka, va, kt, q8)
    loads = [
        pltpu.make_async_copy(src, dst, input_sems.at[k])
        for k, (src, dst) in enumerate(zip((qat_in, do_in, wide_in, ka_in, va_in, kt_in, q8_in), held))
    ]
    shard_others = [shard_device(d)[1] for d in range(1, 8)]
    greet_signal(shard_others)
    start_all(loads)
    dq[...] = jnp.zeros_like(dq)
    greet_wait(shard_others)
    for part in range(3):
        reduce_start(part, net)
    wait_all(loads)
    load_x.start()
    back_prepare(qat, do, wide, lse, queries, grads, grad_rows)
    far = Transfers(send, recv)
    small_out = [far.copy(smalls.at[shard_device(d)[0]], small_buf.at[shard_at], shard_device(d)[1]) for d in range(1, 8)]
    start_all(small_out)
    small_buf[shard_at] = smalls[shard_at]
    rows = half_rows(core)
    weights = far.copy(qkv_all.at[:, rows], qkv_all.at[:, rows], sibling())
    weights.start()

    def landing(first, count):
        return projected.at[pl.ds(first, count), pl.ds(aligned(seq * HD, HD), HD), pl.ds(aligned((x // 2) * TB, TB), TB)]

    def block_device(b):
        return (y, b // 2, b % 2)

    def dk_copy(b, recv_at):
        return remote(d_ref.at[b, pl.ds(1, 2)], landing(1, 2), dk_send.at[b], dk_recv.at[recv_at], block_device(b))

    def dq_copy(b, recv_at):
        return remote(d_ref.at[b, pl.ds(0, 1)], landing(0, 1), dq_send.at[b], dq_recv.at[recv_at], block_device(b))

    dk_own = pltpu.make_async_copy(d_ref.at[mine, pl.ds(1, 2)], landing(1, 2), dk_local)
    dq_own = pltpu.make_async_copy(d_ref.at[mine, pl.ds(0, 1)], landing(0, 1), dq_local)

    steps = [
        spread_steps(part, reduce_refs[6 + part].at[0], (local.at[pl.ds(1, 3)], spread_send, spread_recv), shard_out)
        for part in range(3)
    ]

    @pl.loop(0, BACK_STEPS)
    def _(step):
        at = (step + seq) % BACK_STEPS
        keys = pl.ds(aligned(at * BACK_KEYS, BACK_KEYS), BACK_KEYS)
        ka_part, va_part, kt_part = ka[keys, :], va[keys, :], kt[:, keys]
        dk = jnp.zeros((BACK_KEYS, HD), F32)
        dv = jnp.zeros((BACK_KEYS, HD), F32)
        for j in range(L // BACK_WIDTH):
            columns = slice(j * BACK_WIDTH, (j + 1) * BACK_WIDTH)
            probs = jnp.exp(dot(ka_part, queries[:, columns]))
            raw = (probs * dot(va_part, grads[:, columns])).astype(BF)
            dv = dv + dot(probs.astype(BF), grad_rows[columns, :])
            dk = dk + dot(raw, q8[columns, :])
            dq[:, columns] += dot(kt_part, raw)
        dk_t, dv_t = dk.T.astype(BF), dv.T.astype(BF)
        for i in range(BACK_KEYS // TB):
            b = at * (BACK_KEYS // TB) + i
            d_ref[b, 1] = dk_t[:, i * TB : (i + 1) * TB]
            d_ref[b, 2] = dv_t[:, i * TB : (i + 1) * TB]

            @pl.when(b != mine)
            def _():
                dk_copy(b, mine).start()

            @pl.when(b == mine)
            def _():
                dk_own.start()

        @pl.when(step == 3)
        def _():
            for part in (1, 2, 0):
                first_relay(part, net)

        @pl.when(step == 8)
        def _():
            reduce_step(0, 1, net)

        @pl.when(step == 9)
        def _():
            reduce_step(0, 2, net)

        @pl.when(step == 10)
        def _():
            reduce_step(0, 0, net)

        @pl.when(step == 12)
        def _():
            reduce_step(1, 1, net)

        @pl.when(step == 14)
        def _():
            reduce_step(1, 2, net)
            reduce_step(2, 1, net)
            steps[1][0]()

    reduce_step(1, 0, net)
    for b in range(NB):
        d_ref[b, 0] = (dq[:, b * TB : (b + 1) * TB] * 0.125).astype(BF)

    load_x.wait()
    left = jnp.concatenate([d_ref[b].reshape(3 * HD, TB) for b in range(NB)], axis=1)
    sums = dot(jnp.ones((8, L), BF), left, ((1,), (1,)))
    gap = jnp.zeros((1, 128 - HD), F32)
    tail = jnp.concatenate(
        [
            jnp.concatenate([sums[:1, :HD], gap], axis=1),
            jnp.concatenate([sums[:1, 2 * HD :], gap], axis=1),
            jnp.zeros((14, 128), F32),
        ],
        axis=0,
    ).astype(BF)
    for i in range(4):
        total = dot(left, x_buf[:, :, 256 * i : 256 * (i + 1)].reshape(L, 256))
        for k in range(2):
            mine_ref[2 * i + k, : 3 * HD, :] = total[:, 128 * k : 128 * (k + 1)].astype(BF)
            mine_ref[2 * i + k, 3 * HD :, :] = tail
    part_out = [far.copy(mine_ref.at[shard_device(d)[0]], parts_ref.at[d], shard_device(d)[1]) for d in range(1, 8)]
    start_all(part_out)
    for part in (2, 0):
        reduce_step(2, part, net)
        steps[part][0]()

    @pl.loop(1, NB)
    def _(shift):
        dq_copy((mine + shift) % NB, mine).start()

    dq_own.start()
    wait_all(small_out)
    small_sum[...] = jnp.sum(small_buf[...], axis=0)
    wait_all(part_out)
    added = mine_ref[shard_at].astype(F32)
    for d in range(1, 8):
        added = added + parts_ref[d].astype(F32)
    sum_ref[...] = added.astype(BF)
    heads_buf[seq // 2, core] = sum_ref[...]
    small_all[seq // 2, core] = small_sum[...]
    head_out = []
    for d in range(1, 8):
        target = (y, (seq + 2 * d) % 16, x // 2)
        head_out.append(far.copy(sum_ref, heads_buf.at[seq // 2, core], target))
        head_out.append(far.copy(small_sum, small_all.at[seq // 2, core], target))
    start_all(head_out)
    for part in (1, 2, 0):
        steps[part][1]()
    wait_all(head_out)
    across = [
        far.copy(heads_buf.at[:, core], heads_buf.at[:, core], sibling()),
        far.copy(small_all.at[:, core], small_all.at[:, core], sibling()),
    ]
    start_all(across)
    shared = []
    for part in (1, 2, 0):
        steps[part][2]()
        piece = shard_out.at[core, pl.ds(FIRST[part], 8 * PIECE[part])]
        shared.append(far.copy(piece, piece, sibling()))
        shared[-1].start()

    @pl.loop(1, NB)
    def _(shift):
        b = (mine + shift) % NB
        dk_copy(b, b).wait()
        dq_copy(b, b).wait()

    dk_own.wait()
    dq_own.wait()
    weights.wait()
    wait_all(across)
    for i in range(8):
        heads_out[2 * i] = heads_buf[i, 0]
        heads_out[2 * i + 1] = heads_buf[i, 1]
    smalls_out[...] = jnp.sum(small_all[...].reshape(16, 16, 128), axis=0)
    wait_all(shared)


def back(qat, ka, va, kt, q8, do, wide, lse, smalls, x_seq, g, qkv_all):
    shape = jax.ShapeDtypeStruct
    in_vmem = pl.BlockSpec(memory_space=pltpu.VMEM)
    dma = pltpu.SemaphoreType.DMA
    return pl.pallas_call(
        back_kernel,
        in_specs=[ANY] * 7 + [in_vmem] * 2 + [ANY] * 3,
        out_specs=[ANY, in_vmem, ANY, in_vmem, ANY],
        out_shape=[
            shape((3, D, 2 * TB), BF),
            shape((H, 208, 128), BF),
            shape((2, 1152, 512), BF),
            shape((16, 128), F32),
            shape(qkv_all.shape, BF),
        ],
        input_output_aliases={11: 4},
        scratch_shapes=[
            pltpu.VMEM((128, L), BF),
            pltpu.VMEM((L, 128), BF),
            pltpu.VMEM((L, 128), BF),
            pltpu.VMEM((HD, L), BF),
            pltpu.VMEM((L, HD), BF),
            pltpu.VMEM((NB, HD, TB), BF),
            pltpu.VMEM((HD, L), F32),
            dma((7,)),
            pltpu.VMEM((NB, TB, D), BF),
            pltpu.VMEM((128, L), BF),
            pltpu.VMEM((128, L), BF),
            pltpu.VMEM((L, HD), BF),
            pltpu.VMEM((HD, L), F32),
            pltpu.VMEM((NB, 3, HD, TB), BF),
            pltpu.VMEM((8, 208, 128), BF),
            pltpu.VMEM((8, 208, 128), BF),
            pltpu.VMEM((208, 128), BF),
            pltpu.VMEM((8, 2, 208, 128), BF),
            pltpu.VMEM((8, 16, 128), F32),
            pltpu.VMEM((16, 128), F32),
            pltpu.VMEM((8, 2, 16, 128), F32),
            dma((40,)),
            dma((40,)),
            dma((4,)),
            *swap_sems(),
            *swap_sems(),
            dma((3, 8)),
            dma((3, 8)),
            *reduce_scratch(),
        ],
        name="attend_back",
        compiler_params=pltpu.CompilerParams(
            collective_id=4, has_side_effects=True, vmem_limit_bytes=VMEM_CAP
        ),
    )(qat, ka, va, kt, q8, do, wide, lse, smalls, x_seq, g, qkv_all)


def finish_kernel(
    projected, qkv_ref, resid_ref, heads_ref, up_ref, down_left, down_right, out_ref, smalls_ref, count_ref, states_ref,
    tokens_ref, grad_qkv, grad_out, grad_up, grad_down, states_out, loss_ref,
    q_bias, v_bias, o_bias, gain_one, bias_one, d_bias, gain_two, bias_two, u_bias,
):
    step = pl.program_id(0)

    @pl.when(step == 0)
    def _():
        x, y, _, _ = place()
        shard_at = y * 2 + x // 2
        for row, out in enumerate((q_bias, v_bias)):
            both = [heads_ref[shard_at * 2 + k, 3 * HD + row, :HD].astype(F32) for k in range(2)]
            out[...] = jnp.concatenate(both)
        for row, out in enumerate((o_bias, gain_one, bias_one, d_bias, gain_two, bias_two)):
            out[...] = smalls_ref[row, :]
        u_bias[...] = jnp.concatenate([smalls_ref[6 + k, :] for k in range(4)])
        loss_ref[...] = smalls_ref[10:11, :1] / (D * count_ref[:1, :1])
        for p in range(3):
            for pair in range(8):
                both = [heads_ref[2 * pair + k, p * HD : (p + 1) * HD, :].astype(F32) for k in range(2)]
                at = p * D + pair * 128
                grad_qkv[:, at : at + 128] = jnp.concatenate(both, axis=0).T

    states_out[...] = states_ref[...]
    tokens_ref[...] = resid_ref[...] + dot(qkv_ref[...], projected[...]).T
    for c in range(2):
        columns = slice(512 * c, 512 * (c + 1))
        for j in range(2):
            grad_up[:, 512 * j + 256 * c : 512 * j + 256 * (c + 1)] = up_ref[c, :, 256 * j : 256 * (j + 1)].astype(F32)
        grad_down[:, columns] = (down_left, down_right)[c][0].astype(F32)
        grad_out[:, columns] = out_ref[c].astype(F32)


def finish(projected, qkv, resid, heads, shard, smalls, count, states):
    shape = jax.ShapeDtypeStruct

    def whole(*dims):
        return pl.BlockSpec(dims, lambda i: (0,) * len(dims))

    part = pl.BlockSpec((2 * TB, 256), lambda i: (0, i))
    return pl.pallas_call(
        finish_kernel,
        grid=(4,),
        in_specs=[
            whole(3 * D, 2 * TB),
            pl.BlockSpec((256, 3 * D), lambda i: (i, 0)),
            part,
            whole(H, 208, 128),
            pl.BlockSpec((2, 128, 512), lambda i: (0, i, 0)),
            pl.BlockSpec((1, 128, 512), lambda i: (i // 2, 4 + i % 2, 0)),
            pl.BlockSpec((1, 128, 512), lambda i: (i // 2, 6 + i % 2, 0)),
            pl.BlockSpec((2, 32, 512), lambda i: (0, 32 + i, 0)),
            whole(16, 128),
            whole(8, 128),
            part,
        ],
        out_specs=[
            part,
            whole(128, 3 * D),
            pl.BlockSpec((32, D), lambda i: (i, 0)),
            pl.BlockSpec((128, 1024), lambda i: (0, i)),
            pl.BlockSpec((128, D), lambda i: (i, 0)),
            part,
            whole(1, 1),
        ]
        + [whole(128)] * 8
        + [whole(512)],
        out_shape=[
            shape((2 * TB, D), F32),
            shape((128, 3 * D), F32),
            shape((128, D), F32),
            shape((128, FF), F32),
            shape((512, D), F32),
            shape((2 * TB, D), BF),
            shape((1, 1), F32),
        ]
        + [shape((128,), F32)] * 8
        + [shape((512,), F32)],
        name="finish",
        compiler_params=pltpu.CompilerParams(vmem_limit_bytes=VMEM_CAP),
    )(projected, qkv, resid, heads, shard, shard, shard, shard, smalls, count, states)


def on_device(
    tokens,
    segments,
    valid_flags,
    teacher,
    w_qkv,
    b_query,
    b_value,
    w_out,
    b_out,
    ln1_gain,
    ln1_bias,
    w_up,
    b_up,
    w_down,
    b_down,
    ln2_gain,
    ln2_bias,
):
    seq_local, row_local, _ = tokens.shape
    token_rows = seq_local * row_local

    vectors = [b_query, b_value, b_out, ln1_gain, ln1_bias, b_down, ln2_gain, ln2_bias]
    vectors = [vector.reshape(1, 128) for vector in vectors] + [b_up]
    (
        x_seq, meta_all, smalls_all, out_all, up_all, down_all, qkv_all, qat, ka, va, kt, q8, context, wide, lse
    ) = front(
        tokens, segments, valid_flags, vectors, w_out, w_up, w_down, w_qkv
    )
    x_seq = x_seq.reshape(NB, TB, D)
    states, grad_resid_one, do, g, small_sums, count, qkv_all = middle(
        context,
        meta_all,
        tokens.reshape(token_rows, D),
        teacher.reshape(token_rows, D),
        valid_flags,
        smalls_all,
        out_all,
        up_all,
        down_all,
        qkv_all,
    )
    projected, heads_out, shard_out, small_out, qkv_all = back(
        qat, ka, va, kt, q8, do, wide, lse, small_sums, x_seq, g, qkv_all
    )
    (
        grad_tokens, grad_qkv, grad_out, grad_up, grad_down, states, mean_loss,
        q_bias, v_bias, o_bias, gain_one, bias_one, d_bias, gain_two, bias_two, u_bias,
    ) = finish(
        projected.reshape(3 * D, token_rows), qkv_all.reshape(D, 3 * D), grad_resid_one, heads_out, shard_out, small_out,
        count, states,
    )
    return (
        states.reshape(seq_local, row_local, D),
        mean_loss.reshape(()),
        grad_tokens.reshape(seq_local, row_local, D),
        grad_qkv,
        q_bias,
        v_bias,
        grad_out,
        o_bias,
        gain_one,
        bias_one,
        grad_up,
        u_bias,
        grad_down,
        d_bias,
        gain_two,
        bias_two,
    )


def solution(mesh):
    rows = P("dp", ("seq", "wshard"), None)
    flags = P("dp", ("seq", "wshard"))
    matrix = P(("dp", "wshard"), None)
    vector = P(("dp", "wshard"))
    return jax.shard_map(
        on_device,
        mesh=mesh,
        in_specs=(
            rows,
            flags,
            flags,
            rows,
            matrix,
            vector,
            vector,
            matrix,
            vector,
            vector,
            vector,
            matrix,
            vector,
            matrix,
            vector,
            vector,
            vector,
        ),
        out_specs=(
            rows,
            P(),
            rows,
            matrix,
            vector,
            vector,
            matrix,
            vector,
            vector,
            vector,
            matrix,
            vector,
            matrix,
            vector,
            vector,
            vector,
        ),
        check_vma=False,
    )
```

```python
import functools

import jax
import jax.numpy as jnp
from jax import lax
from jax.experimental import pallas as pl
from jax.experimental.pallas import tpu as pltpu
from jax.sharding import PartitionSpec as P

D = 1024
H = 16
HD = 64
FF = 4096
L = 4096
EPS = 1e-06
F32 = jnp.float32
BF = jnp.bfloat16
MASKED = 1000000000.0
VMEM_CAP = 60 * 1024 * 1024
MESH = pl.DeviceIdType.MESH
ANY = pl.BlockSpec(memory_space=pl.ANY)
TB = 128
NB = L // TB


def dot(first, second, dims=((1,), (0,))):
    return lax.dot_general(first, second, (dims, ((), ())), preferred_element_type=F32)


def three_pieces(row):
    high = row.astype(BF)
    rest = row - high.astype(F32)
    middle = rest.astype(BF)
    lowest = (rest - middle.astype(F32)).astype(BF)
    return jnp.concatenate([high, middle, lowest], axis=0)


def place():
    at = lax.axis_index("seq")
    return (lax.axis_index("wshard") * 2 + (at // 2) % 2, lax.axis_index("dp"), at // 4, at % 2)


def device_at(x, y, z, core):
    return (y, (z * 2 + x % 2) * 2 + core, x // 2)


def along(axis, shift):
    x, y, z, core = place()
    if axis == "x":
        return device_at((x + shift) % 4, y, z, core)
    if axis == "y":
        return device_at(x, (y + shift) % 4, z, core)
    return device_at(x, y, (z + shift) % 4, core)


def sibling():
    x, y, z, core = place()
    return device_at(x, y, z, 1 - core)


def greet(partners):
    barrier = pltpu.get_barrier_semaphore()
    for partner in partners:
        pl.semaphore_signal(barrier, inc=1, device_id=partner, device_id_type=MESH)
    pl.semaphore_wait(barrier, len(partners))


def remote(src, dst, send_sem, recv_sem, target):
    return pltpu.make_async_remote_copy(
        src_ref=src, dst_ref=dst, send_sem=send_sem, recv_sem=recv_sem, device_id=target, device_id_type=MESH
    )


ORDERS = ("yzx", "zxy", "xyz")
PIECE = (48, 48, 48)
FIRST = (0, 384, 768)


def ring_partners():
    return [along(axis, shift) for axis in "xyz" for shift in (1, 2, 3)] + [sibling()]


def reduce_scratch():
    a, b, c = PIECE
    return [
        pltpu.VMEM((4, 2, 8 * a, 512), BF),
        pltpu.VMEM((4, 4, 2, 2 * b, 512), BF),
        pltpu.VMEM((4, 4, 4 * c, 512), BF),
        pltpu.VMEM((4, 2, 2 * a, 512), BF),
        pltpu.VMEM((4, 4, b, 512), BF),
        pltpu.VMEM((4, 4 * c, 512), BF),
        pltpu.VMEM((4, a, 512), BF),
        pltpu.VMEM((4, b, 512), BF),
        pltpu.VMEM((4, c, 512), BF),
        pltpu.SemaphoreType.DMA((3, 3, 3)),
        pltpu.SemaphoreType.DMA((3, 3, 3)),
        pltpu.SemaphoreType.DMA((3, 2)),
        pltpu.VMEM((2, 8 * a, 512), BF),
        pltpu.VMEM((2, 2, 2, 2 * b, 512), BF),
        pltpu.VMEM((2, 2, 4 * c, 512), BF),
        pltpu.SemaphoreType.DMA((3, 6)),
        pltpu.SemaphoreType.DMA((3, 6)),
        pltpu.SemaphoreType.DMA((3, 2)),
    ]


def aligned(value, unit):
    return pl.multiple_of(value, unit)


def reduce_piece(stage, part, refs, at):
    half, low, n = at // 2, at % 2, PIECE[part]
    held = refs[1 + 3 * (stage - 1) + part]
    if stage == 1:
        if part == 0:
            return held.at[0, :, pl.ds(aligned(at * 2 * n, 16), 2 * n), :]
        if part == 1:
            return held.at[0, :, half, pl.ds(aligned(low * n, 16), n), :]
        return held.at[0, at]
    if part == 0:
        return held.at[0, half, pl.ds(aligned(low * n, 16), n), :]
    if part == 1:
        return held.at[0, at]
    return held.at[0, pl.ds(aligned(at * n, 16), n), :]


def ring_at(axis):
    x, y, z, _ = place()
    return {"x": x, "y": y, "z": z}[axis]


def reduce_copies(stage, part, refs):
    send, recv = refs[10], refs[11]
    axis = ORDERS[part][stage]
    return [
        remote(
            reduce_piece(stage, part, refs, (ring_at(axis) + shift) % 4),
            refs[1 + 3 * stage + part].at[shift],
            send.at[stage, part, shift - 1],
            recv.at[stage, part, shift - 1],
            along(axis, shift),
        )
        for shift in (1, 3, 2)
    ]


def first_piece(part, refs, at, half):
    g_ref, n, first = refs[0], PIECE[part], FIRST[part]
    if part == 0:
        return g_ref.at[at, half, pl.ds(0, 8 * n)]
    if part == 1:
        return g_ref.at[pl.ds(2 * half, 2), :, pl.ds(aligned(first + at * 2 * n, 16), 2 * n)]
    return g_ref.at[pl.ds(2 * half, 2), at // 2, pl.ds(aligned(first + at % 2 * 4 * n, 16), 4 * n)]


def first_landing(part, refs, slot, half):
    held = refs[1 + part]
    return held.at[slot, half] if part == 0 else held.at[slot, pl.ds(2 * half, 2)]


def first_copies(part, refs):
    relay, send, recv = refs[13 + part], refs[16], refs[17]
    axis = ORDERS[part][0]
    at = ring_at(axis)
    up, down, far = (at + 1) % 4, (at + 3) % 4, (at + 2) % 4
    moves = [
        (first_piece(part, refs, far, 0), 2, 0, 1),
        (first_piece(part, refs, far, 1), 2, 1, 3),
        (first_piece(part, refs, up, 1), 1, 1, 1),
        (first_piece(part, refs, down, 0), 3, 0, 3),
        (relay.at[0], 1, 0, 1),
        (relay.at[1], 3, 1, 3),
    ]
    return [
        remote(src, first_landing(part, refs, slot, half), send.at[part, k], recv.at[part, k], along(axis, d))
        for k, (src, slot, half, d) in enumerate(moves)
    ]


def first_loads(part, refs):
    relay, local = refs[13 + part], refs[18]
    at = ring_at(ORDERS[part][0])
    return [
        pltpu.make_async_copy(first_piece(part, refs, (at + 1) % 4, 0), relay.at[0], local.at[part, 0]),
        pltpu.make_async_copy(first_piece(part, refs, (at + 3) % 4, 1), relay.at[1], local.at[part, 1]),
    ]


def first_own(part, refs):
    at = ring_at(ORDERS[part][0])
    return [
        pltpu.make_async_copy(first_piece(part, refs, at, h), first_landing(part, refs, 0, h), refs[12].at[part, h])
        for h in range(2)
    ]


def reduce_start(part, refs):
    start_all(first_copies(part, refs)[:4] + first_loads(part, refs) + first_own(part, refs))


def add_two(first, second):
    return (first.astype(F32) + second.astype(F32)).astype(BF)


def first_relay(part, refs):
    held, relay, n = refs[1 + part], refs[13 + part], PIECE[part]
    copies = first_copies(part, refs)
    wait_all(first_loads(part, refs))
    for copy in copies[:2]:
        copy.wait_recv()

    @pl.loop(0, 8 if part == 1 else 16)
    def _(i):
        if part == 0:
            rows = pl.ds(aligned(i % 8 * n, 16), n)
            relay[i // 8, rows, :] = add_two(relay[i // 8, rows, :], held[2, i // 8, rows, :])
        elif part == 1:
            half, k, e = i // 4, i // 2 % 2, i % 2
            relay[half, k, e] = add_two(relay[half, k, e], held[2, 2 * half + k, e])
        else:
            half, k, rows = i // 8, i // 4 % 2, pl.ds(aligned(i % 4 * n, 16), n)
            relay[half, k, rows, :] = add_two(relay[half, k, rows, :], held[2, 2 * half + k, rows, :])

    start_all(copies[4:])


def first_end(part, refs):
    copies = first_copies(part, refs)
    for copy in copies[:2]:
        copy.wait_send()
    wait_all(copies[2:] + first_own(part, refs))


def add_three(values):
    return (values[0].astype(F32) + values[1].astype(F32) + values[2].astype(F32)).astype(BF)


def add_four(values):
    total = values[0].astype(F32) + values[1].astype(F32)
    return (total + values[2].astype(F32) + values[3].astype(F32)).astype(BF)


def reduce_step(stage, part, refs):
    a1, b1, c1, a2, b2, c2, a3, b3, c3 = refs[1:10]
    if stage == 0:
        first_end(part, refs)
    else:
        wait_all(reduce_copies(stage, part, refs))
    x, y, z, _ = place()
    n = PIECE[part]
    rest = (1, 2, 3)
    near = (0, 1, 3)
    if stage == 0:

        @pl.loop(0, 16)
        def _(i):
            if part == 0:
                rows = pl.ds(aligned((i % 8) * n, 16), n)
                a1[0, i // 8, rows, :] = add_three([a1[s, i // 8, rows, :] for s in near])
            elif part == 1:
                rows = pl.ds(aligned((i % 2) * n, 16), n)
                b1[0, i // 4, (i // 2) % 2, rows, :] = add_three([b1[s, i // 4, (i // 2) % 2, rows, :] for s in near])
            else:
                rows = pl.ds(aligned((i % 4) * n, 16), n)
                c1[0, i // 4, rows, :] = add_three([c1[s, i // 4, rows, :] for s in near])

    elif stage == 1:

        @pl.loop(0, 4)
        def _(i):
            if part == 0:
                rows = pl.ds(aligned((i % 2) * n, 16), n)
                own = a1[0, i // 2, pl.ds(aligned(z * 2 * n + (i % 2) * n, 16), n), :]
                a2[0, i // 2, rows, :] = add_four([own] + [a2[s, i // 2, rows, :] for s in rest])
            elif part == 1:
                own = b1[0, i, x // 2, pl.ds(aligned((x % 2) * n, 16), n), :]
                b2[0, i] = add_four([own] + [b2[s, i] for s in rest])
            else:
                rows = pl.ds(aligned(i * n, 16), n)
                own = c1[0, y, rows, :]
                c2[0, rows, :] = add_four([own] + [c2[s, rows, :] for s in rest])

    elif part == 0:
        own = a2[0, x // 2, pl.ds(aligned((x % 2) * n, 16), n), :]
        a3[0] = add_four([own] + [a3[s] for s in rest])
    elif part == 1:
        b3[0] = add_four([b2[0, y]] + [b3[s] for s in rest])
    else:
        own = c2[0, pl.ds(aligned(z * n, 16), n), :]
        c3[0] = add_four([own] + [c3[s] for s in rest])
    if stage < 2:
        start_all(reduce_copies(stage + 1, part, refs))


def shard_rows(o_ref, part, x_low, z, core):
    sub = x_low * 4 + z if part == 2 else z * 2 + x_low
    return o_ref.at[core, pl.ds(aligned(FIRST[part] + sub * PIECE[part], 16), PIECE[part]), :]


def spread_steps(part, mine, sems, o_ref):
    local, send, recv = sems
    x, y, z, core = place()
    low = x % 2
    pair = device_at(x // 2 * 2 + 1 - low, y, z, core)
    spot = shard_rows(o_ref, part, low, z, core)
    own = pltpu.make_async_copy(mine, spot, local.at[part])
    first = remote(mine, spot, send.at[part, 0], recv.at[part, 0], pair)
    second = [remote(mine, spot, send.at[part, d], recv.at[part, d], along("z", d)) for d in (1, 3, 2)]
    spot = shard_rows(o_ref, part, 1 - low, z, core)
    third = [remote(spot, spot, send.at[part, 3 + d], recv.at[part, 3 + d], along("z", d)) for d in (1, 3, 2)]

    def begin():
        start_all([own, first] + second)

    def middle():
        first.wait()
        start_all(third)

    def end():
        wait_all([own] + second + third)

    return begin, middle, end


def swap_partner(shift):
    mine = lax.axis_index("seq") * 2 + lax.axis_index("wshard")
    other = (mine + shift) % NB
    return other, (lax.axis_index("dp"), other // 2, other % 2)


def swap_greet():
    barrier = pltpu.get_barrier_semaphore()

    @pl.loop(1, NB)
    def _(shift):
        pl.semaphore_signal(barrier, inc=1, device_id=swap_partner(shift)[1], device_id_type=MESH)

    pl.semaphore_wait(barrier, NB - 1)


def swap_copies(piece_for, landing_from, sems):
    mine = lax.axis_index("seq") * 2 + lax.axis_index("wshard")
    send, recv, local = sems

    def copy(shift):
        other, device = swap_partner(shift)
        return remote(piece_for(other), landing_from(mine), send.at[shift], recv.at[shift], device)

    own = pltpu.make_async_copy(piece_for(mine), landing_from(mine), local)

    def start():
        @pl.loop(1, NB)
        def _(shift):
            copy(shift).start()

        own.start()

    def wait():
        @pl.loop(1, NB)
        def _(shift):
            copy(shift).wait()

        own.wait()

    return start, wait


def swap_sems():
    return [pltpu.SemaphoreType.DMA((NB,)), pltpu.SemaphoreType.DMA((NB,)), pltpu.SemaphoreType.DMA]


def block_of(ref, b):
    return ref.at[b]


def head_tile(ref, b):
    return ref.at[pl.ds(aligned((b // 2) * HD, HD), HD), pl.ds(aligned((b % 2) * TB, TB), TB)]


def head_tile3(ref, b):
    return ref.at[:, pl.ds(aligned((b // 2) * HD, HD), HD), pl.ds(aligned((b % 2) * TB, TB), TB)]


HALVES = ((128, 2048), (256, 1024))


class Transfers:
    def __init__(self, send, recv):
        self.send, self.recv, self.used = send, recv, 0

    def copy(self, src, dst, target):
        made = remote(src, dst, self.send.at[self.used], self.recv.at[self.used], target)
        self.used += 1
        return made


def start_all(copies):
    for copy in copies:
        copy.start()


def wait_all(copies):
    for copy in copies:
        copy.wait()


def unit_rows(matrix, unit, count=1):
    rows = HALVES[matrix][0] // 4
    return pl.ds(unit * rows, count * rows)


def columns_part(matrix, at, parts):
    width = HALVES[matrix][1] // parts
    return pl.ds(aligned(at * width, 128), width)


def half_rows(core, rows=64):
    return pl.ds(aligned(core * rows, rows), rows)


def shard_greet():
    x, y, z, core = place()
    return [device_at(x, (y + d) % 4, z, core) for d in (1, 2, 3)] + [
        device_at(3 - x, (y + d) % 4, z, core) for d in range(4)
    ]


def greet_signal(others):
    barrier = pltpu.get_barrier_semaphore()

    @pl.loop(1, NB)
    def _(shift):
        pl.semaphore_signal(barrier, inc=1, device_id=swap_partner(shift)[1], device_id_type=MESH)

    for other in others:
        pl.semaphore_signal(barrier, inc=1, device_id=other, device_id_type=MESH)


def greet_wait(others):
    pl.semaphore_wait(pltpu.get_barrier_semaphore(), NB - 1 + len(others))


FRONT_COPIES = 144


def front_kernel(
    tokens, segments, flags, b_query, b_value, b_out, gain_one, bias_one, b_down, gain_two, bias_two, b_up,
    w_out, w_up, w_down, w_qkv,
    x_seq, meta_out, smalls_out, out_all, up_all, down_all, qkv_all, qat_ref, ka_ref, va_ref, kt_ref, q_ref,
    context, wide_ref, lse_ref,
    vat_ref, blocks, x_buf, tok_buf, out_buf, up_buf, down_buf, qkv_buf, meta, heads, smalls, meta_all, heads_all, smalls_all, w_ref, b_ref,
    send, recv, local, meta_send, meta_recv, meta_local, back_send, back_recv, back_local,
):
    x, y, z, core = place()
    hi, lo = x // 2, x % 2
    mine, across = y * 2 + hi, y * 2 + 1 - hi
    wrap, pair, other_core = device_at(3 - x, y, z, core), device_at(hi * 2 + 1 - lo, y, z, core), sibling()
    shards, wholes = (up_buf.at[core], down_buf), (up_all, down_all)
    rows_out = half_rows(core)
    greet_signal(shard_greet())
    load_tokens = pltpu.make_async_copy(tokens, tok_buf, local.at[0])
    load_qkv = pltpu.make_async_copy(w_qkv, qkv_buf, local.at[11])
    loads = [
        pltpu.make_async_copy(w_out, out_buf, local.at[9]),
        pltpu.make_async_copy(w_down.at[half_rows(core, 256)], down_buf, local.at[10]),
    ]
    for j in range(8):
        piece = w_up.at[:, pl.ds(aligned(j * 512 + core * 256, 256), 256)]
        loads.append(pltpu.make_async_copy(piece, up_buf.at[core, :, pl.ds(j * 256, 256)], local.at[1 + j]))
    start_all([load_tokens, load_qkv] + loads)
    meta[...] = jnp.zeros_like(meta)
    for s in range(2):
        meta[s, 0:1, :] = segments[s : s + 1, :]
        meta[s, 1:2, :] = flags[s : s + 1, :]
    smalls[...] = jnp.zeros_like(smalls)
    for k, vector in enumerate((b_query, b_value, b_out, gain_one, bias_one, b_down, gain_two, bias_two)):
        smalls[k : k + 1, :] = vector[...].astype(F32)
    for k in range(4):
        smalls[8 + k, :] = b_up[128 * k : 128 * (k + 1)].astype(F32)
    greet_wait(shard_greet())
    load_tokens.wait()
    net = Transfers(send, recv)
    first, second = pl.ds(0, 64), pl.ds(64, 64)

    def block(at, low, w, rows=slice(None)):
        return x_buf.at[at, low, core, w, rows]

    own = tok_buf.at[hi]
    swap = net.copy(tok_buf.at[1 - hi], block(z, lo, hi), wrap)
    own_z = [net.copy(own, block(z, lo, hi), along("z", d)) for d in (1, 3, 2)]
    own_pair = [net.copy(own.at[rows], block(z, lo, hi, rows), pair) for rows in (first, second)]
    start_all([swap, own_pair[0]] + own_z)
    x_buf[z, lo, core, hi] = tok_buf[hi]
    load_qkv.wait()
    for p in range(3):
        for k, pair_at in ((0, z * 2 + lo), (1, z * 2 + 1 - lo)):
            heads[k, :, 128 * p : 128 * (p + 1)] = qkv_buf[:, pl.ds(aligned(p * D + pair_at * 128, 128), 128)]
    cross_first = [
        net.copy(heads.at[1], heads_all.at[mine], wrap),
        net.copy(smalls, smalls_all.at[mine], wrap),
    ]
    start_all(cross_first)
    wait_all(loads)
    cross_early, cross_late = [], []
    for m in range(2):
        for unit, columns in ((0, columns_part(m, z, 4)), (3, columns_part(m, 1 - lo, 2))):
            rows = unit_rows(m, unit)
            cross_early.append(net.copy(shards[m].at[rows, columns], wholes[m].at[mine, rows, columns], wrap))

    def small_y(shard, heads_source, smalls_source):
        copies = []
        for d in (1, 3, 2):
            copies.append(net.copy(heads_source, heads_all.at[shard], along("y", d)))
            copies.append(net.copy(smalls_source, smalls_all.at[shard], along("y", d)))
        return copies

    own_small = small_y(mine, heads.at[0], smalls)
    start_all(own_small + cross_early)
    heads_all[mine] = heads[0]
    smalls_all[mine] = smalls[...]
    meta_start, meta_wait = swap_copies(
        lambda b: meta.at[b % 2], lambda b: meta_all.at[b], (meta_send, meta_recv, meta_local)
    )
    meta_start()
    keep = [
        pltpu.make_async_copy(out_buf.at[rows_out], out_all.at[mine, rows_out], local.at[9]),
        pltpu.make_async_copy(qkv_buf, qkv_all.at[mine], local.at[11]),
    ]
    for m in range(2):
        parts = [
            (unit_rows(m, 0), columns_part(m, z, 4)),
            (unit_rows(m, 3), columns_part(m, lo, 2)),
            (unit_rows(m, 1, 2), slice(None)),
        ]
        for k, (rows, columns) in enumerate(parts):
            piece = wholes[m].at[mine, rows, columns]
            keep.append(pltpu.make_async_copy(shards[m].at[rows, columns], piece, local.at[1 + 3 * m + k]))
    start_all(keep)

    def outer_y(shard, source):
        copies = []
        for d in (1, 3, 2):
            there = along("y", d)
            for m in range(2):
                for unit, columns in ((0, columns_part(m, z, 4)), (3, columns_part(m, lo, 2))):
                    rows = unit_rows(m, unit)
                    copies.append(net.copy(source(m).at[rows, columns], wholes[m].at[shard, rows, columns], there))
        return copies

    def inner_y(m, shard, source, shifts):
        rows = unit_rows(m, 1, 2)
        return [net.copy(source.at[rows], wholes[m].at[shard, rows], along("y", d)) for d in shifts]

    def out_y(shard, source):
        return [net.copy(source.at[rows_out], out_all.at[shard, rows_out], along("y", d)) for d in (1, 3, 2)]

    def relay_y(m, w):
        copies = []
        for unit, d in ((1, 1), (2, 3)):
            piece = wholes[m].at[(y + 4 - d) % 4 * 2 + w, unit_rows(m, unit)]
            copies.append(net.copy(piece, piece, along("y", d)))
        return copies

    swap.wait_recv()
    came = block(z, 1 - lo, 1 - hi)
    came_pair = [
        net.copy(block(z, 1 - lo, 1 - hi, rows), block(z, 1 - lo, 1 - hi, rows), pair) for rows in (first, second)
    ]
    came_z = [net.copy(came, came, along("z", d)) for d in (1, 3, 2)]
    start_all([came_pair[0]] + came_z + [own_pair[1], came_pair[1]])
    for copy in cross_first:
        copy.wait_recv()
    across_small = small_y(across, heads_all.at[across], smalls_all.at[across])
    own_y = outer_y(mine, lambda m: shards[m])
    start_all(across_small + own_y)
    pair_late = []

    def forward(got, d, low, w):
        got.wait_recv()
        piece = block((z + 4 - d) % 4, low, w, second)
        pair_late.append(net.copy(piece, piece, pair))
        pair_late[-1].start()

    for i, d in enumerate((1, 3, 2)):
        forward(own_z[i], d, lo, hi)
    half_z = []

    def halves(got, low, w):
        got.wait_recv()
        piece = block(z, low, w, first)
        copies = [net.copy(piece, piece, along("z", d)) for d in (1, 3, 2)]
        start_all(copies)
        half_z.extend(copies)

    halves(own_pair[0], 1 - lo, hi)
    for copy in cross_early:
        copy.wait_recv()
    across_y = outer_y(across, lambda m: wholes[m].at[across])
    inner_down = inner_y(1, mine, down_buf, (1, 3, 2))
    out_own = out_y(mine, out_buf)
    inner_up = inner_y(0, mine, up_buf.at[core], (1, 3))
    cross_late.append(net.copy(out_buf.at[rows_out], out_all.at[mine, rows_out], wrap))
    rows = unit_rows(0, 1, 2)
    cross_late.append(net.copy(up_buf.at[core, rows], up_all.at[mine, rows], wrap))
    rows = half_rows(core)
    cross_late.append(net.copy(qkv_buf.at[rows], qkv_all.at[mine, rows], wrap))
    start_all(across_y + cross_late + inner_down + out_own + inner_up)
    for i, d in enumerate((1, 3, 2)):
        forward(came_z[i], d, 1 - lo, 1 - hi)
    halves(came_pair[0], lo, 1 - hi)
    share, rest = [], []
    for low, w in ((lo, hi), (1 - lo, 1 - hi)):
        piece = x_buf.at[:, low, core, w]
        share.append(net.copy(piece, piece, other_core))
    start_all(share)
    for copy in cross_late[:2]:
        copy.wait_recv()
    out_across = out_y(across, out_all.at[across])
    across_up = inner_y(0, across, up_all.at[across], (1, 3))
    start_all(out_across + across_up)

    for copy in own_small + across_small:
        copy.wait_recv()
    meta_wait()
    at_first = core == 0
    both = heads_all[...].reshape(D, 384)
    parts = [jnp.where(at_first, both[:, 128 * p : 128 * p + HD], both[:, 128 * p + HD : 128 * (p + 1)]) for p in range(3)]
    w_ref[...] = jnp.concatenate(parts, axis=1)
    biases = smalls_all[lax.axis_index("seq") // 2]
    bias = [jnp.where(at_first, biases[k : k + 1, :HD], biases[k : k + 1, HD:]) for k in range(2)]
    b_ref[...] = jnp.broadcast_to(jnp.concatenate([bias[0], jnp.zeros((1, HD), F32), bias[1]], axis=1), (8, 3 * HD))

    def project(low, at_core, w):
        sides = dot(x_buf[:, low, at_core, w].reshape(4 * TB, D), w_ref[...]) + b_ref[:1, :]
        for at in range(4):
            b = at * 8 + low * 4 + at_core * 2 + w
            rows = pl.ds(aligned(b * TB, TB), TB)
            side = sides[at * TB : (at + 1) * TB]
            q8 = side[:, :HD].astype(BF).astype(F32) * 0.125
            hot = jnp.where(lax.broadcasted_iota(jnp.int32, (32, TB), 0) == meta_all[b, 0:1, :], 1.0, 0.0)
            lane = lax.broadcasted_iota(jnp.int32, (TB, HD), 1)
            ones3 = jnp.where(lane < 3, 1.0, 0.0)
            apart = (hot.T - 1.0) * MASKED
            key = side[:, HD : 2 * HD]
            value = side[:, 2 * HD :]
            q_ref[rows, :] = q8.astype(BF)
            ka_ref[rows, :] = jnp.concatenate([key, apart, ones3[:, :32]], axis=1).astype(BF)
            va_ref[rows, :] = jnp.concatenate([value, ones3], axis=1).astype(BF)
            qat_ref[:, rows] = jnp.concatenate([q8.T, hot, jnp.zeros((32, TB), F32)], axis=0).astype(BF)
            kt_ref[:, rows] = key.T.astype(BF)
            ones_row = jnp.where(lax.broadcasted_iota(jnp.int32, (16, TB), 0) == 0, 1.0, 0.0)
            vat_ref[:, rows] = jnp.concatenate([value.T, ones_row], axis=0).astype(BF)

    project(lo, core, hi)
    project(1 - lo, core, 1 - hi)
    for copy in half_z + [own_pair[1], came_pair[1]] + pair_late:
        copy.wait_recv()
    for low, w in ((1 - lo, hi), (lo, 1 - hi)):
        piece = x_buf.at[:, low, core, w]
        rest.append(net.copy(piece, piece, other_core))
    start_all(rest)
    for copy in share:
        copy.wait_recv()
    project(1 - lo, core, hi)
    project(lo, core, 1 - hi)
    project(lo, 1 - core, hi)
    project(1 - lo, 1 - core, 1 - hi)
    for copy in rest:
        copy.wait_recv()
    store = pltpu.make_async_copy(x_buf, x_seq, local.at[0])
    store.start()
    project(1 - lo, 1 - core, hi)
    project(lo, 1 - core, 1 - hi)
    meta_out[...] = meta_all[...]
    smalls_out[...] = smalls_all[...]

    wait_all(keep)
    for copy in own_y + across_y:
        copy.wait_recv()
    later, inner_wrap = [], []
    for m in range(2):
        piece = wholes[m].at[:, unit_rows(m, 3), columns_part(m, lo, 2)]
        later.append(net.copy(piece, piece, pair))
        for d in (1, 3, 2):
            piece = wholes[m].at[:, unit_rows(m, 0), columns_part(m, z, 4)]
            later.append(net.copy(piece, piece, along("z", d)))
    for d in range(4):
        piece = down_all.at[(y + d) % 4 * 2 + hi, unit_rows(1, 1, 2)]
        inner_wrap.append(net.copy(piece, piece, wrap))
    piece = out_all.at[:, half_rows(core)]
    share_out = net.copy(piece, piece, other_core)
    relay_up = relay_y(0, hi) + relay_y(0, 1 - hi)
    start_all(later)

    position = lax.axis_index("seq") * 2 + hi

    def result(b, recv_at):
        there = head_tile(context, position)
        return remote(blocks.at[b], there, back_send.at[b], back_recv.at[recv_at], (y, b // 2, b % 2))

    own_result = pltpu.make_async_copy(blocks.at[position], head_tile(context, position), back_local)

    @pl.loop(0, 4)
    def _(step):
        at = (step + z + 1) % 4
        columns = pl.ds(aligned(at * 1024, 1024), 1024)
        queries = qat_ref[:, columns]
        peak = jnp.full((1, 1024), -jnp.inf, F32)
        total = jnp.zeros((80, 1024), F32)
        for j in range(4):
            keys = slice(j * 1024, (j + 1) * 1024)
            logits = dot(ka_ref[keys, :], queries)
            new_peak = jnp.maximum(peak, jnp.max(logits, axis=0, keepdims=True))
            expos = jnp.exp(logits - new_peak).astype(BF)
            total = total * jnp.exp(peak - new_peak) + dot(vat_ref[:, keys], expos)
            peak = new_peak
        sums = total[HD : HD + 1]
        found = total[:HD] / sums
        wide_ref[:, columns] = found
        lse_ref[:, columns] = peak + jnp.log(sums)
        low = found.astype(BF)
        for j in range(8):
            b = at * 8 + j
            blocks[b] = low[:, j * TB : (j + 1) * TB]

            @pl.when(b != position)
            def _():
                result(b, position).start()

            @pl.when(b == position)
            def _():
                own_result.start()

        @pl.when(step == 0)
        def _():
            for copy in inner_down:
                copy.wait_recv()
            start_all(inner_wrap)

        @pl.when(step == 2)
        def _():
            for copy in out_own + out_across + inner_up + across_up:
                copy.wait_recv()
            start_all([share_out] + relay_up)

    store.wait()
    for copy in [swap] + own_pair + own_z + came_pair + came_z + half_z + pair_late + share + rest:
        copy.wait_send()
    for copy in cross_first + cross_early + cross_late + own_small + across_small + own_y + across_y + inner_down:
        copy.wait_send()
    for copy in out_own + out_across + inner_up + across_up:
        copy.wait_send()
    cross_late[2].wait_recv()
    wait_all([share_out] + relay_up + later + inner_wrap)

    @pl.loop(1, NB)
    def _(shift):
        b = (position + shift) % NB
        result(b, b).wait()

    own_result.wait()


def front(tokens, segments, flags, vectors, w_out, w_up, w_down, w_qkv):
    shape = jax.ShapeDtypeStruct
    in_vmem = pl.BlockSpec(memory_space=pltpu.VMEM)
    return pl.pallas_call(
        front_kernel,
        in_specs=[ANY] + [in_vmem] * 11 + [ANY] * 4,
        out_specs=[ANY] + [in_vmem] * 2 + [ANY] * 4 + [in_vmem] * 5 + [ANY] + [in_vmem] * 2,
        out_shape=[
            shape((4, 2, 2, 2, TB, D), BF),
            shape((NB, 8, TB), jnp.int32),
            shape((8, 16, 128), F32),
            shape((8, 128, D), BF),
            shape((8, 128, 2048), BF),
            shape((8, 256, D), BF),
            shape((8, 128, 3 * D), BF),
            shape((128, L), BF),
            shape((L, 128), BF),
            shape((L, 128), BF),
            shape((HD, L), BF),
            shape((L, HD), BF),
            shape((D, 2 * TB), BF),
            shape((HD, L), F32),
            shape((1, L), F32),
        ],
        scratch_shapes=[
            pltpu.VMEM((80, L), BF),
            pltpu.VMEM((NB, HD, TB), BF),
            pltpu.VMEM((4, 2, 2, 2, TB, D), BF),
            pltpu.VMEM((2, TB, D), BF),
            pltpu.VMEM((128, D), BF),
            pltpu.VMEM((2, 128, 2048), BF),
            pltpu.VMEM((256, D), BF),
            pltpu.VMEM((128, 3 * D), BF),
            pltpu.VMEM((2, 8, TB), jnp.int32),
            pltpu.VMEM((2, 128, 384), BF),
            pltpu.VMEM((16, 128), F32),
            pltpu.VMEM((NB, 8, TB), jnp.int32),
            pltpu.VMEM((8, 128, 384), BF),
            pltpu.VMEM((8, 16, 128), F32),
            pltpu.VMEM((D, 3 * HD), BF),
            pltpu.VMEM((8, 3 * HD), F32),
            pltpu.SemaphoreType.DMA((FRONT_COPIES,)),
            pltpu.SemaphoreType.DMA((FRONT_COPIES,)),
            pltpu.SemaphoreType.DMA((12,)),
            *swap_sems(),
            *swap_sems(),
        ],
        name="front",
        compiler_params=pltpu.CompilerParams(
            collective_id=1, has_side_effects=True, vmem_limit_bytes=VMEM_CAP
        ),
    )(tokens, segments, flags, *vectors, w_out, w_up, w_down, w_qkv)


def qkv_along_y(qkv_all, net):
    _, y, _, core = place()
    copies = []
    for d in (1, 3, 2):
        for w in range(2):
            piece = qkv_all.at[y * 2 + w, half_rows(core)]
            copies.append(net.copy(piece, piece, along("y", d)))
    return copies


def turned(first, second):
    return dot(first, second, ((0,), (0,)))


def gelu_both(u):
    rate = 0.7978845608028654
    square = u * u
    curve = jnp.tanh(rate * (u + 0.044715 * (square * u)))
    half = 0.5 * (1.0 + curve)
    slope = half + 0.5 * u * (1.0 - curve * curve) * (rate * (1.0 + 0.134145 * square))
    return u * half, slope


def fold(values):
    return jnp.sum(values.reshape(values.shape[0] // 8, 8, values.shape[1]), axis=0)


ROWS = 256
CHUNK = 64
SMALLS = 16


def middle_kernel(
    context_in, meta, tokens, teacher, flags, smalls, out_all, up_all, down_all, a0,
    states, resid_out, do, g_ref, sums_out, count_out, qkv_all,
    context, context_s, w_out, w_up, w_down, h, act, slope, send_one, come_one, send_two, come_two,
    gb, gu, ga, ga_s, normed, hidden, rate, work, resid, gct, stage, count, counts, valid,
    send, recv, local, back_send, back_recv, back_local,
):
    x, y, z, core = place()
    mine = y * 2 + x // 2
    twin = sibling()
    loads = [
        pltpu.make_async_copy(context_in, context, local.at[6]),
        pltpu.make_async_copy(out_all, w_out, local.at[0]),
        pltpu.make_async_copy(up_all, w_up, local.at[1]),
    ]
    load_down = pltpu.make_async_copy(down_all, w_down, local.at[2])
    start_all(loads + [load_down])
    greet_signal(shard_greet())
    greet_wait(shard_greet())
    net = Transfers(send, recv)
    later = qkv_along_y(qkv_all, net)
    valid_here = jnp.sum(meta[:, 1, :].astype(F32), axis=0, keepdims=True)
    count[...] = jnp.broadcast_to(jnp.sum(valid_here, axis=1, keepdims=True), (8, 128))
    ahead = [net.copy(count, counts.at[mine], target) for target in shard_greet()]
    start_all(ahead + later)
    own_count = pltpu.make_async_copy(count, counts.at[mine], local.at[3])
    own_count.start()
    for s in range(2):
        column = jnp.broadcast_to(flags[s : s + 1, :].astype(F32), (128, 128)).T
        valid[128 * s : 128 * (s + 1), :] = column

    def vector(row):
        return jnp.concatenate([smalls[i, row : row + 1, :] for i in range(8)], axis=1)

    out_bias, gain_one, offset_one, down_bias, gain_two, offset_two = [vector(row) for row in range(2, 8)]
    zeros = jnp.zeros((8, D), F32)
    wait_all(loads)
    give_context = net.copy(context, context_s, twin)
    give_context.start()
    work[...] = turned(context[...], w_out[...].reshape(D, D))

    @pl.loop(0, ROWS // CHUNK)
    def _(i):
        rows = pl.ds(aligned(i * CHUNK, CHUNK), CHUNK)
        total = tokens[rows, :].astype(F32) + work[rows, :] + out_bias
        centre = total - jnp.mean(total, axis=1, keepdims=True)
        scale = lax.rsqrt(jnp.mean(centre * centre, axis=1, keepdims=True) + EPS)
        unit = centre * scale
        normed[rows, :] = unit
        rate[rows, :] = jnp.broadcast_to(scale, (CHUNK, 128))
        full = unit * gain_one + offset_one
        hidden[rows, :] = full
        h[0, rows, :] = full.astype(BF)

    give_hidden = net.copy(h.at[0], h.at[1], twin)
    give_hidden.start()
    for slot in range(2):
        if slot == 1:
            give_hidden.wait()
        for k in range(8):
            columns = slice(256 * k, 256 * (k + 1))
            bias = jnp.concatenate([smalls[k, pl.ds(8 + 2 * core + e, 1), :] for e in range(2)], axis=1)
            u = dot(h[slot], w_up[:, :, columns].reshape(D, 256)) + bias
            value, incline = gelu_both(u)
            act[slot, :, columns] = value.astype(BF)
            slope[slot, :, columns] = incline
    load_down.wait()
    send_one[...] = dot(act[1], w_down[...].reshape(2048, D))
    give_one = net.copy(send_one, come_one, twin)
    give_one.start()
    work[...] = dot(act[0], w_down[...].reshape(2048, D))
    give_one.wait()
    wait_all(ahead)
    own_count.wait()
    total_count = jnp.sum(counts[...], axis=0)
    count_out[...] = total_count
    factor = (128 * ROWS) / total_count[:1, :1]

    def loss_rows(i, carried):
        rows = pl.ds(aligned(i * CHUNK, CHUNK), CHUNK)
        total = hidden[rows, :] + (work[rows, :] + come_one[rows, :] + down_bias)
        centre = total - jnp.mean(total, axis=1, keepdims=True)
        scale = lax.rsqrt(jnp.mean(centre * centre, axis=1, keepdims=True) + EPS)
        unit = centre * scale
        final = unit * gain_two + offset_two
        states[rows, :] = final.astype(BF)
        differ = final - teacher[rows, :].astype(F32)
        held = valid[rows, :1] * differ
        grad = factor * held
        weighted = grad * gain_two
        back = weighted - jnp.mean(weighted, axis=1, keepdims=True)
        back = scale * (back - unit * jnp.mean(weighted * unit, axis=1, keepdims=True))
        resid[rows, :] = back
        low = back.astype(BF)
        gb[0, rows, :] = low
        return (
            carried[0] + fold(grad * unit),
            carried[1] + fold(grad),
            carried[2] + fold(low.astype(F32)),
            carried[3] + fold(held * differ),
        )

    gain_two_sum, offset_two_sum, down_sum, error = lax.fori_loop(
        0, ROWS // CHUNK, loss_rows, (zeros, zeros, zeros, zeros)
    )
    give_branch = net.copy(gb.at[0], gb.at[1], twin)
    give_branch.start()
    up_sums = []
    for slot in range(2):
        if slot == 1:
            give_branch.wait()
        for k in range(8):
            columns = slice(256 * k, 256 * (k + 1))
            pulled = dot(gb[slot], w_down[k], ((1,), (1,))) * slope[slot, :, columns]
            low = pulled.astype(BF)
            gu[slot, :, columns] = low
            up_sums.append(fold(low.astype(F32)))
    for i in range(8):
        send_two[:, 128 * i : 128 * (i + 1)] = dot(gu[1], w_up[i], ((1,), (1,)))
    give_two = net.copy(send_two, come_two, twin)
    give_two.start()
    for i in range(8):
        work[:, 128 * i : 128 * (i + 1)] = dot(gu[0], w_up[i], ((1,), (1,)))
    give_two.wait()

    def first_norm_rows(i, carried):
        rows = pl.ds(aligned(i * CHUNK, CHUNK), CHUNK)
        grad = resid[rows, :] + (work[rows, :] + come_two[rows, :])
        unit = normed[rows, :]
        weighted = grad * gain_one
        back = weighted - jnp.mean(weighted, axis=1, keepdims=True)
        back = rate[rows, :1] * (back - unit * jnp.mean(weighted * unit, axis=1, keepdims=True))
        resid_out[rows, :] = back
        low = back.astype(BF)
        ga[rows, :] = low
        return (carried[0] + fold(grad * unit), carried[1] + fold(grad), carried[2] + fold(low.astype(F32)))

    gain_one_sum, offset_one_sum, out_sum = lax.fori_loop(0, ROWS // CHUNK, first_norm_rows, (zeros, zeros, zeros))
    give_attended = net.copy(ga.at[:, pl.ds(aligned((1 - core) * 512, 512), 512)], ga_s, twin)
    give_attended.start()
    gct[...] = dot(w_out[...].reshape(D, D), ga[...], ((1,), (1,))).astype(BF)
    back_start, back_wait = swap_copies(
        lambda b: head_tile(gct, b), lambda b: do.at[b], (back_send, back_recv, back_local)
    )
    back_start()

    error = jnp.broadcast_to(jnp.sum(jnp.sum(error, axis=0, keepdims=True), axis=1, keepdims=True), (1, 128))
    lines = [out_sum, gain_one_sum, offset_one_sum, down_sum, gain_two_sum, offset_two_sum]
    lines = [jnp.sum(line, axis=0, keepdims=True) for line in lines]
    for i in range(8):
        columns = slice(128 * i, 128 * (i + 1))
        sums_out[i] = jnp.zeros((SMALLS, 128), F32)
        for row, line in enumerate(lines):
            sums_out[i, row : row + 1, :] = line[:, columns]
        both = jnp.sum(up_sums[i] + up_sums[8 + i], axis=0, keepdims=True)
        for e in range(2):
            sums_out[i, pl.ds(6 + 2 * core + e, 1), :] = both[:, 128 * e : 128 * (e + 1)]
        sums_out[i, 10:11, :] = error

    give_context.wait()
    give_attended.wait()

    def stored(i):
        return pltpu.make_async_copy(stage.at[i % 2], g_ref.at[i // 2, i % 2], local.at[4 + i % 2])

    for i in range(8):
        if i >= 2:
            stored(i - 2).wait()
        tall = slice(128 * i, 128 * (i + 1))
        wide = slice(256 * i, 256 * (i + 1))
        up = turned(h[0, :, tall], gu[0]) + turned(h[1, :, tall], gu[1])
        for k in range(4):
            stage[i % 2, 128 * k : 128 * (k + 1), :] = up[:, 512 * k : 512 * (k + 1)].astype(BF)
        down = turned(act[0, :, wide], gb[0]) + turned(act[1, :, wide], gb[1])
        for k in range(2):
            stage[i % 2, 512 + 256 * k : 768 + 256 * k, :] = down[:, 512 * k : 512 * (k + 1)].astype(BF)
        own_half = ga[:, pl.ds(aligned(core * 512, 512), 512)]
        out = dot(context[tall, :], own_half) + dot(context_s[tall, :], ga_s[...])
        stage[i % 2, 1024:, :] = out.astype(BF)
        stored(i).start()
    stored(6).wait()
    stored(7).wait()
    back_wait()
    wait_all(later)


def middle(context, meta, tokens, teacher, flags, smalls, out_all, up_all, down_all, qkv_all):
    shape = jax.ShapeDtypeStruct
    in_vmem = pl.BlockSpec(memory_space=pltpu.VMEM)
    dma = pltpu.SemaphoreType.DMA
    wide = pltpu.VMEM((ROWS, D), F32)
    return pl.pallas_call(
        middle_kernel,
        in_specs=[ANY] + [in_vmem] * 5 + [ANY] * 4,
        out_specs=[in_vmem, in_vmem, ANY, ANY, in_vmem, in_vmem, ANY],
        out_shape=[
            shape((ROWS, D), BF),
            shape((ROWS, D), F32),
            shape((NB, HD, TB), BF),
            shape((4, 2, 1152, 512), BF),
            shape((8, SMALLS, 128), F32),
            shape((8, 128), F32),
            shape(qkv_all.shape, BF),
        ],
        input_output_aliases={9: 6},
        scratch_shapes=[
            pltpu.VMEM((D, ROWS), BF),
            pltpu.VMEM((D, ROWS), BF),
            pltpu.VMEM((8, 128, D), BF),
            pltpu.VMEM((8, 128, 2048), BF),
            pltpu.VMEM((8, 256, D), BF),
            pltpu.VMEM((2, ROWS, D), BF),
            pltpu.VMEM((2, ROWS, 2048), BF),
            pltpu.VMEM((2, ROWS, 2048), F32),
            wide,
            wide,
            wide,
            wide,
            pltpu.VMEM((2, ROWS, D), BF),
            pltpu.VMEM((2, ROWS, 2048), BF),
            pltpu.VMEM((ROWS, D), BF),
            pltpu.VMEM((ROWS, 512), BF),
            wide,
            wide,
            pltpu.VMEM((ROWS, 128), F32),
            wide,
            wide,
            pltpu.VMEM((D, ROWS), BF),
            pltpu.VMEM((2, 1152, 512), BF),
            pltpu.VMEM((8, 128), F32),
            pltpu.VMEM((8, 8, 128), F32),
            pltpu.VMEM((ROWS, 128), F32),
            dma((32,)),
            dma((32,)),
            dma((10,)),
            *swap_sems(),
        ],
        name="middle",
        compiler_params=pltpu.CompilerParams(
            collective_id=3, has_side_effects=True, vmem_limit_bytes=VMEM_CAP
        ),
    )(context, meta, tokens, teacher, flags, smalls, out_all, up_all, down_all, qkv_all)


BACK_KEYS = 256
BACK_STEPS = L // BACK_KEYS
BACK_WIDTH = 1024


def back_prepare(qat, do, wide, lse, queries, grads, grad_rows):
    for j in range(L // BACK_WIDTH):
        columns = slice(j * BACK_WIDTH, (j + 1) * BACK_WIDTH)
        grad_t = jnp.concatenate([do[j * (BACK_WIDTH // TB) + i] for i in range(BACK_WIDTH // TB)], axis=1)
        wider = grad_t.astype(F32)
        delta = jnp.sum(wider * wide[:, columns], axis=0, keepdims=True)
        grads[:HD, columns] = grad_t
        grads[HD:, columns] = jnp.concatenate([three_pieces(-delta), jnp.zeros((61, BACK_WIDTH), BF)], axis=0)
        queries[:96, columns] = qat[:96, columns]
        queries[96:, columns] = jnp.concatenate(
            [three_pieces(-lse[:, columns]), jnp.zeros((29, BACK_WIDTH), BF)], axis=0
        )
        grad_rows[columns, :] = wider.T.astype(BF)


def back_kernel(
    qat_in, ka_in, va_in, kt_in, q8_in, do_in, wide_in, lse, smalls, x_seq, g_ref, a0,
    projected, heads_out, shard_out, smalls_out, qkv_all,
    qat, ka, va, kt, q8, do, wide, input_sems,
    x_buf, queries, grads, grad_rows, dq, d_ref, mine_ref, parts_ref, sum_ref, heads_buf, small_buf, small_sum, small_all,
    send, recv, local, dk_send, dk_recv, dk_local, dq_send, dq_recv, dq_local, spread_send, spread_recv, *reduce_refs,
):
    x, y, z, core = place()
    shard_at = y * 2 + x // 2
    seq = lax.axis_index("seq")
    mine = seq * 2 + x // 2
    net = (g_ref,) + reduce_refs

    def shard_device(d):
        other = (shard_at + d) % 8
        return other, (other // 2, seq, other % 2)

    load_x = pltpu.make_async_copy(x_seq, x_buf, local.at[0])
    held = (qat, do, wide, ka, va, kt, q8)
    loads = [
        pltpu.make_async_copy(src, dst, input_sems.at[k])
        for k, (src, dst) in enumerate(zip((qat_in, do_in, wide_in, ka_in, va_in, kt_in, q8_in), held))
    ]
    shard_others = [shard_device(d)[1] for d in range(1, 8)]
    greet_signal(shard_others)
    start_all(loads)
    dq[...] = jnp.zeros_like(dq)
    greet_wait(shard_others)
    for part in range(3):
        reduce_start(part, net)
    wait_all(loads)
    load_x.start()
    back_prepare(qat, do, wide, lse, queries, grads, grad_rows)
    far = Transfers(send, recv)
    small_out = [far.copy(smalls.at[shard_device(d)[0]], small_buf.at[shard_at], shard_device(d)[1]) for d in range(1, 8)]
    start_all(small_out)
    small_buf[shard_at] = smalls[shard_at]
    rows = half_rows(core)
    weights = far.copy(qkv_all.at[:, rows], qkv_all.at[:, rows], sibling())
    weights.start()

    def landing(first, count):
        return projected.at[pl.ds(first, count), pl.ds(aligned(seq * HD, HD), HD), pl.ds(aligned((x // 2) * TB, TB), TB)]

    def block_device(b):
        return (y, b // 2, b % 2)

    def dk_copy(b, recv_at):
        return remote(d_ref.at[b, pl.ds(1, 2)], landing(1, 2), dk_send.at[b], dk_recv.at[recv_at], block_device(b))

    def dq_copy(b, recv_at):
        return remote(d_ref.at[b, pl.ds(0, 1)], landing(0, 1), dq_send.at[b], dq_recv.at[recv_at], block_device(b))

    dk_own = pltpu.make_async_copy(d_ref.at[mine, pl.ds(1, 2)], landing(1, 2), dk_local)
    dq_own = pltpu.make_async_copy(d_ref.at[mine, pl.ds(0, 1)], landing(0, 1), dq_local)

    steps = [
        spread_steps(part, reduce_refs[6 + part].at[0], (local.at[pl.ds(1, 3)], spread_send, spread_recv), shard_out)
        for part in range(3)
    ]

    @pl.loop(0, BACK_STEPS)
    def _(step):
        at = (step + seq) % BACK_STEPS
        keys = pl.ds(aligned(at * BACK_KEYS, BACK_KEYS), BACK_KEYS)
        ka_part, va_part, kt_part = ka[keys, :], va[keys, :], kt[:, keys]
        dk = jnp.zeros((BACK_KEYS, HD), F32)
        dv = jnp.zeros((BACK_KEYS, HD), F32)
        for j in range(L // BACK_WIDTH):
            columns = slice(j * BACK_WIDTH, (j + 1) * BACK_WIDTH)
            probs = jnp.exp(dot(ka_part, queries[:, columns]))
            raw = (probs * dot(va_part, grads[:, columns])).astype(BF)
            dv = dv + dot(probs.astype(BF), grad_rows[columns, :])
            dk = dk + dot(raw, q8[columns, :])
            dq[:, columns] += dot(kt_part, raw)
        dk_t, dv_t = dk.T.astype(BF), dv.T.astype(BF)
        for i in range(BACK_KEYS // TB):
            b = at * (BACK_KEYS // TB) + i
            d_ref[b, 1] = dk_t[:, i * TB : (i + 1) * TB]
            d_ref[b, 2] = dv_t[:, i * TB : (i + 1) * TB]

            @pl.when(b != mine)
            def _():
                dk_copy(b, mine).start()

            @pl.when(b == mine)
            def _():
                dk_own.start()

        @pl.when(step == 3)
        def _():
            for part in (1, 2, 0):
                first_relay(part, net)

        @pl.when(step == 8)
        def _():
            reduce_step(0, 1, net)

        @pl.when(step == 9)
        def _():
            reduce_step(0, 2, net)

        @pl.when(step == 10)
        def _():
            reduce_step(0, 0, net)

        @pl.when(step == 12)
        def _():
            reduce_step(1, 1, net)

        @pl.when(step == 14)
        def _():
            reduce_step(1, 2, net)
            reduce_step(2, 1, net)
            steps[1][0]()

    reduce_step(1, 0, net)
    for b in range(NB):
        d_ref[b, 0] = (dq[:, b * TB : (b + 1) * TB] * 0.125).astype(BF)

    load_x.wait()
    left = jnp.concatenate([d_ref[b].reshape(3 * HD, TB) for b in range(NB)], axis=1)
    sums = dot(jnp.ones((8, L), BF), left, ((1,), (1,)))
    gap = jnp.zeros((1, 128 - HD), F32)
    tail = jnp.concatenate(
        [
            jnp.concatenate([sums[:1, :HD], gap], axis=1),
            jnp.concatenate([sums[:1, 2 * HD :], gap], axis=1),
            jnp.zeros((14, 128), F32),
        ],
        axis=0,
    ).astype(BF)
    for i in range(4):
        total = dot(left, x_buf[:, :, 256 * i : 256 * (i + 1)].reshape(L, 256))
        for k in range(2):
            mine_ref[2 * i + k, : 3 * HD, :] = total[:, 128 * k : 128 * (k + 1)].astype(BF)
            mine_ref[2 * i + k, 3 * HD :, :] = tail
    part_out = [far.copy(mine_ref.at[shard_device(d)[0]], parts_ref.at[d], shard_device(d)[1]) for d in range(1, 8)]
    start_all(part_out)
    for part in (2, 0):
        reduce_step(2, part, net)
        steps[part][0]()

    @pl.loop(1, NB)
    def _(shift):
        dq_copy((mine + shift) % NB, mine).start()

    dq_own.start()
    wait_all(small_out)
    small_sum[...] = jnp.sum(small_buf[...], axis=0)
    wait_all(part_out)
    added = mine_ref[shard_at].astype(F32)
    for d in range(1, 8):
        added = added + parts_ref[d].astype(F32)
    sum_ref[...] = added.astype(BF)
    heads_buf[seq // 2, core] = sum_ref[...]
    small_all[seq // 2, core] = small_sum[...]
    head_out = []
    for d in range(1, 8):
        target = (y, (seq + 2 * d) % 16, x // 2)
        head_out.append(far.copy(sum_ref, heads_buf.at[seq // 2, core], target))
        head_out.append(far.copy(small_sum, small_all.at[seq // 2, core], target))
    start_all(head_out)
    for part in (1, 2, 0):
        steps[part][1]()
    wait_all(head_out)
    across = [
        far.copy(heads_buf.at[:, core], heads_buf.at[:, core], sibling()),
        far.copy(small_all.at[:, core], small_all.at[:, core], sibling()),
    ]
    start_all(across)
    shared = []
    for part in (1, 2, 0):
        steps[part][2]()
        piece = shard_out.at[core, pl.ds(FIRST[part], 8 * PIECE[part])]
        shared.append(far.copy(piece, piece, sibling()))
        shared[-1].start()

    @pl.loop(1, NB)
    def _(shift):
        b = (mine + shift) % NB
        dk_copy(b, b).wait()
        dq_copy(b, b).wait()

    dk_own.wait()
    dq_own.wait()
    weights.wait()
    wait_all(across)
    for i in range(8):
        heads_out[2 * i] = heads_buf[i, 0]
        heads_out[2 * i + 1] = heads_buf[i, 1]
    smalls_out[...] = jnp.sum(small_all[...].reshape(16, 16, 128), axis=0)
    wait_all(shared)


def back(qat, ka, va, kt, q8, do, wide, lse, smalls, x_seq, g, qkv_all):
    shape = jax.ShapeDtypeStruct
    in_vmem = pl.BlockSpec(memory_space=pltpu.VMEM)
    dma = pltpu.SemaphoreType.DMA
    return pl.pallas_call(
        back_kernel,
        in_specs=[ANY] * 7 + [in_vmem] * 2 + [ANY] * 3,
        out_specs=[ANY, in_vmem, ANY, in_vmem, ANY],
        out_shape=[
            shape((3, D, 2 * TB), BF),
            shape((H, 208, 128), BF),
            shape((2, 1152, 512), BF),
            shape((16, 128), F32),
            shape(qkv_all.shape, BF),
        ],
        input_output_aliases={11: 4},
        scratch_shapes=[
            pltpu.VMEM((128, L), BF),
            pltpu.VMEM((L, 128), BF),
            pltpu.VMEM((L, 128), BF),
            pltpu.VMEM((HD, L), BF),
            pltpu.VMEM((L, HD), BF),
            pltpu.VMEM((NB, HD, TB), BF),
            pltpu.VMEM((HD, L), F32),
            dma((7,)),
            pltpu.VMEM((NB, TB, D), BF),
            pltpu.VMEM((128, L), BF),
            pltpu.VMEM((128, L), BF),
            pltpu.VMEM((L, HD), BF),
            pltpu.VMEM((HD, L), F32),
            pltpu.VMEM((NB, 3, HD, TB), BF),
            pltpu.VMEM((8, 208, 128), BF),
            pltpu.VMEM((8, 208, 128), BF),
            pltpu.VMEM((208, 128), BF),
            pltpu.VMEM((8, 2, 208, 128), BF),
            pltpu.VMEM((8, 16, 128), F32),
            pltpu.VMEM((16, 128), F32),
            pltpu.VMEM((8, 2, 16, 128), F32),
            dma((40,)),
            dma((40,)),
            dma((4,)),
            *swap_sems(),
            *swap_sems(),
            dma((3, 8)),
            dma((3, 8)),
            *reduce_scratch(),
        ],
        name="attend_back",
        compiler_params=pltpu.CompilerParams(
            collective_id=4, has_side_effects=True, vmem_limit_bytes=VMEM_CAP
        ),
    )(qat, ka, va, kt, q8, do, wide, lse, smalls, x_seq, g, qkv_all)


def finish_kernel(
    projected, qkv_ref, resid_ref, heads_ref, up_ref, down_left, down_right, out_ref, smalls_ref, count_ref, states_ref,
    tokens_ref, grad_qkv, grad_out, grad_up, grad_down, states_out, loss_ref,
    q_bias, v_bias, o_bias, gain_one, bias_one, d_bias, gain_two, bias_two, u_bias,
):
    step = pl.program_id(0)

    @pl.when(step == 0)
    def _():
        x, y, _, _ = place()
        shard_at = y * 2 + x // 2
        for row, out in enumerate((q_bias, v_bias)):
            both = [heads_ref[shard_at * 2 + k, 3 * HD + row, :HD].astype(F32) for k in range(2)]
            out[...] = jnp.concatenate(both)
        for row, out in enumerate((o_bias, gain_one, bias_one, d_bias, gain_two, bias_two)):
            out[...] = smalls_ref[row, :]
        u_bias[...] = jnp.concatenate([smalls_ref[6 + k, :] for k in range(4)])
        loss_ref[...] = smalls_ref[10:11, :1] / (D * count_ref[:1, :1])
        for p in range(3):
            for pair in range(8):
                both = [heads_ref[2 * pair + k, p * HD : (p + 1) * HD, :].astype(F32) for k in range(2)]
                at = p * D + pair * 128
                grad_qkv[:, at : at + 128] = jnp.concatenate(both, axis=0).T

    states_out[...] = states_ref[...]
    tokens_ref[...] = resid_ref[...] + dot(qkv_ref[...], projected[...]).T
    for c in range(2):
        columns = slice(512 * c, 512 * (c + 1))
        for j in range(2):
            grad_up[:, 512 * j + 256 * c : 512 * j + 256 * (c + 1)] = up_ref[c, :, 256 * j : 256 * (j + 1)].astype(F32)
        grad_down[:, columns] = (down_left, down_right)[c][0].astype(F32)
        grad_out[:, columns] = out_ref[c].astype(F32)


def finish(projected, qkv, resid, heads, shard, smalls, count, states):
    shape = jax.ShapeDtypeStruct

    def whole(*dims):
        return pl.BlockSpec(dims, lambda i: (0,) * len(dims))

    part = pl.BlockSpec((2 * TB, 256), lambda i: (0, i))
    return pl.pallas_call(
        finish_kernel,
        grid=(4,),
        in_specs=[
            whole(3 * D, 2 * TB),
            pl.BlockSpec((256, 3 * D), lambda i: (i, 0)),
            part,
            whole(H, 208, 128),
            pl.BlockSpec((2, 128, 512), lambda i: (0, i, 0)),
            pl.BlockSpec((1, 128, 512), lambda i: (i // 2, 4 + i % 2, 0)),
            pl.BlockSpec((1, 128, 512), lambda i: (i // 2, 6 + i % 2, 0)),
            pl.BlockSpec((2, 32, 512), lambda i: (0, 32 + i, 0)),
            whole(16, 128),
            whole(8, 128),
            part,
        ],
        out_specs=[
            part,
            whole(128, 3 * D),
            pl.BlockSpec((32, D), lambda i: (i, 0)),
            pl.BlockSpec((128, 1024), lambda i: (0, i)),
            pl.BlockSpec((128, D), lambda i: (i, 0)),
            part,
            whole(1, 1),
        ]
        + [whole(128)] * 8
        + [whole(512)],
        out_shape=[
            shape((2 * TB, D), F32),
            shape((128, 3 * D), F32),
            shape((128, D), F32),
            shape((128, FF), F32),
            shape((512, D), F32),
            shape((2 * TB, D), BF),
            shape((1, 1), F32),
        ]
        + [shape((128,), F32)] * 8
        + [shape((512,), F32)],
        name="finish",
        compiler_params=pltpu.CompilerParams(vmem_limit_bytes=VMEM_CAP),
    )(projected, qkv, resid, heads, shard, shard, shard, shard, smalls, count, states)


def on_device(
    tokens,
    segments,
    valid_flags,
    teacher,
    w_qkv,
    b_query,
    b_value,
    w_out,
    b_out,
    ln1_gain,
    ln1_bias,
    w_up,
    b_up,
    w_down,
    b_down,
    ln2_gain,
    ln2_bias,
):
    seq_local, row_local, _ = tokens.shape
    token_rows = seq_local * row_local

    vectors = [b_query, b_value, b_out, ln1_gain, ln1_bias, b_down, ln2_gain, ln2_bias]
    vectors = [vector.reshape(1, 128) for vector in vectors] + [b_up]
    (
        x_seq, meta_all, smalls_all, out_all, up_all, down_all, qkv_all, qat, ka, va, kt, q8, context, wide, lse
    ) = front(
        tokens, segments, valid_flags, vectors, w_out, w_up, w_down, w_qkv
    )
    x_seq = x_seq.reshape(NB, TB, D)
    states, grad_resid_one, do, g, small_sums, count, qkv_all = middle(
        context,
        meta_all,
        tokens.reshape(token_rows, D),
        teacher.reshape(token_rows, D),
        valid_flags,
        smalls_all,
        out_all,
        up_all,
        down_all,
        qkv_all,
    )
    projected, heads_out, shard_out, small_out, qkv_all = back(
        qat, ka, va, kt, q8, do, wide, lse, small_sums, x_seq, g, qkv_all
    )
    (
        grad_tokens, grad_qkv, grad_out, grad_up, grad_down, states, mean_loss,
        q_bias, v_bias, o_bias, gain_one, bias_one, d_bias, gain_two, bias_two, u_bias,
    ) = finish(
        projected.reshape(3 * D, token_rows), qkv_all.reshape(D, 3 * D), grad_resid_one, heads_out, shard_out, small_out,
        count, states,
    )
    return (
        states.reshape(seq_local, row_local, D),
        mean_loss.reshape(()),
        grad_tokens.reshape(seq_local, row_local, D),
        grad_qkv,
        q_bias,
        v_bias,
        grad_out,
        o_bias,
        gain_one,
        bias_one,
        grad_up,
        u_bias,
        grad_down,
        d_bias,
        gain_two,
        bias_two,
    )


def solution(mesh):
    rows = P("dp", ("seq", "wshard"), None)
    flags = P("dp", ("seq", "wshard"))
    matrix = P(("dp", "wshard"), None)
    vector = P(("dp", "wshard"))
    return jax.shard_map(
        on_device,
        mesh=mesh,
        in_specs=(
            rows,
            flags,
            flags,
            rows,
            matrix,
            vector,
            vector,
            matrix,
            vector,
            vector,
            vector,
            matrix,
            vector,
            matrix,
            vector,
            vector,
            vector,
        ),
        out_specs=(
            rows,
            P(),
            rows,
            matrix,
            vector,
            vector,
            matrix,
            vector,
            vector,
            vector,
            matrix,
            vector,
            matrix,
            vector,
            vector,
            vector,
        ),
        check_vma=False,
    )
```
